128 devices in a mesh: seq: 2 (over x_lo), ctx: 16 (over x_hi, z, core), fsdp: 4 (over y).
Axes of the slice: x: 4 (x_hi: 2, x_lo: 2; x = x_hi * 2 + x_lo), y: 4, z: 4, core: 2. Of those that a mesh axis runs over, the one named last changes fastest.
Arguments:
- tokens: bfloat16 [8, 2048, 960], P(('seq', 'fsdp'), 'ctx'), may hold values from -6 to 6
- gain_attn: bfloat16 [960], P('fsdp'), may hold values from 0.099609375 to 1.8984375
- w_q: bfloat16 [960, 960], P('fsdp'), may hold values from -0.375 to 0.375
- w_kv: bfloat16 [960, 640], P('fsdp'), may hold values from -0.1875 to 0.1875
- w_o: bfloat16 [960, 960], P('fsdp'), may hold values from -0.75 to 0.75
- gain_mlp: bfloat16 [960], P('fsdp'), may hold values from 0.099609375 to 1.8984375
- w_gate_up: bfloat16 [960, 5120], P('fsdp'), may hold values from -0.1875 to 0.1875
- w_down: bfloat16 [2560, 960], P('fsdp'), may hold values from -0.125 to 0.125
- block_order: int32 [8, 32], P(('seq', 'fsdp')), may hold values from 0 to 31, as said below
- cotangent: bfloat16 [8, 2048, 960], P(('seq', 'fsdp'), 'ctx'), may hold values from -6 to 6
Outputs:
- activations: bfloat16 [8, 2048, 960], P(('seq', 'fsdp'), 'ctx')
- input_grad: float32 [8, 2048, 960], P(('seq', 'fsdp'), 'ctx')
- grad_gain_attn: float32 [960], P('fsdp')
- grad_w_q: float32 [960, 960], P('fsdp')
- grad_w_kv: float32 [960, 640], P('fsdp')
- grad_w_o: float32 [960, 960], P('fsdp')
- grad_gain_mlp: float32 [960], P('fsdp')
- grad_w_gate_up: float32 [960, 5120], P('fsdp')
- grad_w_down: float32 [2560, 960], P('fsdp')
The draws below stay inside these ranges and needn't reach their ends.
Inputs may be any that keep to these rules, and one draw needn't show every extreme that they name: `block_order`: each row is an order of the 32 causal blocks of its sequence; stored blocks 2 i and 2 i + 1 are causal blocks c and 31 - c for some c.
All inputs are finite; a program needn't handle non-finite values.
Results may differ from the reference program's by a relative error of at most 0.03.
Values may be sent and summed in bfloat16 or wider, within the bound.
No kernel may reach another device: no remote copies, remote signals or barrier semaphores. Data moves between devices by JAX's collectives and lax.ppermute only.
A program may use at most 128 MiB of HBM per device.

```python
import math
import jax
import jax.numpy as jnp
from jax import lax

D = 960
HEADS = 15
KV_HEADS = 5
HEAD = 64
FF = 2560
BLK = 64
NBLK = 32
L = 2048
SEQS = 8


def draw_block_order(key, part):
    pairs = NBLK // 2

    def one_row(row_key):
        first_key, second_key = jax.random.split(row_key)
        early = jax.random.permutation(first_key, pairs).astype(jnp.int32)
        flip = jax.random.randint(second_key, (pairs,), 0, 2, dtype=jnp.int32)
        front = jnp.where(flip == 1, NBLK - 1 - early, early)
        back = NBLK - 1 - front
        return jnp.stack([front, back], axis=1).reshape(NBLK).astype(jnp.int32)
    return jax.vmap(one_row)(jax.random.split(jax.random.fold_in(key, 11), SEQS))


def levels(stream_key, dims, pieces, smallest, top_value):
    gain = 1.0
    for dim, shards_of in pieces:
        steps = jax.random.uniform(jax.random.fold_in(jax.random.fold_in(stream_key, 6), dim), (shards_of,), jnp.float32, smallest / len(pieces), top_value / len(pieces))
        gain = gain * jnp.repeat(jnp.exp(steps), dims[dim] // shards_of).reshape((-1,) + (1,) * (len(dims) - 1 - dim))
    return gain


def gaussian(own_key, dims, deviation, limit, pieces=(), held_as=jnp.bfloat16):
    array = jax.random.normal(own_key, dims, jnp.float32) * deviation
    if len(pieces) > 0:
        array = levels(own_key, dims, pieces, -0.22, 0.18) * array
    return jnp.clip(array, min=-limit, max=limit).astype(held_as)


def setup_inputs(seed: int = 0) -> dict:
    key_list = jax.random.split(jax.random.key(seed), 11)
    tokens = gaussian(key_list[0], (SEQS, L, D), 1.0, 6.0, ((0, 8), (1, 16)))
    gain_attn = jnp.clip(1.0 + 0.18 * jax.random.normal(key_list[1], (D,), jnp.float32), 0.099609375, 1.8984375).astype(jnp.bfloat16)
    w_q = gaussian(key_list[2], (D, HEADS * HEAD), (D // 4) ** -0.5, 0.375, ((0, 4),))
    w_kv = gaussian(key_list[3], (D, 2 * KV_HEADS * HEAD), D ** -0.5, 0.1875, ((0, 4),))
    w_o = gaussian(key_list[4], (HEADS * HEAD, D), (4 * HEADS) ** -0.5, 0.75, ((0, 4),))
    gain_mlp = jnp.clip(1.0 + 0.18 * jax.random.normal(key_list[5], (D,), jnp.float32), 0.099609375, 1.8984375).astype(jnp.bfloat16)
    w_gate_up = gaussian(key_list[6], (D, 2 * FF), D ** -0.5, 0.1875, ((0, 4),))
    w_down = gaussian(key_list[7], (FF, D), FF ** -0.5, 0.125, ((0, 4),))
    block_order = draw_block_order(jax.random.fold_in(key_list[10], 71), 0)
    cotangent = gaussian(key_list[9], (SEQS, L, D), 1.0, 6.0, ((0, 8), (1, 16)))
    return {"tokens": tokens, "gain_attn": gain_attn, "w_q": w_q, "w_kv": w_kv, "w_o": w_o, "gain_mlp": gain_mlp, "w_gate_up": w_gate_up, "w_down": w_down, "block_order": block_order, "cotangent": cotangent}


EPS = 1e-05
THETA = 100000.0
HIGH = lax.Precision.HIGHEST

@jax.custom_vjp
def low(v):
    return lax.optimization_barrier(v.astype(jnp.bfloat16)).astype(jnp.float32)

@jax.custom_vjp
def low_back(v):
    return v

def low_keep(v):
    return (low(v), None)

def low_pass(kept, grad):
    return (grad,)

def back_keep(v):
    return (v, None)

def back_low(kept, grad):
    return (low(grad),)
low.defvjp(low_keep, low_pass)
low_back.defvjp(back_keep, back_low)

def tables(places):
    half = HEAD // 2
    freq = THETA ** (-(jnp.arange(half, dtype=jnp.float32) * 2.0 / HEAD))
    angle = places.astype(jnp.float32)[:, None] * freq[None, :]
    return (jnp.cos(angle)[:, None, :], jnp.sin(angle)[:, None, :])

def rotate(value, cosine, sine):
    half = HEAD // 2
    first, second = (value[..., :half], value[..., half:])
    return jnp.concatenate([first * cosine - second * sine, second * cosine + first * sine], axis=-1)

def layer(inputs, gain_attn, w_q, w_kv, w_o, gain_mlp, w_gate_up, w_down, places):
    length = inputs.shape[0]
    group = HEADS // KV_HEADS
    kv_width = KV_HEADS * HEAD
    scale = HEAD ** (-0.5)
    inv_one = lax.rsqrt(lax.optimization_barrier(jnp.mean(inputs * inputs, axis=-1, keepdims=True)) + EPS)
    normed = low(inputs * inv_one * gain_attn)
    cosine, sine = tables(places)
    queries = low(rotate(low_back(jnp.dot(normed, w_q, precision=HIGH)).reshape(length, HEADS, HEAD), cosine, sine))
    kv_lin = low_back(jnp.dot(normed, w_kv, precision=HIGH))
    keys = low(rotate(kv_lin[:, :kv_width].reshape(length, KV_HEADS, HEAD), cosine, sine))
    values = low(kv_lin[:, kv_width:].reshape(length, KV_HEADS, HEAD))
    keys_wide = jnp.repeat(keys, group, axis=1)
    values_wide = jnp.repeat(values, group, axis=1)
    row_block = math.gcd(length, 512)

    def attend(item):
        block, block_places = item
        scores = low_back(jnp.einsum('qhe,khe->hqk', block, keys_wide, precision=HIGH) * scale)
        allowed = places[None, None, :] <= block_places[None, :, None]
        scores = jnp.where(allowed, scores, -1e+30)
        row_max = lax.optimization_barrier(jnp.max(scores, axis=-1, keepdims=True))
        expo = jnp.exp(scores - row_max)
        probs = low(expo / lax.optimization_barrier(jnp.sum(expo, axis=-1, keepdims=True)))
        return low_back(low(jnp.einsum('hqk,khe->qhe', probs, values_wide, precision=HIGH)))
    mixed = lax.map(jax.checkpoint(attend), (queries.reshape(length // row_block, row_block, HEADS, HEAD), places.reshape(length // row_block, row_block)))
    mixed = mixed.reshape(length, HEADS * HEAD)
    resid = inputs + low_back(jnp.dot(mixed, w_o, precision=HIGH))
    inv_two = lax.rsqrt(lax.optimization_barrier(jnp.mean(resid * resid, axis=-1, keepdims=True)) + EPS)
    normed_two = low(resid * inv_two * gain_mlp)
    gate_up = low_back(jnp.dot(normed_two, w_gate_up, precision=HIGH))
    hidden = low(jax.nn.silu(gate_up[:, :FF]) * gate_up[:, FF:])
    return resid + low_back(jnp.dot(hidden, w_down, precision=HIGH))

def reference(tokens, gain_attn, w_q, w_kv, w_o, gain_mlp, w_gate_up, w_down, block_order, cotangent):
    params = tuple((t.astype(jnp.float32) for t in (gain_attn, w_q, w_kv, w_o, gain_mlp, w_gate_up, w_down)))
    offsets = jnp.arange(BLK, dtype=jnp.int32)
    places = (block_order[:, :, None] * BLK + offsets[None, None, :]).reshape(block_order.shape[0], -1).astype(jnp.int32)

    def whole(inputs_all, *weights):

        def one(carry, item):
            return (carry, layer(item[0], *weights, item[1]))
        return lax.scan(one, jnp.zeros((), jnp.float32), (inputs_all, places))[1]
    outputs, pull = jax.vjp(whole, tokens.astype(jnp.float32), *params)
    grads = pull(cotangent.astype(jnp.float32))
    return (outputs.astype(jnp.bfloat16), grads[0], grads[1], grads[2], grads[3], grads[4], grads[5], grads[6], grads[7])
```

```python
import functools

import jax
import jax.numpy as jnp
from jax import lax
from jax.experimental import pallas as pl
from jax.experimental.pallas import tpu as pltpu
from jax.sharding import PartitionSpec as P

D = 960
HEADS = 15
KV_HEADS = 5
GROUP = 3
HEAD = 64
HALF = 32
FF = 2560
BLK = 64
L = 2048
CTX = 16
FS = 4
ROWS = 128
QKV = 1600
WIDE = 1664
SHARD = D // FS
FSL = FF // FS
TILE = 256
NT = L // TILE
EPS = 1e-05
THETA = 100000.0
SCALE = HEAD**-0.5
F32 = jnp.float32
BF16 = jnp.bfloat16
VMEM_BYTES = 56 * 1024 * 1024


def call(kernel, outs, args, smem=0, scratch=(), flops=0):
    specs = [pl.BlockSpec(memory_space=pltpu.SMEM)] * smem
    specs += [pl.BlockSpec(memory_space=pltpu.VMEM)] * (len(args) - smem)
    moved = sum(a.size * a.dtype.itemsize for a in list(args) + list(outs))
    return pl.pallas_call(
        kernel,
        out_shape=outs,
        in_specs=specs,
        out_specs=[pl.BlockSpec(memory_space=pltpu.VMEM)] * len(outs),
        scratch_shapes=list(scratch),
        cost_estimate=pl.CostEstimate(flops=flops, bytes_accessed=moved, transcendentals=0),
        compiler_params=pltpu.CompilerParams(vmem_limit_bytes=VMEM_BYTES),
    )(*args)


def shape(*dims, dtype=BF16):
    return jax.ShapeDtypeStruct(dims, dtype)


def dot(left, right, a=1, b=0):
    return lax.dot_general(left, right, (((a,), (b,)), ((), ())), preferred_element_type=F32)


def inv_norm(rows):
    return lax.rsqrt(jnp.mean(rows * rows, axis=-1, keepdims=True) + EPS)


def qkv_kernel(x_ref, w_ref, cos_ref, sin_ref, at_ref, out_ref, gains_ref):
    x = x_ref[...].astype(F32)
    gains = w_ref[:, WIDE - 128 : WIDE].astype(F32).T
    gains_ref[...] = gains[64:72, :]
    a = (x * inv_norm(x) * gains[64:65, :]).astype(BF16)
    at_ref[...] = a.astype(F32).T.astype(BF16)
    lin = dot(a, w_ref[...]).T
    cos = cos_ref[...]
    sin = sin_ref[...]

    def turned(base):
        first = lin[base : base + HALF]
        second = lin[base + HALF : base + HEAD]
        return jnp.concatenate(
            [first * cos - second * sin, second * cos + first * sin], axis=0
        ).astype(BF16)

    for j in range(KV_HEADS):
        key = turned(D + HEAD * j)
        value = lin[D + HEAD * (KV_HEADS + j) : D + HEAD * (KV_HEADS + j + 1)].astype(BF16)
        for g in range(GROUP):
            head = j * GROUP + g
            out_ref[head, 0:HEAD, :] = turned(HEAD * head)
            out_ref[head, HEAD : 2 * HEAD, :] = key
            out_ref[head, 2 * HEAD : 3 * HEAD, :] = value
    out_ref[HEADS, :, :] = jnp.zeros((3 * HEAD, ROWS), BF16)


def pick_pair(load, first, second):
    left = load(first // 2).astype(F32)
    right = load(second // 2).astype(F32)
    left = pltpu.roll(left, (first % 2) * BLK, 1)
    right = pltpu.roll(right, (1 - second % 2) * BLK, 1)
    lane = lax.broadcasted_iota(jnp.int32, left.shape, 1)
    return jnp.where(lane < BLK, left, right)


def causal(size):
    key = lax.broadcasted_iota(jnp.int32, (size, size), 0)
    query = lax.broadcasted_iota(jnp.int32, (size, size), 1)
    return key <= query


def attend_kernel(
    order_ref, inv_ref, recv_ref, out_ref, qt_ref, kt_ref, k_ref, vt_ref, of_ref, lse_ref, s_ref
):
    for m in range(CTX):
        got = pick_pair(lambda i: recv_ref[i], inv_ref[2 * m], inv_ref[2 * m + 1])
        at = slice(2 * BLK * m, 2 * BLK * (m + 1))
        qt_ref[:, at] = (got[0:HEAD] * SCALE).astype(BF16)
        key = got[HEAD : 2 * HEAD]
        kt_ref[:, at] = key.astype(BF16)
        k_ref[at, :] = key.T.astype(BF16)
        vt_ref[:, at] = got[2 * HEAD : 3 * HEAD].astype(BF16)
    allowed = causal(TILE)
    for n in range(NT):
        span = slice(TILE * n, TILE * (n + 1))
        query = qt_ref[:, span]
        top = None
        for c in range(n + 1):
            rows = slice(TILE * c, TILE * (c + 1))
            s = dot(k_ref[rows, :], query)
            if c == n:
                s = jnp.where(allowed, s, -1e30)
            s_ref[rows, :] = s
            part = jnp.max(s, axis=0, keepdims=True)
            top = part if top is None else jnp.maximum(top, part)
        total = None
        for c in range(n + 1):
            rows = slice(TILE * c, TILE * (c + 1))
            e = jnp.exp(s_ref[rows, :] - top)
            s_ref[rows, :] = e
            part = jnp.sum(e, axis=0, keepdims=True)
            total = part if total is None else total + part
        recip = 1.0 / total
        lse_ref[n] = jnp.broadcast_to(top + jnp.log(total), (8, TILE))
        prob = (s_ref[0 : TILE * (n + 1), :] * recip).astype(BF16)
        o = dot(vt_ref[:, 0 : TILE * (n + 1)], prob)
        of_ref[2 * n] = o[:, 0 : 2 * BLK]
        of_ref[2 * n + 1] = o[:, 2 * BLK :]
    for i in range(CTX):
        got = pick_pair(lambda g: of_ref[g], order_ref[2 * i], order_ref[2 * i + 1])
        out_ref[i] = got.astype(BF16)


def attend_back_kernel(
    order_ref,
    inv_ref,
    recv_ref,
    qt_ref,
    q_ref,
    kt_ref,
    k_ref,
    v_ref,
    of_ref,
    lse_ref,
    cos_ref,
    sin_ref,
    out_ref,
    dot_ref,
    do_ref,
    delta_ref,
    dk_ref,
    dv_ref,
    st_ref,
):
    for m in range(CTX):
        got = pick_pair(lambda i: recv_ref[i], inv_ref[2 * m], inv_ref[2 * m + 1])
        at = slice(2 * BLK * m, 2 * BLK * (m + 1))
        dot_ref[:, at] = got.astype(BF16)
        do_ref[at, :] = got.T.astype(BF16)
        delta_ref[:, at] = jnp.broadcast_to(
            jnp.sum(got * of_ref[m], axis=0, keepdims=True), (8, 2 * BLK)
        )
    allowed = causal(TILE)
    for n in range(NT):
        span = slice(TILE * n, TILE * (n + 1))
        query = qt_ref[:, span]
        out_grad = dot_ref[:, span]
        lse = lse_ref[n][0:1, :]
        delta = delta_ref[0:1, span]
        dq = None
        for c in range(n + 1):
            rows = slice(TILE * c, TILE * (c + 1))
            prob = jnp.exp(dot(k_ref[rows, :], query) - lse)
            if c == n:
                prob = jnp.where(allowed, prob, 0.0)
            ds = (prob * (dot(v_ref[rows, :], out_grad) - delta)).astype(BF16)
            part = dot(kt_ref[:, rows], ds)
            dq = part if dq is None else dq + part
            dk = dot(ds, q_ref[span, :])
            dv = dot(prob.astype(BF16), do_ref[span, :])
            if c == n:
                dk_ref[rows, :] = dk
                dv_ref[rows, :] = dv
            else:
                dk_ref[rows, :] += dk
                dv_ref[rows, :] += dv
        st_ref[2 * n, 0:HEAD, :] = dq[:, 0 : 2 * BLK] * SCALE
        st_ref[2 * n + 1, 0:HEAD, :] = dq[:, 2 * BLK :] * SCALE
    for m in range(CTX):
        at = slice(2 * BLK * m, 2 * BLK * (m + 1))
        cos = cos_ref[:, at]
        sin = sin_ref[:, at]

        def turned(value):
            first = value[0:HALF]
            second = value[HALF:HEAD]
            return jnp.concatenate(
                [first * cos + second * sin, second * cos - first * sin], axis=0
            )

        st_ref[m, 0:HEAD, :] = turned(st_ref[m, 0:HEAD, :])
        st_ref[m, HEAD : 2 * HEAD, :] = turned(dk_ref[at, :].T)
        st_ref[m, 2 * HEAD : 3 * HEAD, :] = dv_ref[at, :].T
    for i in range(CTX):
        got = pick_pair(lambda g: st_ref[g], order_ref[2 * i], order_ref[2 * i + 1])
        out_ref[i] = got.astype(BF16)


def resid_kernel(ot_ref, w_ref, x_ref, gains_ref, h_ref, b_ref, flat_ref):
    flat = jnp.concatenate([ot_ref[h] for h in range(HEADS)], axis=0)
    flat_ref[...] = flat
    mixed = flat.astype(F32).T.astype(BF16)
    h = x_ref[...].astype(F32) + dot(mixed, w_ref[...])
    h_ref[...] = h
    b_ref[...] = (h * inv_norm(h) * gains_ref[1:2, :]).astype(BF16)


def mlp_kernel(b_ref, g_ref, gu_ref, down_ref, y_ref, db_ref, mm_ref, dgu_ref):
    tokens = b_ref.shape[0] * ROWS
    for s in range(FS):
        b = b_ref[s]
        g = g_ref[s]
        gu = dot(b, gu_ref[...])
        gate = gu[:, :FSL]
        up = gu[:, FSL:]
        sig = 1.0 / (1.0 + jnp.exp(-gate))
        act = gate * sig
        mm = (act * up).astype(BF16)
        dm = dot(g, down_ref[...], 1, 1)
        dgate = dm * up * sig * (1.0 + gate * (1.0 - sig))
        dgu = jnp.concatenate([dgate, dm * act], axis=1).astype(BF16)
        rows = slice(ROWS * s, ROWS * (s + 1))
        mm_ref[rows, :] = mm
        dgu_ref[rows, :] = dgu
        db_ref[s] = dot(dgu, gu_ref[...], 1, 1).astype(BF16)
        y_ref[s] = dot(mm, down_ref[...]).astype(BF16)


def mlp_grad_kernel(b_ref, g_ref, mm_ref, dgu_ref, dgu_w_ref, dd_w_ref):
    b = b_ref[...].reshape(FS * ROWS, D)
    dgu_w_ref[...] = dot(b, dgu_ref[...], 0, 0).astype(BF16)
    dd_w_ref[...] = dot(mm_ref[...], g_ref[...].reshape(FS * ROWS, D), 0, 0).astype(BF16)


def mid_kernel(db0, db1, db2, db3, h_ref, g_ref, gains_ref, w_ref, dh_ref, e_ref, do_ref, dg_ref):
    db = db0[...].astype(F32) + db1[...].astype(F32) + db2[...].astype(F32) + db3[...].astype(F32)
    h = h_ref[...]
    r2 = inv_norm(h)
    dg_ref[...] = jnp.broadcast_to(jnp.sum(db * h * r2, axis=0, keepdims=True), (8, D))
    scaled = gains_ref[1:2, :] * db
    dh = (
        g_ref[...].astype(F32)
        + r2 * scaled
        - h * (r2 * r2 * r2) * jnp.mean(scaled * h, axis=-1, keepdims=True)
    )
    dh_ref[...] = dh
    e = dh.astype(BF16)
    e_ref[...] = e
    back = dot(w_ref[...], e, 1, 1).astype(BF16)
    for head in range(HEADS):
        do_ref[head] = back[HEAD * head : HEAD * (head + 1)]
    do_ref[HEADS] = jnp.zeros((HEAD, ROWS), BF16)


def out_grad_kernel(ot_ref, e_ref, out_ref):
    total = dot(ot_ref[0], e_ref[0])
    for f in range(1, FS):
        total += dot(ot_ref[f], e_ref[f])
    out_ref[...] = total.astype(BF16)


def last_kernel(recv_ref, w_ref, x_ref, dh_ref, gains_ref, dg2_ref, ig_ref, msg_ref):
    for head in range(HEADS):
        msg_ref[HEAD * head : HEAD * (head + 1), :] = recv_ref[head, 0:HEAD, :]
    for part in range(2):
        for j in range(KV_HEADS):
            total = None
            for g in range(GROUP):
                piece = recv_ref[j * GROUP + g, HEAD * (part + 1) : HEAD * (part + 2), :]
                piece = piece.astype(F32)
                total = piece if total is None else total + piece
            base = D + HEAD * (KV_HEADS * part + j)
            msg_ref[base : base + HEAD, :] = total.astype(BF16)
    da = dot(w_ref[:, 0:QKV], msg_ref[0:QKV, :]).T
    x = x_ref[...].astype(F32)
    r1 = inv_norm(x)
    dg1 = jnp.sum(da * x * r1, axis=0, keepdims=True)
    scaled = gains_ref[0:1, :] * da
    ig_ref[...] = (
        dh_ref[...]
        + r1 * scaled
        - x * (r1 * r1 * r1) * jnp.mean(scaled * x, axis=-1, keepdims=True)
    )
    pad = jnp.zeros((1, 1024 - D), F32)
    rows = []
    for row in (dg1, dg2_ref[0:1, :]):
        full = jnp.concatenate([row, pad], axis=1)
        rows += [full[:, 128 * i : 128 * (i + 1)] for i in range(8)]
    msg_ref[QKV : QKV + 16, :] = jnp.concatenate(rows, axis=0).astype(BF16)


def qkv_grad_kernel(at_ref, d_ref, out_ref):
    total = dot(at_ref[0], d_ref[0, 0:QKV, :], 1, 1)
    gains = d_ref[0, QKV : QKV + 16, :].astype(F32)
    for f in range(1, FS):
        total += dot(at_ref[f], d_ref[f, 0:QKV, :], 1, 1)
        gains += d_ref[f, QKV : QKV + 16, :].astype(F32)
    out_ref[0:SHARD, 0:QKV] = total.astype(BF16)
    out_ref[0:SHARD, QKV:WIDE] = jnp.zeros((SHARD, WIDE - QKV), BF16)
    rows = []
    for part in range(2):
        row = [gains[8 * part + i : 8 * part + i + 1, :] for i in range(8)]
        rows.append(jnp.concatenate(row + [jnp.zeros((1, WIDE - 1024), F32)], axis=1))
    rows.append(jnp.zeros((14, WIDE), F32))
    out_ref[SHARD : SHARD + 16, :] = jnp.concatenate(rows, axis=0).astype(BF16)


def swap_core(value):
    return lax.ppermute(value, "ctx", [(i, i ^ 1) for i in range(CTX)])


def shift(value, step):
    return lax.ppermute(value, "fsdp", [((i + step) % FS, i) for i in range(FS)])


def to_all(value, axis, count):
    return lax.all_to_all(jnp.broadcast_to(value[None], (count,) + value.shape), axis, 0, 0)


def gather_weights(shard):
    core = lax.axis_index("ctx") % 2
    half = shard.shape[0] // 2
    mine = to_all(lax.dynamic_slice_in_dim(shard, core * half, half, 0), "fsdp", FS)
    other = swap_core(mine)
    low = jnp.where(core == 0, mine, other)
    high = jnp.where(core == 0, other, mine)
    return jnp.concatenate([low, high], axis=1).reshape((2 * FS * half,) + shard.shape[1:])


def gather_rolled(value):
    return jnp.stack([value] + [shift(value, s) for s in range(1, FS)])


def scatter_rolled(pieces):
    return [pieces[0]] + [shift(pieces[s], -s) for s in range(1, FS)]


def shards(tokens, gain_attn, w_q, w_kv, w_o, gain_mlp, w_gate_up, w_down, block_order, cotangent):
    x = tokens[0]
    g_own = cotangent[0]
    order = block_order[0]
    place = lax.axis_index("ctx")
    fs = lax.axis_index("fsdp")

    slots = jnp.arange(2 * CTX, dtype=jnp.int32)
    inverse = jnp.sum(jnp.where(order[None, :] == slots[:, None], slots[None, :], 0), axis=1)
    mine = lax.dynamic_slice_in_dim(order, place * 2, 2)
    places = (mine[:, None] * BLK + jnp.arange(BLK, dtype=jnp.int32)[None, :]).reshape(ROWS)
    freq = THETA ** (-(jnp.arange(HALF, dtype=F32) * 2.0 / HEAD))
    angle = freq[:, None] * places.astype(F32)[None, :]
    angle_all = freq[:, None] * jnp.arange(L, dtype=F32)[None, :]

    message = jnp.concatenate(
        [w_q, w_kv, gain_attn[:, None], gain_mlp[:, None], jnp.zeros((SHARD, 62), BF16)], axis=1
    )
    w_qkv = gather_weights(message)
    w_out = lax.all_gather(w_o, "fsdp", axis=0, tiled=True)
    chunks = w_gate_up.reshape(SHARD, 2, FS, FSL).transpose(2, 0, 1, 3).reshape(FS, SHARD, 2 * FSL)
    chunks = jnp.roll(chunks, -fs, axis=0)
    pieces = scatter_rolled([chunks[s] for s in range(FS)])
    w_gu = jnp.roll(
        jnp.stack([pieces[0], pieces[3], pieces[2], pieces[1]]), fs, axis=0
    ).reshape(D, 2 * FSL)
    g_all = gather_rolled(g_own)

    a_t, packed, gains = call(
        qkv_kernel,
        [shape(D, ROWS), shape(CTX, 3 * HEAD, ROWS), shape(8, D, dtype=F32)],
        [x, w_qkv, jnp.cos(angle), jnp.sin(angle)],
        flops=2 * ROWS * D * QKV,
    )
    received = lax.all_to_all(packed, "ctx", 0, 0)
    o_part, q_t, k_t, k_n, v_t, o_f, lse = call(
        attend_kernel,
        [
            shape(CTX, HEAD, ROWS),
            shape(HEAD, L),
            shape(HEAD, L),
            shape(L, HEAD),
            shape(HEAD, L),
            shape(CTX, HEAD, ROWS, dtype=F32),
            shape(NT, 8, TILE, dtype=F32),
        ],
        [order, inverse, received],
        smem=2,
        scratch=[pltpu.VMEM((L, TILE), F32)],
        flops=2 * L * L * HEAD,
    )
    o_all = lax.all_to_all(o_part, "ctx", 0, 0)
    h, b, o_flat = call(
        resid_kernel,
        [shape(ROWS, D, dtype=F32), shape(ROWS, D), shape(D, ROWS)],
        [o_all, w_out, x, gains],
        flops=2 * ROWS * D * D,
    )
    a_all = lax.all_gather(a_t, "fsdp", axis=0)
    o_flat_all = lax.all_gather(o_flat, "fsdp", axis=0)
    b_all = gather_rolled(b)
    y_part, db_part, mm, dgu = call(
        mlp_kernel,
        [shape(FS, ROWS, D), shape(FS, ROWS, D), shape(FS * ROWS, FSL), shape(FS * ROWS, 2 * FSL)],
        [b_all, g_all, w_gu, w_down],
        flops=12 * FS * ROWS * D * FSL,
    )
    db = scatter_rolled([db_part[s] for s in range(FS)])
    y = scatter_rolled([y_part[s] for s in range(FS)])
    gu_grad, down_grad = call(
        mlp_grad_kernel,
        [shape(D, 2 * FSL), shape(FSL, D)],
        [b_all, g_all, mm, dgu],
        flops=6 * FS * ROWS * D * FSL,
    )
    dh, e, do_part, dgain_two = call(
        mid_kernel,
        [
            shape(ROWS, D, dtype=F32),
            shape(ROWS, D),
            shape(CTX, HEAD, ROWS),
            shape(8, D, dtype=F32),
        ],
        [db[0], db[1], db[2], db[3], h, g_own, gains, w_out],
        flops=2 * ROWS * D * D,
    )
    do_all = lax.all_to_all(do_part, "ctx", 0, 0)
    e_all = lax.all_gather(e, "fsdp", axis=0)
    result = h
    for piece in y:
        result = result + piece.astype(F32)
    (dqkv_part,) = call(
        attend_back_kernel,
        [shape(CTX, 3 * HEAD, ROWS)],
        [
            order,
            inverse,
            do_all,
            q_t,
            q_t.T,
            k_t,
            k_n,
            v_t.T,
            o_f,
            lse,
            jnp.cos(angle_all),
            jnp.sin(angle_all),
        ],
        smem=2,
        scratch=[
            pltpu.VMEM((HEAD, L), BF16),
            pltpu.VMEM((L, HEAD), BF16),
            pltpu.VMEM((8, L), F32),
            pltpu.VMEM((L, HEAD), F32),
            pltpu.VMEM((L, HEAD), F32),
            pltpu.VMEM((CTX, 3 * HEAD, ROWS), F32),
        ],
        flops=5 * L * L * HEAD,
    )
    gu_grad = lax.all_to_all(gu_grad.reshape(FS, SHARD, 2 * FSL), "fsdp", 0, 0)
    (o_grad,) = call(
        out_grad_kernel,
        [shape(SHARD, D)],
        [lax.dynamic_slice_in_dim(o_flat_all, fs * SHARD, SHARD, 1), e_all],
        flops=2 * FS * ROWS * SHARD * D,
    )
    gu_sum, down_sum, o_sum = (
        lax.psum(part, ("seq", "ctx")) for part in (gu_grad, down_grad, o_grad)
    )

    dqkv = lax.all_to_all(dqkv_part, "ctx", 0, 0)
    input_grad, low = call(
        last_kernel,
        [shape(ROWS, D, dtype=F32), shape(QKV + 16, ROWS)],
        [dqkv, w_qkv, x, dh, gains, dgain_two],
        flops=2 * ROWS * D * QKV,
    )
    low_all = to_all(low, "fsdp", FS)
    (grads,) = call(
        qkv_grad_kernel,
        [shape(SHARD + 16, WIDE)],
        [lax.dynamic_slice_in_dim(a_all, fs * SHARD, SHARD, 1), low_all],
        flops=2 * FS * ROWS * SHARD * QKV,
    )
    parts = lax.all_to_all(grads.reshape(32, 8, WIDE), ("seq", "ctx"), 0, 0)
    summed = jnp.sum(parts.astype(F32), axis=0).astype(BF16)
    grads = to_all(summed, ("seq", "ctx"), 32).reshape(SHARD + 16, WIDE).astype(F32)
    own_gains = lax.dynamic_slice(grads, (SHARD, fs * SHARD), (2, SHARD))
    gu_out = gu_sum.reshape(FS, SHARD, 2, FSL).transpose(1, 2, 0, 3).reshape(SHARD, 2 * FF)
    return (
        result.astype(BF16)[None],
        input_grad[None],
        own_gains[0],
        grads[:SHARD, :D],
        grads[:SHARD, D:QKV],
        o_sum.astype(F32),
        own_gains[1],
        gu_out.astype(F32),
        down_sum.astype(F32),
    )


def solution(mesh):
    tokens = P(("seq", "fsdp"), "ctx", None)
    return jax.shard_map(
        shards,
        mesh=mesh,
        in_specs=(
            tokens,
            P("fsdp"),
            P("fsdp", None),
            P("fsdp", None),
            P("fsdp", None),
            P("fsdp"),
            P("fsdp", None),
            P("fsdp", None),
            P(("seq", "fsdp"), None),
            tokens,
        ),
        out_specs=(
            tokens,
            tokens,
            P("fsdp"),
            P("fsdp", None),
            P("fsdp", None),
            P("fsdp", None),
            P("fsdp"),
            P("fsdp", None),
            P("fsdp", None),
        ),
        check_vma=False,
    )
```

```python
import jax
import jax.numpy as jnp
from jax import lax
from jax.experimental import pallas as pl
from jax.experimental.pallas import tpu as pltpu
from jax.sharding import PartitionSpec as P

D = 960
HEADS = 15
KV_HEADS = 5
GROUP = 3
HEAD = 64
HALF = 32
FF = 2560
BLK = 64
L = 2048
CTX = 16
FS = 4
ROWS = 128
QKV = 1600
WIDE = 1664
HALFW = 896
KVW = 640
TAIL = 2688
HALF_ROWS = D + D // 2
SHARD = D // FS
FSL = FF // FS
TILE = 256
NT = L // TILE
EPS = 1e-05
THETA = 100000.0
SCALE = HEAD**-0.5
F32 = jnp.float32
BF16 = jnp.bfloat16
VMEM_BYTES = 56 * 1024 * 1024


def call(kernel, outs, args, smem=0, scratch=(), flops=0):
    specs = [pl.BlockSpec(memory_space=pltpu.SMEM)] * smem
    specs += [pl.BlockSpec(memory_space=pltpu.VMEM)] * (len(args) - smem)
    moved = sum(a.size * a.dtype.itemsize for a in list(args) + list(outs))
    return pl.pallas_call(
        kernel,
        out_shape=outs,
        in_specs=specs,
        out_specs=[pl.BlockSpec(memory_space=pltpu.VMEM)] * len(outs),
        scratch_shapes=list(scratch),
        cost_estimate=pl.CostEstimate(flops=flops, bytes_accessed=moved, transcendentals=0),
        compiler_params=pltpu.CompilerParams(vmem_limit_bytes=VMEM_BYTES),
    )(*args)


def shape(*dims, dtype=BF16):
    return jax.ShapeDtypeStruct(dims, dtype)


def dot(left, right, a=1, b=0):
    return lax.dot_general(left, right, (((a,), (b,)), ((), ())), preferred_element_type=F32)


def inv_norm(rows):
    return lax.rsqrt(jnp.mean(rows * rows, axis=-1, keepdims=True) + EPS)


def message_kernel(ids_ref, wq_ref, wkv_ref, g1_ref, g2_ref, out_ref):
    core = ids_ref[1]

    @pl.when(core == 0)
    def _():
        out_ref[...] = wq_ref[:, 0:HALFW]

    @pl.when(core == 1)
    def _():
        out_ref[:, 0:KVW] = wkv_ref[...]
        one = jnp.broadcast_to(g1_ref[...].astype(F32), (128, SHARD)).T
        two = jnp.broadcast_to(g2_ref[...].astype(F32), (128, SHARD)).T
        lane = lax.broadcasted_iota(jnp.int32, (SHARD, 128), 1)
        rest = wq_ref[:, HALFW:D].astype(F32)
        rest = jnp.concatenate([rest, jnp.zeros((SHARD, 64), F32)], axis=1)
        rest = jnp.where(lane == 64, one, jnp.where(lane == 65, two, rest))
        out_ref[:, KVW : KVW + 128] = rest.astype(BF16)
        out_ref[:, KVW + 128 : HALFW] = jnp.zeros((SHARD, HALFW - KVW - 128), BF16)


def chunk_kernel(ids_ref, gu_ref, *out_refs):
    fs = ids_ref[0]
    for s in range(FS):
        at = pl.multiple_of(lax.rem(fs + s, FS) * FSL, 128)
        out_refs[s][:, 0:FSL] = gu_ref[:, pl.ds(at, FSL)]
        out_refs[s][:, FSL : 2 * FSL] = gu_ref[:, pl.ds(FF + at, FSL)]


def place_kernel(ids_ref, p0, p1, p2, p3, out_ref):
    fs = ids_ref[0]
    for s, piece in enumerate((p0, p1, p2, p3)):
        at = pl.multiple_of(lax.rem(fs + FS - s, FS) * SHARD, 16)
        out_ref[pl.ds(at, SHARD), :] = piece[...]


def qkv_kernel(ids_ref, x_ref, *refs):
    mine = refs[0:FS]
    other = refs[FS : 2 * FS]
    cos_ref, sin_ref = refs[2 * FS : 2 * FS + 2]
    out_ref, gains_ref, wa_ref, wb_ref = refs[2 * FS + 2 : 2 * FS + 6]
    at_refs = refs[2 * FS + 6 : 3 * FS + 6]
    full_ref = refs[3 * FS + 6]
    fs = ids_ref[0]
    core = ids_ref[1]

    def fill(first, second):
        for s in range(FS):
            at = pl.multiple_of(lax.rem(fs + s, FS) * SHARD, 16)
            wa_ref[pl.ds(at, SHARD), :] = first[s][...]
            wb_ref[pl.ds(at, SHARD), :] = second[s][...]

    @pl.when(core == 0)
    def _():
        fill(mine, other)

    @pl.when(core == 1)
    def _():
        fill(other, mine)

    x = x_ref[...].astype(F32)
    gains = wb_ref[:, KVW : KVW + 128].astype(F32).T
    gains_ref[...] = gains[64:72, :]
    a = (x * inv_norm(x) * gains[64:65, :]).astype(BF16)
    full_ref[...] = a.astype(F32).T.astype(BF16)
    for s in range(FS):
        at = pl.multiple_of(lax.rem(fs + s, FS) * SHARD, 16)
        at_refs[s][...] = full_ref[pl.ds(at, SHARD), :]
    lin_a = dot(a, wa_ref[...]).T
    lin_b = dot(a, wb_ref[...]).T
    cos = cos_ref[...]
    sin = sin_ref[...]

    def turned(rows):
        first = rows[0:HALF]
        second = rows[HALF:HEAD]
        return jnp.concatenate(
            [first * cos - second * sin, second * cos + first * sin], axis=0
        ).astype(BF16)

    for j in range(KV_HEADS):
        key = turned(lin_b[HEAD * j : HEAD * (j + 1)])
        value = lin_b[HEAD * (KV_HEADS + j) : HEAD * (KV_HEADS + j + 1)].astype(BF16)
        for g in range(GROUP):
            head = j * GROUP + g
            if head < HEADS - 1:
                rows = lin_a[HEAD * head : HEAD * (head + 1)]
            else:
                rows = lin_b[KVW : KVW + HEAD]
            out_ref[head, 0:HEAD, :] = turned(rows)
            out_ref[head, HEAD : 2 * HEAD, :] = key
            out_ref[head, 2 * HEAD : 3 * HEAD, :] = value
    out_ref[HEADS, :, :] = jnp.zeros((3 * HEAD, ROWS), BF16)


def pick_pair(load, first, second):
    left = load(first // 2).astype(F32)
    right = load(second // 2).astype(F32)
    left = pltpu.roll(left, (first % 2) * BLK, 1)
    right = pltpu.roll(right, (1 - second % 2) * BLK, 1)
    lane = lax.broadcasted_iota(jnp.int32, left.shape, 1)
    return jnp.where(lane < BLK, left, right)


def causal(size):
    key = lax.broadcasted_iota(jnp.int32, (size, size), 0)
    query = lax.broadcasted_iota(jnp.int32, (size, size), 1)
    return key <= query


def attend_kernel(
    order_ref, inv_ref, recv_ref, out_ref, qt_ref, kt_ref, k_ref, vt_ref, of_ref, lse_ref, s_ref
):
    for m in range(CTX):
        got = pick_pair(lambda i: recv_ref[i], inv_ref[2 * m], inv_ref[2 * m + 1])
        at = slice(2 * BLK * m, 2 * BLK * (m + 1))
        qt_ref[:, at] = (got[0:HEAD] * SCALE).astype(BF16)
        key = got[HEAD : 2 * HEAD]
        kt_ref[:, at] = key.astype(BF16)
        k_ref[at, :] = key.T.astype(BF16)
        vt_ref[:, at] = got[2 * HEAD : 3 * HEAD].astype(BF16)
    allowed = causal(TILE)
    for n in range(NT):
        span = slice(TILE * n, TILE * (n + 1))
        query = qt_ref[:, span]
        top = None
        for c in range(n + 1):
            rows = slice(TILE * c, TILE * (c + 1))
            s = dot(k_ref[rows, :], query)
            if c == n:
                s = jnp.where(allowed, s, -1e30)
            s_ref[rows, :] = s
            part = jnp.max(s, axis=0, keepdims=True)
            top = part if top is None else jnp.maximum(top, part)
        total = None
        for c in range(n + 1):
            rows = slice(TILE * c, TILE * (c + 1))
            e = jnp.exp(s_ref[rows, :] - top)
            s_ref[rows, :] = e
            part = jnp.sum(e, axis=0, keepdims=True)
            total = part if total is None else total + part
        recip = 1.0 / total
        lse_ref[n] = jnp.broadcast_to(top + jnp.log(total), (8, TILE))
        prob = (s_ref[0 : TILE * (n + 1), :] * recip).astype(BF16)
        o = dot(vt_ref[:, 0 : TILE * (n + 1)], prob)
        of_ref[2 * n] = o[:, 0 : 2 * BLK]
        of_ref[2 * n + 1] = o[:, 2 * BLK :]
    for i in range(CTX):
        got = pick_pair(lambda g: of_ref[g], order_ref[2 * i], order_ref[2 * i + 1])
        out_ref[i] = got.astype(BF16)


def attend_back_kernel(
    order_ref,
    inv_ref,
    recv_ref,
    qt_ref,
    q_ref,
    kt_ref,
    k_ref,
    v_ref,
    of_ref,
    lse_ref,
    cos_ref,
    sin_ref,
    out_ref,
    dot_ref,
    do_ref,
    delta_ref,
    dk_ref,
    dv_ref,
    st_ref,
):
    for m in range(CTX):
        got = pick_pair(lambda i: recv_ref[i], inv_ref[2 * m], inv_ref[2 * m + 1])
        at = slice(2 * BLK * m, 2 * BLK * (m + 1))
        dot_ref[:, at] = got.astype(BF16)
        do_ref[at, :] = got.T.astype(BF16)
        delta_ref[:, at] = jnp.broadcast_to(
            jnp.sum(got * of_ref[m], axis=0, keepdims=True), (8, 2 * BLK)
        )
    allowed = causal(TILE)
    for n in range(NT):
        span = slice(TILE * n, TILE * (n + 1))
        query = qt_ref[:, span]
        out_grad = dot_ref[:, span]
        lse = lse_ref[n][0:1, :]
        delta = delta_ref[0:1, span]
        dq = None
        for c in range(n + 1):
            rows = slice(TILE * c, TILE * (c + 1))
            prob = jnp.exp(dot(k_ref[rows, :], query) - lse)
            if c == n:
                prob = jnp.where(allowed, prob, 0.0)
            ds = (prob * (dot(v_ref[rows, :], out_grad) - delta)).astype(BF16)
            part = dot(kt_ref[:, rows], ds)
            dq = part if dq is None else dq + part
            dk = dot(ds, q_ref[span, :])
            dv = dot(prob.astype(BF16), do_ref[span, :])
            if c == n:
                dk_ref[rows, :] = dk
                dv_ref[rows, :] = dv
            else:
                dk_ref[rows, :] += dk
                dv_ref[rows, :] += dv
        st_ref[2 * n, 0:HEAD, :] = dq[:, 0 : 2 * BLK] * SCALE
        st_ref[2 * n + 1, 0:HEAD, :] = dq[:, 2 * BLK :] * SCALE
    for m in range(CTX):
        at = slice(2 * BLK * m, 2 * BLK * (m + 1))
        cos = cos_ref[:, at]
        sin = sin_ref[:, at]

        def turned(value):
            first = value[0:HALF]
            second = value[HALF:HEAD]
            return jnp.concatenate(
                [first * cos + second * sin, second * cos - first * sin], axis=0
            )

        st_ref[m, 0:HEAD, :] = turned(st_ref[m, 0:HEAD, :])
        st_ref[m, HEAD : 2 * HEAD, :] = turned(dk_ref[at, :].T)
        st_ref[m, 2 * HEAD : 3 * HEAD, :] = dv_ref[at, :].T
    for i in range(CTX):
        got = pick_pair(lambda g: st_ref[g], order_ref[2 * i], order_ref[2 * i + 1])
        out_ref[i] = got.astype(BF16)


def resid_kernel(ids_ref, ot_ref, w_ref, x_ref, gains_ref, h_ref, b_ref, *refs):
    full_ref = refs[FS]
    flat = jnp.concatenate([ot_ref[h] for h in range(HEADS)], axis=0)
    full_ref[...] = flat
    for s in range(FS):
        at = pl.multiple_of(lax.rem(ids_ref[0] + s, FS) * SHARD, 16)
        refs[s][...] = full_ref[pl.ds(at, SHARD), :]
    mixed = flat.astype(F32).T.astype(BF16)
    h = x_ref[...].astype(F32) + dot(mixed, w_ref[...])
    h_ref[...] = h
    b_ref[...] = (h * inv_norm(h) * gains_ref[1:2, :]).astype(BF16)


def mlp_kernel(*refs):
    b_refs = refs[0:FS]
    g_refs = refs[FS : 2 * FS]
    gu_ref, down_ref = refs[2 * FS : 2 * FS + 2]
    db_refs = refs[2 * FS + 2 : 3 * FS + 2]
    mm_ref, dgu_ref = refs[3 * FS + 2 :]
    for s in range(FS):
        gu = dot(b_refs[s][...], gu_ref[...])
        gate = gu[:, :FSL]
        up = gu[:, FSL:]
        sig = 1.0 / (1.0 + jnp.exp(-gate))
        act = gate * sig
        dm = dot(g_refs[s][...], down_ref[...], 1, 1)
        dgate = dm * up * sig * (1.0 + gate * (1.0 - sig))
        dgu = jnp.concatenate([dgate, dm * act], axis=1).astype(BF16)
        rows = slice(ROWS * s, ROWS * (s + 1))
        mm_ref[rows, :] = (act * up).astype(BF16)
        dgu_ref[rows, :] = dgu
        db_refs[s][...] = dot(dgu, gu_ref[...], 1, 1).astype(BF16)


def mlp_grad_kernel(ids_ref, *refs):
    b_refs = refs[0:FS]
    g_refs = refs[FS : 2 * FS]
    mm_ref, dgu_ref, down_ref = refs[2 * FS : 2 * FS + 3]
    y_refs = refs[2 * FS + 3 : 3 * FS + 3]
    keep_ref, give_ref, gu_ref, dd_ref = refs[3 * FS + 3 :]
    b = jnp.concatenate([r[...] for r in b_refs], axis=0)
    g = jnp.concatenate([r[...] for r in g_refs], axis=0)
    gu_ref[...] = dot(b, dgu_ref[...], 0, 0).astype(BF16)
    dd_ref[...] = dot(g, mm_ref[...], 0, 0).astype(BF16)

    def put(out_ref, half):
        out_ref[0:D, :] = gu_ref[:, FSL * half : FSL * (half + 1)]
        out_ref[D : D + D // 2, :] = dd_ref[D // 2 * half : D // 2 * (half + 1), :]

    for core in range(2):

        @pl.when(ids_ref[1] == core)
        def _(core=core):
            put(keep_ref, core)
            put(give_ref, 1 - core)

    for s in range(FS):
        y_refs[s][...] = dot(mm_ref[ROWS * s : ROWS * (s + 1), :], down_ref[...]).astype(BF16)


def pack_kernel(keep_ref, got_ref, out_ref, sum_ref):
    for at in range(0, HALF_ROWS, 240):
        rows = slice(at, at + 240)
        sum_ref[rows, :] = keep_ref[rows, :].astype(F32) + got_ref[rows, :].astype(F32)
    sum_ref[HALF_ROWS:, :] = jnp.zeros((16, FSL), F32)
    for r in range(CTX):
        for k in range(FS):
            at = SHARD * k + 15 * r
            out_ref[r, 16 * k : 16 * (k + 1), :] = sum_ref[at : at + 16, :].astype(BF16)
        at = D + 30 * r
        out_ref[r, 64:96, :] = sum_ref[at : at + 32, :].astype(BF16)


def reduce_kernel(ids_ref, parts_ref, p0, p1, p2, p3, rest_ref, sum_ref):
    total = parts_ref[0].astype(F32)
    for r in range(1, CTX):
        total += parts_ref[r].astype(F32)
    sum_ref[...] = total.astype(BF16)
    for s, piece in enumerate((p0, p1, p2, p3)):
        at = pl.multiple_of(lax.rem(ids_ref[0] + s, FS) * 16, 16)
        piece[...] = sum_ref[pl.ds(at, 16), :]
    rest_ref[...] = sum_ref[64:96, :]


def mid_kernel(db0, db1, db2, db3, h_ref, g_ref, gains_ref, w_ref, dh_ref, e_ref, do_ref, dg_ref):
    db = db0[...].astype(F32) + db1[...].astype(F32) + db2[...].astype(F32) + db3[...].astype(F32)
    h = h_ref[...]
    r2 = inv_norm(h)
    dg_ref[...] = jnp.broadcast_to(jnp.sum(db * h * r2, axis=0, keepdims=True), (8, D))
    scaled = gains_ref[1:2, :] * db
    dh = (
        g_ref[...].astype(F32)
        + r2 * scaled
        - h * (r2 * r2 * r2) * jnp.mean(scaled * h, axis=-1, keepdims=True)
    )
    dh_ref[...] = dh
    e = dh.astype(BF16)
    e_ref[...] = e
    back = dot(w_ref[...], e, 1, 1).astype(BF16)
    for head in range(HEADS):
        do_ref[head] = back[HEAD * head : HEAD * (head + 1)]
    do_ref[HEADS] = jnp.zeros((HEAD, ROWS), BF16)


def out_grad_kernel(*refs):
    total = None
    for s in range(FS):
        part = dot(refs[(FS - s) % FS][...], refs[FS + s][...])
        total = part if total is None else total + part
    refs[2 * FS][...] = total.astype(BF16)


def last_kernel(
    recv_ref, wa_ref, wb_ref, x_ref, dh_ref, gains_ref, dg2_ref, ig_ref, msg_ref
):
    for head in range(HEADS):
        msg_ref[HEAD * head : HEAD * (head + 1), :] = recv_ref[head, 0:HEAD, :]
    for part in range(2):
        for j in range(KV_HEADS):
            total = None
            for g in range(GROUP):
                piece = recv_ref[j * GROUP + g, HEAD * (part + 1) : HEAD * (part + 2), :]
                piece = piece.astype(F32)
                total = piece if total is None else total + piece
            base = D + HEAD * (KV_HEADS * part + j)
            msg_ref[base : base + HEAD, :] = total.astype(BF16)
    da = dot(wa_ref[...], msg_ref[0:HALFW, :])
    da += dot(wb_ref[:, 0:KVW], msg_ref[D:QKV, :])
    da += dot(wb_ref[:, KVW : KVW + HEAD], msg_ref[HALFW:D, :])
    da = da.T
    x = x_ref[...].astype(F32)
    r1 = inv_norm(x)
    dg1 = jnp.sum(da * x * r1, axis=0, keepdims=True)
    scaled = gains_ref[0:1, :] * da
    ig_ref[...] = (
        dh_ref[...]
        + r1 * scaled
        - x * (r1 * r1 * r1) * jnp.mean(scaled * x, axis=-1, keepdims=True)
    )
    pad = jnp.zeros((1, 1024 - D), F32)
    rows = []
    for row in (dg1, dg2_ref[0:1, :]):
        full = jnp.concatenate([row, pad], axis=1)
        rows += [full[:, 128 * i : 128 * (i + 1)] for i in range(8)]
    msg_ref[QKV : QKV + 16, :] = jnp.concatenate(rows, axis=0).astype(BF16)


def qkv_grad_kernel(ids_ref, *refs):
    o_ref, keep_ref, give_ref, full_ref = refs[2 * FS :]
    total = None
    gains = None
    for s in range(FS):
        d_ref = refs[FS + s]
        part = dot(refs[(FS - s) % FS][...], d_ref[0:QKV, :], 1, 1)
        total = part if total is None else total + part
        part = d_ref[QKV : QKV + 16, :].astype(F32)
        gains = part if gains is None else gains + part
    full_ref[0:SHARD, 0:QKV] = total.astype(BF16)
    full_ref[0:SHARD, QKV:WIDE] = jnp.zeros((SHARD, WIDE - QKV), BF16)
    full_ref[0:SHARD, WIDE : WIDE + D] = o_ref[...]
    full_ref[0:SHARD, WIDE + D : TAIL] = jnp.zeros((SHARD, TAIL - WIDE - D), BF16)
    rows = []
    for part in range(2):
        row = [gains[8 * part + i : 8 * part + i + 1, :] for i in range(8)]
        rows.append(jnp.concatenate(row + [jnp.zeros((1, TAIL - 1024), F32)], axis=1))
    rows.append(jnp.zeros((14, TAIL), F32))
    full_ref[SHARD : SHARD + 16, :] = jnp.concatenate(rows, axis=0).astype(BF16)
    core = ids_ref[1]
    keep_ref[...] = full_ref[pl.ds(pl.multiple_of(core * 128, 128), 128), :]
    give_ref[...] = full_ref[pl.ds(pl.multiple_of((1 - core) * 128, 128), 128), :]


def unpack_kernel(ids_ref, mine_ref, other_ref, q_ref, kv_ref, o_ref, gain_ref, full_ref):
    core = ids_ref[1]
    full_ref[pl.ds(pl.multiple_of(core * 128, 128), 128), :] = mine_ref[...]
    full_ref[pl.ds(pl.multiple_of((1 - core) * 128, 128), 128), :] = other_ref[...]
    q_ref[...] = full_ref[0:SHARD, 0:D].astype(F32)
    kv_ref[...] = full_ref[0:SHARD, D:QKV].astype(F32)
    o_ref[...] = full_ref[0:SHARD, WIDE : WIDE + D].astype(F32)
    rows = full_ref[SHARD : SHARD + 16, 0:1024].astype(F32)
    rows = pltpu.roll(rows, lax.rem(1024 - ids_ref[0] * SHARD, 1024), 1)
    gain_ref[...] = rows[0:8, 0:SHARD]


def widen_kernel(ids_ref, mine_ref, other_ref, gu_out, down_out):
    for core in range(2):

        @pl.when(ids_ref[1] == core)
        def _(core=core):
            halves = (mine_ref, other_ref) if core == 0 else (other_ref, mine_ref)
            down = []
            for half, src in enumerate(halves):
                for s in range(FS):
                    at = lax.rem(ids_ref[0] + FS - s, FS) * FSL + FF * half
                    at = pl.multiple_of(at, 128)
                    rows = [
                        src[r, 16 * s : 16 * (s + 1), :].astype(F32)[0:15] for r in range(CTX)
                    ]
                    gu_out[:, pl.ds(at, FSL)] = jnp.concatenate(rows, axis=0)
                down += [src[r, 64:96, :].astype(F32)[0:30] for r in range(CTX)]
            down_out[...] = jnp.concatenate(down, axis=0).T


def swap_core(value):
    return lax.ppermute(value, "ctx", [(i, i ^ 1) for i in range(CTX)])


def shift(value, step):
    return lax.ppermute(value, "fsdp", [((i + step) % FS, i) for i in range(FS)])


def same_core(value):
    groups = [[2 * i + core for i in range(CTX)] for core in range(2)]
    return lax.all_to_all(value, ("seq", "ctx"), 0, 0, axis_index_groups=groups)


def gather_rolled(value):
    return [value] + [shift(value, s) for s in range(1, FS)]


def scatter_rolled(pieces):
    return [pieces[0]] + [shift(pieces[s], -s) for s in range(1, FS)]


def shards(tokens, gain_attn, w_q, w_kv, w_o, gain_mlp, w_gate_up, w_down, block_order, cotangent):
    x = tokens[0]
    g_own = cotangent[0]
    order = block_order[0]
    place = lax.axis_index("ctx")
    ids = jnp.stack([lax.axis_index("fsdp"), place % 2]).astype(jnp.int32)

    slots = jnp.arange(2 * CTX, dtype=jnp.int32)
    inverse = jnp.sum(jnp.where(order[None, :] == slots[:, None], slots[None, :], 0), axis=1)
    mine = lax.dynamic_slice_in_dim(order, place * 2, 2)
    places = (mine[:, None] * BLK + jnp.arange(BLK, dtype=jnp.int32)[None, :]).reshape(ROWS)
    freq = THETA ** (-(jnp.arange(HALF, dtype=F32) * 2.0 / HEAD))
    angle = freq[:, None] * places.astype(F32)[None, :]
    angle_all = freq[:, None] * jnp.arange(L, dtype=F32)[None, :]

    (message,) = call(
        message_kernel,
        [shape(SHARD, HALFW)],
        [ids, w_q, w_kv, gain_attn[None], gain_mlp[None]],
        smem=1,
    )
    w_mine = gather_rolled(message)
    w_other = [swap_core(piece) for piece in w_mine]
    w_out = lax.all_gather(w_o, "fsdp", axis=0, tiled=True)
    chunks = call(chunk_kernel, [shape(SHARD, 2 * FSL)] * FS, [ids, w_gate_up], smem=1)
    (w_gu,) = call(
        place_kernel, [shape(D, 2 * FSL)], [ids] + scatter_rolled(chunks), smem=1
    )
    g_all = gather_rolled(g_own)

    packed, gains, w_a, w_b, *a_pieces = call(
        qkv_kernel,
        [
            shape(CTX, 3 * HEAD, ROWS),
            shape(8, D, dtype=F32),
            shape(D, HALFW),
            shape(D, HALFW),
        ]
        + [shape(SHARD, ROWS)] * FS,
        [ids, x] + w_mine + w_other + [jnp.cos(angle), jnp.sin(angle)],
        smem=1,
        scratch=[pltpu.VMEM((D, ROWS), BF16)],
        flops=2 * ROWS * D * QKV,
    )
    received = lax.all_to_all(packed, "ctx", 0, 0)
    o_part, q_t, k_t, k_n, v_t, o_f, lse = call(
        attend_kernel,
        [
            shape(CTX, HEAD, ROWS),
            shape(HEAD, L),
            shape(HEAD, L),
            shape(L, HEAD),
            shape(HEAD, L),
            shape(CTX, HEAD, ROWS, dtype=F32),
            shape(NT, 8, TILE, dtype=F32),
        ],
        [order, inverse, received],
        smem=2,
        scratch=[pltpu.VMEM((L, TILE), F32)],
        flops=2 * L * L * HEAD,
    )
    o_all = lax.all_to_all(o_part, "ctx", 0, 0)
    o_all, g_all, w_gu = lax.optimization_barrier((o_all, g_all, w_gu))
    h, b, *o_pieces = call(
        resid_kernel,
        [shape(ROWS, D, dtype=F32), shape(ROWS, D)] + [shape(SHARD, ROWS)] * FS,
        [ids, o_all, w_out, x, gains],
        smem=1,
        scratch=[pltpu.VMEM((D, ROWS), BF16)],
        flops=2 * ROWS * D * D,
    )
    b_all = gather_rolled(b)
    *db_parts, mm, dgu = call(
        mlp_kernel,
        [shape(ROWS, D)] * FS + [shape(FS * ROWS, FSL), shape(FS * ROWS, 2 * FSL)],
        b_all + g_all + [w_gu, w_down],
        flops=10 * FS * ROWS * D * FSL,
    )
    db = scatter_rolled(db_parts)
    *y_parts, keep, give = call(
        mlp_grad_kernel,
        [shape(ROWS, D)] * FS + [shape(HALF_ROWS, FSL)] * 2,
        [ids] + b_all + g_all + [mm, dgu, w_down],
        smem=1,
        scratch=[pltpu.VMEM((D, 2 * FSL), BF16), pltpu.VMEM((D, FSL), BF16)],
        flops=8 * FS * ROWS * D * FSL,
    )
    got = swap_core(give)
    db, keep = lax.optimization_barrier((db, keep))
    dh, e, do_part, dgain_two = call(
        mid_kernel,
        [
            shape(ROWS, D, dtype=F32),
            shape(ROWS, D),
            shape(CTX, HEAD, ROWS),
            shape(8, D, dtype=F32),
        ],
        db + [h, g_own, gains, w_out],
        flops=2 * ROWS * D * D,
    )
    do_all = lax.all_to_all(do_part, "ctx", 0, 0)
    (half_sum,) = call(
        pack_kernel,
        [shape(CTX, 96, FSL)],
        [keep, got],
        scratch=[pltpu.VMEM((HALF_ROWS + 16, FSL), F32)],
    )
    a_all = scatter_rolled(a_pieces)
    o_slices = scatter_rolled(o_pieces)
    do_all, half_sum, a_all, o_slices = lax.optimization_barrier(
        (do_all, half_sum, a_all, o_slices)
    )
    half_parts = same_core(half_sum)
    e_all = gather_rolled(e)
    y = scatter_rolled(y_parts)
    (dqkv_part,) = call(
        attend_back_kernel,
        [shape(CTX, 3 * HEAD, ROWS)],
        [
            order,
            inverse,
            do_all,
            q_t,
            q_t.T,
            k_t,
            k_n,
            v_t.T,
            o_f,
            lse,
            jnp.cos(angle_all),
            jnp.sin(angle_all),
        ],
        smem=2,
        scratch=[
            pltpu.VMEM((HEAD, L), BF16),
            pltpu.VMEM((L, HEAD), BF16),
            pltpu.VMEM((8, L), F32),
            pltpu.VMEM((L, HEAD), F32),
            pltpu.VMEM((L, HEAD), F32),
            pltpu.VMEM((CTX, 3 * HEAD, ROWS), F32),
        ],
        flops=5 * L * L * HEAD,
    )
    dqkv = lax.all_to_all(dqkv_part, "ctx", 0, 0)
    (o_grad,) = call(
        out_grad_kernel,
        [shape(SHARD, D)],
        o_slices + e_all,
        flops=2 * FS * ROWS * SHARD * D,
    )
    *pieces, down_sum = call(
        reduce_kernel,
        [shape(16, FSL)] * FS + [shape(32, FSL)],
        [ids, half_parts],
        smem=1,
        scratch=[pltpu.VMEM((96, FSL), BF16)],
    )
    dqkv, o_grad, pieces, y = lax.optimization_barrier((dqkv, o_grad, pieces, y))
    result = h
    for piece in y:
        result = result + piece.astype(F32)
    pieces = scatter_rolled(pieces)
    own = jnp.concatenate(pieces + [down_sum], axis=0)
    mine_all = same_core(jnp.broadcast_to(own[None], (CTX, 96, FSL)))
    input_grad, low = call(
        last_kernel,
        [shape(ROWS, D, dtype=F32), shape(QKV + 16, ROWS)],
        [dqkv, w_a, w_b, x, dh, gains, dgain_two],
        flops=2 * ROWS * D * QKV,
    )
    low_all = gather_rolled(low)
    low_all, mine_all = lax.optimization_barrier((low_all, mine_all))
    other_all = swap_core(mine_all)
    keep, give = call(
        qkv_grad_kernel,
        [shape(128, TAIL)] * 2,
        [ids] + a_all + low_all + [o_grad],
        smem=1,
        scratch=[pltpu.VMEM((SHARD + 16, TAIL), BF16)],
        flops=2 * FS * ROWS * SHARD * QKV,
    )
    half = (keep.astype(F32) + swap_core(give).astype(F32)).astype(BF16)
    parts = same_core(half.reshape(CTX, 8, TAIL))
    summed = jnp.sum(parts.astype(F32), axis=0).astype(BF16)
    mine_tail = same_core(jnp.broadcast_to(summed[None], (CTX, 8, TAIL))).reshape(128, TAIL)
    gu_out, down_out = call(
        widen_kernel,
        [shape(SHARD, 2 * FF, dtype=F32), shape(FSL, D, dtype=F32)],
        [ids, mine_all, other_all],
        smem=1,
    )
    q_out, kv_out, o_out, gain_out = call(
        unpack_kernel,
        [
            shape(SHARD, D, dtype=F32),
            shape(SHARD, KVW, dtype=F32),
            shape(SHARD, D, dtype=F32),
            shape(8, SHARD, dtype=F32),
        ],
        [ids, mine_tail, swap_core(mine_tail)],
        smem=1,
        scratch=[pltpu.VMEM((SHARD + 16, TAIL), BF16)],
    )
    return (
        result.astype(BF16)[None],
        input_grad[None],
        gain_out[0],
        q_out,
        kv_out,
        o_out,
        gain_out[1],
        gu_out,
        down_out,
    )


def solution(mesh):
    tokens = P(("seq", "fsdp"), "ctx", None)
    return jax.shard_map(
        shards,
        mesh=mesh,
        in_specs=(
            tokens,
            P("fsdp"),
            P("fsdp", None),
            P("fsdp", None),
            P("fsdp", None),
            P("fsdp"),
            P("fsdp", None),
            P("fsdp", None),
            P(("seq", "fsdp"), None),
            tokens,
        ),
        out_specs=(
            tokens,
            tokens,
            P("fsdp"),
            P("fsdp", None),
            P("fsdp", None),
            P("fsdp", None),
            P("fsdp"),
            P("fsdp", None),
            P("fsdp", None),
        ),
        check_vma=False,
    )
```

```python
import jax
import jax.numpy as jnp
from jax import lax
from jax.experimental import pallas as pl
from jax.experimental.pallas import tpu as pltpu
from jax.sharding import PartitionSpec as P

D = 960
HEADS = 15
KV_HEADS = 5
GROUP = 3
HEAD = 64
HALF = 32
FF = 2560
BLK = 64
L = 2048
CTX = 16
FS = 4
ROWS = 128
QKV = 1600
WIDE = 1664
HALFW = 896
KVW = 640
TAIL = 2688
HALF_ROWS = D + D // 2
SHARD = D // FS
FSL = FF // FS
TILE = 256
NT = L // TILE
EPS = 1e-05
THETA = 100000.0
SCALE = HEAD**-0.5
F32 = jnp.float32
BF16 = jnp.bfloat16
VMEM_BYTES = 56 * 1024 * 1024


def call(kernel, outs, args, smem=0, scratch=(), flops=0):
    specs = [pl.BlockSpec(memory_space=pltpu.SMEM)] * smem
    specs += [pl.BlockSpec(memory_space=pltpu.VMEM)] * (len(args) - smem)
    moved = sum(a.size * a.dtype.itemsize for a in list(args) + list(outs))
    return pl.pallas_call(
        kernel,
        out_shape=outs,
        in_specs=specs,
        out_specs=[pl.BlockSpec(memory_space=pltpu.VMEM)] * len(outs),
        scratch_shapes=list(scratch),
        cost_estimate=pl.CostEstimate(flops=flops, bytes_accessed=moved, transcendentals=0),
        compiler_params=pltpu.CompilerParams(vmem_limit_bytes=VMEM_BYTES),
    )(*args)


def shape(*dims, dtype=BF16):
    return jax.ShapeDtypeStruct(dims, dtype)


def dot(left, right, a=1, b=0):
    return lax.dot_general(left, right, (((a,), (b,)), ((), ())), preferred_element_type=F32)


def inv_norm(rows):
    return lax.rsqrt(jnp.mean(rows * rows, axis=-1, keepdims=True) + EPS)


def message_kernel(ids_ref, wq_ref, wkv_ref, g1_ref, g2_ref, out_ref):
    core = ids_ref[1]

    @pl.when(core == 0)
    def _():
        out_ref[...] = wq_ref[:, 0:HALFW]

    @pl.when(core == 1)
    def _():
        out_ref[:, 0:KVW] = wkv_ref[...]
        one = jnp.broadcast_to(g1_ref[...].astype(F32), (128, SHARD)).T
        two = jnp.broadcast_to(g2_ref[...].astype(F32), (128, SHARD)).T
        lane = lax.broadcasted_iota(jnp.int32, (SHARD, 128), 1)
        rest = wq_ref[:, HALFW:D].astype(F32)
        rest = jnp.concatenate([rest, jnp.zeros((SHARD, 64), F32)], axis=1)
        rest = jnp.where(lane == 64, one, jnp.where(lane == 65, two, rest))
        out_ref[:, KVW : KVW + 128] = rest.astype(BF16)
        out_ref[:, KVW + 128 : HALFW] = jnp.zeros((SHARD, HALFW - KVW - 128), BF16)


def chunk_kernel(ids_ref, gu_ref, wo_ref, *out_refs):
    fs = ids_ref[0]
    core = ids_ref[1]
    for s in range(FS):
        at = lax.rem(fs + s, FS) * FSL + core * FF
        out_refs[s][...] = gu_ref[:, pl.ds(pl.multiple_of(at, 128), FSL)]
    at = fs * FSL + (1 - core) * FF
    out_refs[FS][...] = gu_ref[:, pl.ds(pl.multiple_of(at, 128), FSL)]
    out_refs[FS + 1][...] = wo_ref[pl.ds(pl.multiple_of(core * 112, 16), 128), :]
    out_refs[FS + 2][...] = wo_ref[pl.ds(pl.multiple_of((1 - core) * 112, 16), 128), :]


def place_kernel(ids_ref, *refs):
    fs = ids_ref[0]
    core = ids_ref[1]
    out_ref, wo_ref = refs[4 * FS :]
    for half in range(2):

        @pl.when(core == half)
        def _(half=half):
            for s in range(FS):
                at = pl.multiple_of(lax.rem(fs + FS - s, FS) * SHARD, 16)
                for other in range(2):
                    cols = slice(FSL * (half ^ other), FSL * ((half ^ other) + 1))
                    out_ref[pl.ds(at, SHARD), cols] = refs[FS * other + s][...]

    for s in range(FS):
        at = lax.rem(fs + s, FS) * SHARD
        for other in range(2):
            first = at + 112 * (core if other == 0 else 1 - core)
            wo_ref[pl.ds(pl.multiple_of(first, 16), 128), :] = refs[FS * (2 + other) + s][...]


def qkv_kernel(ids_ref, x_ref, *refs):
    mine = refs[0:FS]
    other = refs[FS : 2 * FS]
    cos_ref, sin_ref = refs[2 * FS : 2 * FS + 2]
    out_ref, gains_ref, wa_ref, wb_ref = refs[2 * FS + 2 : 2 * FS + 6]
    at_refs = refs[2 * FS + 6 : 3 * FS + 6]
    full_ref = refs[3 * FS + 6]
    fs = ids_ref[0]
    core = ids_ref[1]

    def fill(first, second):
        for s in range(FS):
            at = pl.multiple_of(lax.rem(fs + s, FS) * SHARD, 16)
            wa_ref[pl.ds(at, SHARD), :] = first[s][...]
            wb_ref[pl.ds(at, SHARD), :] = second[s][...]

    @pl.when(core == 0)
    def _():
        fill(mine, other)

    @pl.when(core == 1)
    def _():
        fill(other, mine)

    x = x_ref[...].astype(F32)
    gains = wb_ref[:, KVW : KVW + 128].astype(F32).T
    gains_ref[...] = gains[64:72, :]
    a = (x * inv_norm(x) * gains[64:65, :]).astype(BF16)
    full_ref[...] = a.astype(F32).T.astype(BF16)
    for s in range(FS):
        at = pl.multiple_of(lax.rem(fs + s, FS) * SHARD, 16)
        at_refs[s][...] = full_ref[pl.ds(at, SHARD), :]
    lin_a = dot(a, wa_ref[...]).T
    lin_b = dot(a, wb_ref[...]).T
    cos = cos_ref[...]
    sin = sin_ref[...]

    def turned(rows):
        first = rows[0:HALF]
        second = rows[HALF:HEAD]
        return jnp.concatenate(
            [first * cos - second * sin, second * cos + first * sin], axis=0
        ).astype(BF16)

    for j in range(KV_HEADS):
        key = turned(lin_b[HEAD * j : HEAD * (j + 1)])
        value = lin_b[HEAD * (KV_HEADS + j) : HEAD * (KV_HEADS + j + 1)].astype(BF16)
        for g in range(GROUP):
            head = j * GROUP + g
            if head < HEADS - 1:
                rows = lin_a[HEAD * head : HEAD * (head + 1)]
            else:
                rows = lin_b[KVW : KVW + HEAD]
            out_ref[head, 0:HEAD, :] = turned(rows)
            out_ref[head, HEAD : 2 * HEAD, :] = key
            out_ref[head, 2 * HEAD : 3 * HEAD, :] = value
    out_ref[HEADS, :, :] = jnp.zeros((3 * HEAD, ROWS), BF16)


def pick_pair(load, first, second):
    left = load(first // 2).astype(F32)
    right = load(second // 2).astype(F32)
    left = pltpu.roll(left, (first % 2) * BLK, 1)
    right = pltpu.roll(right, (1 - second % 2) * BLK, 1)
    lane = lax.broadcasted_iota(jnp.int32, left.shape, 1)
    return jnp.where(lane < BLK, left, right)


def causal(size):
    key = lax.broadcasted_iota(jnp.int32, (size, size), 0)
    query = lax.broadcasted_iota(jnp.int32, (size, size), 1)
    return key <= query


def attend_kernel(
    order_ref, inv_ref, recv_ref, out_ref, qt_ref, kt_ref, k_ref, vt_ref, of_ref, lse_ref, s_ref
):
    for m in range(CTX):
        got = pick_pair(lambda i: recv_ref[i], inv_ref[2 * m], inv_ref[2 * m + 1])
        at = slice(2 * BLK * m, 2 * BLK * (m + 1))
        qt_ref[:, at] = (got[0:HEAD] * SCALE).astype(BF16)
        key = got[HEAD : 2 * HEAD]
        kt_ref[:, at] = key.astype(BF16)
        k_ref[at, :] = key.T.astype(BF16)
        vt_ref[:, at] = got[2 * HEAD : 3 * HEAD].astype(BF16)
    allowed = causal(TILE)
    for n in range(NT):
        span = slice(TILE * n, TILE * (n + 1))
        query = qt_ref[:, span]
        top = None
        for c in range(n + 1):
            rows = slice(TILE * c, TILE * (c + 1))
            s = dot(k_ref[rows, :], query)
            if c == n:
                s = jnp.where(allowed, s, -1e30)
            s_ref[rows, :] = s
            part = jnp.max(s, axis=0, keepdims=True)
            top = part if top is None else jnp.maximum(top, part)
        total = None
        for c in range(n + 1):
            rows = slice(TILE * c, TILE * (c + 1))
            e = jnp.exp(s_ref[rows, :] - top)
            s_ref[rows, :] = e
            part = jnp.sum(e, axis=0, keepdims=True)
            total = part if total is None else total + part
        recip = 1.0 / total
        lse_ref[n] = jnp.broadcast_to(top + jnp.log(total), (8, TILE))
        prob = (s_ref[0 : TILE * (n + 1), :] * recip).astype(BF16)
        o = dot(vt_ref[:, 0 : TILE * (n + 1)], prob)
        of_ref[2 * n] = o[:, 0 : 2 * BLK]
        of_ref[2 * n + 1] = o[:, 2 * BLK :]
    for i in range(CTX):
        got = pick_pair(lambda g: of_ref[g], order_ref[2 * i], order_ref[2 * i + 1])
        out_ref[i] = got.astype(BF16)


def attend_back_kernel(
    order_ref,
    inv_ref,
    recv_ref,
    qt_ref,
    q_ref,
    kt_ref,
    k_ref,
    v_ref,
    of_ref,
    lse_ref,
    cos_ref,
    sin_ref,
    out_ref,
    dot_ref,
    do_ref,
    delta_ref,
    dk_ref,
    dv_ref,
    st_ref,
):
    for m in range(CTX):
        got = pick_pair(lambda i: recv_ref[i], inv_ref[2 * m], inv_ref[2 * m + 1])
        at = slice(2 * BLK * m, 2 * BLK * (m + 1))
        dot_ref[:, at] = got.astype(BF16)
        do_ref[at, :] = got.T.astype(BF16)
        delta_ref[:, at] = jnp.broadcast_to(
            jnp.sum(got * of_ref[m], axis=0, keepdims=True), (8, 2 * BLK)
        )
    allowed = causal(TILE)
    for n in range(NT):
        span = slice(TILE * n, TILE * (n + 1))
        query = qt_ref[:, span]
        out_grad = dot_ref[:, span]
        lse = lse_ref[n][0:1, :]
        delta = delta_ref[0:1, span]
        dq = None
        for c in range(n + 1):
            rows = slice(TILE * c, TILE * (c + 1))
            prob = jnp.exp(dot(k_ref[rows, :], query) - lse)
            if c == n:
                prob = jnp.where(allowed, prob, 0.0)
            ds = (prob * (dot(v_ref[rows, :], out_grad) - delta)).astype(BF16)
            part = dot(kt_ref[:, rows], ds)
            dq = part if dq is None else dq + part
            dk = dot(ds, q_ref[span, :])
            dv = dot(prob.astype(BF16), do_ref[span, :])
            if c == n:
                dk_ref[rows, :] = dk
                dv_ref[rows, :] = dv
            else:
                dk_ref[rows, :] += dk
                dv_ref[rows, :] += dv
        st_ref[2 * n, 0:HEAD, :] = dq[:, 0 : 2 * BLK] * SCALE
        st_ref[2 * n + 1, 0:HEAD, :] = dq[:, 2 * BLK :] * SCALE
    for m in range(CTX):
        at = slice(2 * BLK * m, 2 * BLK * (m + 1))
        cos = cos_ref[:, at]
        sin = sin_ref[:, at]

        def turned(value):
            first = value[0:HALF]
            second = value[HALF:HEAD]
            return jnp.concatenate(
                [first * cos + second * sin, second * cos - first * sin], axis=0
            )

        st_ref[m, 0:HEAD, :] = turned(st_ref[m, 0:HEAD, :])
        st_ref[m, HEAD : 2 * HEAD, :] = turned(dk_ref[at, :].T)
        st_ref[m, 2 * HEAD : 3 * HEAD, :] = dv_ref[at, :].T
    for i in range(CTX):
        got = pick_pair(lambda g: st_ref[g], order_ref[2 * i], order_ref[2 * i + 1])
        out_ref[i] = got.astype(BF16)


def resid_kernel(ids_ref, ot_ref, w_ref, x_ref, gains_ref, *refs):
    a_refs = refs[0:FS]
    h_ref, b_ref = refs[FS : FS + 2]
    out_refs = refs[FS + 2 : 2 * FS + 2]
    full_ref = refs[2 * FS + 2]
    flat = jnp.concatenate([ot_ref[h] for h in range(HEADS)], axis=0)
    full_ref[...] = flat
    for s in range(FS):
        at = pl.multiple_of(lax.rem(ids_ref[0] + s, FS) * SHARD, 16)
        out_refs[s][0:SHARD, :] = full_ref[pl.ds(at, SHARD), :]
        out_refs[s][SHARD : 2 * SHARD, :] = a_refs[s][...]
    mixed = flat.astype(F32).T.astype(BF16)
    h = x_ref[...].astype(F32) + dot(mixed, w_ref[...])
    h_ref[...] = h
    b_ref[...] = (h * inv_norm(h) * gains_ref[1:2, :]).astype(BF16)


def mlp_kernel(*refs):
    b_refs = refs[0:FS]
    g_refs = refs[FS : 2 * FS]
    gu_ref, down_ref = refs[2 * FS : 2 * FS + 2]
    db_refs = refs[2 * FS + 2 : 3 * FS + 2]
    mm_ref, dgu_ref = refs[3 * FS + 2 :]
    for s in range(FS):
        gu = dot(b_refs[s][...], gu_ref[...])
        gate = gu[:, :FSL]
        up = gu[:, FSL:]
        sig = 1.0 / (1.0 + jnp.exp(-gate))
        act = gate * sig
        dm = dot(g_refs[s][...], down_ref[...], 1, 1)
        dgate = dm * up * sig * (1.0 + gate * (1.0 - sig))
        dgu = jnp.concatenate([dgate, dm * act], axis=1).astype(BF16)
        rows = slice(ROWS * s, ROWS * (s + 1))
        mm_ref[rows, :] = (act * up).astype(BF16)
        dgu_ref[rows, :] = dgu
        db_refs[s][...] = dot(dgu, gu_ref[...], 1, 1).astype(BF16)


def mlp_grad_kernel(ids_ref, *refs):
    b_refs = refs[0:FS]
    g_refs = refs[FS : 2 * FS]
    mm_ref, dgu_ref, down_ref = refs[2 * FS : 2 * FS + 3]
    y_refs = refs[2 * FS + 3 : 3 * FS + 3]
    keep_ref, give_ref, gu_ref, dd_ref = refs[3 * FS + 3 :]
    b = jnp.concatenate([r[...] for r in b_refs], axis=0)
    g = jnp.concatenate([r[...] for r in g_refs], axis=0)
    gu_ref[...] = dot(b, dgu_ref[...], 0, 0).astype(BF16)
    dd_ref[...] = dot(g, mm_ref[...], 0, 0).astype(BF16)

    def put(out_ref, half):
        out_ref[0:D, :] = gu_ref[:, FSL * half : FSL * (half + 1)]
        out_ref[D : D + D // 2, :] = dd_ref[D // 2 * half : D // 2 * (half + 1), :]

    for core in range(2):

        @pl.when(ids_ref[1] == core)
        def _(core=core):
            put(keep_ref, core)
            put(give_ref, 1 - core)

    for s in range(FS):
        y_refs[s][...] = dot(mm_ref[ROWS * s : ROWS * (s + 1), :], down_ref[...]).astype(BF16)


def pack_kernel(ids_ref, keep_ref, got_ref, *refs):
    sum_ref = refs[4]
    for at in range(0, HALF_ROWS, 240):
        rows = slice(at, at + 240)
        sum_ref[rows, :] = keep_ref[rows, :].astype(F32) + got_ref[rows, :].astype(F32)
    sum_ref[HALF_ROWS:, :] = jnp.zeros((16, FSL), F32)

    def put(out_ref, first):
        for r in range(first, first + 4):
            for k in range(FS):
                at = SHARD * k + 15 * r
                out_ref[r - first, 16 * k : 16 * (k + 1), :] = sum_ref[at : at + 16, :].astype(BF16)
            at = D + 30 * r
            out_ref[r - first, 64:96, :] = sum_ref[at : at + 32, :].astype(BF16)

    for x in range(4):

        @pl.when(ids_ref[2] == x)
        def _(x=x):
            for step in range(4):
                put(refs[step], 4 * ((x + step) % 4))


def sum_x_kernel(ids_ref, *refs):
    total = refs[0][...].astype(F32)
    for step in range(1, 4):
        total += refs[step][...].astype(F32)
    refs[8][...] = total.astype(BF16)
    for step in range(4):
        refs[4 + step][...] = refs[8][lax.rem(ids_ref[3] + step, 4)]


def sum_z_kernel(ids_ref, *refs):
    total = refs[0][...].astype(F32)
    for step in range(1, 4):
        total += refs[step][...].astype(F32)
    sum_ref = refs[9]
    sum_ref[...] = total.astype(BF16)
    for s in range(FS):
        at = pl.multiple_of(lax.rem(ids_ref[0] + s, FS) * 16, 16)
        refs[4 + s][...] = sum_ref[pl.ds(at, 16), :]
    refs[8][...] = sum_ref[64:96, :]


def mid_kernel(db0, db1, db2, db3, h_ref, g_ref, gains_ref, w_ref, dh_ref, e_ref, do_ref):
    db = db0[...].astype(F32) + db1[...].astype(F32) + db2[...].astype(F32) + db3[...].astype(F32)
    h = h_ref[...]
    r2 = inv_norm(h)
    scaled = gains_ref[1:2, :] * db
    dh = (
        g_ref[...].astype(F32)
        + r2 * scaled
        - h * (r2 * r2 * r2) * jnp.mean(scaled * h, axis=-1, keepdims=True)
    )
    dh_ref[...] = dh
    e = dh.astype(BF16)
    e_ref[...] = e
    back = dot(w_ref[...], e, 1, 1).astype(BF16)
    for head in range(HEADS):
        do_ref[head] = back[HEAD * head : HEAD * (head + 1)]
    do_ref[HEADS] = jnp.zeros((HEAD, ROWS), BF16)


def last_kernel(recv_ref, wa_ref, wb_ref, x_ref, dh_ref, gains_ref, ig_ref, msg_ref):
    for head in range(HEADS):
        msg_ref[HEAD * head : HEAD * (head + 1), :] = recv_ref[head, 0:HEAD, :]
    for part in range(2):
        for j in range(KV_HEADS):
            total = None
            for g in range(GROUP):
                piece = recv_ref[j * GROUP + g, HEAD * (part + 1) : HEAD * (part + 2), :]
                piece = piece.astype(F32)
                total = piece if total is None else total + piece
            base = D + HEAD * (KV_HEADS * part + j)
            msg_ref[base : base + HEAD, :] = total.astype(BF16)
    da = dot(wa_ref[...], msg_ref[0:HALFW, :])
    da += dot(wb_ref[:, 0:KVW], msg_ref[D:QKV, :])
    da += dot(wb_ref[:, KVW : KVW + HEAD], msg_ref[HALFW:D, :])
    da = da.T
    x = x_ref[...].astype(F32)
    r1 = inv_norm(x)
    scaled = gains_ref[0:1, :] * da
    ig_ref[...] = (
        dh_ref[...]
        + r1 * scaled
        - x * (r1 * r1 * r1) * jnp.mean(scaled * x, axis=-1, keepdims=True)
    )


def out_grad_kernel(*refs):
    total = None
    for s in range(FS):
        part = dot(refs[(FS - s) % FS][0:SHARD, :], refs[FS + s][...])
        total = part if total is None else total + part
    refs[2 * FS][...] = total.astype(BF16)


def qkv_grad_kernel(ids_ref, *refs):
    o_ref, keep_ref, give_ref, full_ref = refs[2 * FS :]
    total = None
    for s in range(FS):
        part = dot(refs[(FS - s) % FS][SHARD:, :], refs[FS + s][...], 1, 1)
        total = part if total is None else total + part
    full_ref[0:SHARD, 0:QKV] = total.astype(BF16)
    full_ref[0:SHARD, QKV:WIDE] = jnp.zeros((SHARD, WIDE - QKV), BF16)
    full_ref[0:SHARD, WIDE : WIDE + D] = o_ref[...]
    full_ref[0:SHARD, WIDE + D : TAIL] = jnp.zeros((SHARD, TAIL - WIDE - D), BF16)
    full_ref[SHARD : SHARD + 16, :] = jnp.zeros((16, TAIL), BF16)
    core = ids_ref[1]
    keep_ref[...] = full_ref[pl.ds(pl.multiple_of(core * 128, 128), 128), :]
    give_ref[...] = full_ref[pl.ds(pl.multiple_of((1 - core) * 128, 128), 128), :]


def unpack_kernel(
    ids_ref, mine_ref, other_ref, wq_ref, wkv_ref, gain_in, q_ref, kv_ref, o_ref, gain_ref, full_ref
):
    core = ids_ref[1]
    full_ref[pl.ds(pl.multiple_of(core * 128, 128), 128), :] = mine_ref[...]
    full_ref[pl.ds(pl.multiple_of((1 - core) * 128, 128), 128), :] = other_ref[...]
    q = full_ref[0:SHARD, 0:D].astype(F32)
    kv = full_ref[0:SHARD, D:QKV].astype(F32)
    q_ref[...] = q
    kv_ref[...] = kv
    o_ref[...] = full_ref[0:SHARD, WIDE : WIDE + D].astype(F32)
    total = jnp.sum(q * wq_ref[...].astype(F32), axis=1, keepdims=True)
    total += jnp.sum(kv * wkv_ref[...].astype(F32), axis=1, keepdims=True)
    gain_ref[...] = jnp.broadcast_to(total, (SHARD, 128)).T[0:8] / gain_in[...].astype(F32)


def widen_kernel(ids_ref, *refs):
    gu_in, gain_in, gu_out, down_out, gain_ref, all_ref = refs[8:]
    for half in range(2):
        core = ids_ref[1] if half == 0 else 1 - ids_ref[1]
        for xs in range(4):
            for zs in range(4):
                r = lax.rem(ids_ref[2] + xs, 4) * 4 + lax.rem(ids_ref[3] + zs, 4)
                all_ref[core * CTX + r] = refs[4 * half + xs][zs]
    total = None
    down = []
    for half in range(2):
        for s in range(FS):
            at = lax.rem(ids_ref[0] + FS - s, FS) * FSL + FF * half
            cols = pl.ds(pl.multiple_of(at, 128), FSL)
            rows = [
                all_ref[CTX * half + r, 16 * s : 16 * (s + 1), :].astype(F32)[0:15]
                for r in range(CTX)
            ]
            rows = jnp.concatenate(rows, axis=0)
            gu_out[:, cols] = rows
            part = jnp.sum(rows * gu_in[:, cols].astype(F32), axis=1, keepdims=True)
            total = part if total is None else total + part
        down += [all_ref[CTX * half + r, 64:96, :].astype(F32)[0:30] for r in range(CTX)]
    down_out[...] = jnp.concatenate(down, axis=0).T
    gain_ref[...] = jnp.broadcast_to(total, (SHARD, 128)).T[0:8] / gain_in[...].astype(F32)


def swap_core(value):
    return lax.ppermute(value, "ctx", [(i, i ^ 1) for i in range(CTX)])


def shift(value, step):
    return lax.ppermute(value, "fsdp", [((i + step) % FS, i) for i in range(FS)])


def same_core(value):
    groups = [[2 * i + core for i in range(CTX)] for core in range(2)]
    return lax.all_to_all(value, ("seq", "ctx"), 0, 0, axis_index_groups=groups)


def shift_x(value, step):
    def at(x, z, core):
        return (x % 2) * CTX + (x // 2) * 8 + z * 2 + core

    pairs = [
        (at((x + step) % 4, z, core), at(x, z, core))
        for x in range(4)
        for z in range(4)
        for core in range(2)
    ]
    return lax.ppermute(value, ("seq", "ctx"), pairs)


def shift_z(value, step):
    def at(high, z, core):
        return high * 8 + z * 2 + core

    pairs = [
        (at(high, (z + step) % 4, core), at(high, z, core))
        for high in range(2)
        for z in range(4)
        for core in range(2)
    ]
    return lax.ppermute(value, "ctx", pairs)


def gather_by(move, value):
    return [value] + [move(value, s) for s in range(1, 4)]


def scatter_by(move, pieces):
    return [pieces[0]] + [move(pieces[s], -s) for s in range(1, 4)]


def gather_rolled(value):
    return gather_by(shift, value)


def scatter_rolled(pieces):
    return scatter_by(shift, pieces)


def together(*values):
    return lax.optimization_barrier(values)


def shards(tokens, gain_attn, w_q, w_kv, w_o, gain_mlp, w_gate_up, w_down, block_order, cotangent):
    x = tokens[0]
    g_own = cotangent[0]
    order = block_order[0]
    place = lax.axis_index("ctx")
    x_place = place // 8 * 2 + lax.axis_index("seq")
    ids = jnp.stack([lax.axis_index("fsdp"), place % 2, x_place, place // 2 % 4])
    ids = ids.astype(jnp.int32)

    slots = jnp.arange(2 * CTX, dtype=jnp.int32)
    inverse = jnp.sum(jnp.where(order[None, :] == slots[:, None], slots[None, :], 0), axis=1)
    mine = lax.dynamic_slice_in_dim(order, place * 2, 2)
    places = (mine[:, None] * BLK + jnp.arange(BLK, dtype=jnp.int32)[None, :]).reshape(ROWS)
    freq = THETA ** (-(jnp.arange(HALF, dtype=F32) * 2.0 / HEAD))
    angle = freq[:, None] * places.astype(F32)[None, :]
    angle_all = freq[:, None] * jnp.arange(L, dtype=F32)[None, :]

    (message,) = call(
        message_kernel,
        [shape(SHARD, HALFW)],
        [ids, w_q, w_kv, gain_attn[None], gain_mlp[None]],
        smem=1,
    )
    w_mine = gather_rolled(message)
    w_other = [swap_core(piece) for piece in w_mine]
    *chunks, gu_local, wo_mine, wo_other = call(
        chunk_kernel,
        [shape(SHARD, FSL)] * (FS + 1) + [shape(128, D)] * 2,
        [ids, w_gate_up, w_o],
        smem=1,
    )
    w_mine, chunks, wo_mine = together(w_mine, chunks, wo_mine)
    wo_mine = gather_rolled(wo_mine)
    wo_other = [wo_other] + [swap_core(piece) for piece in wo_mine[1:]]
    gu_mine = scatter_rolled(chunks)
    gu_other = [gu_local] + [swap_core(piece) for piece in gu_mine[1:]]
    w_gu, w_out = call(
        place_kernel,
        [shape(D, 2 * FSL), shape(D, D)],
        [ids] + gu_mine + gu_other + wo_mine + wo_other,
        smem=1,
    )
    g_all = gather_rolled(g_own)

    packed, gains, w_a, w_b, *a_pieces = call(
        qkv_kernel,
        [
            shape(CTX, 3 * HEAD, ROWS),
            shape(8, D, dtype=F32),
            shape(D, HALFW),
            shape(D, HALFW),
        ]
        + [shape(SHARD, ROWS)] * FS,
        [ids, x] + w_mine + w_other + [jnp.cos(angle), jnp.sin(angle)],
        smem=1,
        scratch=[pltpu.VMEM((D, ROWS), BF16)],
        flops=2 * ROWS * D * QKV,
    )
    received = lax.all_to_all(packed, "ctx", 0, 0)
    o_part, q_t, k_t, k_n, v_t, o_f, lse = call(
        attend_kernel,
        [
            shape(CTX, HEAD, ROWS),
            shape(HEAD, L),
            shape(HEAD, L),
            shape(L, HEAD),
            shape(HEAD, L),
            shape(CTX, HEAD, ROWS, dtype=F32),
            shape(NT, 8, TILE, dtype=F32),
        ],
        [order, inverse, received],
        smem=2,
        scratch=[pltpu.VMEM((L, TILE), F32)],
        flops=2 * L * L * HEAD,
    )
    o_all = lax.all_to_all(o_part, "ctx", 0, 0)
    o_all, g_all, w_gu, w_out = together(o_all, g_all, w_gu, w_out)
    h, b, *ao_pieces = call(
        resid_kernel,
        [shape(ROWS, D, dtype=F32), shape(ROWS, D)] + [shape(2 * SHARD, ROWS)] * FS,
        [ids, o_all, w_out, x, gains] + a_pieces,
        smem=1,
        scratch=[pltpu.VMEM((D, ROWS), BF16)],
        flops=2 * ROWS * D * D,
    )
    b_all = gather_rolled(b)
    *db_parts, mm, dgu = call(
        mlp_kernel,
        [shape(ROWS, D)] * FS + [shape(FS * ROWS, FSL), shape(FS * ROWS, 2 * FSL)],
        b_all + g_all + [w_gu, w_down],
        flops=10 * FS * ROWS * D * FSL,
    )
    db = scatter_rolled(db_parts)
    db[1], mm = together(db[1], mm)
    *y_parts, keep, give = call(
        mlp_grad_kernel,
        [shape(ROWS, D)] * FS + [shape(HALF_ROWS, FSL)] * 2,
        [ids] + b_all + g_all + [mm, dgu, w_down],
        smem=1,
        scratch=[pltpu.VMEM((D, 2 * FSL), BF16), pltpu.VMEM((D, FSL), BF16)],
        flops=8 * FS * ROWS * D * FSL,
    )
    db, keep, give = together(db, keep, give)
    got = swap_core(give)
    dh, e, do_part = call(
        mid_kernel,
        [shape(ROWS, D, dtype=F32), shape(ROWS, D), shape(CTX, HEAD, ROWS)],
        db + [h, g_own, gains, w_out],
        flops=2 * ROWS * D * D,
    )
    do_all = lax.all_to_all(do_part, "ctx", 0, 0)
    x_pieces = call(
        pack_kernel,
        [shape(4, 96, FSL)] * 4,
        [ids, keep, got],
        smem=1,
        scratch=[pltpu.VMEM((HALF_ROWS + 16, FSL), F32)],
    )
    do_all, x_pieces = together(do_all, x_pieces)
    x_pieces = scatter_by(shift_x, x_pieces)
    e_all = gather_rolled(e)
    (dqkv_part,) = call(
        attend_back_kernel,
        [shape(CTX, 3 * HEAD, ROWS)],
        [
            order,
            inverse,
            do_all,
            q_t,
            q_t.T,
            k_t,
            k_n,
            v_t.T,
            o_f,
            lse,
            jnp.cos(angle_all),
            jnp.sin(angle_all),
        ],
        smem=2,
        scratch=[
            pltpu.VMEM((HEAD, L), BF16),
            pltpu.VMEM((L, HEAD), BF16),
            pltpu.VMEM((8, L), F32),
            pltpu.VMEM((L, HEAD), F32),
            pltpu.VMEM((L, HEAD), F32),
            pltpu.VMEM((CTX, 3 * HEAD, ROWS), F32),
        ],
        flops=5 * L * L * HEAD,
    )
    dqkv_part, x_pieces, e_all = together(dqkv_part, x_pieces, e_all)
    dqkv = lax.all_to_all(dqkv_part, "ctx", 0, 0)
    z_pieces = call(
        sum_x_kernel,
        [shape(96, FSL)] * 4,
        [ids] + x_pieces,
        smem=1,
        scratch=[pltpu.VMEM((4, 96, FSL), BF16)],
    )
    z_pieces = scatter_by(shift_z, z_pieces)
    y = scatter_rolled(y_parts)
    ao_all = scatter_rolled(ao_pieces)
    (o_grad,) = call(
        out_grad_kernel,
        [shape(SHARD, D)],
        ao_all + e_all,
        flops=2 * FS * ROWS * SHARD * D,
    )
    dqkv, o_grad, z_pieces, y = together(dqkv, o_grad, z_pieces, y)
    result = h
    for piece in y:
        result = result + piece.astype(F32)
    input_grad, low = call(
        last_kernel,
        [shape(ROWS, D, dtype=F32), shape(QKV, ROWS)],
        [dqkv, w_a, w_b, x, dh, gains],
        flops=2 * ROWS * D * QKV,
    )
    low_all = gather_rolled(low)
    *pieces, down_sum = call(
        sum_z_kernel,
        [shape(16, FSL)] * FS + [shape(32, FSL)],
        [ids] + z_pieces,
        smem=1,
        scratch=[pltpu.VMEM((96, FSL), BF16)],
    )
    own = jnp.concatenate(scatter_rolled(pieces) + [down_sum], axis=0)
    z_all = jnp.stack(gather_by(shift_z, own))
    low_all, z_all = together(low_all, z_all)
    keep, give = call(
        qkv_grad_kernel,
        [shape(128, TAIL)] * 2,
        [ids] + ao_all + low_all + [o_grad],
        smem=1,
        scratch=[pltpu.VMEM((SHARD + 16, TAIL), BF16)],
        flops=2 * FS * ROWS * SHARD * QKV,
    )
    half = (keep.astype(F32) + swap_core(give).astype(F32)).astype(BF16)
    parts = same_core(half.reshape(CTX, 8, TAIL))
    x_mine = gather_by(shift_x, z_all)
    parts, x_mine = together(parts, x_mine)
    summed = jnp.sum(parts.astype(F32), axis=0).astype(BF16)
    mine_tail = same_core(jnp.broadcast_to(summed[None], (CTX, 8, TAIL))).reshape(128, TAIL)
    x_other = [swap_core(piece) for piece in x_mine]
    gu_out, down_out, gain_two = call(
        widen_kernel,
        [
            shape(SHARD, 2 * FF, dtype=F32),
            shape(FSL, D, dtype=F32),
            shape(8, SHARD, dtype=F32),
        ],
        [ids] + x_mine + x_other + [w_gate_up, gain_mlp[None]],
        smem=1,
        scratch=[pltpu.VMEM((2 * CTX, 96, FSL), BF16)],
    )
    mine_tail, gu_out, down_out, gain_two, result = together(
        mine_tail, gu_out, down_out, gain_two, result
    )
    q_out, kv_out, o_out, gain_one = call(
        unpack_kernel,
        [
            shape(SHARD, D, dtype=F32),
            shape(SHARD, KVW, dtype=F32),
            shape(SHARD, D, dtype=F32),
            shape(8, SHARD, dtype=F32),
        ],
        [ids, mine_tail, swap_core(mine_tail), w_q, w_kv, gain_attn[None]],
        smem=1,
        scratch=[pltpu.VMEM((SHARD + 16, TAIL), BF16)],
    )
    return (
        result.astype(BF16)[None],
        input_grad[None],
        gain_one[0],
        q_out,
        kv_out,
        o_out,
        gain_two[0],
        gu_out,
        down_out,
    )


def solution(mesh):
    tokens = P(("seq", "fsdp"), "ctx", None)
    return jax.shard_map(
        shards,
        mesh=mesh,
        in_specs=(
            tokens,
            P("fsdp"),
            P("fsdp", None),
            P("fsdp", None),
            P("fsdp", None),
            P("fsdp"),
            P("fsdp", None),
            P("fsdp", None),
            P(("seq", "fsdp"), None),
            tokens,
        ),
        out_specs=(
            tokens,
            tokens,
            P("fsdp"),
            P("fsdp", None),
            P("fsdp", None),
            P("fsdp", None),
            P("fsdp"),
            P("fsdp", None),
            P("fsdp", None),
        ),
        check_vma=False,
    )
```

```python
import jax
import jax.numpy as jnp
from jax import lax
from jax.experimental import pallas as pl
from jax.experimental.pallas import tpu as pltpu
from jax.sharding import PartitionSpec as P

D = 960
HEADS = 15
KV_HEADS = 5
GROUP = 3
HEAD = 64
HALF = 32
FF = 2560
BLK = 64
L = 2048
CTX = 16
FS = 4
ROWS = 128
QKV = 1600
HEADROWS = 368
HALFW = 896
KVW = 640
HALF_ROWS = D + D // 2
SHARD = D // FS
FSL = FF // FS
TILE = 256
NT = L // TILE
EPS = 1e-05
THETA = 100000.0
SCALE = HEAD**-0.5
F32 = jnp.float32
BF16 = jnp.bfloat16
VMEM_BYTES = 56 * 1024 * 1024


def call(kernel, outs, args, smem=0, scratch=(), flops=0):
    specs = [pl.BlockSpec(memory_space=pltpu.SMEM)] * smem
    specs += [pl.BlockSpec(memory_space=pltpu.VMEM)] * (len(args) - smem)
    moved = sum(a.size * a.dtype.itemsize for a in list(args) + list(outs))
    return pl.pallas_call(
        kernel,
        out_shape=outs,
        in_specs=specs,
        out_specs=[pl.BlockSpec(memory_space=pltpu.VMEM)] * len(outs),
        scratch_shapes=list(scratch),
        cost_estimate=pl.CostEstimate(flops=flops, bytes_accessed=moved, transcendentals=0),
        compiler_params=pltpu.CompilerParams(vmem_limit_bytes=VMEM_BYTES),
    )(*args)


def shape(*dims, dtype=BF16):
    return jax.ShapeDtypeStruct(dims, dtype)


def dot(left, right, a=1, b=0):
    return lax.dot_general(left, right, (((a,), (b,)), ((), ())), preferred_element_type=F32)


def inv_norm(rows):
    return lax.rsqrt(jnp.mean(rows * rows, axis=-1, keepdims=True) + EPS)


def message_kernel(ids_ref, wq_ref, wkv_ref, g1_ref, g2_ref, out_ref):
    core = ids_ref[1]

    @pl.when(core == 0)
    def _():
        out_ref[...] = wq_ref[:, 0:HALFW]

    @pl.when(core == 1)
    def _():
        out_ref[:, 0:KVW] = wkv_ref[...]
        one = jnp.broadcast_to(g1_ref[...].astype(F32)[None], (128, SHARD)).T
        two = jnp.broadcast_to(g2_ref[...].astype(F32)[None], (128, SHARD)).T
        lane = lax.broadcasted_iota(jnp.int32, (SHARD, 128), 1)
        rest = wq_ref[:, HALFW:D].astype(F32)
        rest = jnp.concatenate([rest, jnp.zeros((SHARD, 64), F32)], axis=1)
        rest = jnp.where(lane == 64, one, jnp.where(lane == 65, two, rest))
        out_ref[:, KVW : KVW + 128] = rest.astype(BF16)
        out_ref[:, KVW + 128 : HALFW] = jnp.zeros((SHARD, HALFW - KVW - 128), BF16)


def chunk_kernel(ids_ref, gu_ref, wo_ref, *out_refs):
    fs = ids_ref[0]
    core = ids_ref[1]
    for s in range(FS):
        at = lax.rem(fs + s, FS) * FSL + core * FF
        out_refs[s][...] = gu_ref[:, pl.ds(pl.multiple_of(at, 128), FSL)]
    at = fs * FSL + (1 - core) * FF
    out_refs[FS][...] = gu_ref[:, pl.ds(pl.multiple_of(at, 128), FSL)]
    out_refs[FS + 1][...] = wo_ref[pl.ds(pl.multiple_of(core * 112, 16), 128), :]
    out_refs[FS + 2][...] = wo_ref[pl.ds(pl.multiple_of((1 - core) * 112, 16), 128), :]


def place_kernel(ids_ref, *refs):
    fs = ids_ref[0]
    core = ids_ref[1]
    out_ref, wo_ref = refs[4 * FS :]
    for half in range(2):

        @pl.when(core == half)
        def _(half=half):
            for s in range(FS):
                at = pl.multiple_of(lax.rem(fs + FS - s, FS) * SHARD, 16)
                for other in range(2):
                    cols = slice(FSL * (half ^ other), FSL * ((half ^ other) + 1))
                    out_ref[pl.ds(at, SHARD), cols] = refs[FS * other + s][...]

    for s in range(FS):
        at = lax.rem(fs + s, FS) * SHARD
        for other in range(2):
            first = at + 112 * (core if other == 0 else 1 - core)
            wo_ref[pl.ds(pl.multiple_of(first, 16), 128), :] = refs[FS * (2 + other) + s][...]


def qkv_kernel(ids_ref, xt_ref, *refs):
    mine = refs[0:FS]
    other = refs[FS : 2 * FS]
    cos_ref, sin_ref, out_ref, gains_ref, wa_ref, wb_ref, at_ref = refs[2 * FS :]
    fs = ids_ref[0]
    core = ids_ref[1]

    def fill(first, second):
        for s in range(FS):
            at = pl.multiple_of(lax.rem(fs + s, FS) * SHARD, 16)
            wa_ref[pl.ds(at, SHARD), :] = first[s][...]
            wb_ref[pl.ds(at, SHARD), :] = second[s][...]

    @pl.when(core == 0)
    def _():
        fill(mine, other)

    @pl.when(core == 1)
    def _():
        fill(other, mine)

    xt = xt_ref[...].astype(F32)
    gains = wb_ref[:, KVW : KVW + 128].astype(F32)
    gains_ref[...] = gains.T[64:72, :]
    r1 = lax.rsqrt(jnp.mean(xt * xt, axis=0, keepdims=True) + EPS)
    at = xt * r1 * gains[:, 64:65]
    at_ref[...] = at.astype(BF16)
    a = at.T.astype(BF16)
    lin_a = dot(a, wa_ref[...]).T
    lin_b = dot(a, wb_ref[...]).T
    cos = cos_ref[...]
    sin = sin_ref[...]

    def turned(rows):
        first = rows[0:HALF]
        second = rows[HALF:HEAD]
        return jnp.concatenate(
            [first * cos - second * sin, second * cos + first * sin], axis=0
        ).astype(BF16)

    for j in range(KV_HEADS):
        key = turned(lin_b[HEAD * j : HEAD * (j + 1)])
        value = lin_b[HEAD * (KV_HEADS + j) : HEAD * (KV_HEADS + j + 1)].astype(BF16)
        for g in range(GROUP):
            head = j * GROUP + g
            if head < HEADS - 1:
                rows = lin_a[HEAD * head : HEAD * (head + 1)]
            else:
                rows = lin_b[KVW : KVW + HEAD]
            out_ref[head, 0:HEAD, :] = turned(rows)
            out_ref[head, HEAD : 2 * HEAD, :] = key
            out_ref[head, 2 * HEAD : 3 * HEAD, :] = value
    out_ref[HEADS, :, :] = jnp.zeros((3 * HEAD, ROWS), BF16)


def pick_pair(load, first, second):
    left = load(first // 2).astype(F32)
    right = load(second // 2).astype(F32)
    left = pltpu.roll(left, (first % 2) * BLK, 1)
    right = pltpu.roll(right, (1 - second % 2) * BLK, 1)
    lane = lax.broadcasted_iota(jnp.int32, left.shape, 1)
    return jnp.where(lane < BLK, left, right)


def causal(size):
    key = lax.broadcasted_iota(jnp.int32, (size, size), 0)
    query = lax.broadcasted_iota(jnp.int32, (size, size), 1)
    return key <= query


def attend_kernel(
    order_ref, inv_ref, recv_ref, out_ref, qt_ref, kt_ref, k_ref, vt_ref, of_ref, lse_ref, s_ref
):
    for m in range(CTX):
        got = pick_pair(lambda i: recv_ref[i], inv_ref[2 * m], inv_ref[2 * m + 1])
        at = slice(2 * BLK * m, 2 * BLK * (m + 1))
        qt_ref[:, at] = (got[0:HEAD] * SCALE).astype(BF16)
        key = got[HEAD : 2 * HEAD]
        kt_ref[:, at] = key.astype(BF16)
        k_ref[at, :] = key.T.astype(BF16)
        vt_ref[:, at] = got[2 * HEAD : 3 * HEAD].astype(BF16)
    allowed = causal(TILE)
    for n in range(NT):
        span = slice(TILE * n, TILE * (n + 1))
        query = qt_ref[:, span]
        top = None
        for c in range(n + 1):
            rows = slice(TILE * c, TILE * (c + 1))
            s = dot(k_ref[rows, :], query)
            if c == n:
                s = jnp.where(allowed, s, -1e30)
            s_ref[rows, :] = s
            part = jnp.max(s, axis=0, keepdims=True)
            top = part if top is None else jnp.maximum(top, part)
        total = None
        for c in range(n + 1):
            rows = slice(TILE * c, TILE * (c + 1))
            e = jnp.exp(s_ref[rows, :] - top)
            s_ref[rows, :] = e
            part = jnp.sum(e, axis=0, keepdims=True)
            total = part if total is None else total + part
        recip = 1.0 / total
        lse_ref[n] = jnp.broadcast_to(top + jnp.log(total), (8, TILE))
        prob = (s_ref[0 : TILE * (n + 1), :] * recip).astype(BF16)
        o = dot(vt_ref[:, 0 : TILE * (n + 1)], prob)
        of_ref[2 * n] = o[:, 0 : 2 * BLK]
        of_ref[2 * n + 1] = o[:, 2 * BLK :]
    for i in range(CTX):
        got = pick_pair(lambda g: of_ref[g], order_ref[2 * i], order_ref[2 * i + 1])
        out_ref[i] = got.astype(BF16)


def attend_back_kernel(
    order_ref,
    inv_ref,
    recv_ref,
    qt_ref,
    q_ref,
    kt_ref,
    k_ref,
    v_ref,
    of_ref,
    lse_ref,
    cos_ref,
    sin_ref,
    out_ref,
    dot_ref,
    do_ref,
    delta_ref,
    dk_ref,
    dv_ref,
    st_ref,
):
    for m in range(CTX):
        got = pick_pair(lambda i: recv_ref[i], inv_ref[2 * m], inv_ref[2 * m + 1])
        at = slice(2 * BLK * m, 2 * BLK * (m + 1))
        dot_ref[:, at] = got.astype(BF16)
        do_ref[at, :] = got.T.astype(BF16)
        delta_ref[:, at] = jnp.broadcast_to(
            jnp.sum(got * of_ref[m], axis=0, keepdims=True), (8, 2 * BLK)
        )
    allowed = causal(TILE)
    for n in range(NT):
        span = slice(TILE * n, TILE * (n + 1))
        query = qt_ref[:, span]
        out_grad = dot_ref[:, span]
        lse = lse_ref[n][0:1, :]
        delta = delta_ref[0:1, span]
        dq = None
        for c in range(n + 1):
            rows = slice(TILE * c, TILE * (c + 1))
            prob = jnp.exp(dot(k_ref[rows, :], query) - lse)
            if c == n:
                prob = jnp.where(allowed, prob, 0.0)
            ds = (prob * (dot(v_ref[rows, :], out_grad) - delta)).astype(BF16)
            part = dot(kt_ref[:, rows], ds)
            dq = part if dq is None else dq + part
            dk = dot(ds, q_ref[span, :])
            dv = dot(prob.astype(BF16), do_ref[span, :])
            if c == n:
                dk_ref[rows, :] = dk
                dv_ref[rows, :] = dv
            else:
                dk_ref[rows, :] += dk
                dv_ref[rows, :] += dv
        st_ref[2 * n, 0:HEAD, :] = dq[:, 0 : 2 * BLK] * SCALE
        st_ref[2 * n + 1, 0:HEAD, :] = dq[:, 2 * BLK :] * SCALE
    for m in range(CTX):
        at = slice(2 * BLK * m, 2 * BLK * (m + 1))
        cos = cos_ref[:, at]
        sin = sin_ref[:, at]

        def turned(value):
            first = value[0:HALF]
            second = value[HALF:HEAD]
            return jnp.concatenate(
                [first * cos + second * sin, second * cos - first * sin], axis=0
            )

        st_ref[m, 0:HEAD, :] = turned(st_ref[m, 0:HEAD, :])
        st_ref[m, HEAD : 2 * HEAD, :] = turned(dk_ref[at, :].T)
        st_ref[m, 2 * HEAD : 3 * HEAD, :] = dv_ref[at, :].T
    for i in range(CTX):
        got = pick_pair(lambda g: st_ref[g], order_ref[2 * i], order_ref[2 * i + 1])
        out_ref[i] = got.astype(BF16)


def resid_kernel(ids_ref, ot_ref, w_ref, xt_ref, gains_ref, h_ref, b_ref, *refs):
    full_ref = refs[FS]
    flat = jnp.concatenate([ot_ref[h] for h in range(HEADS)], axis=0)
    full_ref[...] = flat
    for s in range(FS):
        at = pl.multiple_of(lax.rem(ids_ref[0] + s, FS) * SHARD, 16)
        refs[s][...] = full_ref[pl.ds(at, SHARD), :]
    mixed = flat.astype(F32).T.astype(BF16)
    h = xt_ref[...].astype(F32).T + dot(mixed, w_ref[...])
    h_ref[...] = h
    b_ref[...] = (h * inv_norm(h) * gains_ref[1:2, :]).astype(BF16)


def mlp_kernel(b_ref, gt_ref, gu_ref, down_ref, db_ref, mm_ref, dgu_ref):
    gu = dot(b_ref[...], gu_ref[...])
    gate = gu[:, :FSL]
    up = gu[:, FSL:]
    sig = 1.0 / (1.0 + jnp.exp(-gate))
    act = gate * sig
    dm = dot(gt_ref[...], down_ref[...], 0, 0)
    dgate = dm * up * sig * (1.0 + gate * (1.0 - sig))
    dgu = jnp.concatenate([dgate, dm * act], axis=1).astype(BF16)
    mm_ref[...] = (act * up).astype(BF16)
    dgu_ref[...] = dgu
    db_ref[...] = dot(dgu, gu_ref[...], 1, 1).astype(BF16)


def mlp_grad_kernel(ids_ref, *refs):
    b_refs = refs[0:FS]
    g_refs = refs[FS : 2 * FS]
    mm_refs = refs[2 * FS : 3 * FS]
    dgu_refs = refs[3 * FS : 4 * FS]
    down_ref = refs[4 * FS]
    y_refs = refs[4 * FS + 1 : 5 * FS + 1]
    keep_ref, give_ref, gu_ref, dd_ref = refs[5 * FS + 1 :]
    b = jnp.concatenate([r[...] for r in b_refs], axis=0)
    gt = jnp.concatenate([r[...] for r in g_refs], axis=1)
    mm = jnp.concatenate([r[...] for r in mm_refs], axis=0)
    dgu = jnp.concatenate([r[...] for r in dgu_refs], axis=0)
    gu_ref[...] = dot(b, dgu, 0, 0).astype(BF16)
    dd_ref[...] = dot(gt, mm).astype(BF16)

    def put(out_ref, half):
        out_ref[0:D, :] = gu_ref[:, FSL * half : FSL * (half + 1)]
        out_ref[D : D + D // 2, :] = dd_ref[D // 2 * half : D // 2 * (half + 1), :]

    for core in range(2):

        @pl.when(ids_ref[1] == core)
        def _(core=core):
            put(keep_ref, core)
            put(give_ref, 1 - core)

    for s in range(FS):
        y_refs[s][...] = dot(mm_refs[s][...], down_ref[...], 1, 1).astype(BF16)


def result_kernel(h_ref, y0, y1, y2, y3, out_ref):
    total = h_ref[...]
    for piece in (y0, y1, y2, y3):
        total += piece[...].astype(F32)
    out_ref[...] = total.T.astype(BF16)


def pack_kernel(keep_ref, got_ref, out_ref, sum_ref):
    for at in range(0, HALF_ROWS, 240):
        rows = slice(at, at + 240)
        sum_ref[rows, :] = keep_ref[rows, :].astype(F32) + got_ref[rows, :].astype(F32)
    sum_ref[HALF_ROWS:, :] = jnp.zeros((16, FSL), F32)
    for r in range(CTX):
        for k in range(FS):
            at = SHARD * k + 15 * r
            out_ref[r, 16 * k : 16 * (k + 1), :] = sum_ref[at : at + 16, :].astype(BF16)
        at = D + 30 * r
        out_ref[r, 64:96, :] = sum_ref[at : at + 32, :].astype(BF16)


def reduce_kernel(ids_ref, parts_ref, p0, p1, p2, p3, rest_ref, sum_ref):
    total = parts_ref[0].astype(F32)
    for r in range(1, CTX):
        total += parts_ref[r].astype(F32)
    sum_ref[...] = total.astype(BF16)
    for s, piece in enumerate((p0, p1, p2, p3)):
        at = pl.multiple_of(lax.rem(ids_ref[0] + s, FS) * 16, 16)
        piece[...] = sum_ref[pl.ds(at, 16), :]
    rest_ref[...] = sum_ref[64:96, :]


def mid_kernel(db0, db1, db2, db3, h_ref, gt_ref, gains_ref, w_ref, dh_ref, e_ref, do_ref):
    db = db0[...].astype(F32) + db1[...].astype(F32) + db2[...].astype(F32) + db3[...].astype(F32)
    h = h_ref[...]
    r2 = inv_norm(h)
    scaled = gains_ref[1:2, :] * db
    dh = (
        gt_ref[...].astype(F32).T
        + r2 * scaled
        - h * (r2 * r2 * r2) * jnp.mean(scaled * h, axis=-1, keepdims=True)
    )
    dh_ref[...] = dh
    e = dh.astype(BF16)
    e_ref[...] = e
    back = dot(w_ref[...], e, 1, 1).astype(BF16)
    for head in range(HEADS):
        do_ref[head] = back[HEAD * head : HEAD * (head + 1)]
    do_ref[HEADS] = jnp.zeros((HEAD, ROWS), BF16)


def head_grad_kernel(ids_ref, at_ref, d_ref, *refs):
    full_ref = refs[FS]
    total = None
    for i in range(0, CTX, 2):
        left = jnp.concatenate([at_ref[i], at_ref[i + 1]], axis=1)
        right = jnp.concatenate([d_ref[i], d_ref[i + 1]], axis=1)
        part = dot(left, right, 1, 1)
        total = part if total is None else total + part
    full_ref[...] = total.astype(BF16)
    for s in range(FS):
        at = pl.multiple_of(lax.rem(ids_ref[0] + s, FS) * SHARD, 16)
        rows = full_ref[pl.ds(at, SHARD), :]
        refs[s][0:SHARD, :] = rows[:, 0:128]
        value = rows[:, 128:192].astype(F32)
        value = jnp.concatenate([value[0 : SHARD // 2], value[SHARD // 2 :]], axis=1)
        value = jnp.concatenate([value, jnp.zeros((8, 128), F32)], axis=0)
        refs[s][SHARD:HEADROWS, :] = value.astype(BF16)


def out_grad_kernel(*refs):
    total = None
    for s in range(FS):
        part = dot(refs[(FS - s) % FS][...], refs[FS + s][...])
        total = part if total is None else total + part
    out_ref = refs[2 * FS]
    pad = jnp.zeros((SHARD, 64), F32)
    total = jnp.concatenate([total, pad], axis=1).astype(BF16)
    for i in range(HEADS):
        for j in range(8):
            out_ref[i, 16 * j : 16 * (j + 1), :] = total[
                16 * i : 16 * (i + 1), 128 * j : 128 * (j + 1)
            ]
    out_ref[HEADS, :, :] = jnp.zeros((128, 128), BF16)


def head_sum_kernel(p0, p1, p2, p3, recv_ref, out_ref):
    total = p0[...].astype(F32)
    for piece in (p1, p2, p3):
        total += piece[...].astype(F32)
    out_ref[0:HEADROWS, :] = total.astype(BF16)
    total = recv_ref[0, 3 * HEAD :, :].astype(F32)
    for i in range(1, CTX):
        total += recv_ref[i, 3 * HEAD :, :].astype(F32)
    out_ref[HEADROWS:, :] = total.astype(BF16)


def last_kernel(recv_ref, wa_ref, wb_ref, xt_ref, dh_ref, gains_ref, ig_ref, msg_ref):
    for head in range(HEADS):
        msg_ref[HEAD * head : HEAD * (head + 1), :] = recv_ref[head, 0:HEAD, :]
    for part in range(2):
        for j in range(KV_HEADS):
            total = None
            for g in range(GROUP):
                piece = recv_ref[j * GROUP + g, HEAD * (part + 1) : HEAD * (part + 2), :]
                piece = piece.astype(F32)
                total = piece if total is None else total + piece
            base = D + HEAD * (KV_HEADS * part + j)
            msg_ref[base : base + HEAD, :] = total.astype(BF16)
    da = dot(wa_ref[...], msg_ref[0:HALFW, :])
    da += dot(wb_ref[:, 0:KVW], msg_ref[D:QKV, :])
    da += dot(wb_ref[:, KVW : KVW + HEAD], msg_ref[HALFW:D, :])
    x = xt_ref[...].astype(F32)
    r1 = lax.rsqrt(jnp.mean(x * x, axis=0, keepdims=True) + EPS)
    scaled = wb_ref[:, KVW : KVW + 128].astype(F32)[:, 64:65] * da
    ig_ref[...] = (
        dh_ref[...].T
        + r1 * scaled
        - x * (r1 * r1 * r1) * jnp.mean(scaled * x, axis=0, keepdims=True)
    )


def unpack_kernel(
    ids_ref, mine_ref, other_ref, wq_ref, wkv_ref, gain_in, q_ref, kv_ref, o_ref, gain_ref
):
    for core in range(2):

        @pl.when(ids_ref[1] == core)
        def _(core=core):
            blocks = []
            for head in range(HEADS):
                src = mine_ref if head % 2 == core else other_ref
                blocks.append(src[head // 2].astype(F32))
            parts = [b[0:SHARD] for b in blocks]
            tails = [b[SHARD : SHARD + SHARD // 2] for b in blocks]
            zero = jnp.zeros((SHARD, HEAD), F32)
            query = [p[:, 0:HEAD] for p in parts]
            key = []
            value = []
            for j in range(KV_HEADS):
                group = parts[GROUP * j] + parts[GROUP * j + 1] + parts[GROUP * j + 2]
                key.append(group[:, HEAD:])
                group = tails[GROUP * j] + tails[GROUP * j + 1] + tails[GROUP * j + 2]
                value.append(jnp.concatenate([group[:, 0:HEAD], group[:, HEAD:]], axis=0))
            q = jnp.concatenate(query + [zero], axis=1)[:, 0:D]
            kv = jnp.concatenate(key + value, axis=1)
            q_ref[...] = q
            kv_ref[...] = kv
            total = jnp.sum(q * wq_ref[...].astype(F32), axis=1, keepdims=True)
            total += jnp.sum(kv * wkv_ref[...].astype(F32), axis=1, keepdims=True)
            total = jnp.broadcast_to(total, (SHARD, 128)).T[0:8]
            gain_ref[...] = total / gain_in[...].astype(F32)[None]
            for i, b in enumerate(blocks):
                cols = [b[HEADROWS + 16 * j : HEADROWS + 16 * (j + 1)] for j in range(8)]
                o_ref[16 * i : 16 * (i + 1), :] = jnp.concatenate(cols, axis=1)[:, 0:D]


def widen_kernel(
    ids_ref, mine_ref, other_ref, gu_in, gain_in, gu_out, down_out, gain_ref
):
    for core in range(2):

        @pl.when(ids_ref[1] == core)
        def _(core=core):
            halves = (mine_ref, other_ref) if core == 0 else (other_ref, mine_ref)
            total = None
            down = []
            for half, src in enumerate(halves):
                for s in range(FS):
                    at = lax.rem(ids_ref[0] + FS - s, FS) * FSL + FF * half
                    cols = pl.ds(pl.multiple_of(at, 128), FSL)
                    rows = [
                        src[r, 16 * s : 16 * (s + 1), :].astype(F32)[0:15] for r in range(CTX)
                    ]
                    rows = jnp.concatenate(rows, axis=0)
                    gu_out[:, cols] = rows
                    part = jnp.sum(rows * gu_in[:, cols].astype(F32), axis=1, keepdims=True)
                    total = part if total is None else total + part
                down += [src[r, 64:96, :].astype(F32)[0:30] for r in range(CTX)]
            down_out[...] = jnp.concatenate(down, axis=0)
            total = jnp.broadcast_to(total, (SHARD, 128)).T[0:8]
            gain_ref[...] = total / gain_in[...].astype(F32)[None]


def swap_core(value):
    return lax.ppermute(value, "ctx", [(i, i ^ 1) for i in range(CTX)])


def shift(value, step):
    return lax.ppermute(value, "fsdp", [((i + step) % FS, i) for i in range(FS)])


def same_core(value):
    groups = [[2 * i + core for i in range(CTX)] for core in range(2)]
    return lax.all_to_all(value, ("seq", "ctx"), 0, 0, axis_index_groups=groups)


def same_core_row(value):
    groups = [[2 * i + core for i in range(CTX // 2)] for core in range(2)]
    return lax.all_to_all(value, "ctx", 0, 0, axis_index_groups=groups)


def swap_seq(value):
    return lax.ppermute(value, "seq", [(0, 1), (1, 0)])


def gather_by(move, value):
    return [value] + [move(value, s) for s in range(1, 4)]


def scatter_by(move, pieces):
    return [pieces[0]] + [move(pieces[s], -s) for s in range(1, 4)]


def gather_rolled(value):
    return gather_by(shift, value)


def scatter_rolled(pieces):
    return scatter_by(shift, pieces)


def together(*values):
    return lax.optimization_barrier(values)


def shards(tokens, gain_attn, w_q, w_kv, w_o, gain_mlp, w_gate_up, w_down, block_order, cotangent):
    x_t = tokens[0].T
    g_t = cotangent[0].T
    down_t = w_down.T
    order = block_order[0]
    place = lax.axis_index("ctx")
    x_place = place // 8 * 2 + lax.axis_index("seq")
    ids = jnp.stack([lax.axis_index("fsdp"), place % 2, x_place, place // 2 % 4])
    ids = ids.astype(jnp.int32)

    slots = jnp.arange(2 * CTX, dtype=jnp.int32)
    inverse = jnp.sum(jnp.where(order[None, :] == slots[:, None], slots[None, :], 0), axis=1)
    mine = lax.dynamic_slice_in_dim(order, place * 2, 2)
    places = (mine[:, None] * BLK + jnp.arange(BLK, dtype=jnp.int32)[None, :]).reshape(ROWS)
    freq = THETA ** (-(jnp.arange(HALF, dtype=F32) * 2.0 / HEAD))
    angle = freq[:, None] * places.astype(F32)[None, :]
    angle_all = freq[:, None] * jnp.arange(L, dtype=F32)[None, :]

    (message,) = call(
        message_kernel,
        [shape(SHARD, HALFW)],
        [ids, w_q, w_kv, gain_attn, gain_mlp],
        smem=1,
    )
    w_mine = gather_rolled(message)
    w_other = [swap_core(piece) for piece in w_mine]
    *chunks, gu_local, wo_mine, wo_other = call(
        chunk_kernel,
        [shape(SHARD, FSL)] * (FS + 1) + [shape(128, D)] * 2,
        [ids, w_gate_up, w_o],
        smem=1,
    )
    w_mine, chunks, wo_mine, g_t = together(w_mine, chunks, wo_mine, g_t)
    gu_mine = scatter_rolled(chunks)
    wo_mine = gather_rolled(wo_mine)
    g_all = gather_rolled(g_t)

    packed, gains, w_a, w_b, a_t = call(
        qkv_kernel,
        [
            shape(CTX, 3 * HEAD, ROWS),
            shape(8, D, dtype=F32),
            shape(D, HALFW),
            shape(D, HALFW),
            shape(D, ROWS),
        ],
        [ids, x_t] + w_mine + w_other + [jnp.cos(angle), jnp.sin(angle)],
        smem=1,
        flops=2 * ROWS * D * QKV,
    )
    a_all = lax.all_gather(a_t, "ctx", axis=0)
    received = lax.all_to_all(packed, "ctx", 0, 0)
    o_part, q_t, k_t, k_n, v_t, o_f, lse = call(
        attend_kernel,
        [
            shape(CTX, HEAD, ROWS),
            shape(HEAD, L),
            shape(HEAD, L),
            shape(L, HEAD),
            shape(HEAD, L),
            shape(CTX, HEAD, ROWS, dtype=F32),
            shape(NT, 8, TILE, dtype=F32),
        ],
        [order, inverse, received],
        smem=2,
        scratch=[pltpu.VMEM((L, TILE), F32)],
        flops=2 * L * L * HEAD,
    )
    o_all = lax.all_to_all(o_part, "ctx", 0, 0)
    q_t, v_t, gu_mine, wo_mine = together(q_t, v_t, gu_mine, wo_mine)
    wo_other = [wo_other] + [swap_core(piece) for piece in wo_mine[1:]]
    gu_other = [gu_local] + [swap_core(piece) for piece in gu_mine[1:]]
    w_gu, w_out = call(
        place_kernel,
        [shape(D, 2 * FSL), shape(D, D)],
        [ids] + gu_mine + gu_other + wo_mine + wo_other,
        smem=1,
    )
    q_n, v_n, cos_all, sin_all = q_t.T, v_t.T, jnp.cos(angle_all), jnp.sin(angle_all)
    o_all, w_gu, w_out, q_n, v_n, cos_all, sin_all = together(
        o_all, w_gu, w_out, q_n, v_n, cos_all, sin_all
    )
    h, b, *o_pieces = call(
        resid_kernel,
        [shape(ROWS, D, dtype=F32), shape(ROWS, D)] + [shape(SHARD, ROWS)] * FS,
        [ids, o_all, w_out, x_t, gains],
        smem=1,
        scratch=[pltpu.VMEM((D, ROWS), BF16)],
        flops=2 * ROWS * D * D,
    )
    b_all = gather_rolled(b)
    db, mm, dgu = [None] * FS, [None] * FS, [None] * FS
    before = None
    for s in (0, 1, 3, 2):
        if before is not None:
            b_all[s], before = together(b_all[s], before)
        db[s], mm[s], dgu[s] = call(
            mlp_kernel,
            [shape(ROWS, D), shape(ROWS, FSL), shape(ROWS, 2 * FSL)],
            [b_all[s], g_all[s], w_gu, down_t],
            flops=10 * ROWS * D * FSL,
        )
        before = mm[s]
    db = scatter_rolled(db)
    *y_parts, keep, give = call(
        mlp_grad_kernel,
        [shape(ROWS, D)] * FS + [shape(HALF_ROWS, FSL)] * 2,
        [ids] + b_all + g_all + mm + dgu + [down_t],
        smem=1,
        scratch=[pltpu.VMEM((D, 2 * FSL), BF16), pltpu.VMEM((D, FSL), BF16)],
        flops=8 * FS * ROWS * D * FSL,
    )
    db, keep, give = together(db, keep, give)
    got = swap_core(give)
    dh, e, do_part = call(
        mid_kernel,
        [shape(ROWS, D, dtype=F32), shape(ROWS, D), shape(CTX, HEAD, ROWS)],
        db + [h, g_t, gains, w_out],
        flops=2 * ROWS * D * D,
    )
    do_all = lax.all_to_all(do_part, "ctx", 0, 0)
    (half_sum,) = call(
        pack_kernel,
        [shape(CTX, 96, FSL)],
        [keep, got],
        scratch=[pltpu.VMEM((HALF_ROWS + 16, FSL), F32)],
    )
    e_all = gather_rolled(e)
    do_all, half_sum = together(do_all, half_sum)
    half_parts = same_core(half_sum)
    (dqkv_part,) = call(
        attend_back_kernel,
        [shape(CTX, 3 * HEAD, ROWS)],
        [order, inverse, do_all, q_t, q_n, k_t, k_n, v_n, o_f, lse, cos_all, sin_all],
        smem=2,
        scratch=[
            pltpu.VMEM((HEAD, L), BF16),
            pltpu.VMEM((L, HEAD), BF16),
            pltpu.VMEM((8, L), F32),
            pltpu.VMEM((L, HEAD), F32),
            pltpu.VMEM((L, HEAD), F32),
            pltpu.VMEM((CTX, 3 * HEAD, ROWS), F32),
        ],
        flops=5 * L * L * HEAD,
    )
    o_slices = scatter_rolled(o_pieces)
    (o_grad,) = call(
        out_grad_kernel,
        [shape(CTX, 128, 128)],
        o_slices + e_all,
        flops=2 * FS * ROWS * SHARD * D,
    )
    half_parts, message = together(half_parts, jnp.concatenate([dqkv_part, o_grad], axis=1))
    dqkv = lax.all_to_all(message, "ctx", 0, 0)
    head_pieces = call(
        head_grad_kernel,
        [shape(HEADROWS, 128)] * FS,
        [ids, a_all, dqkv_part],
        smem=1,
        scratch=[pltpu.VMEM((D, 3 * HEAD), BF16)],
        flops=2 * L * D * 3 * HEAD,
    )
    head_pieces = scatter_rolled(head_pieces)
    *pieces, down_sum = call(
        reduce_kernel,
        [shape(16, FSL)] * FS + [shape(32, FSL)],
        [ids, half_parts],
        smem=1,
        scratch=[pltpu.VMEM((96, FSL), BF16)],
    )
    own = jnp.concatenate(scatter_rolled(pieces) + [down_sum], axis=0)
    y = scatter_rolled(y_parts)
    dqkv, own, head_pieces = together(dqkv, own, head_pieces)
    mine_all = same_core(jnp.broadcast_to(own[None], (CTX, 96, FSL)))
    (head_sum,) = call(head_sum_kernel, [shape(HEADROWS + 128, 128)], head_pieces + [dqkv])
    head_sum = (head_sum.astype(F32) + swap_seq(head_sum).astype(F32)).astype(BF16)
    (input_grad,) = call(
        last_kernel,
        [shape(D, ROWS, dtype=F32)],
        [dqkv, w_a, w_b, x_t, dh, gains],
        scratch=[pltpu.VMEM((QKV, ROWS), BF16)],
        flops=2 * ROWS * D * QKV,
    )
    (result,) = call(result_kernel, [shape(D, ROWS)], [h] + y)
    mine_all, head_sum, input_grad, result = together(mine_all, head_sum, input_grad, result)
    head_mine = same_core_row(jnp.broadcast_to(head_sum[None], (CTX // 2, HEADROWS + 128, 128)))
    gu_out, down_out, gain_two = call(
        widen_kernel,
        [
            shape(SHARD, 2 * FF, dtype=F32),
            shape(D, FSL, dtype=F32),
            shape(8, SHARD, dtype=F32),
        ],
        [ids, mine_all, swap_core(mine_all), w_gate_up, gain_mlp],
        smem=1,
    )
    head_mine, gu_out, down_out, gain_two = together(head_mine, gu_out, down_out, gain_two)
    q_out, kv_out, o_out, gain_one = call(
        unpack_kernel,
        [
            shape(SHARD, D, dtype=F32),
            shape(SHARD, KVW, dtype=F32),
            shape(SHARD, D, dtype=F32),
            shape(8, SHARD, dtype=F32),
        ],
        [ids, head_mine, swap_core(head_mine), w_q, w_kv, gain_attn],
        smem=1,
    )
    return (
        result.T[None],
        input_grad.T[None],
        gain_one[0],
        q_out,
        kv_out,
        o_out,
        gain_two[0],
        gu_out,
        down_out.T,
    )


def solution(mesh):
    tokens = P(("seq", "fsdp"), "ctx", None)
    return jax.shard_map(
        shards,
        mesh=mesh,
        in_specs=(
            tokens,
            P("fsdp"),
            P("fsdp", None),
            P("fsdp", None),
            P("fsdp", None),
            P("fsdp"),
            P("fsdp", None),
            P("fsdp", None),
            P(("seq", "fsdp"), None),
            tokens,
        ),
        out_specs=(
            tokens,
            tokens,
            P("fsdp"),
            P("fsdp", None),
            P("fsdp", None),
            P("fsdp", None),
            P("fsdp"),
            P("fsdp", None),
            P("fsdp", None),
        ),
        check_vma=False,
    )
```

```python
import jax
import jax.numpy as jnp
from jax import lax
from jax.experimental import pallas as pl
from jax.experimental.pallas import tpu as pltpu
from jax.sharding import PartitionSpec as P

D = 960
HEADS = 15
KV_HEADS = 5
GROUP = 3
HEAD = 64
HALF = 32
FF = 2560
BLK = 64
L = 2048
CTX = 16
FS = 4
ROWS = 128
QKV = 1600
HEADROWS = 368
EO = 1280
HALFW = 896
KVW = 640
HALF_ROWS = D + D // 2
SHARD = D // FS
FSL = FF // FS
TILE = 256
NT = L // TILE
EPS = 1e-05
THETA = 100000.0
SCALE = HEAD**-0.5
F32 = jnp.float32
BF16 = jnp.bfloat16
VMEM_BYTES = 32 * 1024 * 1024


def call(kernel, outs, args, smem=0, scratch=(), flops=0):
    specs = [pl.BlockSpec(memory_space=pltpu.SMEM)] * smem
    specs += [pl.BlockSpec(memory_space=pltpu.VMEM)] * (len(args) - smem)
    moved = sum(a.size * a.dtype.itemsize for a in list(args) + list(outs))
    return pl.pallas_call(
        kernel,
        out_shape=outs,
        in_specs=specs,
        out_specs=[pl.BlockSpec(memory_space=pltpu.VMEM)] * len(outs),
        scratch_shapes=list(scratch),
        cost_estimate=pl.CostEstimate(flops=flops, bytes_accessed=moved, transcendentals=0),
        compiler_params=pltpu.CompilerParams(vmem_limit_bytes=VMEM_BYTES),
    )(*args)


def shape(*dims, dtype=BF16):
    return jax.ShapeDtypeStruct(dims, dtype)


def dot(left, right, a=1, b=0):
    return lax.dot_general(left, right, (((a,), (b,)), ((), ())), preferred_element_type=F32)


def inv_norm(rows):
    return lax.rsqrt(jnp.mean(rows * rows, axis=-1, keepdims=True) + EPS)


def message_kernel(ids_ref, wq_ref, wkv_ref, g1_ref, g2_ref, out_ref):
    core = ids_ref[1]

    @pl.when(core == 0)
    def _():
        out_ref[...] = wq_ref[:, 0:HALFW]

    @pl.when(core == 1)
    def _():
        out_ref[:, 0:KVW] = wkv_ref[...]
        one = jnp.broadcast_to(g1_ref[...].astype(F32)[None], (128, SHARD)).T
        two = jnp.broadcast_to(g2_ref[...].astype(F32)[None], (128, SHARD)).T
        lane = lax.broadcasted_iota(jnp.int32, (SHARD, 128), 1)
        rest = wq_ref[:, HALFW:D].astype(F32)
        rest = jnp.concatenate([rest, jnp.zeros((SHARD, 64), F32)], axis=1)
        rest = jnp.where(lane == 64, one, jnp.where(lane == 65, two, rest))
        out_ref[:, KVW : KVW + 128] = rest.astype(BF16)
        out_ref[:, KVW + 128 : HALFW] = jnp.zeros((SHARD, HALFW - KVW - 128), BF16)


def chunk_kernel(ids_ref, gu_ref, *out_refs):
    fs = ids_ref[0]
    for s in range(FS):
        at = pl.multiple_of(lax.rem(fs + s, FS) * FSL, 128)
        out_refs[s][:, 0:FSL] = gu_ref[:, pl.ds(at, FSL)]
        out_refs[s][:, FSL : 2 * FSL] = gu_ref[:, pl.ds(FF + at, FSL)]


def place_gate_up_kernel(ids_ref, *refs):
    for s in range(FS):
        at = pl.multiple_of(lax.rem(ids_ref[0] + FS - s, FS) * SHARD, 16)
        refs[FS][pl.ds(at, SHARD), :] = refs[s][...]


def qkv_kernel(ids_ref, xt_ref, *refs):
    mine = refs[0:FS]
    other = refs[FS : 2 * FS]
    cos_ref, sin_ref, out_ref, gains_ref, wa_ref, wb_ref, at_ref = refs[2 * FS :]
    fs = ids_ref[0]
    core = ids_ref[1]

    def fill(first, second):
        for s in range(FS):
            at = pl.multiple_of(lax.rem(fs + s, FS) * SHARD, 16)
            wa_ref[pl.ds(at, SHARD), :] = first[s][...]
            wb_ref[pl.ds(at, SHARD), :] = second[s][...]

    @pl.when(core == 0)
    def _():
        fill(mine, other)

    @pl.when(core == 1)
    def _():
        fill(other, mine)

    xt = xt_ref[...].astype(F32)
    gains = wb_ref[:, KVW : KVW + 128].astype(F32)
    gains_ref[...] = gains.T[64:72, :]
    r1 = lax.rsqrt(jnp.mean(xt * xt, axis=0, keepdims=True) + EPS)
    at = xt * r1 * gains[:, 64:65]
    at_ref[...] = at.astype(BF16)
    a = at.T.astype(BF16)
    lin_a = dot(a, wa_ref[...]).T
    lin_b = dot(a, wb_ref[...]).T
    cos = cos_ref[...]
    sin = sin_ref[...]

    def turned(rows):
        first = rows[0:HALF]
        second = rows[HALF:HEAD]
        return jnp.concatenate(
            [first * cos - second * sin, second * cos + first * sin], axis=0
        ).astype(BF16)

    for j in range(KV_HEADS):
        key = turned(lin_b[HEAD * j : HEAD * (j + 1)])
        value = lin_b[HEAD * (KV_HEADS + j) : HEAD * (KV_HEADS + j + 1)].astype(BF16)
        for g in range(GROUP):
            head = j * GROUP + g
            if head < HEADS - 1:
                rows = lin_a[HEAD * head : HEAD * (head + 1)]
            else:
                rows = lin_b[KVW : KVW + HEAD]
            out_ref[head, 0:HEAD, :] = turned(rows)
            out_ref[head, HEAD : 2 * HEAD, :] = key
            out_ref[head, 2 * HEAD : 3 * HEAD, :] = value
    out_ref[HEADS, :, :] = jnp.zeros((3 * HEAD, ROWS), BF16)


def pick_pair(load, first, second):
    left = load(first // 2).astype(F32)
    right = load(second // 2).astype(F32)
    left = pltpu.roll(left, (first % 2) * BLK, 1)
    right = pltpu.roll(right, (1 - second % 2) * BLK, 1)
    lane = lax.broadcasted_iota(jnp.int32, left.shape, 1)
    return jnp.where(lane < BLK, left, right)


def causal(size):
    key = lax.broadcasted_iota(jnp.int32, (size, size), 0)
    query = lax.broadcasted_iota(jnp.int32, (size, size), 1)
    return key <= query


def attend_kernel(
    order_ref, inv_ref, recv_ref, out_ref, qt_ref, kt_ref, k_ref, vt_ref, of_ref, lse_ref, s_ref
):
    for m in range(CTX):
        got = pick_pair(lambda i: recv_ref[i], inv_ref[2 * m], inv_ref[2 * m + 1])
        at = slice(2 * BLK * m, 2 * BLK * (m + 1))
        qt_ref[:, at] = (got[0:HEAD] * SCALE).astype(BF16)
        key = got[HEAD : 2 * HEAD]
        kt_ref[:, at] = key.astype(BF16)
        k_ref[at, :] = key.T.astype(BF16)
        vt_ref[:, at] = got[2 * HEAD : 3 * HEAD].astype(BF16)
    allowed = causal(TILE)
    for n in range(NT):
        span = slice(TILE * n, TILE * (n + 1))
        query = qt_ref[:, span]
        top = None
        for c in range(n + 1):
            rows = slice(TILE * c, TILE * (c + 1))
            s = dot(k_ref[rows, :], query)
            if c == n:
                s = jnp.where(allowed, s, -1e30)
            s_ref[rows, :] = s
            part = jnp.max(s, axis=0, keepdims=True)
            top = part if top is None else jnp.maximum(top, part)
        total = None
        for c in range(n + 1):
            rows = slice(TILE * c, TILE * (c + 1))
            e = jnp.exp(s_ref[rows, :] - top)
            s_ref[rows, :] = e
            part = jnp.sum(e, axis=0, keepdims=True)
            total = part if total is None else total + part
        recip = 1.0 / total
        lse_ref[n] = jnp.broadcast_to(top + jnp.log(total), (8, TILE))
        prob = (s_ref[0 : TILE * (n + 1), :] * recip).astype(BF16)
        o = dot(vt_ref[:, 0 : TILE * (n + 1)], prob)
        of_ref[2 * n] = o[:, 0 : 2 * BLK]
        of_ref[2 * n + 1] = o[:, 2 * BLK :]
    for i in range(CTX):
        got = pick_pair(lambda g: of_ref[g], order_ref[2 * i], order_ref[2 * i + 1])
        out_ref[i] = got.astype(BF16)


def attend_back_kernel(
    order_ref,
    inv_ref,
    recv_ref,
    qt_ref,
    q_ref,
    kt_ref,
    k_ref,
    v_ref,
    of_ref,
    lse_ref,
    cos_ref,
    sin_ref,
    out_ref,
    dot_ref,
    do_ref,
    delta_ref,
    dk_ref,
    dv_ref,
    st_ref,
):
    for m in range(CTX):
        got = pick_pair(lambda i: recv_ref[i], inv_ref[2 * m], inv_ref[2 * m + 1])
        at = slice(2 * BLK * m, 2 * BLK * (m + 1))
        dot_ref[:, at] = got.astype(BF16)
        do_ref[at, :] = got.T.astype(BF16)
        delta_ref[:, at] = jnp.broadcast_to(
            jnp.sum(got * of_ref[m], axis=0, keepdims=True), (8, 2 * BLK)
        )
    allowed = causal(TILE)
    for n in range(NT):
        span = slice(TILE * n, TILE * (n + 1))
        query = qt_ref[:, span]
        out_grad = dot_ref[:, span]
        lse = lse_ref[n][0:1, :]
        delta = delta_ref[0:1, span]
        dq = None
        for c in range(n + 1):
            rows = slice(TILE * c, TILE * (c + 1))
            prob = jnp.exp(dot(k_ref[rows, :], query) - lse)
            if c == n:
                prob = jnp.where(allowed, prob, 0.0)
            ds = (prob * (dot(v_ref[rows, :], out_grad) - delta)).astype(BF16)
            part = dot(kt_ref[:, rows], ds)
            dq = part if dq is None else dq + part
            dk = dot(ds, q_ref[span, :])
            dv = dot(prob.astype(BF16), do_ref[span, :])
            if c == n:
                dk_ref[rows, :] = dk
                dv_ref[rows, :] = dv
            else:
                dk_ref[rows, :] += dk
                dv_ref[rows, :] += dv
        st_ref[2 * n, 0:HEAD, :] = dq[:, 0 : 2 * BLK] * SCALE
        st_ref[2 * n + 1, 0:HEAD, :] = dq[:, 2 * BLK :] * SCALE
    for m in range(CTX):
        at = slice(2 * BLK * m, 2 * BLK * (m + 1))
        cos = cos_ref[:, at]
        sin = sin_ref[:, at]

        def turned(value):
            first = value[0:HALF]
            second = value[HALF:HEAD]
            return jnp.concatenate(
                [first * cos + second * sin, second * cos - first * sin], axis=0
            )

        st_ref[m, 0:HEAD, :] = turned(st_ref[m, 0:HEAD, :])
        st_ref[m, HEAD : 2 * HEAD, :] = turned(dk_ref[at, :].T)
        st_ref[m, 2 * HEAD : 3 * HEAD, :] = dv_ref[at, :].T
    for i in range(CTX):
        got = pick_pair(lambda g: st_ref[g], order_ref[2 * i], order_ref[2 * i + 1])
        out_ref[i] = got.astype(BF16)


def resid_kernel(ids_ref, ot_ref, w_ref, xt_ref, gains_ref, h_ref, b_ref, *refs):
    full_ref = refs[FS]
    flat = jnp.concatenate([ot_ref[h] for h in range(HEADS)], axis=0)
    full_ref[...] = flat
    for s in range(FS):
        at = pl.multiple_of(lax.rem(ids_ref[0] + s, FS) * SHARD, 16)
        refs[s][...] = full_ref[pl.ds(at, SHARD), :]
    mixed = flat.astype(F32).T.astype(BF16)
    h = xt_ref[...].astype(F32).T + dot(mixed, w_ref[...])
    h_ref[...] = h
    b_ref[...] = (h * inv_norm(h) * gains_ref[1:2, :]).astype(BF16)


def mlp_kernel(*refs):
    count = (len(refs) - 2) // 5
    b_refs = refs[0:count]
    g_refs = refs[count : 2 * count]
    gu_ref, down_ref = refs[2 * count : 2 * count + 2]
    outs = refs[2 * count + 2 :]
    for i in range(count):
        db_ref, mm_ref, dgu_ref = outs[3 * i : 3 * i + 3]
        gu = dot(b_refs[i][...], gu_ref[...])
        gate = gu[:, :FSL]
        up = gu[:, FSL:]
        sig = 1.0 / (1.0 + jnp.exp(-gate))
        act = gate * sig
        dm = dot(g_refs[i][...], down_ref[...], 0, 0)
        dgate = dm * up * sig * (1.0 + gate * (1.0 - sig))
        dgu = jnp.concatenate([dgate, dm * act], axis=1).astype(BF16)
        mm_ref[...] = (act * up).astype(BF16)
        dgu_ref[...] = dgu
        db_ref[...] = dot(dgu, gu_ref[...], 1, 1).astype(BF16)


def mlp_grad_kernel(ids_ref, *refs):
    b_refs = refs[0:FS]
    g_refs = refs[FS : 2 * FS]
    mm_refs = refs[2 * FS : 3 * FS]
    dgu_refs = refs[3 * FS : 4 * FS]
    down_ref = refs[4 * FS]
    y_refs = refs[4 * FS + 1 : 5 * FS + 1]
    keep_ref, give_ref, gu_ref, dd_ref = refs[5 * FS + 1 :]
    b = jnp.concatenate([r[...] for r in b_refs], axis=0)
    gt = jnp.concatenate([r[...] for r in g_refs], axis=1)
    mm = jnp.concatenate([r[...] for r in mm_refs], axis=0)
    dgu = jnp.concatenate([r[...] for r in dgu_refs], axis=0)
    gu_ref[...] = dot(b, dgu, 0, 0).astype(BF16)
    dd_ref[...] = dot(gt, mm).astype(BF16)

    def put(out_ref, half):
        out_ref[0:D, :] = gu_ref[:, FSL * half : FSL * (half + 1)]
        out_ref[D : D + D // 2, :] = dd_ref[D // 2 * half : D // 2 * (half + 1), :]

    for core in range(2):

        @pl.when(ids_ref[1] == core)
        def _(core=core):
            put(keep_ref, core)
            put(give_ref, 1 - core)

    for s in range(FS):
        y_refs[s][...] = dot(mm_refs[s][...], down_ref[...], 1, 1).astype(BF16)


def result_kernel(h_ref, y0, y1, y2, y3, out_ref):
    total = h_ref[...]
    for piece in (y0, y1, y2, y3):
        total += piece[...].astype(F32)
    out_ref[...] = total.T.astype(BF16)


def pack_kernel(keep_ref, got_ref, out_ref, sum_ref):
    for at in range(0, HALF_ROWS, 240):
        rows = slice(at, at + 240)
        sum_ref[rows, :] = keep_ref[rows, :].astype(F32) + got_ref[rows, :].astype(F32)
    sum_ref[HALF_ROWS:, :] = jnp.zeros((16, FSL), F32)
    for r in range(CTX):
        for k in range(FS):
            at = SHARD * k + 15 * r
            out_ref[r, 16 * k : 16 * (k + 1), :] = sum_ref[at : at + 16, :].astype(BF16)
        at = D + 30 * r
        out_ref[r, 64:96, :] = sum_ref[at : at + 32, :].astype(BF16)


def reduce_kernel(ids_ref, parts_ref, p0, p1, p2, p3, rest_ref, sum_ref):
    total = parts_ref[0].astype(F32)
    for r in range(1, CTX):
        total += parts_ref[r].astype(F32)
    sum_ref[...] = total.astype(BF16)
    for s, piece in enumerate((p0, p1, p2, p3)):
        at = pl.multiple_of(lax.rem(ids_ref[0] + s, FS) * 16, 16)
        piece[...] = sum_ref[pl.ds(at, 16), :]
    rest_ref[...] = sum_ref[64:96, :]


def mid_kernel(*refs):
    db_refs = refs[0:FS]
    h_ref, gt_ref, gains_ref, w_ref = refs[FS : FS + 4]
    o_refs = refs[FS + 4 : 2 * FS + 4]
    dh_ref, do_ref = refs[2 * FS + 4 : 2 * FS + 6]
    out_refs = refs[2 * FS + 6 :]
    db = db_refs[0][...].astype(F32)
    for ref in db_refs[1:]:
        db += ref[...].astype(F32)
    h = h_ref[...]
    r2 = inv_norm(h)
    scaled = gains_ref[1:2, :] * db
    dh = (
        gt_ref[...].astype(F32).T
        + r2 * scaled
        - h * (r2 * r2 * r2) * jnp.mean(scaled * h, axis=-1, keepdims=True)
    )
    dh_ref[...] = dh
    e = dh.astype(BF16)
    back = dot(w_ref[...], e, 1, 1).astype(BF16)
    for head in range(HEADS):
        do_ref[head] = back[HEAD * head : HEAD * (head + 1)]
    do_ref[HEADS] = jnp.zeros((HEAD, ROWS), BF16)
    for s in range(FS):
        out_refs[s][:, 0:D] = e
        o = jnp.concatenate([o_refs[s][...].astype(F32), jnp.zeros((80, ROWS), F32)], axis=0)
        out_refs[s][:, D:EO] = o.T.astype(BF16)


def head_grad_kernel(ids_ref, at_ref, d_ref, *refs):
    full_ref = refs[FS]
    total = None
    for i in range(0, CTX, 2):
        left = jnp.concatenate([at_ref[i], at_ref[i + 1]], axis=1)
        right = jnp.concatenate([d_ref[i], d_ref[i + 1]], axis=1)
        part = dot(left, right, 1, 1)
        total = part if total is None else total + part
    full_ref[...] = total.astype(BF16)
    for s in range(FS):
        at = pl.multiple_of(lax.rem(ids_ref[0] + s, FS) * SHARD, 16)
        rows = full_ref[pl.ds(at, SHARD), :]
        refs[s][0:SHARD, :] = rows[:, 0:128]
        value = rows[:, 128:192].astype(F32)
        value = jnp.concatenate([value[0 : SHARD // 2], value[SHARD // 2 :]], axis=1)
        value = jnp.concatenate([value, jnp.zeros((8, 128), F32)], axis=0)
        refs[s][SHARD:HEADROWS, :] = value.astype(BF16)


def out_grad_kernel(*refs):
    part_ref, out_ref = refs[FS:]
    total = None
    for s in range(FS):
        message = refs[s]
        part = dot(message[:, D:EO], message[:, 0:D], 0, 0)[0:SHARD]
        total = part if total is None else total + part
    pad = jnp.zeros((SHARD, 64), F32)
    total = jnp.concatenate([total, pad], axis=1).astype(BF16)
    out_ref[:, 0 : 3 * HEAD, :] = part_ref[...]
    for i in range(HEADS):
        for j in range(8):
            at = 3 * HEAD + 16 * j
            out_ref[i, at : at + 16, :] = total[16 * i : 16 * (i + 1), 128 * j : 128 * (j + 1)]
    out_ref[HEADS, 3 * HEAD :, :] = jnp.zeros((128, 128), BF16)


def head_sum_kernel(p0, p1, p2, p3, recv_ref, out_ref):
    total = p0[...].astype(F32)
    for piece in (p1, p2, p3):
        total += piece[...].astype(F32)
    out_ref[0:HEADROWS, :] = total.astype(BF16)
    total = recv_ref[0, 3 * HEAD :, :].astype(F32)
    for i in range(1, CTX):
        total += recv_ref[i, 3 * HEAD :, :].astype(F32)
    out_ref[HEADROWS:, :] = total.astype(BF16)


def last_kernel(recv_ref, wa_ref, wb_ref, xt_ref, dh_ref, gains_ref, ig_ref, msg_ref):
    for head in range(HEADS):
        msg_ref[HEAD * head : HEAD * (head + 1), :] = recv_ref[head, 0:HEAD, :]
    for part in range(2):
        for j in range(KV_HEADS):
            total = None
            for g in range(GROUP):
                piece = recv_ref[j * GROUP + g, HEAD * (part + 1) : HEAD * (part + 2), :]
                piece = piece.astype(F32)
                total = piece if total is None else total + piece
            base = D + HEAD * (KV_HEADS * part + j)
            msg_ref[base : base + HEAD, :] = total.astype(BF16)
    da = dot(wa_ref[...], msg_ref[0:HALFW, :])
    da += dot(wb_ref[:, 0:KVW], msg_ref[D:QKV, :])
    da += dot(wb_ref[:, KVW : KVW + HEAD], msg_ref[HALFW:D, :])
    x = xt_ref[...].astype(F32)
    r1 = lax.rsqrt(jnp.mean(x * x, axis=0, keepdims=True) + EPS)
    scaled = wb_ref[:, KVW : KVW + 128].astype(F32)[:, 64:65] * da
    ig_ref[...] = (
        dh_ref[...].T
        + r1 * scaled
        - x * (r1 * r1 * r1) * jnp.mean(scaled * x, axis=0, keepdims=True)
    )


def unpack_kernel(
    ids_ref, mine_ref, other_ref, wq_ref, wkv_ref, gain_in, q_ref, kv_ref, o_ref, gain_ref
):
    for core in range(2):

        @pl.when(ids_ref[1] == core)
        def _(core=core):
            blocks = []
            for head in range(HEADS):
                src = mine_ref if head % 2 == core else other_ref
                blocks.append(src[head // 2].astype(F32))
            parts = [b[0:SHARD] for b in blocks]
            tails = [b[SHARD : SHARD + SHARD // 2] for b in blocks]
            zero = jnp.zeros((SHARD, HEAD), F32)
            query = [p[:, 0:HEAD] for p in parts]
            key = []
            value = []
            for j in range(KV_HEADS):
                group = parts[GROUP * j] + parts[GROUP * j + 1] + parts[GROUP * j + 2]
                key.append(group[:, HEAD:])
                group = tails[GROUP * j] + tails[GROUP * j + 1] + tails[GROUP * j + 2]
                value.append(jnp.concatenate([group[:, 0:HEAD], group[:, HEAD:]], axis=0))
            q = jnp.concatenate(query + [zero], axis=1)[:, 0:D]
            kv = jnp.concatenate(key + value, axis=1)
            q_ref[...] = q
            kv_ref[...] = kv
            total = jnp.sum(q * wq_ref[...].astype(F32), axis=1, keepdims=True)
            total += jnp.sum(kv * wkv_ref[...].astype(F32), axis=1, keepdims=True)
            total = jnp.broadcast_to(total, (SHARD, 128)).T[0:8]
            gain_ref[...] = total[0] / gain_in[...].astype(F32)
            for i, b in enumerate(blocks):
                cols = [b[HEADROWS + 16 * j : HEADROWS + 16 * (j + 1)] for j in range(8)]
                o_ref[16 * i : 16 * (i + 1), :] = jnp.concatenate(cols, axis=1)[:, 0:D]


def widen_kernel(
    ids_ref, mine_ref, other_ref, gu_in, gain_in, gu_out, down_out, gain_ref
):
    for core in range(2):

        @pl.when(ids_ref[1] == core)
        def _(core=core):
            halves = (mine_ref, other_ref) if core == 0 else (other_ref, mine_ref)
            total = None
            down = []
            for half, src in enumerate(halves):
                for s in range(FS):
                    at = lax.rem(ids_ref[0] + FS - s, FS) * FSL + FF * half
                    cols = pl.ds(pl.multiple_of(at, 128), FSL)
                    rows = [
                        src[r, 16 * s : 16 * (s + 1), :].astype(F32)[0:15] for r in range(CTX)
                    ]
                    rows = jnp.concatenate(rows, axis=0)
                    gu_out[:, cols] = rows
                    part = jnp.sum(rows * gu_in[:, cols].astype(F32), axis=1, keepdims=True)
                    total = part if total is None else total + part
                down += [src[r, 64:96, :].astype(F32)[0:30] for r in range(CTX)]
            down_out[...] = jnp.concatenate(down, axis=0)
            total = jnp.broadcast_to(total, (SHARD, 128)).T[0:8]
            gain_ref[...] = total[0] / gain_in[...].astype(F32)


def swap_core(value):
    return lax.ppermute(value, "ctx", [(i, i ^ 1) for i in range(CTX)])


def shift(value, step):
    return lax.ppermute(value, "fsdp", [((i + step) % FS, i) for i in range(FS)])


def same_core(value):
    groups = [[2 * i + core for i in range(CTX)] for core in range(2)]
    return lax.all_to_all(value, ("seq", "ctx"), 0, 0, axis_index_groups=groups)


def same_core_row(value):
    groups = [[2 * i + core for i in range(CTX // 2)] for core in range(2)]
    return lax.all_to_all(value, "ctx", 0, 0, axis_index_groups=groups)


def swap_seq(value):
    return lax.ppermute(value, "seq", [(0, 1), (1, 0)])


def gather_by(move, value):
    return [value] + [move(value, s) for s in range(1, 4)]


def scatter_by(move, pieces):
    return [pieces[0]] + [move(pieces[s], -s) for s in range(1, 4)]


def gather_rolled(value):
    return gather_by(shift, value)


def scatter_rolled(pieces):
    return scatter_by(shift, pieces)


def together(*values):
    return lax.optimization_barrier(values)


def shards(tokens, gain_attn, w_q, w_kv, w_o, gain_mlp, w_gate_up, w_down, block_order, cotangent):
    x_t = tokens[0].T
    g_t = cotangent[0].T
    down_t = w_down.T
    order = block_order[0]
    place = lax.axis_index("ctx")
    x_place = place // 8 * 2 + lax.axis_index("seq")
    ids = jnp.stack([lax.axis_index("fsdp"), place % 2, x_place, place // 2 % 4])
    ids = ids.astype(jnp.int32)

    slots = jnp.arange(2 * CTX, dtype=jnp.int32)
    inverse = jnp.sum(jnp.where(order[None, :] == slots[:, None], slots[None, :], 0), axis=1)
    mine = lax.dynamic_slice_in_dim(order, place * 2, 2)
    places = (mine[:, None] * BLK + jnp.arange(BLK, dtype=jnp.int32)[None, :]).reshape(ROWS)
    freq = THETA ** (-(jnp.arange(HALF, dtype=F32) * 2.0 / HEAD))
    angle = freq[:, None] * places.astype(F32)[None, :]
    angle_all = freq[:, None] * jnp.arange(L, dtype=F32)[None, :]

    (message,) = call(
        message_kernel,
        [shape(SHARD, HALFW)],
        [ids, w_q, w_kv, gain_attn, gain_mlp],
        smem=1,
    )
    w_mine = gather_rolled(message)
    chunks = call(chunk_kernel, [shape(SHARD, 2 * FSL)] * FS, [ids, w_gate_up], smem=1)
    w_mine, chunks, w_o, g_t = together(w_mine, chunks, w_o, g_t)
    w_other = [swap_core(message)] + [swap_core(piece) for piece in w_mine[1:]]
    w_out = lax.all_gather(w_o, "fsdp", axis=0, tiled=True)
    gu_pieces = scatter_rolled(chunks)
    g_all = gather_rolled(g_t)

    packed, gains, w_a, w_b, a_t = call(
        qkv_kernel,
        [
            shape(CTX, 3 * HEAD, ROWS),
            shape(8, D, dtype=F32),
            shape(D, HALFW),
            shape(D, HALFW),
            shape(D, ROWS),
        ],
        [ids, x_t] + w_mine + w_other + [jnp.cos(angle), jnp.sin(angle)],
        smem=1,
        flops=2 * ROWS * D * QKV,
    )
    a_all = lax.all_gather(a_t, "ctx", axis=0)
    received = lax.all_to_all(packed, "ctx", 0, 0)
    o_part, q_t, k_t, k_n, v_t, o_f, lse = call(
        attend_kernel,
        [
            shape(CTX, HEAD, ROWS),
            shape(HEAD, L),
            shape(HEAD, L),
            shape(L, HEAD),
            shape(HEAD, L),
            shape(CTX, HEAD, ROWS, dtype=F32),
            shape(NT, 8, TILE, dtype=F32),
        ],
        [order, inverse, received],
        smem=2,
        scratch=[pltpu.VMEM((L, TILE), F32)],
        flops=2 * L * L * HEAD,
    )
    o_all = lax.all_to_all(o_part, "ctx", 0, 0)
    q_n, v_n = q_t.T, v_t.T
    (w_gu,) = call(place_gate_up_kernel, [shape(D, 2 * FSL)], [ids] + gu_pieces, smem=1)
    cos_all, sin_all = jnp.cos(angle_all), jnp.sin(angle_all)
    o_all, w_out, q_n, v_n, cos_all, sin_all = together(
        o_all, w_out, q_n, v_n, cos_all, sin_all
    )
    h, b, *o_pieces = call(
        resid_kernel,
        [shape(ROWS, D, dtype=F32), shape(ROWS, D)] + [shape(SHARD, ROWS)] * FS,
        [ids, o_all, w_out, x_t, gains],
        smem=1,
        scratch=[pltpu.VMEM((D, ROWS), BF16)],
        flops=2 * ROWS * D * D,
    )
    b, w_gu, g_all = together(b, w_gu, g_all)
    b_all = gather_rolled(b)
    db, mm, dgu = [None] * FS, [None] * FS, [None] * FS
    before = None
    for partners in ((0,), (1, 3), (2,)):
        if before is not None:
            b_all[partners[0]], before = together(b_all[partners[0]], before)
        outs = call(
            mlp_kernel,
            [shape(ROWS, D), shape(ROWS, FSL), shape(ROWS, 2 * FSL)] * len(partners),
            [b_all[s] for s in partners] + [g_all[s] for s in partners] + [w_gu, down_t],
            flops=10 * len(partners) * ROWS * D * FSL,
        )
        for i, s in enumerate(partners):
            db[s], mm[s], dgu[s] = outs[3 * i : 3 * i + 3]
        before = mm[partners[0]]
    db = scatter_rolled(db)
    *y_parts, keep, give = call(
        mlp_grad_kernel,
        [shape(ROWS, D)] * FS + [shape(HALF_ROWS, FSL)] * 2,
        [ids] + b_all + g_all + mm + dgu + [down_t],
        smem=1,
        scratch=[pltpu.VMEM((D, 2 * FSL), BF16), pltpu.VMEM((D, FSL), BF16)],
        flops=8 * FS * ROWS * D * FSL,
    )
    db, keep, give = together(db, keep, give)
    got = swap_core(give)
    dh, do_part, *eo_parts = call(
        mid_kernel,
        [shape(ROWS, D, dtype=F32), shape(CTX, HEAD, ROWS)] + [shape(ROWS, EO)] * FS,
        db + [h, g_t, gains, w_out] + o_pieces,
        flops=2 * ROWS * D * D,
    )
    do_all = lax.all_to_all(do_part, "ctx", 0, 0)
    (half_sum,) = call(
        pack_kernel,
        [shape(CTX, 96, FSL)],
        [keep, got],
        scratch=[pltpu.VMEM((HALF_ROWS + 16, FSL), F32)],
    )
    do_all, half_sum = together(do_all, half_sum)
    half_parts = same_core(half_sum)
    eo_all = scatter_rolled(eo_parts)
    (dqkv_part,) = call(
        attend_back_kernel,
        [shape(CTX, 3 * HEAD, ROWS)],
        [order, inverse, do_all, q_t, q_n, k_t, k_n, v_n, o_f, lse, cos_all, sin_all],
        smem=2,
        scratch=[
            pltpu.VMEM((HEAD, L), BF16),
            pltpu.VMEM((L, HEAD), BF16),
            pltpu.VMEM((8, L), F32),
            pltpu.VMEM((L, HEAD), F32),
            pltpu.VMEM((L, HEAD), F32),
            pltpu.VMEM((CTX, 3 * HEAD, ROWS), F32),
        ],
        flops=5 * L * L * HEAD,
    )
    dqkv_part, eo_all = together(dqkv_part, eo_all)
    (message,) = call(
        out_grad_kernel,
        [shape(CTX, 3 * HEAD + 128, ROWS)],
        eo_all + [dqkv_part],
        flops=2 * FS * ROWS * SHARD * D,
    )
    head_pieces = call(
        head_grad_kernel,
        [shape(HEADROWS, 128)] * FS,
        [ids, a_all, dqkv_part],
        smem=1,
        scratch=[pltpu.VMEM((D, 3 * HEAD), BF16)],
        flops=2 * L * D * 3 * HEAD,
    )
    half_parts, message, head_pieces = together(half_parts, message, head_pieces)
    dqkv = lax.all_to_all(message, "ctx", 0, 0)
    head_pieces = scatter_rolled(head_pieces)
    *pieces, down_sum = call(
        reduce_kernel,
        [shape(16, FSL)] * FS + [shape(32, FSL)],
        [ids, half_parts],
        smem=1,
        scratch=[pltpu.VMEM((96, FSL), BF16)],
    )
    own = jnp.concatenate(scatter_rolled(pieces) + [down_sum], axis=0)
    dqkv, head_pieces = together(dqkv, head_pieces)
    groups = [[2 * i + core for i in range(CTX)] for core in range(2)]
    mine_all = lax.all_gather(own, ("seq", "ctx"), axis=0, axis_index_groups=groups)
    (head_sum,) = call(head_sum_kernel, [shape(HEADROWS + 128, 128)], head_pieces + [dqkv])
    head_sum = (head_sum.astype(F32) + swap_seq(head_sum).astype(F32)).astype(BF16)
    (input_grad,) = call(
        last_kernel,
        [shape(D, ROWS, dtype=F32)],
        [dqkv, w_a, w_b, x_t, dh, gains],
        scratch=[pltpu.VMEM((QKV, ROWS), BF16)],
        flops=2 * ROWS * D * QKV,
    )
    head_sum, input_grad, y_parts = together(head_sum, input_grad, y_parts)
    y = scatter_rolled(y_parts)
    (result,) = call(result_kernel, [shape(D, ROWS)], [h] + y)
    head_mine = same_core_row(jnp.broadcast_to(head_sum[None], (CTX // 2, HEADROWS + 128, 128)))
    head_mine, result, mine_all = together(head_mine, result, mine_all)
    gu_out, down_out, gain_two = call(
        widen_kernel,
        [
            shape(SHARD, 2 * FF, dtype=F32),
            shape(D, FSL, dtype=F32),
            shape(SHARD, dtype=F32),
        ],
        [ids, mine_all, swap_core(mine_all), w_gate_up, gain_mlp],
        smem=1,
    )
    q_out, kv_out, o_out, gain_one = call(
        unpack_kernel,
        [
            shape(SHARD, D, dtype=F32),
            shape(SHARD, KVW, dtype=F32),
            shape(SHARD, D, dtype=F32),
            shape(SHARD, dtype=F32),
        ],
        [ids, head_mine, swap_core(head_mine), w_q, w_kv, gain_attn],
        smem=1,
    )
    return (
        result.T[None],
        input_grad.T[None],
        gain_one,
        q_out,
        kv_out,
        o_out,
        gain_two,
        gu_out,
        down_out.T,
    )


def solution(mesh):
    tokens = P(("seq", "fsdp"), "ctx", None)
    return jax.shard_map(
        shards,
        mesh=mesh,
        in_specs=(
            tokens,
            P("fsdp"),
            P("fsdp", None),
            P("fsdp", None),
            P("fsdp", None),
            P("fsdp"),
            P("fsdp", None),
            P("fsdp", None),
            P(("seq", "fsdp"), None),
            tokens,
        ),
        out_specs=(
            tokens,
            tokens,
            P("fsdp"),
            P("fsdp", None),
            P("fsdp", None),
            P("fsdp", None),
            P("fsdp"),
            P("fsdp", None),
            P("fsdp", None),
        ),
        check_vma=False,
    )
```

```python
import jax
import jax.numpy as jnp
from jax import lax
from jax.experimental import pallas as pl
from jax.experimental.pallas import tpu as pltpu
from jax.sharding import PartitionSpec as P

D = 960
HEADS = 15
KV_HEADS = 5
GROUP = 3
HEAD = 64
HALF = 32
FF = 2560
BLK = 64
L = 2048
CTX = 16
FS = 4
ROWS = 128
QKV = 1600
HEADROWS = 368
EO = 1280
HALFW = 896
KVW = 640
HALF_ROWS = D + D // 2
SHARD = D // FS
FSL = FF // FS
TILE = 256
NT = L // TILE
EPS = 1e-05
THETA = 100000.0
SCALE = HEAD**-0.5
F32 = jnp.float32
BF16 = jnp.bfloat16
VMEM_BYTES = 56 * 1024 * 1024
MLP_BYTES = 24 * 1024 * 1024


def call(kernel, outs, args, smem=0, scratch=(), flops=0, limit=VMEM_BYTES):
    specs = [pl.BlockSpec(memory_space=pltpu.SMEM)] * smem
    specs += [pl.BlockSpec(memory_space=pltpu.VMEM)] * (len(args) - smem)
    moved = sum(a.size * a.dtype.itemsize for a in list(args) + list(outs))
    return pl.pallas_call(
        kernel,
        out_shape=outs,
        in_specs=specs,
        out_specs=[pl.BlockSpec(memory_space=pltpu.VMEM)] * len(outs),
        scratch_shapes=list(scratch),
        cost_estimate=pl.CostEstimate(flops=flops, bytes_accessed=moved, transcendentals=0),
        compiler_params=pltpu.CompilerParams(vmem_limit_bytes=limit),
    )(*args)


def shape(*dims, dtype=BF16):
    return jax.ShapeDtypeStruct(dims, dtype)


def dot(left, right, a=1, b=0):
    return lax.dot_general(left, right, (((a,), (b,)), ((), ())), preferred_element_type=F32)


def inv_norm(rows):
    return lax.rsqrt(jnp.mean(rows * rows, axis=-1, keepdims=True) + EPS)


def message_kernel(ids_ref, wq_ref, wkv_ref, g1_ref, g2_ref, out_ref):
    core = ids_ref[1]

    @pl.when(core == 0)
    def _():
        out_ref[...] = wq_ref[:, 0:HALFW]

    @pl.when(core == 1)
    def _():
        out_ref[:, 0:KVW] = wkv_ref[...]
        one = jnp.broadcast_to(g1_ref[...].astype(F32)[None], (128, SHARD)).T
        two = jnp.broadcast_to(g2_ref[...].astype(F32)[None], (128, SHARD)).T
        lane = lax.broadcasted_iota(jnp.int32, (SHARD, 128), 1)
        rest = wq_ref[:, HALFW:D].astype(F32)
        rest = jnp.concatenate([rest, jnp.zeros((SHARD, 64), F32)], axis=1)
        rest = jnp.where(lane == 64, one, jnp.where(lane == 65, two, rest))
        out_ref[:, KVW : KVW + 128] = rest.astype(BF16)
        out_ref[:, KVW + 128 : HALFW] = jnp.zeros((SHARD, HALFW - KVW - 128), BF16)


def chunk_kernel(ids_ref, gu_ref, *out_refs):
    fs = ids_ref[0]
    for s in range(FS):
        at = pl.multiple_of(lax.rem(fs + s, FS) * FSL, 128)
        out_refs[s][:, 0:FSL] = gu_ref[:, pl.ds(at, FSL)]
        out_refs[s][:, FSL : 2 * FSL] = gu_ref[:, pl.ds(FF + at, FSL)]


def place_gate_up_kernel(ids_ref, *refs):
    for s in range(FS):
        at = pl.multiple_of(lax.rem(ids_ref[0] + FS - s, FS) * SHARD, 16)
        refs[FS][pl.ds(at, SHARD), :] = refs[s][...]


def qkv_kernel(ids_ref, xt_ref, *refs):
    mine = refs[0:FS]
    other = refs[FS : 2 * FS]
    cos_ref, sin_ref, out_ref, gains_ref, wa_ref, wb_ref, at_ref = refs[2 * FS :]
    fs = ids_ref[0]
    core = ids_ref[1]

    def fill(first, second):
        for s in range(FS):
            at = pl.multiple_of(lax.rem(fs + s, FS) * SHARD, 16)
            wa_ref[pl.ds(at, SHARD), :] = first[s][...]
            wb_ref[pl.ds(at, SHARD), :] = second[s][...]

    @pl.when(core == 0)
    def _():
        fill(mine, other)

    @pl.when(core == 1)
    def _():
        fill(other, mine)

    xt = xt_ref[...].astype(F32)
    gains = wb_ref[:, KVW : KVW + 128].astype(F32)
    gains_ref[...] = gains.T[64:72, :]
    r1 = lax.rsqrt(jnp.mean(xt * xt, axis=0, keepdims=True) + EPS)
    at = xt * r1 * gains[:, 64:65]
    at_ref[...] = at.astype(BF16)
    a = at.T.astype(BF16)
    lin_a = dot(a, wa_ref[...]).T
    lin_b = dot(a, wb_ref[...]).T
    cos = cos_ref[...]
    sin = sin_ref[...]

    def turned(rows):
        first = rows[0:HALF]
        second = rows[HALF:HEAD]
        return jnp.concatenate(
            [first * cos - second * sin, second * cos + first * sin], axis=0
        ).astype(BF16)

    for j in range(KV_HEADS):
        key = turned(lin_b[HEAD * j : HEAD * (j + 1)])
        value = lin_b[HEAD * (KV_HEADS + j) : HEAD * (KV_HEADS + j + 1)].astype(BF16)
        for g in range(GROUP):
            head = j * GROUP + g
            if head < HEADS - 1:
                rows = lin_a[HEAD * head : HEAD * (head + 1)]
            else:
                rows = lin_b[KVW : KVW + HEAD]
            out_ref[head, 0:HEAD, :] = turned(rows)
            out_ref[head, HEAD : 2 * HEAD, :] = key
            out_ref[head, 2 * HEAD : 3 * HEAD, :] = value
    out_ref[HEADS, :, :] = jnp.zeros((3 * HEAD, ROWS), BF16)


def pick_pair(load, first, second):
    left = load(first // 2).astype(F32)
    right = load(second // 2).astype(F32)
    left = pltpu.roll(left, (first % 2) * BLK, 1)
    right = pltpu.roll(right, (1 - second % 2) * BLK, 1)
    lane = lax.broadcasted_iota(jnp.int32, left.shape, 1)
    return jnp.where(lane < BLK, left, right)


def causal(size):
    key = lax.broadcasted_iota(jnp.int32, (size, size), 0)
    query = lax.broadcasted_iota(jnp.int32, (size, size), 1)
    return key <= query


def attend_kernel(
    order_ref, inv_ref, recv_ref, out_ref, qt_ref, kt_ref, k_ref, vt_ref, of_ref, lse_ref, s_ref
):
    for m in range(CTX):
        got = pick_pair(lambda i: recv_ref[i], inv_ref[2 * m], inv_ref[2 * m + 1])
        at = slice(2 * BLK * m, 2 * BLK * (m + 1))
        qt_ref[:, at] = (got[0:HEAD] * SCALE).astype(BF16)
        key = got[HEAD : 2 * HEAD]
        kt_ref[:, at] = key.astype(BF16)
        k_ref[at, :] = key.T.astype(BF16)
        vt_ref[:, at] = got[2 * HEAD : 3 * HEAD].astype(BF16)
    allowed = causal(TILE)
    for n in range(NT):
        span = slice(TILE * n, TILE * (n + 1))
        query = qt_ref[:, span]
        top = None
        for c in range(n + 1):
            rows = slice(TILE * c, TILE * (c + 1))
            s = dot(k_ref[rows, :], query)
            if c == n:
                s = jnp.where(allowed, s, -1e30)
            s_ref[rows, :] = s
            part = jnp.max(s, axis=0, keepdims=True)
            top = part if top is None else jnp.maximum(top, part)
        total = None
        for c in range(n + 1):
            rows = slice(TILE * c, TILE * (c + 1))
            e = jnp.exp(s_ref[rows, :] - top)
            s_ref[rows, :] = e
            part = jnp.sum(e, axis=0, keepdims=True)
            total = part if total is None else total + part
        recip = 1.0 / total
        lse_ref[n] = jnp.broadcast_to(top + jnp.log(total), (8, TILE))
        prob = (s_ref[0 : TILE * (n + 1), :] * recip).astype(BF16)
        o = dot(vt_ref[:, 0 : TILE * (n + 1)], prob)
        of_ref[2 * n] = o[:, 0 : 2 * BLK]
        of_ref[2 * n + 1] = o[:, 2 * BLK :]
    for i in range(CTX):
        got = pick_pair(lambda g: of_ref[g], order_ref[2 * i], order_ref[2 * i + 1])
        out_ref[i] = got.astype(BF16)


def attend_back_kernel(
    order_ref,
    inv_ref,
    recv_ref,
    qt_ref,
    q_ref,
    kt_ref,
    k_ref,
    v_ref,
    of_ref,
    lse_ref,
    cos_ref,
    sin_ref,
    out_ref,
    dot_ref,
    do_ref,
    delta_ref,
    dk_ref,
    dv_ref,
    st_ref,
):
    for m in range(CTX):
        got = pick_pair(lambda i: recv_ref[i], inv_ref[2 * m], inv_ref[2 * m + 1])
        at = slice(2 * BLK * m, 2 * BLK * (m + 1))
        dot_ref[:, at] = got.astype(BF16)
        do_ref[at, :] = got.T.astype(BF16)
        delta_ref[:, at] = jnp.broadcast_to(
            jnp.sum(got * of_ref[m], axis=0, keepdims=True), (8, 2 * BLK)
        )
    allowed = causal(TILE)
    for n in range(NT):
        span = slice(TILE * n, TILE * (n + 1))
        query = qt_ref[:, span]
        out_grad = dot_ref[:, span]
        lse = lse_ref[n][0:1, :]
        delta = delta_ref[0:1, span]
        dq = None
        for c in range(n + 1):
            rows = slice(TILE * c, TILE * (c + 1))
            prob = jnp.exp(dot(k_ref[rows, :], query) - lse)
            if c == n:
                prob = jnp.where(allowed, prob, 0.0)
            ds = (prob * (dot(v_ref[rows, :], out_grad) - delta)).astype(BF16)
            part = dot(kt_ref[:, rows], ds)
            dq = part if dq is None else dq + part
            dk = dot(ds, q_ref[span, :])
            dv = dot(prob.astype(BF16), do_ref[span, :])
            if c == n:
                dk_ref[rows, :] = dk
                dv_ref[rows, :] = dv
            else:
                dk_ref[rows, :] += dk
                dv_ref[rows, :] += dv
        st_ref[2 * n, 0:HEAD, :] = dq[:, 0 : 2 * BLK] * SCALE
        st_ref[2 * n + 1, 0:HEAD, :] = dq[:, 2 * BLK :] * SCALE
    for m in range(CTX):
        at = slice(2 * BLK * m, 2 * BLK * (m + 1))
        cos = cos_ref[:, at]
        sin = sin_ref[:, at]

        def turned(value):
            first = value[0:HALF]
            second = value[HALF:HEAD]
            return jnp.concatenate(
                [first * cos + second * sin, second * cos - first * sin], axis=0
            )

        st_ref[m, 0:HEAD, :] = turned(st_ref[m, 0:HEAD, :])
        st_ref[m, HEAD : 2 * HEAD, :] = turned(dk_ref[at, :].T)
        st_ref[m, 2 * HEAD : 3 * HEAD, :] = dv_ref[at, :].T
    for i in range(CTX):
        got = pick_pair(lambda g: st_ref[g], order_ref[2 * i], order_ref[2 * i + 1])
        out_ref[i] = got.astype(BF16)


def resid_kernel(ids_ref, ot_ref, w_ref, xt_ref, gains_ref, h_ref, b_ref, *refs):
    full_ref = refs[FS]
    flat = jnp.concatenate([ot_ref[h] for h in range(HEADS)], axis=0)
    full_ref[...] = flat
    for s in range(FS):
        at = pl.multiple_of(lax.rem(ids_ref[0] + s, FS) * SHARD, 16)
        refs[s][...] = full_ref[pl.ds(at, SHARD), :]
    mixed = flat.astype(F32).T.astype(BF16)
    h = xt_ref[...].astype(F32).T + dot(mixed, w_ref[...])
    h_ref[...] = h
    b_ref[...] = (h * inv_norm(h) * gains_ref[1:2, :]).astype(BF16)


def mlp_kernel(*refs):
    count = (len(refs) - 2) // 5
    b_refs = refs[0:count]
    g_refs = refs[count : 2 * count]
    gu_ref, down_ref = refs[2 * count : 2 * count + 2]
    outs = refs[2 * count + 2 :]
    for i in range(count):
        db_ref, mm_ref, dgu_ref = outs[3 * i : 3 * i + 3]
        gu = dot(b_refs[i][...], gu_ref[...])
        gate = gu[:, :FSL]
        up = gu[:, FSL:]
        sig = 1.0 / (1.0 + jnp.exp(-gate))
        act = gate * sig
        dm = dot(g_refs[i][...], down_ref[...], 0, 0)
        dgate = dm * up * sig * (1.0 + gate * (1.0 - sig))
        dgu = jnp.concatenate([dgate, dm * act], axis=1).astype(BF16)
        mm_ref[...] = (act * up).astype(BF16)
        dgu_ref[...] = dgu
        db_ref[...] = dot(dgu, gu_ref[...], 1, 1).astype(BF16)


def mlp_grad_kernel(ids_ref, *refs):
    b_refs = refs[0:FS]
    g_refs = refs[FS : 2 * FS]
    mm_refs = refs[2 * FS : 3 * FS]
    dgu_refs = refs[3 * FS : 4 * FS]
    down_ref = refs[4 * FS]
    y_refs = refs[4 * FS + 1 : 5 * FS + 1]
    keep_ref, give_ref, gu_ref, dd_ref = refs[5 * FS + 1 :]
    b = jnp.concatenate([r[...] for r in b_refs], axis=0)
    gt = jnp.concatenate([r[...] for r in g_refs], axis=1)
    mm = jnp.concatenate([r[...] for r in mm_refs], axis=0)
    dgu = jnp.concatenate([r[...] for r in dgu_refs], axis=0)
    gu_ref[...] = dot(b, dgu, 0, 0).astype(BF16)
    dd_ref[...] = dot(gt, mm).astype(BF16)

    def put(out_ref, half):
        out_ref[0:D, :] = gu_ref[:, FSL * half : FSL * (half + 1)]
        out_ref[D : D + D // 2, :] = dd_ref[D // 2 * half : D // 2 * (half + 1), :]

    for core in range(2):

        @pl.when(ids_ref[1] == core)
        def _(core=core):
            put(keep_ref, core)
            put(give_ref, 1 - core)

    for s in range(FS):
        y_refs[s][...] = dot(mm_refs[s][...], down_ref[...], 1, 1).astype(BF16)


def result_kernel(h_ref, y0, y1, y2, y3, out_ref):
    total = h_ref[...]
    for piece in (y0, y1, y2, y3):
        total += piece[...].astype(F32)
    out_ref[...] = total.T.astype(BF16)


def pack_kernel(ids_ref, keep_ref, got_ref, *refs):
    sum_ref = refs[4]
    for at in range(0, HALF_ROWS, 240):
        rows = slice(at, at + 240)
        sum_ref[rows, :] = keep_ref[rows, :].astype(F32) + got_ref[rows, :].astype(F32)
    sum_ref[HALF_ROWS:, :] = jnp.zeros((16, FSL), F32)

    def put(out_ref, first):
        for r in range(first, first + 4):
            for k in range(FS):
                at = SHARD * k + 15 * r
                out_ref[r - first, 16 * k : 16 * (k + 1), :] = sum_ref[at : at + 16, :].astype(BF16)
            at = D + 30 * r
            out_ref[r - first, 64:96, :] = sum_ref[at : at + 32, :].astype(BF16)

    for x in range(4):

        @pl.when(ids_ref[2] == x)
        def _(x=x):
            for step in range(4):
                owner = (x + step) % 4
                put(refs[step], 4 * (owner % 2 * 2 + owner // 2))


def sum_x_kernel(ids_ref, *refs):
    total = refs[0][...].astype(F32)
    for step in range(1, 4):
        total += refs[step][...].astype(F32)
    refs[8][...] = total.astype(BF16)
    for step in range(4):
        refs[4 + step][...] = refs[8][lax.rem(ids_ref[3] + step, 4)]


def sum_z_kernel(ids_ref, *refs):
    total = refs[0][...].astype(F32)
    for step in range(1, 4):
        total += refs[step][...].astype(F32)
    sum_ref = refs[9]
    sum_ref[...] = total.astype(BF16)
    for s in range(FS):
        at = pl.multiple_of(lax.rem(ids_ref[0] + s, FS) * 16, 16)
        refs[4 + s][...] = sum_ref[pl.ds(at, 16), :]
    refs[8][...] = sum_ref[64:96, :]


def mid_kernel(*refs):
    db_refs = refs[0:FS]
    h_ref, gt_ref, gains_ref, w_ref = refs[FS : FS + 4]
    o_refs = refs[FS + 4 : 2 * FS + 4]
    dh_ref, do_ref = refs[2 * FS + 4 : 2 * FS + 6]
    out_refs = refs[2 * FS + 6 :]
    db = db_refs[0][...].astype(F32)
    for ref in db_refs[1:]:
        db += ref[...].astype(F32)
    h = h_ref[...]
    r2 = inv_norm(h)
    scaled = gains_ref[1:2, :] * db
    dh = (
        gt_ref[...].astype(F32).T
        + r2 * scaled
        - h * (r2 * r2 * r2) * jnp.mean(scaled * h, axis=-1, keepdims=True)
    )
    dh_ref[...] = dh
    e = dh.astype(BF16)
    back = dot(w_ref[...], e, 1, 1).astype(BF16)
    for head in range(HEADS):
        do_ref[head] = back[HEAD * head : HEAD * (head + 1)]
    do_ref[HEADS] = jnp.zeros((HEAD, ROWS), BF16)
    for s in range(FS):
        out_refs[s][:, 0:D] = e
        o = jnp.concatenate([o_refs[s][...].astype(F32), jnp.zeros((80, ROWS), F32)], axis=0)
        out_refs[s][:, D:EO] = o.T.astype(BF16)


def head_grad_kernel(ids_ref, at_ref, d_ref, *refs):
    full_ref = refs[FS]
    total = None
    for i in range(0, CTX, 2):
        left = jnp.concatenate([at_ref[i], at_ref[i + 1]], axis=1)
        right = jnp.concatenate([d_ref[i], d_ref[i + 1]], axis=1)
        part = dot(left, right, 1, 1)
        total = part if total is None else total + part
    full_ref[...] = total.astype(BF16)
    for s in range(FS):
        at = pl.multiple_of(lax.rem(ids_ref[0] + s, FS) * SHARD, 16)
        rows = full_ref[pl.ds(at, SHARD), :]
        refs[s][0:SHARD, :] = rows[:, 0:128]
        value = rows[:, 128:192].astype(F32)
        value = jnp.concatenate([value[0 : SHARD // 2], value[SHARD // 2 :]], axis=1)
        value = jnp.concatenate([value, jnp.zeros((8, 128), F32)], axis=0)
        refs[s][SHARD:HEADROWS, :] = value.astype(BF16)


def out_grad_kernel(*refs):
    part_ref, out_ref = refs[FS:]
    total = None
    for s in range(FS):
        message = refs[s]
        part = dot(message[:, D:EO], message[:, 0:D], 0, 0)[0:SHARD]
        total = part if total is None else total + part
    pad = jnp.zeros((SHARD, 64), F32)
    total = jnp.concatenate([total, pad], axis=1).astype(BF16)
    out_ref[:, 0 : 3 * HEAD, :] = part_ref[...]
    for i in range(HEADS):
        for j in range(8):
            at = 3 * HEAD + 16 * j
            out_ref[i, at : at + 16, :] = total[16 * i : 16 * (i + 1), 128 * j : 128 * (j + 1)]
    out_ref[HEADS, 3 * HEAD :, :] = jnp.zeros((128, 128), BF16)


def head_sum_kernel(p0, p1, p2, p3, recv_ref, out_ref):
    total = p0[...].astype(F32)
    for piece in (p1, p2, p3):
        total += piece[...].astype(F32)
    out_ref[0:HEADROWS, :] = total.astype(BF16)
    total = recv_ref[0, 3 * HEAD :, :].astype(F32)
    for i in range(1, CTX):
        total += recv_ref[i, 3 * HEAD :, :].astype(F32)
    out_ref[HEADROWS:, :] = total.astype(BF16)


def last_kernel(recv_ref, wa_ref, wb_ref, xt_ref, dh_ref, gains_ref, ig_ref, msg_ref):
    for head in range(HEADS):
        msg_ref[HEAD * head : HEAD * (head + 1), :] = recv_ref[head, 0:HEAD, :]
    for part in range(2):
        for j in range(KV_HEADS):
            total = None
            for g in range(GROUP):
                piece = recv_ref[j * GROUP + g, HEAD * (part + 1) : HEAD * (part + 2), :]
                piece = piece.astype(F32)
                total = piece if total is None else total + piece
            base = D + HEAD * (KV_HEADS * part + j)
            msg_ref[base : base + HEAD, :] = total.astype(BF16)
    da = dot(wa_ref[...], msg_ref[0:HALFW, :])
    da += dot(wb_ref[:, 0:KVW], msg_ref[D:QKV, :])
    da += dot(wb_ref[:, KVW : KVW + HEAD], msg_ref[HALFW:D, :])
    x = xt_ref[...].astype(F32)
    r1 = lax.rsqrt(jnp.mean(x * x, axis=0, keepdims=True) + EPS)
    scaled = wb_ref[:, KVW : KVW + 128].astype(F32)[:, 64:65] * da
    ig_ref[...] = (
        dh_ref[...].T
        + r1 * scaled
        - x * (r1 * r1 * r1) * jnp.mean(scaled * x, axis=0, keepdims=True)
    )


def unpack_kernel(
    ids_ref, mine_ref, other_ref, wq_ref, wkv_ref, gain_in, q_ref, kv_ref, o_ref, gain_ref
):
    for core in range(2):

        @pl.when(ids_ref[1] == core)
        def _(core=core):
            blocks = []
            for head in range(HEADS):
                src = mine_ref if head % 2 == core else other_ref
                blocks.append(src[head // 2].astype(F32))
            parts = [b[0:SHARD] for b in blocks]
            tails = [b[SHARD : SHARD + SHARD // 2] for b in blocks]
            zero = jnp.zeros((SHARD, HEAD), F32)
            query = [p[:, 0:HEAD] for p in parts]
            key = []
            value = []
            for j in range(KV_HEADS):
                group = parts[GROUP * j] + parts[GROUP * j + 1] + parts[GROUP * j + 2]
                key.append(group[:, HEAD:])
                group = tails[GROUP * j] + tails[GROUP * j + 1] + tails[GROUP * j + 2]
                value.append(jnp.concatenate([group[:, 0:HEAD], group[:, HEAD:]], axis=0))
            q = jnp.concatenate(query + [zero], axis=1)[:, 0:D]
            kv = jnp.concatenate(key + value, axis=1)
            q_ref[...] = q
            kv_ref[...] = kv
            total = jnp.sum(q * wq_ref[...].astype(F32), axis=1, keepdims=True)
            total += jnp.sum(kv * wkv_ref[...].astype(F32), axis=1, keepdims=True)
            total = jnp.broadcast_to(total, (SHARD, 128)).T[0:8]
            gain_ref[...] = total[0] / gain_in[...].astype(F32)
            for i, b in enumerate(blocks):
                cols = [b[HEADROWS + 16 * j : HEADROWS + 16 * (j + 1)] for j in range(8)]
                o_ref[16 * i : 16 * (i + 1), :] = jnp.concatenate(cols, axis=1)[:, 0:D]


def widen_kernel(
    ids_ref, mine_ref, other_ref, gu_in, gain_in, gu_out, down_out, gain_ref
):
    for core in range(2):

        @pl.when(ids_ref[1] == core)
        def _(core=core):
            halves = (mine_ref, other_ref) if core == 0 else (other_ref, mine_ref)
            total = None
            down = []
            for half, src in enumerate(halves):
                for s in range(FS):
                    at = lax.rem(ids_ref[0] + FS - s, FS) * FSL + FF * half
                    cols = pl.ds(pl.multiple_of(at, 128), FSL)
                    rows = [
                        src[r, 16 * s : 16 * (s + 1), :].astype(F32)[0:15] for r in range(CTX)
                    ]
                    rows = jnp.concatenate(rows, axis=0)
                    gu_out[:, cols] = rows
                    part = jnp.sum(rows * gu_in[:, cols].astype(F32), axis=1, keepdims=True)
                    total = part if total is None else total + part
                down += [src[r, 64:96, :].astype(F32)[0:30] for r in range(CTX)]
            down_out[...] = jnp.concatenate(down, axis=0)
            total = jnp.broadcast_to(total, (SHARD, 128)).T[0:8]
            gain_ref[...] = total[0] / gain_in[...].astype(F32)


def swap_core(value):
    return lax.ppermute(value, "ctx", [(i, i ^ 1) for i in range(CTX)])


def shift(value, step):
    return lax.ppermute(value, "fsdp", [((i + step) % FS, i) for i in range(FS)])


def same_core(value):
    groups = [[2 * i + core for i in range(CTX)] for core in range(2)]
    return lax.all_to_all(value, ("seq", "ctx"), 0, 0, axis_index_groups=groups)


def shift_x(value, step):
    def at(x, z, core):
        return (x % 2) * CTX + (x // 2) * 8 + z * 2 + core

    pairs = [
        (at((x + step) % 4, z, core), at(x, z, core))
        for x in range(4)
        for z in range(4)
        for core in range(2)
    ]
    return lax.ppermute(value, ("seq", "ctx"), pairs)


def shift_z(value, step):
    def at(high, z, core):
        return high * 8 + z * 2 + core

    pairs = [
        (at(high, (z + step) % 4, core), at(high, z, core))
        for high in range(2)
        for z in range(4)
        for core in range(2)
    ]
    return lax.ppermute(value, "ctx", pairs)


def same_core_row(value):
    groups = [[2 * i + core for i in range(CTX // 2)] for core in range(2)]
    return lax.all_to_all(value, "ctx", 0, 0, axis_index_groups=groups)


def swap_seq(value):
    return lax.ppermute(value, "seq", [(0, 1), (1, 0)])


def gather_by(move, value):
    return [value] + [move(value, s) for s in range(1, 4)]


def scatter_by(move, pieces):
    return [pieces[0]] + [move(pieces[s], -s) for s in range(1, 4)]


def gather_rolled(value):
    return gather_by(shift, value)


def scatter_rolled(pieces):
    return scatter_by(shift, pieces)


def together(*values):
    return lax.optimization_barrier(values)


def shards(tokens, gain_attn, w_q, w_kv, w_o, gain_mlp, w_gate_up, w_down, block_order, cotangent):
    x_t = tokens[0].T
    g_t = cotangent[0].T
    down_t = w_down.T
    order = block_order[0]
    place = lax.axis_index("ctx")
    x_place = place // 8 * 2 + lax.axis_index("seq")
    ids = jnp.stack([lax.axis_index("fsdp"), place % 2, x_place, place // 2 % 4])
    ids = ids.astype(jnp.int32)

    slots = jnp.arange(2 * CTX, dtype=jnp.int32)
    inverse = jnp.sum(jnp.where(order[None, :] == slots[:, None], slots[None, :], 0), axis=1)
    mine = lax.dynamic_slice_in_dim(order, place * 2, 2)
    places = (mine[:, None] * BLK + jnp.arange(BLK, dtype=jnp.int32)[None, :]).reshape(ROWS)
    freq = THETA ** (-(jnp.arange(HALF, dtype=F32) * 2.0 / HEAD))
    angle = freq[:, None] * places.astype(F32)[None, :]
    angle_all = freq[:, None] * jnp.arange(L, dtype=F32)[None, :]

    (message,) = call(
        message_kernel,
        [shape(SHARD, HALFW)],
        [ids, w_q, w_kv, gain_attn, gain_mlp],
        smem=1,
    )
    w_mine = gather_rolled(message)
    chunks = call(chunk_kernel, [shape(SHARD, 2 * FSL)] * FS, [ids, w_gate_up], smem=1)
    w_mine, chunks, w_o, g_t = together(w_mine, chunks, w_o, g_t)
    w_other = [swap_core(message)] + [swap_core(piece) for piece in w_mine[1:]]
    w_out = lax.all_gather(w_o, "fsdp", axis=0, tiled=True)
    gu_pieces = scatter_rolled(chunks)
    g_all = gather_rolled(g_t)

    packed, gains, w_a, w_b, a_t = call(
        qkv_kernel,
        [
            shape(CTX, 3 * HEAD, ROWS),
            shape(8, D, dtype=F32),
            shape(D, HALFW),
            shape(D, HALFW),
            shape(D, ROWS),
        ],
        [ids, x_t] + w_mine + w_other + [jnp.cos(angle), jnp.sin(angle)],
        smem=1,
        flops=2 * ROWS * D * QKV,
    )
    a_all = lax.all_gather(a_t, "ctx", axis=0)
    received = lax.all_to_all(packed, "ctx", 0, 0)
    o_part, q_t, k_t, k_n, v_t, o_f, lse = call(
        attend_kernel,
        [
            shape(CTX, HEAD, ROWS),
            shape(HEAD, L),
            shape(HEAD, L),
            shape(L, HEAD),
            shape(HEAD, L),
            shape(CTX, HEAD, ROWS, dtype=F32),
            shape(NT, 8, TILE, dtype=F32),
        ],
        [order, inverse, received],
        smem=2,
        scratch=[pltpu.VMEM((L, TILE), F32)],
        flops=2 * L * L * HEAD,
    )
    o_all = lax.all_to_all(o_part, "ctx", 0, 0)
    q_n, v_n = q_t.T, v_t.T
    (w_gu,) = call(place_gate_up_kernel, [shape(D, 2 * FSL)], [ids] + gu_pieces, smem=1)
    cos_all, sin_all = jnp.cos(angle_all), jnp.sin(angle_all)
    o_all, w_out, q_n, v_n, cos_all, sin_all = together(
        o_all, w_out, q_n, v_n, cos_all, sin_all
    )
    h, b, *o_pieces = call(
        resid_kernel,
        [shape(ROWS, D, dtype=F32), shape(ROWS, D)] + [shape(SHARD, ROWS)] * FS,
        [ids, o_all, w_out, x_t, gains],
        smem=1,
        scratch=[pltpu.VMEM((D, ROWS), BF16)],
        flops=2 * ROWS * D * D,
    )
    b, w_gu, g_all = together(b, w_gu, g_all)
    b_all = gather_rolled(b)
    db, mm, dgu = [None] * FS, [None] * FS, [None] * FS
    before = None
    for partners in ((0,), (1, 3), (2,)):
        if before is not None:
            b_all[partners[0]], before = together(b_all[partners[0]], before)
        outs = call(
            mlp_kernel,
            [shape(ROWS, D), shape(ROWS, FSL), shape(ROWS, 2 * FSL)] * len(partners),
            [b_all[s] for s in partners] + [g_all[s] for s in partners] + [w_gu, down_t],
            flops=10 * len(partners) * ROWS * D * FSL,
            limit=MLP_BYTES,
        )
        for i, s in enumerate(partners):
            db[s], mm[s], dgu[s] = outs[3 * i : 3 * i + 3]
        before = mm[partners[0]]
    db = scatter_rolled(db)
    *y_parts, keep, give = call(
        mlp_grad_kernel,
        [shape(ROWS, D)] * FS + [shape(HALF_ROWS, FSL)] * 2,
        [ids] + b_all + g_all + mm + dgu + [down_t],
        smem=1,
        scratch=[pltpu.VMEM((D, 2 * FSL), BF16), pltpu.VMEM((D, FSL), BF16)],
        flops=8 * FS * ROWS * D * FSL,
        limit=MLP_BYTES,
    )
    db, keep = together(db, keep)
    dh, do_part, *eo_parts = call(
        mid_kernel,
        [shape(ROWS, D, dtype=F32), shape(CTX, HEAD, ROWS)] + [shape(ROWS, EO)] * FS,
        db + [h, g_t, gains, w_out] + o_pieces,
        flops=2 * ROWS * D * D,
    )
    do_all = lax.all_to_all(do_part, "ctx", 0, 0)
    eo_parts, give = together(eo_parts, give)
    got = swap_core(give)
    x_pieces = call(
        pack_kernel,
        [shape(4, 96, FSL)] * 4,
        [ids, keep, got],
        smem=1,
        scratch=[pltpu.VMEM((HALF_ROWS + 16, FSL), F32)],
    )
    eo_all = scatter_rolled(eo_parts)
    do_all, x_pieces, eo_all[1], eo_all[3] = together(do_all, x_pieces, eo_all[1], eo_all[3])
    x_pieces = scatter_by(shift_x, x_pieces)
    (dqkv_part,) = call(
        attend_back_kernel,
        [shape(CTX, 3 * HEAD, ROWS)],
        [order, inverse, do_all, q_t, q_n, k_t, k_n, v_n, o_f, lse, cos_all, sin_all],
        smem=2,
        scratch=[
            pltpu.VMEM((HEAD, L), BF16),
            pltpu.VMEM((L, HEAD), BF16),
            pltpu.VMEM((8, L), F32),
            pltpu.VMEM((L, HEAD), F32),
            pltpu.VMEM((L, HEAD), F32),
            pltpu.VMEM((CTX, 3 * HEAD, ROWS), F32),
        ],
        flops=5 * L * L * HEAD,
    )
    head_pieces = call(
        head_grad_kernel,
        [shape(HEADROWS, 128)] * FS,
        [ids, a_all, dqkv_part],
        smem=1,
        scratch=[pltpu.VMEM((D, 3 * HEAD), BF16)],
        flops=2 * L * D * 3 * HEAD,
    )
    dqkv_part, head_pieces, eo_all, x_pieces = together(dqkv_part, head_pieces, eo_all, x_pieces)
    (message,) = call(
        out_grad_kernel,
        [shape(CTX, 3 * HEAD + 128, ROWS)],
        eo_all + [dqkv_part],
        flops=2 * FS * ROWS * SHARD * D,
    )
    dqkv = lax.all_to_all(message, "ctx", 0, 0)
    head_pieces = scatter_rolled(head_pieces)
    z_pieces = call(
        sum_x_kernel,
        [shape(96, FSL)] * 4,
        [ids] + x_pieces,
        smem=1,
        scratch=[pltpu.VMEM((4, 96, FSL), BF16)],
    )
    *pieces, down_sum = call(
        sum_z_kernel,
        [shape(16, FSL)] * FS + [shape(32, FSL)],
        [ids] + scatter_by(shift_z, z_pieces),
        smem=1,
        scratch=[pltpu.VMEM((96, FSL), BF16)],
    )
    own = jnp.concatenate(scatter_rolled(pieces) + [down_sum], axis=0)
    dqkv, own, head_pieces = together(dqkv, own, head_pieces)
    mine_all = same_core(jnp.broadcast_to(own[None], (CTX, 96, FSL)))
    (head_sum,) = call(head_sum_kernel, [shape(HEADROWS + 128, 128)], head_pieces + [dqkv])
    head_sum = (head_sum.astype(F32) + swap_seq(head_sum).astype(F32)).astype(BF16)
    (input_grad,) = call(
        last_kernel,
        [shape(D, ROWS, dtype=F32)],
        [dqkv, w_a, w_b, x_t, dh, gains],
        scratch=[pltpu.VMEM((QKV, ROWS), BF16)],
        flops=2 * ROWS * D * QKV,
    )
    head_sum, y_parts = together(head_sum, y_parts)
    y = scatter_rolled(y_parts)
    (result,) = call(result_kernel, [shape(D, ROWS)], [h] + y)
    mine_all, head_sum, input_grad, result = together(mine_all, head_sum, input_grad, result)
    head_mine = same_core_row(jnp.broadcast_to(head_sum[None], (CTX // 2, HEADROWS + 128, 128)))
    gu_out, down_out, gain_two = call(
        widen_kernel,
        [
            shape(SHARD, 2 * FF, dtype=F32),
            shape(D, FSL, dtype=F32),
            shape(SHARD, dtype=F32),
        ],
        [ids, mine_all, swap_core(mine_all), w_gate_up, gain_mlp],
        smem=1,
    )
    head_mine, gu_out, down_out, gain_two = together(head_mine, gu_out, down_out, gain_two)
    q_out, kv_out, o_out, gain_one = call(
        unpack_kernel,
        [
            shape(SHARD, D, dtype=F32),
            shape(SHARD, KVW, dtype=F32),
            shape(SHARD, D, dtype=F32),
            shape(SHARD, dtype=F32),
        ],
        [ids, head_mine, swap_core(head_mine), w_q, w_kv, gain_attn],
        smem=1,
    )
    return (
        result.T[None],
        input_grad.T[None],
        gain_one,
        q_out,
        kv_out,
        o_out,
        gain_two,
        gu_out,
        down_out.T,
    )


def solution(mesh):
    tokens = P(("seq", "fsdp"), "ctx", None)
    return jax.shard_map(
        shards,
        mesh=mesh,
        in_specs=(
            tokens,
            P("fsdp"),
            P("fsdp", None),
            P("fsdp", None),
            P("fsdp", None),
            P("fsdp"),
            P("fsdp", None),
            P("fsdp", None),
            P(("seq", "fsdp"), None),
            tokens,
        ),
        out_specs=(
            tokens,
            tokens,
            P("fsdp"),
            P("fsdp", None),
            P("fsdp", None),
            P("fsdp", None),
            P("fsdp"),
            P("fsdp", None),
            P("fsdp", None),
        ),
        check_vma=False,
    )
```

```python
import jax
import jax.numpy as jnp
from jax import lax
from jax.experimental import pallas as pl
from jax.experimental.pallas import tpu as pltpu
from jax.sharding import PartitionSpec as P

D = 960
HEADS = 15
KV_HEADS = 5
GROUP = 3
HEAD = 64
HALF = 32
FF = 2560
BLK = 64
L = 2048
CTX = 16
FS = 4
ROWS = 128
QKV = 1600
HEADROWS = 368
EO = 1280
HALFW = 896
KVW = 640
HALF_ROWS = D + D // 2
SHARD = D // FS
FSL = FF // FS
TILE = 256
NT = L // TILE
EPS = 1e-05
THETA = 100000.0
SCALE = HEAD**-0.5
F32 = jnp.float32
BF16 = jnp.bfloat16
VMEM_BYTES = 56 * 1024 * 1024
MLP_BYTES = 24 * 1024 * 1024


def call(kernel, outs, args, smem=0, scratch=(), flops=0, limit=VMEM_BYTES):
    specs = [pl.BlockSpec(memory_space=pltpu.SMEM)] * smem
    specs += [pl.BlockSpec(memory_space=pltpu.VMEM)] * (len(args) - smem)
    moved = sum(a.size * a.dtype.itemsize for a in list(args) + list(outs))
    return pl.pallas_call(
        kernel,
        out_shape=outs,
        in_specs=specs,
        out_specs=[pl.BlockSpec(memory_space=pltpu.VMEM)] * len(outs),
        scratch_shapes=list(scratch),
        cost_estimate=pl.CostEstimate(flops=flops, bytes_accessed=moved, transcendentals=0),
        compiler_params=pltpu.CompilerParams(vmem_limit_bytes=limit),
    )(*args)


def shape(*dims, dtype=BF16):
    return jax.ShapeDtypeStruct(dims, dtype)


def dot(left, right, a=1, b=0):
    return lax.dot_general(left, right, (((a,), (b,)), ((), ())), preferred_element_type=F32)


def inv_norm(rows):
    return lax.rsqrt(jnp.mean(rows * rows, axis=-1, keepdims=True) + EPS)


def message_kernel(ids_ref, wq_ref, wkv_ref, g1_ref, g2_ref, out_ref):
    core = ids_ref[1]

    @pl.when(core == 0)
    def _():
        out_ref[...] = wq_ref[:, 0:HALFW]

    @pl.when(core == 1)
    def _():
        out_ref[:, 0:KVW] = wkv_ref[...]
        one = jnp.broadcast_to(g1_ref[...].astype(F32)[None], (128, SHARD)).T
        two = jnp.broadcast_to(g2_ref[...].astype(F32)[None], (128, SHARD)).T
        lane = lax.broadcasted_iota(jnp.int32, (SHARD, 128), 1)
        rest = wq_ref[:, HALFW:D].astype(F32)
        rest = jnp.concatenate([rest, jnp.zeros((SHARD, 64), F32)], axis=1)
        rest = jnp.where(lane == 64, one, jnp.where(lane == 65, two, rest))
        out_ref[:, KVW : KVW + 128] = rest.astype(BF16)
        out_ref[:, KVW + 128 : HALFW] = jnp.zeros((SHARD, HALFW - KVW - 128), BF16)


def chunk_kernel(ids_ref, gu_ref, *out_refs):
    fs = ids_ref[0]
    for s in range(FS):
        at = pl.multiple_of(lax.rem(fs + s, FS) * FSL, 128)
        out_refs[s][:, 0:FSL] = gu_ref[:, pl.ds(at, FSL)]
        out_refs[s][:, FSL : 2 * FSL] = gu_ref[:, pl.ds(FF + at, FSL)]


def place_gate_up_kernel(ids_ref, *refs):
    for s in range(FS):
        at = pl.multiple_of(lax.rem(ids_ref[0] + FS - s, FS) * SHARD, 16)
        refs[FS][pl.ds(at, SHARD), :] = refs[s][...]


def qkv_kernel(ids_ref, xt_ref, *refs):
    mine = refs[0:FS]
    other = refs[FS : 2 * FS]
    cos_ref, sin_ref, out_ref, gains_ref, wa_ref, wb_ref, at_ref = refs[2 * FS :]
    fs = ids_ref[0]
    core = ids_ref[1]

    def fill(first, second):
        for s in range(FS):
            at = pl.multiple_of(lax.rem(fs + s, FS) * SHARD, 16)
            wa_ref[pl.ds(at, SHARD), :] = first[s][...]
            wb_ref[pl.ds(at, SHARD), :] = second[s][...]

    @pl.when(core == 0)
    def _():
        fill(mine, other)

    @pl.when(core == 1)
    def _():
        fill(other, mine)

    xt = xt_ref[...].astype(F32)
    gains = wb_ref[:, KVW : KVW + 128].astype(F32)
    gains_ref[...] = gains.T[64:72, :]
    r1 = lax.rsqrt(jnp.mean(xt * xt, axis=0, keepdims=True) + EPS)
    at = xt * r1 * gains[:, 64:65]
    at_ref[...] = at.astype(BF16)
    a = at.T.astype(BF16)
    lin_a = dot(a, wa_ref[...]).T
    lin_b = dot(a, wb_ref[...]).T
    cos = cos_ref[...]
    sin = sin_ref[...]

    def turned(rows):
        first = rows[0:HALF]
        second = rows[HALF:HEAD]
        return jnp.concatenate(
            [first * cos - second * sin, second * cos + first * sin], axis=0
        ).astype(BF16)

    for j in range(KV_HEADS):
        key = turned(lin_b[HEAD * j : HEAD * (j + 1)])
        value = lin_b[HEAD * (KV_HEADS + j) : HEAD * (KV_HEADS + j + 1)].astype(BF16)
        for g in range(GROUP):
            head = j * GROUP + g
            if head < HEADS - 1:
                rows = lin_a[HEAD * head : HEAD * (head + 1)]
            else:
                rows = lin_b[KVW : KVW + HEAD]
            out_ref[head, 0:HEAD, :] = turned(rows)
            out_ref[head, HEAD : 2 * HEAD, :] = key
            out_ref[head, 2 * HEAD : 3 * HEAD, :] = value
    out_ref[HEADS, :, :] = jnp.zeros((3 * HEAD, ROWS), BF16)


def pick_pair(load, first, second):
    left = load(first // 2).astype(F32)
    right = load(second // 2).astype(F32)
    left = pltpu.roll(left, (first % 2) * BLK, 1)
    right = pltpu.roll(right, (1 - second % 2) * BLK, 1)
    lane = lax.broadcasted_iota(jnp.int32, left.shape, 1)
    return jnp.where(lane < BLK, left, right)


def causal(size):
    key = lax.broadcasted_iota(jnp.int32, (size, size), 0)
    query = lax.broadcasted_iota(jnp.int32, (size, size), 1)
    return key <= query


def attend_kernel(
    order_ref, inv_ref, recv_ref, out_ref, qt_ref, kt_ref, k_ref, vt_ref, of_ref, lse_ref, s_ref
):
    for m in range(CTX):
        got = pick_pair(lambda i: recv_ref[i], inv_ref[2 * m], inv_ref[2 * m + 1])
        at = slice(2 * BLK * m, 2 * BLK * (m + 1))
        qt_ref[:, at] = (got[0:HEAD] * SCALE).astype(BF16)
        key = got[HEAD : 2 * HEAD]
        kt_ref[:, at] = key.astype(BF16)
        k_ref[at, :] = key.T.astype(BF16)
        vt_ref[:, at] = got[2 * HEAD : 3 * HEAD].astype(BF16)
    allowed = causal(TILE)
    for n in range(NT):
        span = slice(TILE * n, TILE * (n + 1))
        query = qt_ref[:, span]
        top = None
        for c in range(n + 1):
            rows = slice(TILE * c, TILE * (c + 1))
            s = dot(k_ref[rows, :], query)
            if c == n:
                s = jnp.where(allowed, s, -1e30)
            s_ref[rows, :] = s
            part = jnp.max(s, axis=0, keepdims=True)
            top = part if top is None else jnp.maximum(top, part)
        total = None
        for c in range(n + 1):
            rows = slice(TILE * c, TILE * (c + 1))
            e = jnp.exp(s_ref[rows, :] - top)
            s_ref[rows, :] = e
            part = jnp.sum(e, axis=0, keepdims=True)
            total = part if total is None else total + part
        recip = 1.0 / total
        lse_ref[n] = jnp.broadcast_to(top + jnp.log(total), (8, TILE))
        prob = (s_ref[0 : TILE * (n + 1), :] * recip).astype(BF16)
        o = dot(vt_ref[:, 0 : TILE * (n + 1)], prob)
        of_ref[2 * n] = o[:, 0 : 2 * BLK]
        of_ref[2 * n + 1] = o[:, 2 * BLK :]
    for i in range(CTX):
        got = pick_pair(lambda g: of_ref[g], order_ref[2 * i], order_ref[2 * i + 1])
        out_ref[i] = got.astype(BF16)


def attend_back_kernel(
    order_ref,
    inv_ref,
    recv_ref,
    qt_ref,
    q_ref,
    kt_ref,
    k_ref,
    v_ref,
    of_ref,
    lse_ref,
    cos_ref,
    sin_ref,
    out_ref,
    dot_ref,
    do_ref,
    delta_ref,
    dk_ref,
    dv_ref,
    st_ref,
):
    for m in range(CTX):
        got = pick_pair(lambda i: recv_ref[i], inv_ref[2 * m], inv_ref[2 * m + 1])
        at = slice(2 * BLK * m, 2 * BLK * (m + 1))
        dot_ref[:, at] = got.astype(BF16)
        do_ref[at, :] = got.T.astype(BF16)
        delta_ref[:, at] = jnp.broadcast_to(
            jnp.sum(got * of_ref[m], axis=0, keepdims=True), (8, 2 * BLK)
        )
    allowed = causal(TILE)
    for n in range(NT):
        span = slice(TILE * n, TILE * (n + 1))
        query = qt_ref[:, span]
        out_grad = dot_ref[:, span]
        lse = lse_ref[n][0:1, :]
        delta = delta_ref[0:1, span]
        dq = None
        for c in range(n + 1):
            rows = slice(TILE * c, TILE * (c + 1))
            prob = jnp.exp(dot(k_ref[rows, :], query) - lse)
            if c == n:
                prob = jnp.where(allowed, prob, 0.0)
            ds = (prob * (dot(v_ref[rows, :], out_grad) - delta)).astype(BF16)
            part = dot(kt_ref[:, rows], ds)
            dq = part if dq is None else dq + part
            dk = dot(ds, q_ref[span, :])
            dv = dot(prob.astype(BF16), do_ref[span, :])
            if c == n:
                dk_ref[rows, :] = dk
                dv_ref[rows, :] = dv
            else:
                dk_ref[rows, :] += dk
                dv_ref[rows, :] += dv
        st_ref[2 * n, 0:HEAD, :] = dq[:, 0 : 2 * BLK] * SCALE
        st_ref[2 * n + 1, 0:HEAD, :] = dq[:, 2 * BLK :] * SCALE
    for m in range(CTX):
        at = slice(2 * BLK * m, 2 * BLK * (m + 1))
        cos = cos_ref[:, at]
        sin = sin_ref[:, at]

        def turned(value):
            first = value[0:HALF]
            second = value[HALF:HEAD]
            return jnp.concatenate(
                [first * cos + second * sin, second * cos - first * sin], axis=0
            )

        st_ref[m, 0:HEAD, :] = turned(st_ref[m, 0:HEAD, :])
        st_ref[m, HEAD : 2 * HEAD, :] = turned(dk_ref[at, :].T)
        st_ref[m, 2 * HEAD : 3 * HEAD, :] = dv_ref[at, :].T
    for i in range(CTX):
        got = pick_pair(lambda g: st_ref[g], order_ref[2 * i], order_ref[2 * i + 1])
        out_ref[i] = got.astype(BF16)


def resid_kernel(ids_ref, ot_ref, w_ref, xt_ref, gains_ref, h_ref, b_ref, *refs):
    full_ref = refs[FS]
    flat = jnp.concatenate([ot_ref[h] for h in range(HEADS)], axis=0)
    full_ref[...] = flat
    for s in range(FS):
        at = pl.multiple_of(lax.rem(ids_ref[0] + s, FS) * SHARD, 16)
        refs[s][...] = full_ref[pl.ds(at, SHARD), :]
    mixed = flat.astype(F32).T.astype(BF16)
    h = xt_ref[...].astype(F32).T + dot(mixed, w_ref[...])
    h_ref[...] = h
    b_ref[...] = (h * inv_norm(h) * gains_ref[1:2, :]).astype(BF16)


def mlp_kernel(*refs):
    count = (len(refs) - 2) // 5
    b_refs = refs[0:count]
    g_refs = refs[count : 2 * count]
    gu_ref, down_ref = refs[2 * count : 2 * count + 2]
    outs = refs[2 * count + 2 :]
    for i in range(count):
        db_ref, mm_ref, dgu_ref = outs[3 * i : 3 * i + 3]
        gu = dot(b_refs[i][...], gu_ref[...])
        gate = gu[:, :FSL]
        up = gu[:, FSL:]
        sig = 1.0 / (1.0 + jnp.exp(-gate))
        act = gate * sig
        dm = dot(g_refs[i][...], down_ref[...], 0, 0)
        dgate = dm * up * sig * (1.0 + gate * (1.0 - sig))
        dgu = jnp.concatenate([dgate, dm * act], axis=1).astype(BF16)
        mm_ref[...] = (act * up).astype(BF16)
        dgu_ref[...] = dgu
        db_ref[...] = dot(dgu, gu_ref[...], 1, 1).astype(BF16)


def mlp_grad_kernel(ids_ref, *refs):
    b_refs = refs[0:FS]
    g_refs = refs[FS : 2 * FS]
    mm_refs = refs[2 * FS : 3 * FS]
    dgu_refs = refs[3 * FS : 4 * FS]
    down_ref = refs[4 * FS]
    y_refs = refs[4 * FS + 1 : 5 * FS + 1]
    keep_ref, give_ref, gu_ref, dd_ref = refs[5 * FS + 1 :]
    b = jnp.concatenate([r[...] for r in b_refs], axis=0)
    gt = jnp.concatenate([r[...] for r in g_refs], axis=1)
    mm = jnp.concatenate([r[...] for r in mm_refs], axis=0)
    dgu = jnp.concatenate([r[...] for r in dgu_refs], axis=0)
    gu_ref[...] = dot(b, dgu, 0, 0).astype(BF16)
    dd_ref[...] = dot(gt, mm).astype(BF16)

    def put(out_ref, half):
        out_ref[0:D, :] = gu_ref[:, FSL * half : FSL * (half + 1)]
        out_ref[D : D + D // 2, :] = dd_ref[D // 2 * half : D // 2 * (half + 1), :]

    for core in range(2):

        @pl.when(ids_ref[1] == core)
        def _(core=core):
            put(keep_ref, core)
            put(give_ref, 1 - core)

    for s in range(FS):
        y_refs[s][...] = dot(mm_refs[s][...], down_ref[...], 1, 1).astype(BF16)


def result_kernel(h_ref, y0, y1, y2, y3, out_ref):
    total = h_ref[...]
    for piece in (y0, y1, y2, y3):
        total += piece[...].astype(F32)
    out_ref[...] = total.T.astype(BF16)


def pack_kernel(ids_ref, keep_ref, got_ref, *refs):
    sum_ref = refs[4]
    for at in range(0, HALF_ROWS, 240):
        rows = slice(at, at + 240)
        sum_ref[rows, :] = keep_ref[rows, :].astype(F32) + got_ref[rows, :].astype(F32)
    sum_ref[HALF_ROWS:, :] = jnp.zeros((16, FSL), F32)

    def put(out_ref, first):
        for r in range(first, first + 4):
            for k in range(FS):
                at = SHARD * k + 15 * r
                out_ref[r - first, 16 * k : 16 * (k + 1), :] = sum_ref[at : at + 16, :].astype(BF16)
            at = D + 30 * r
            out_ref[r - first, 64:96, :] = sum_ref[at : at + 32, :].astype(BF16)

    for x in range(4):

        @pl.when(ids_ref[2] == x)
        def _(x=x):
            for step in range(4):
                owner = (x + step) % 4
                put(refs[step], 4 * (owner % 2 * 2 + owner // 2))


def sum_x_kernel(ids_ref, *refs):
    total = refs[0][...].astype(F32)
    for step in range(1, 4):
        total += refs[step][...].astype(F32)
    refs[8][...] = total.astype(BF16)
    for step in range(4):
        refs[4 + step][...] = refs[8][lax.rem(ids_ref[3] + step, 4)]


def sum_z_kernel(ids_ref, *refs):
    total = refs[0][...].astype(F32)
    for step in range(1, 4):
        total += refs[step][...].astype(F32)
    sum_ref = refs[9]
    sum_ref[...] = total.astype(BF16)
    for s in range(FS):
        at = pl.multiple_of(lax.rem(ids_ref[0] + s, FS) * 16, 16)
        refs[4 + s][...] = sum_ref[pl.ds(at, 16), :]
    refs[8][...] = sum_ref[64:96, :]


def mid_kernel(*refs):
    db_refs = refs[0:FS]
    h_ref, gt_ref, gains_ref, w_ref = refs[FS : FS + 4]
    o_refs = refs[FS + 4 : 2 * FS + 4]
    dh_ref, do_ref = refs[2 * FS + 4 : 2 * FS + 6]
    out_refs = refs[2 * FS + 6 :]
    db = db_refs[0][...].astype(F32)
    for ref in db_refs[1:]:
        db += ref[...].astype(F32)
    h = h_ref[...]
    r2 = inv_norm(h)
    scaled = gains_ref[1:2, :] * db
    dh = (
        gt_ref[...].astype(F32).T
        + r2 * scaled
        - h * (r2 * r2 * r2) * jnp.mean(scaled * h, axis=-1, keepdims=True)
    )
    dh_ref[...] = dh
    e = dh.astype(BF16)
    back = dot(w_ref[...], e, 1, 1).astype(BF16)
    for head in range(HEADS):
        do_ref[head] = back[HEAD * head : HEAD * (head + 1)]
    do_ref[HEADS] = jnp.zeros((HEAD, ROWS), BF16)
    for s in range(FS):
        out_refs[s][:, 0:D] = e
        o = jnp.concatenate([o_refs[s][...].astype(F32), jnp.zeros((80, ROWS), F32)], axis=0)
        out_refs[s][:, D:EO] = o.T.astype(BF16)


def head_grad_kernel(ids_ref, at_ref, d_ref, *refs):
    full_ref = refs[FS]
    total = None
    for i in range(0, CTX, 2):
        left = jnp.concatenate([at_ref[i], at_ref[i + 1]], axis=1)
        right = jnp.concatenate([d_ref[i], d_ref[i + 1]], axis=1)
        part = dot(left, right, 1, 1)
        total = part if total is None else total + part
    full_ref[...] = total.astype(BF16)
    for s in range(FS):
        at = pl.multiple_of(lax.rem(ids_ref[0] + s, FS) * SHARD, 16)
        rows = full_ref[pl.ds(at, SHARD), :]
        refs[s][0:SHARD, :] = rows[:, 0:128]
        value = rows[:, 128:192].astype(F32)
        value = jnp.concatenate([value[0 : SHARD // 2], value[SHARD // 2 :]], axis=1)
        value = jnp.concatenate([value, jnp.zeros((8, 128), F32)], axis=0)
        refs[s][SHARD:HEADROWS, :] = value.astype(BF16)


def out_grad_kernel(*refs):
    part_ref, out_ref = refs[FS:]
    total = None
    for s in range(FS):
        message = refs[s]
        part = dot(message[:, D:EO], message[:, 0:D], 0, 0)[0:SHARD]
        total = part if total is None else total + part
    pad = jnp.zeros((SHARD, 64), F32)
    total = jnp.concatenate([total, pad], axis=1).astype(BF16)
    out_ref[:, 0 : 3 * HEAD, :] = part_ref[...]
    for i in range(HEADS):
        for j in range(8):
            at = 3 * HEAD + 16 * j
            out_ref[i, at : at + 16, :] = total[16 * i : 16 * (i + 1), 128 * j : 128 * (j + 1)]
    out_ref[HEADS, 3 * HEAD :, :] = jnp.zeros((128, 128), BF16)


def head_sum_kernel(p0, p1, p2, p3, recv_ref, out_ref):
    total = p0[...].astype(F32)
    for piece in (p1, p2, p3):
        total += piece[...].astype(F32)
    out_ref[0:HEADROWS, :] = total.astype(BF16)
    total = recv_ref[0, 3 * HEAD :, :].astype(F32)
    for i in range(1, CTX):
        total += recv_ref[i, 3 * HEAD :, :].astype(F32)
    out_ref[HEADROWS:, :] = total.astype(BF16)


def last_kernel(recv_ref, wa_ref, wb_ref, xt_ref, dh_ref, gains_ref, ig_ref, msg_ref):
    for head in range(HEADS):
        msg_ref[HEAD * head : HEAD * (head + 1), :] = recv_ref[head, 0:HEAD, :]
    for part in range(2):
        for j in range(KV_HEADS):
            total = None
            for g in range(GROUP):
                piece = recv_ref[j * GROUP + g, HEAD * (part + 1) : HEAD * (part + 2), :]
                piece = piece.astype(F32)
                total = piece if total is None else total + piece
            base = D + HEAD * (KV_HEADS * part + j)
            msg_ref[base : base + HEAD, :] = total.astype(BF16)
    da = dot(wa_ref[...], msg_ref[0:HALFW, :])
    da += dot(wb_ref[:, 0:KVW], msg_ref[D:QKV, :])
    da += dot(wb_ref[:, KVW : KVW + HEAD], msg_ref[HALFW:D, :])
    x = xt_ref[...].astype(F32)
    r1 = lax.rsqrt(jnp.mean(x * x, axis=0, keepdims=True) + EPS)
    scaled = wb_ref[:, KVW : KVW + 128].astype(F32)[:, 64:65] * da
    ig_ref[...] = (
        dh_ref[...].T
        + r1 * scaled
        - x * (r1 * r1 * r1) * jnp.mean(scaled * x, axis=0, keepdims=True)
    )


def unpack_kernel(
    ids_ref, mine_ref, other_ref, wq_ref, wkv_ref, gain_in, q_ref, kv_ref, o_ref, gain_ref
):
    for core in range(2):

        @pl.when(ids_ref[1] == core)
        def _(core=core):
            blocks = []
            for head in range(HEADS):
                src = mine_ref if head % 2 == core else other_ref
                blocks.append(src[head // 2].astype(F32))
            parts = [b[0:SHARD] for b in blocks]
            tails = [b[SHARD : SHARD + SHARD // 2] for b in blocks]
            zero = jnp.zeros((SHARD, HEAD), F32)
            query = [p[:, 0:HEAD] for p in parts]
            key = []
            value = []
            for j in range(KV_HEADS):
                group = parts[GROUP * j] + parts[GROUP * j + 1] + parts[GROUP * j + 2]
                key.append(group[:, HEAD:])
                group = tails[GROUP * j] + tails[GROUP * j + 1] + tails[GROUP * j + 2]
                value.append(jnp.concatenate([group[:, 0:HEAD], group[:, HEAD:]], axis=0))
            q = jnp.concatenate(query + [zero], axis=1)[:, 0:D]
            kv = jnp.concatenate(key + value, axis=1)
            q_ref[...] = q
            kv_ref[...] = kv
            total = jnp.sum(q * wq_ref[...].astype(F32), axis=1, keepdims=True)
            total += jnp.sum(kv * wkv_ref[...].astype(F32), axis=1, keepdims=True)
            total = jnp.broadcast_to(total, (SHARD, 128)).T[0:8]
            gain_ref[...] = total[0] / gain_in[...].astype(F32)
            for i, b in enumerate(blocks):
                cols = [b[HEADROWS + 16 * j : HEADROWS + 16 * (j + 1)] for j in range(8)]
                o_ref[16 * i : 16 * (i + 1), :] = jnp.concatenate(cols, axis=1)[:, 0:D]


def widen_kernel(
    ids_ref, mine_ref, other_ref, gu_in, gain_in, gu_out, down_out, gain_ref
):
    for core in range(2):

        @pl.when(ids_ref[1] == core)
        def _(core=core):
            halves = (mine_ref, other_ref) if core == 0 else (other_ref, mine_ref)
            total = None
            down = []
            for half, src in enumerate(halves):
                for s in range(FS):
                    at = lax.rem(ids_ref[0] + FS - s, FS) * FSL + FF * half
                    cols = pl.ds(pl.multiple_of(at, 128), FSL)
                    rows = [
                        src[r, 16 * s : 16 * (s + 1), :].astype(F32)[0:15] for r in range(CTX)
                    ]
                    rows = jnp.concatenate(rows, axis=0)
                    gu_out[:, cols] = rows
                    part = jnp.sum(rows * gu_in[:, cols].astype(F32), axis=1, keepdims=True)
                    total = part if total is None else total + part
                down += [src[r, 64:96, :].astype(F32)[0:30] for r in range(CTX)]
            down_out[...] = jnp.concatenate(down, axis=0)
            total = jnp.broadcast_to(total, (SHARD, 128)).T[0:8]
            gain_ref[...] = total[0] / gain_in[...].astype(F32)


def swap_core(value):
    return lax.ppermute(value, "ctx", [(i, i ^ 1) for i in range(CTX)])


def shift(value, step):
    return lax.ppermute(value, "fsdp", [((i + step) % FS, i) for i in range(FS)])


def same_core(value):
    groups = [[2 * i + core for i in range(CTX)] for core in range(2)]
    return lax.all_to_all(value, ("seq", "ctx"), 0, 0, axis_index_groups=groups)


def shift_x(value, step):
    def at(x, z, core):
        return (x % 2) * CTX + (x // 2) * 8 + z * 2 + core

    pairs = [
        (at((x + step) % 4, z, core), at(x, z, core))
        for x in range(4)
        for z in range(4)
        for core in range(2)
    ]
    return lax.ppermute(value, ("seq", "ctx"), pairs)


def shift_z(value, step):
    def at(high, z, core):
        return high * 8 + z * 2 + core

    pairs = [
        (at(high, (z + step) % 4, core), at(high, z, core))
        for high in range(2)
        for z in range(4)
        for core in range(2)
    ]
    return lax.ppermute(value, "ctx", pairs)


def same_core_row(value):
    groups = [[2 * i + core for i in range(CTX // 2)] for core in range(2)]
    return lax.all_to_all(value, "ctx", 0, 0, axis_index_groups=groups)


def swap_seq(value):
    return lax.ppermute(value, "seq", [(0, 1), (1, 0)])


def gather_by(move, value):
    return [value] + [move(value, s) for s in range(1, 4)]


def scatter_by(move, pieces):
    return [pieces[0]] + [move(pieces[s], -s) for s in range(1, 4)]


def gather_rolled(value):
    return gather_by(shift, value)


def scatter_rolled(pieces):
    return scatter_by(shift, pieces)


def together(*values):
    return lax.optimization_barrier(values)


def shards(tokens, gain_attn, w_q, w_kv, w_o, gain_mlp, w_gate_up, w_down, block_order, cotangent):
    x_t = tokens[0].T
    g_t = cotangent[0].T
    down_t = w_down.T
    order = block_order[0]
    place = lax.axis_index("ctx")
    x_place = place // 8 * 2 + lax.axis_index("seq")
    ids = jnp.stack([lax.axis_index("fsdp"), place % 2, x_place, place // 2 % 4])
    ids = ids.astype(jnp.int32)

    slots = jnp.arange(2 * CTX, dtype=jnp.int32)
    inverse = jnp.sum(jnp.where(order[None, :] == slots[:, None], slots[None, :], 0), axis=1)
    mine = lax.dynamic_slice_in_dim(order, place * 2, 2)
    places = (mine[:, None] * BLK + jnp.arange(BLK, dtype=jnp.int32)[None, :]).reshape(ROWS)
    freq = THETA ** (-(jnp.arange(HALF, dtype=F32) * 2.0 / HEAD))
    angle = freq[:, None] * places.astype(F32)[None, :]
    angle_all = freq[:, None] * jnp.arange(L, dtype=F32)[None, :]

    (message,) = call(
        message_kernel,
        [shape(SHARD, HALFW)],
        [ids, w_q, w_kv, gain_attn, gain_mlp],
        smem=1,
    )
    w_mine = gather_rolled(message)
    chunks = call(chunk_kernel, [shape(SHARD, 2 * FSL)] * FS, [ids, w_gate_up], smem=1)
    w_mine, chunks, w_o, g_t = together(w_mine, chunks, w_o, g_t)
    w_other = [swap_core(message)] + [swap_core(piece) for piece in w_mine[1:]]
    w_out = lax.all_gather(w_o, "fsdp", axis=0, tiled=True)
    gu_pieces = scatter_rolled(chunks)
    g_all = gather_rolled(g_t)

    packed, gains, w_a, w_b, a_t = call(
        qkv_kernel,
        [
            shape(CTX, 3 * HEAD, ROWS),
            shape(8, D, dtype=F32),
            shape(D, HALFW),
            shape(D, HALFW),
            shape(D, ROWS),
        ],
        [ids, x_t] + w_mine + w_other + [jnp.cos(angle), jnp.sin(angle)],
        smem=1,
        flops=2 * ROWS * D * QKV,
    )
    a_all = lax.all_gather(a_t, "ctx", axis=0)
    received = lax.all_to_all(packed, "ctx", 0, 0)
    o_part, q_t, k_t, k_n, v_t, o_f, lse = call(
        attend_kernel,
        [
            shape(CTX, HEAD, ROWS),
            shape(HEAD, L),
            shape(HEAD, L),
            shape(L, HEAD),
            shape(HEAD, L),
            shape(CTX, HEAD, ROWS, dtype=F32),
            shape(NT, 8, TILE, dtype=F32),
        ],
        [order, inverse, received],
        smem=2,
        scratch=[pltpu.VMEM((L, TILE), F32)],
        flops=2 * L * L * HEAD,
    )
    o_all = lax.all_to_all(o_part, "ctx", 0, 0)
    q_n, v_n = q_t.T, v_t.T
    cos_all, sin_all = jnp.cos(angle_all), jnp.sin(angle_all)
    o_all, w_out = together(o_all, w_out)
    h, b, *o_pieces = call(
        resid_kernel,
        [shape(ROWS, D, dtype=F32), shape(ROWS, D)] + [shape(SHARD, ROWS)] * FS,
        [ids, o_all, w_out, x_t, gains],
        smem=1,
        scratch=[pltpu.VMEM((D, ROWS), BF16)],
        flops=2 * ROWS * D * D,
    )
    b, gu_pieces, g_all = together(b, gu_pieces, g_all)
    (w_gu,) = call(place_gate_up_kernel, [shape(D, 2 * FSL)], [ids] + gu_pieces, smem=1)
    b_all = gather_rolled(b)
    db, mm, dgu = [None] * FS, [None] * FS, [None] * FS
    before = None
    for partners in ((0,), (1, 3), (2,)):
        if before is not None:
            b_all[partners[0]], before = together(b_all[partners[0]], before)
        outs = call(
            mlp_kernel,
            [shape(ROWS, D), shape(ROWS, FSL), shape(ROWS, 2 * FSL)] * len(partners),
            [b_all[s] for s in partners] + [g_all[s] for s in partners] + [w_gu, down_t],
            flops=10 * len(partners) * ROWS * D * FSL,
            limit=MLP_BYTES,
        )
        for i, s in enumerate(partners):
            db[s], mm[s], dgu[s] = outs[3 * i : 3 * i + 3]
        before = mm[partners[0]]
    db = scatter_rolled(db)
    *y_parts, keep, give = call(
        mlp_grad_kernel,
        [shape(ROWS, D)] * FS + [shape(HALF_ROWS, FSL)] * 2,
        [ids] + b_all + g_all + mm + dgu + [down_t],
        smem=1,
        scratch=[pltpu.VMEM((D, 2 * FSL), BF16), pltpu.VMEM((D, FSL), BF16)],
        flops=8 * FS * ROWS * D * FSL,
        limit=MLP_BYTES,
    )
    db, keep, q_n, v_n, cos_all, sin_all = together(db, keep, q_n, v_n, cos_all, sin_all)
    dh, do_part, *eo_parts = call(
        mid_kernel,
        [shape(ROWS, D, dtype=F32), shape(CTX, HEAD, ROWS)] + [shape(ROWS, EO)] * FS,
        db + [h, g_t, gains, w_out] + o_pieces,
        flops=2 * ROWS * D * D,
    )
    do_all = lax.all_to_all(do_part, "ctx", 0, 0)
    eo_parts, give = together(eo_parts, give)
    got = swap_core(give)
    x_pieces = call(
        pack_kernel,
        [shape(4, 96, FSL)] * 4,
        [ids, keep, got],
        smem=1,
        scratch=[pltpu.VMEM((HALF_ROWS + 16, FSL), F32)],
    )
    eo_all = scatter_rolled(eo_parts)
    do_all, x_pieces, eo_all[1], eo_all[3] = together(do_all, x_pieces, eo_all[1], eo_all[3])
    x_pieces = scatter_by(shift_x, x_pieces)
    (dqkv_part,) = call(
        attend_back_kernel,
        [shape(CTX, 3 * HEAD, ROWS)],
        [order, inverse, do_all, q_t, q_n, k_t, k_n, v_n, o_f, lse, cos_all, sin_all],
        smem=2,
        scratch=[
            pltpu.VMEM((HEAD, L), BF16),
            pltpu.VMEM((L, HEAD), BF16),
            pltpu.VMEM((8, L), F32),
            pltpu.VMEM((L, HEAD), F32),
            pltpu.VMEM((L, HEAD), F32),
            pltpu.VMEM((CTX, 3 * HEAD, ROWS), F32),
        ],
        flops=5 * L * L * HEAD,
    )
    head_pieces = call(
        head_grad_kernel,
        [shape(HEADROWS, 128)] * FS,
        [ids, a_all, dqkv_part],
        smem=1,
        scratch=[pltpu.VMEM((D, 3 * HEAD), BF16)],
        flops=2 * L * D * 3 * HEAD,
    )
    dqkv_part, head_pieces, eo_all, x_pieces = together(dqkv_part, head_pieces, eo_all, x_pieces)
    (message,) = call(
        out_grad_kernel,
        [shape(CTX, 3 * HEAD + 128, ROWS)],
        eo_all + [dqkv_part],
        flops=2 * FS * ROWS * SHARD * D,
    )
    dqkv = lax.all_to_all(message, "ctx", 0, 0)
    head_pieces = scatter_rolled(head_pieces)
    z_pieces = call(
        sum_x_kernel,
        [shape(96, FSL)] * 4,
        [ids] + x_pieces,
        smem=1,
        scratch=[pltpu.VMEM((4, 96, FSL), BF16)],
    )
    *pieces, down_sum = call(
        sum_z_kernel,
        [shape(16, FSL)] * FS + [shape(32, FSL)],
        [ids] + scatter_by(shift_z, z_pieces),
        smem=1,
        scratch=[pltpu.VMEM((96, FSL), BF16)],
    )
    own = jnp.concatenate(scatter_rolled(pieces) + [down_sum], axis=0)
    dqkv, own, head_pieces, y_parts = together(dqkv, own, head_pieces, y_parts)
    y = scatter_rolled(y_parts)
    mine_all = same_core(jnp.broadcast_to(own[None], (CTX, 96, FSL)))
    (head_sum,) = call(head_sum_kernel, [shape(HEADROWS + 128, 128)], head_pieces + [dqkv])
    head_sum = (head_sum.astype(F32) + swap_seq(head_sum).astype(F32)).astype(BF16)
    (input_grad,) = call(
        last_kernel,
        [shape(D, ROWS, dtype=F32)],
        [dqkv, w_a, w_b, x_t, dh, gains],
        scratch=[pltpu.VMEM((QKV, ROWS), BF16)],
        flops=2 * ROWS * D * QKV,
    )
    (result,) = call(result_kernel, [shape(D, ROWS)], [h] + y)
    mine_all, head_sum, input_grad, result = together(mine_all, head_sum, input_grad, result)
    head_mine = same_core_row(jnp.broadcast_to(head_sum[None], (CTX // 2, HEADROWS + 128, 128)))
    gu_out, down_out, gain_two = call(
        widen_kernel,
        [
            shape(SHARD, 2 * FF, dtype=F32),
            shape(D, FSL, dtype=F32),
            shape(SHARD, dtype=F32),
        ],
        [ids, mine_all, swap_core(mine_all), w_gate_up, gain_mlp],
        smem=1,
    )
    head_mine, gu_out, down_out, gain_two = together(head_mine, gu_out, down_out, gain_two)
    q_out, kv_out, o_out, gain_one = call(
        unpack_kernel,
        [
            shape(SHARD, D, dtype=F32),
            shape(SHARD, KVW, dtype=F32),
            shape(SHARD, D, dtype=F32),
            shape(SHARD, dtype=F32),
        ],
        [ids, head_mine, swap_core(head_mine), w_q, w_kv, gain_attn],
        smem=1,
    )
    return (
        result.T[None],
        input_grad.T[None],
        gain_one,
        q_out,
        kv_out,
        o_out,
        gain_two,
        gu_out,
        down_out.T,
    )


def solution(mesh):
    tokens = P(("seq", "fsdp"), "ctx", None)
    return jax.shard_map(
        shards,
        mesh=mesh,
        in_specs=(
            tokens,
            P("fsdp"),
            P("fsdp", None),
            P("fsdp", None),
            P("fsdp", None),
            P("fsdp"),
            P("fsdp", None),
            P("fsdp", None),
            P(("seq", "fsdp"), None),
            tokens,
        ),
        out_specs=(
            tokens,
            tokens,
            P("fsdp"),
            P("fsdp", None),
            P("fsdp", None),
            P("fsdp", None),
            P("fsdp"),
            P("fsdp", None),
            P("fsdp", None),
        ),
        check_vma=False,
    )
```

```python
import jax
import jax.numpy as jnp
from jax import lax
from jax.experimental import pallas as pl
from jax.experimental.pallas import tpu as pltpu
from jax.sharding import PartitionSpec as P

D = 960
HEADS = 15
KV_HEADS = 5
GROUP = 3
HEAD = 64
HALF = 32
FF = 2560
BLK = 64
L = 2048
CTX = 16
FS = 4
ROWS = 128
QKV = 1600
HEADROWS = 368
EO = 1280
HALFW = 896
KVW = 640
HALF_ROWS = D + D // 2
SHARD = D // FS
FSL = FF // FS
TILE = 256
NT = L // TILE
EPS = 1e-05
THETA = 100000.0
SCALE = HEAD**-0.5
F32 = jnp.float32
BF16 = jnp.bfloat16
VMEM_BYTES = 56 * 1024 * 1024
MLP_BYTES = 24 * 1024 * 1024


def call(kernel, outs, args, smem=0, scratch=(), flops=0, limit=VMEM_BYTES):
    specs = [pl.BlockSpec(memory_space=pltpu.SMEM)] * smem
    specs += [pl.BlockSpec(memory_space=pltpu.VMEM)] * (len(args) - smem)
    moved = sum(a.size * a.dtype.itemsize for a in list(args) + list(outs))
    return pl.pallas_call(
        kernel,
        out_shape=outs,
        in_specs=specs,
        out_specs=[pl.BlockSpec(memory_space=pltpu.VMEM)] * len(outs),
        scratch_shapes=list(scratch),
        cost_estimate=pl.CostEstimate(flops=flops, bytes_accessed=moved, transcendentals=0),
        compiler_params=pltpu.CompilerParams(vmem_limit_bytes=limit),
    )(*args)


def shape(*dims, dtype=BF16):
    return jax.ShapeDtypeStruct(dims, dtype)


def dot(left, right, a=1, b=0):
    return lax.dot_general(left, right, (((a,), (b,)), ((), ())), preferred_element_type=F32)


def inv_norm(rows):
    return lax.rsqrt(jnp.mean(rows * rows, axis=-1, keepdims=True) + EPS)


def message_kernel(ids_ref, wq_ref, wkv_ref, g1_ref, g2_ref, out_ref):
    core = ids_ref[1]

    @pl.when(core == 0)
    def _():
        out_ref[...] = wq_ref[:, 0:HALFW]

    @pl.when(core == 1)
    def _():
        out_ref[:, 0:KVW] = wkv_ref[...]
        one = jnp.broadcast_to(g1_ref[...].astype(F32)[None], (128, SHARD)).T
        two = jnp.broadcast_to(g2_ref[...].astype(F32)[None], (128, SHARD)).T
        lane = lax.broadcasted_iota(jnp.int32, (SHARD, 128), 1)
        rest = wq_ref[:, HALFW:D].astype(F32)
        rest = jnp.concatenate([rest, jnp.zeros((SHARD, 64), F32)], axis=1)
        rest = jnp.where(lane == 64, one, jnp.where(lane == 65, two, rest))
        out_ref[:, KVW : KVW + 128] = rest.astype(BF16)
        out_ref[:, KVW + 128 : HALFW] = jnp.zeros((SHARD, HALFW - KVW - 128), BF16)


def chunk_kernel(ids_ref, gu_ref, *out_refs):
    fs = ids_ref[0]
    for s in range(FS):
        at = pl.multiple_of(lax.rem(fs + s, FS) * FSL, 128)
        out_refs[s][:, 0:FSL] = gu_ref[:, pl.ds(at, FSL)]
        out_refs[s][:, FSL : 2 * FSL] = gu_ref[:, pl.ds(FF + at, FSL)]


def place_gate_up_kernel(ids_ref, *refs):
    for s in range(FS):
        at = pl.multiple_of(lax.rem(ids_ref[0] + FS - s, FS) * SHARD, 16)
        refs[FS][pl.ds(at, SHARD), :] = refs[s][...]


def qkv_kernel(ids_ref, xt_ref, *refs):
    mine = refs[0:FS]
    other = refs[FS : 2 * FS]
    cos_ref, sin_ref, out_ref, gains_ref, wa_ref, wb_ref, at_ref = refs[2 * FS :]
    fs = ids_ref[0]
    core = ids_ref[1]

    def fill(first, second):
        for s in range(FS):
            at = pl.multiple_of(lax.rem(fs + s, FS) * SHARD, 16)
            wa_ref[pl.ds(at, SHARD), :] = first[s][...]
            wb_ref[pl.ds(at, SHARD), :] = second[s][...]

    @pl.when(core == 0)
    def _():
        fill(mine, other)

    @pl.when(core == 1)
    def _():
        fill(other, mine)

    xt = xt_ref[...].astype(F32)
    gains = wb_ref[:, KVW : KVW + 128].astype(F32)
    gains_ref[...] = gains.T[64:72, :]
    r1 = lax.rsqrt(jnp.mean(xt * xt, axis=0, keepdims=True) + EPS)
    at = xt * r1 * gains[:, 64:65]
    at_ref[...] = at.astype(BF16)
    a = at.T.astype(BF16)
    lin_a = dot(a, wa_ref[...]).T
    lin_b = dot(a, wb_ref[...]).T
    cos = cos_ref[...]
    sin = sin_ref[...]

    def turned(rows):
        first = rows[0:HALF]
        second = rows[HALF:HEAD]
        return jnp.concatenate(
            [first * cos - second * sin, second * cos + first * sin], axis=0
        ).astype(BF16)

    for j in range(KV_HEADS):
        key = turned(lin_b[HEAD * j : HEAD * (j + 1)])
        value = lin_b[HEAD * (KV_HEADS + j) : HEAD * (KV_HEADS + j + 1)].astype(BF16)
        for g in range(GROUP):
            head = j * GROUP + g
            if head < HEADS - 1:
                rows = lin_a[HEAD * head : HEAD * (head + 1)]
            else:
                rows = lin_b[KVW : KVW + HEAD]
            out_ref[head, 0:HEAD, :] = turned(rows)
            out_ref[head, HEAD : 2 * HEAD, :] = key
            out_ref[head, 2 * HEAD : 3 * HEAD, :] = value
    out_ref[HEADS, :, :] = jnp.zeros((3 * HEAD, ROWS), BF16)


def pick_pair(load, first, second):
    left = load(first // 2).astype(F32)
    right = load(second // 2).astype(F32)
    left = pltpu.roll(left, (first % 2) * BLK, 1)
    right = pltpu.roll(right, (1 - second % 2) * BLK, 1)
    lane = lax.broadcasted_iota(jnp.int32, left.shape, 1)
    return jnp.where(lane < BLK, left, right)


def causal(size):
    key = lax.broadcasted_iota(jnp.int32, (size, size), 0)
    query = lax.broadcasted_iota(jnp.int32, (size, size), 1)
    return key <= query


def attend_kernel(
    order_ref, inv_ref, recv_ref, out_ref, qt_ref, kt_ref, k_ref, vt_ref, of_ref, lse_ref, s_ref
):
    for m in range(CTX):
        got = pick_pair(lambda i: recv_ref[i], inv_ref[2 * m], inv_ref[2 * m + 1])
        at = slice(2 * BLK * m, 2 * BLK * (m + 1))
        qt_ref[:, at] = (got[0:HEAD] * SCALE).astype(BF16)
        key = got[HEAD : 2 * HEAD]
        kt_ref[:, at] = key.astype(BF16)
        k_ref[at, :] = key.T.astype(BF16)
        vt_ref[:, at] = got[2 * HEAD : 3 * HEAD].astype(BF16)
    allowed = causal(TILE)
    for n in range(NT):
        span = slice(TILE * n, TILE * (n + 1))
        query = qt_ref[:, span]
        top = None
        for c in range(n + 1):
            rows = slice(TILE * c, TILE * (c + 1))
            s = dot(k_ref[rows, :], query)
            if c == n:
                s = jnp.where(allowed, s, -1e30)
            s_ref[rows, :] = s
            part = jnp.max(s, axis=0, keepdims=True)
            top = part if top is None else jnp.maximum(top, part)
        total = None
        for c in range(n + 1):
            rows = slice(TILE * c, TILE * (c + 1))
            e = jnp.exp(s_ref[rows, :] - top)
            s_ref[rows, :] = e
            part = jnp.sum(e, axis=0, keepdims=True)
            total = part if total is None else total + part
        recip = 1.0 / total
        lse_ref[n] = jnp.broadcast_to(top + jnp.log(total), (8, TILE))
        prob = (s_ref[0 : TILE * (n + 1), :] * recip).astype(BF16)
        o = dot(vt_ref[:, 0 : TILE * (n + 1)], prob)
        of_ref[2 * n] = o[:, 0 : 2 * BLK]
        of_ref[2 * n + 1] = o[:, 2 * BLK :]
    for i in range(CTX):
        got = pick_pair(lambda g: of_ref[g], order_ref[2 * i], order_ref[2 * i + 1])
        out_ref[i] = got.astype(BF16)


def attend_back_kernel(
    order_ref,
    inv_ref,
    recv_ref,
    qt_ref,
    q_ref,
    kt_ref,
    k_ref,
    v_ref,
    of_ref,
    lse_ref,
    cos_ref,
    sin_ref,
    out_ref,
    dot_ref,
    do_ref,
    delta_ref,
    dk_ref,
    dv_ref,
    st_ref,
):
    for m in range(CTX):
        got = pick_pair(lambda i: recv_ref[i], inv_ref[2 * m], inv_ref[2 * m + 1])
        at = slice(2 * BLK * m, 2 * BLK * (m + 1))
        dot_ref[:, at] = got.astype(BF16)
        do_ref[at, :] = got.T.astype(BF16)
        delta_ref[:, at] = jnp.broadcast_to(
            jnp.sum(got * of_ref[m], axis=0, keepdims=True), (8, 2 * BLK)
        )
    allowed = causal(TILE)
    for n in range(NT):
        span = slice(TILE * n, TILE * (n + 1))
        query = qt_ref[:, span]
        out_grad = dot_ref[:, span]
        lse = lse_ref[n][0:1, :]
        delta = delta_ref[0:1, span]
        dq = None
        for c in range(n + 1):
            rows = slice(TILE * c, TILE * (c + 1))
            prob = jnp.exp(dot(k_ref[rows, :], query) - lse)
            if c == n:
                prob = jnp.where(allowed, prob, 0.0)
            ds = (prob * (dot(v_ref[rows, :], out_grad) - delta)).astype(BF16)
            part = dot(kt_ref[:, rows], ds)
            dq = part if dq is None else dq + part
            dk = dot(ds, q_ref[span, :])
            dv = dot(prob.astype(BF16), do_ref[span, :])
            if c == n:
                dk_ref[rows, :] = dk
                dv_ref[rows, :] = dv
            else:
                dk_ref[rows, :] += dk
                dv_ref[rows, :] += dv
        st_ref[2 * n, 0:HEAD, :] = dq[:, 0 : 2 * BLK] * SCALE
        st_ref[2 * n + 1, 0:HEAD, :] = dq[:, 2 * BLK :] * SCALE
    for m in range(CTX):
        at = slice(2 * BLK * m, 2 * BLK * (m + 1))
        cos = cos_ref[:, at]
        sin = sin_ref[:, at]

        def turned(value):
            first = value[0:HALF]
            second = value[HALF:HEAD]
            return jnp.concatenate(
                [first * cos + second * sin, second * cos - first * sin], axis=0
            )

        st_ref[m, 0:HEAD, :] = turned(st_ref[m, 0:HEAD, :])
        st_ref[m, HEAD : 2 * HEAD, :] = turned(dk_ref[at, :].T)
        st_ref[m, 2 * HEAD : 3 * HEAD, :] = dv_ref[at, :].T
    for i in range(CTX):
        got = pick_pair(lambda g: st_ref[g], order_ref[2 * i], order_ref[2 * i + 1])
        out_ref[i] = got.astype(BF16)


def resid_kernel(ids_ref, ot_ref, w_ref, xt_ref, gains_ref, h_ref, b_ref, *refs):
    full_ref = refs[FS]
    flat = jnp.concatenate([ot_ref[h] for h in range(HEADS)], axis=0)
    full_ref[...] = flat
    for s in range(FS):
        at = pl.multiple_of(lax.rem(ids_ref[0] + s, FS) * SHARD, 16)
        refs[s][...] = full_ref[pl.ds(at, SHARD), :]
    mixed = flat.astype(F32).T.astype(BF16)
    h = xt_ref[...].astype(F32).T + dot(mixed, w_ref[...])
    h_ref[...] = h
    b_ref[...] = (h * inv_norm(h) * gains_ref[1:2, :]).astype(BF16)


def mlp_kernel(*refs):
    count = (len(refs) - 2) // 5
    b_refs = refs[0:count]
    g_refs = refs[count : 2 * count]
    gu_ref, down_ref = refs[2 * count : 2 * count + 2]
    outs = refs[2 * count + 2 :]
    for i in range(count):
        db_ref, mm_ref, dgu_ref = outs[3 * i : 3 * i + 3]
        gu = dot(b_refs[i][...], gu_ref[...])
        gate = gu[:, :FSL]
        up = gu[:, FSL:]
        sig = 1.0 / (1.0 + jnp.exp(-gate))
        act = gate * sig
        dm = dot(g_refs[i][...], down_ref[...], 0, 0)
        dgate = dm * up * sig * (1.0 + gate * (1.0 - sig))
        dgu = jnp.concatenate([dgate, dm * act], axis=1).astype(BF16)
        mm_ref[...] = (act * up).astype(BF16)
        dgu_ref[...] = dgu
        db_ref[...] = dot(dgu, gu_ref[...], 1, 1).astype(BF16)


def mlp_grad_kernel(ids_ref, *refs):
    b_refs = refs[0:FS]
    g_refs = refs[FS : 2 * FS]
    mm_refs = refs[2 * FS : 3 * FS]
    dgu_refs = refs[3 * FS : 4 * FS]
    down_ref = refs[4 * FS]
    y_refs = refs[4 * FS + 1 : 5 * FS + 1]
    keep_ref, give_ref, gu_ref, dd_ref = refs[5 * FS + 1 :]
    b = jnp.concatenate([r[...] for r in b_refs], axis=0)
    gt = jnp.concatenate([r[...] for r in g_refs], axis=1)
    mm = jnp.concatenate([r[...] for r in mm_refs], axis=0)
    dgu = jnp.concatenate([r[...] for r in dgu_refs], axis=0)
    gu_ref[...] = dot(b, dgu, 0, 0).astype(BF16)
    dd_ref[...] = dot(gt, mm).astype(BF16)

    def put(out_ref, half):
        out_ref[0:D, :] = gu_ref[:, FSL * half : FSL * (half + 1)]
        out_ref[D : D + D // 2, :] = dd_ref[D // 2 * half : D // 2 * (half + 1), :]

    for core in range(2):

        @pl.when(ids_ref[1] == core)
        def _(core=core):
            put(keep_ref, core)
            put(give_ref, 1 - core)

    for s in range(FS):
        y_refs[s][...] = dot(mm_refs[s][...], down_ref[...], 1, 1).astype(BF16)


def result_kernel(h_ref, y0, y1, y2, y3, out_ref):
    total = h_ref[...]
    for piece in (y0, y1, y2, y3):
        total += piece[...].astype(F32)
    out_ref[...] = total.T.astype(BF16)


def pack_kernel(ids_ref, keep_ref, got_ref, *refs):
    sum_ref = refs[4]
    for at in range(0, HALF_ROWS, 240):
        rows = slice(at, at + 240)
        sum_ref[rows, :] = keep_ref[rows, :].astype(F32) + got_ref[rows, :].astype(F32)
    sum_ref[HALF_ROWS:, :] = jnp.zeros((16, FSL), F32)

    def put(out_ref, first):
        for r in range(first, first + 4):
            for k in range(FS):
                at = SHARD * k + 15 * r
                out_ref[r - first, 16 * k : 16 * (k + 1), :] = sum_ref[at : at + 16, :].astype(BF16)
            at = D + 30 * r
            out_ref[r - first, 64:96, :] = sum_ref[at : at + 32, :].astype(BF16)

    for x in range(4):

        @pl.when(ids_ref[2] == x)
        def _(x=x):
            for step in range(4):
                owner = (x + step) % 4
                put(refs[step], 4 * (owner % 2 * 2 + owner // 2))


def sum_x_kernel(ids_ref, *refs):
    total = refs[0][...].astype(F32)
    for step in range(1, 4):
        total += refs[step][...].astype(F32)
    refs[8][...] = total.astype(BF16)
    for step in range(4):
        refs[4 + step][...] = refs[8][lax.rem(ids_ref[3] + step, 4)]


def sum_z_kernel(ids_ref, *refs):
    total = refs[0][...].astype(F32)
    for step in range(1, 4):
        total += refs[step][...].astype(F32)
    sum_ref = refs[9]
    sum_ref[...] = total.astype(BF16)
    for s in range(FS):
        at = pl.multiple_of(lax.rem(ids_ref[0] + s, FS) * 16, 16)
        refs[4 + s][...] = sum_ref[pl.ds(at, 16), :]
    refs[8][...] = sum_ref[64:96, :]


def mid_kernel(*refs):
    db_refs = refs[0:FS]
    h_ref, gt_ref, gains_ref, w_ref = refs[FS : FS + 4]
    o_refs = refs[FS + 4 : 2 * FS + 4]
    dh_ref, do_ref = refs[2 * FS + 4 : 2 * FS + 6]
    out_refs = refs[2 * FS + 6 :]
    db = db_refs[0][...].astype(F32)
    for ref in db_refs[1:]:
        db += ref[...].astype(F32)
    h = h_ref[...]
    r2 = inv_norm(h)
    scaled = gains_ref[1:2, :] * db
    dh = (
        gt_ref[...].astype(F32).T
        + r2 * scaled
        - h * (r2 * r2 * r2) * jnp.mean(scaled * h, axis=-1, keepdims=True)
    )
    dh_ref[...] = dh
    e = dh.astype(BF16)
    back = dot(w_ref[...], e, 1, 1).astype(BF16)
    for head in range(HEADS):
        do_ref[head] = back[HEAD * head : HEAD * (head + 1)]
    do_ref[HEADS] = jnp.zeros((HEAD, ROWS), BF16)
    for s in range(FS):
        out_refs[s][:, 0:D] = e
        o = jnp.concatenate([o_refs[s][...].astype(F32), jnp.zeros((80, ROWS), F32)], axis=0)
        out_refs[s][:, D:EO] = o.T.astype(BF16)


def head_grad_kernel(ids_ref, at_ref, d_ref, *refs):
    full_ref = refs[FS]
    total = None
    for i in range(0, CTX, 2):
        left = jnp.concatenate([at_ref[i], at_ref[i + 1]], axis=1)
        right = jnp.concatenate([d_ref[i], d_ref[i + 1]], axis=1)
        part = dot(left, right, 1, 1)
        total = part if total is None else total + part
    full_ref[...] = total.astype(BF16)
    for s in range(FS):
        at = pl.multiple_of(lax.rem(ids_ref[0] + s, FS) * SHARD, 16)
        rows = full_ref[pl.ds(at, SHARD), :]
        refs[s][0:SHARD, :] = rows[:, 0:128]
        value = rows[:, 128:192].astype(F32)
        value = jnp.concatenate([value[0 : SHARD // 2], value[SHARD // 2 :]], axis=1)
        value = jnp.concatenate([value, jnp.zeros((8, 128), F32)], axis=0)
        refs[s][SHARD:HEADROWS, :] = value.astype(BF16)


def out_grad_kernel(*refs):
    part_ref, out_ref = refs[FS:]
    total = None
    for s in range(FS):
        message = refs[s]
        part = dot(message[:, D:EO], message[:, 0:D], 0, 0)[0:SHARD]
        total = part if total is None else total + part
    pad = jnp.zeros((SHARD, 64), F32)
    total = jnp.concatenate([total, pad], axis=1).astype(BF16)
    out_ref[:, 0 : 3 * HEAD, :] = part_ref[...]
    for i in range(HEADS):
        for j in range(8):
            at = 3 * HEAD + 16 * j
            out_ref[i, at : at + 16, :] = total[16 * i : 16 * (i + 1), 128 * j : 128 * (j + 1)]
    out_ref[HEADS, 3 * HEAD :, :] = jnp.zeros((128, 128), BF16)


def head_sum_kernel(p0, p1, p2, p3, recv_ref, out_ref):
    total = p0[...].astype(F32)
    for piece in (p1, p2, p3):
        total += piece[...].astype(F32)
    out_ref[0:HEADROWS, :] = total.astype(BF16)
    total = recv_ref[0, 3 * HEAD :, :].astype(F32)
    for i in range(1, CTX):
        total += recv_ref[i, 3 * HEAD :, :].astype(F32)
    out_ref[HEADROWS:, :] = total.astype(BF16)


def last_kernel(recv_ref, wa_ref, wb_ref, xt_ref, dh_ref, gains_ref, ig_ref, msg_ref):
    for head in range(HEADS):
        msg_ref[HEAD * head : HEAD * (head + 1), :] = recv_ref[head, 0:HEAD, :]
    for part in range(2):
        for j in range(KV_HEADS):
            total = None
            for g in range(GROUP):
                piece = recv_ref[j * GROUP + g, HEAD * (part + 1) : HEAD * (part + 2), :]
                piece = piece.astype(F32)
                total = piece if total is None else total + piece
            base = D + HEAD * (KV_HEADS * part + j)
            msg_ref[base : base + HEAD, :] = total.astype(BF16)
    da = dot(wa_ref[...], msg_ref[0:HALFW, :])
    da += dot(wb_ref[:, 0:KVW], msg_ref[D:QKV, :])
    da += dot(wb_ref[:, KVW : KVW + HEAD], msg_ref[HALFW:D, :])
    x = xt_ref[...].astype(F32)
    r1 = lax.rsqrt(jnp.mean(x * x, axis=0, keepdims=True) + EPS)
    scaled = wb_ref[:, KVW : KVW + 128].astype(F32)[:, 64:65] * da
    ig_ref[...] = (
        dh_ref[...].T
        + r1 * scaled
        - x * (r1 * r1 * r1) * jnp.mean(scaled * x, axis=0, keepdims=True)
    )


def unpack_kernel(
    ids_ref, mine_ref, other_ref, wq_ref, wkv_ref, gain_in, q_ref, kv_ref, o_ref, gain_ref
):
    for core in range(2):

        @pl.when(ids_ref[1] == core)
        def _(core=core):
            blocks = []
            for head in range(HEADS):
                src = mine_ref if head % 2 == core else other_ref
                blocks.append(src[head // 2].astype(F32))
            parts = [b[0:SHARD] for b in blocks]
            tails = [b[SHARD : SHARD + SHARD // 2] for b in blocks]
            zero = jnp.zeros((SHARD, HEAD), F32)
            query = [p[:, 0:HEAD] for p in parts]
            key = []
            value = []
            for j in range(KV_HEADS):
                group = parts[GROUP * j] + parts[GROUP * j + 1] + parts[GROUP * j + 2]
                key.append(group[:, HEAD:])
                group = tails[GROUP * j] + tails[GROUP * j + 1] + tails[GROUP * j + 2]
                value.append(jnp.concatenate([group[:, 0:HEAD], group[:, HEAD:]], axis=0))
            q = jnp.concatenate(query + [zero], axis=1)[:, 0:D]
            kv = jnp.concatenate(key + value, axis=1)
            q_ref[...] = q
            kv_ref[...] = kv
            total = jnp.sum(q * wq_ref[...].astype(F32), axis=1, keepdims=True)
            total += jnp.sum(kv * wkv_ref[...].astype(F32), axis=1, keepdims=True)
            total = jnp.broadcast_to(total, (SHARD, 128)).T[0:8]
            gain_ref[...] = total[0] / gain_in[...].astype(F32)
            for i, b in enumerate(blocks):
                cols = [b[HEADROWS + 16 * j : HEADROWS + 16 * (j + 1)] for j in range(8)]
                o_ref[16 * i : 16 * (i + 1), :] = jnp.concatenate(cols, axis=1)[:, 0:D]


def widen_kernel(
    ids_ref, mine_ref, other_ref, gu_in, gain_in, gu_out, down_out, gain_ref
):
    for core in range(2):

        @pl.when(ids_ref[1] == core)
        def _(core=core):
            halves = (mine_ref, other_ref) if core == 0 else (other_ref, mine_ref)
            total = None
            down = []
            for half, src in enumerate(halves):
                for s in range(FS):
                    at = lax.rem(ids_ref[0] + FS - s, FS) * FSL + FF * half
                    cols = pl.ds(pl.multiple_of(at, 128), FSL)
                    rows = [
                        src[r, 16 * s : 16 * (s + 1), :].astype(F32)[0:15] for r in range(CTX)
                    ]
                    rows = jnp.concatenate(rows, axis=0)
                    gu_out[:, cols] = rows
                    part = jnp.sum(rows * gu_in[:, cols].astype(F32), axis=1, keepdims=True)
                    total = part if total is None else total + part
                down += [src[r, 64:96, :].astype(F32)[0:30] for r in range(CTX)]
            down_out[...] = jnp.concatenate(down, axis=0)
            total = jnp.broadcast_to(total, (SHARD, 128)).T[0:8]
            gain_ref[...] = total[0] / gain_in[...].astype(F32)


def swap_core(value):
    return lax.ppermute(value, "ctx", [(i, i ^ 1) for i in range(CTX)])


def shift(value, step):
    return lax.ppermute(value, "fsdp", [((i + step) % FS, i) for i in range(FS)])


def same_core(value):
    groups = [[2 * i + core for i in range(CTX)] for core in range(2)]
    return lax.all_to_all(value, ("seq", "ctx"), 0, 0, axis_index_groups=groups)


def shift_x(value, step):
    def at(x, z, core):
        return (x % 2) * CTX + (x // 2) * 8 + z * 2 + core

    pairs = [
        (at((x + step) % 4, z, core), at(x, z, core))
        for x in range(4)
        for z in range(4)
        for core in range(2)
    ]
    return lax.ppermute(value, ("seq", "ctx"), pairs)


def shift_z(value, step):
    def at(high, z, core):
        return high * 8 + z * 2 + core

    pairs = [
        (at(high, (z + step) % 4, core), at(high, z, core))
        for high in range(2)
        for z in range(4)
        for core in range(2)
    ]
    return lax.ppermute(value, "ctx", pairs)


def same_core_row(value):
    groups = [[2 * i + core for i in range(CTX // 2)] for core in range(2)]
    return lax.all_to_all(value, "ctx", 0, 0, axis_index_groups=groups)


def swap_seq(value):
    return lax.ppermute(value, "seq", [(0, 1), (1, 0)])


def gather_by(move, value):
    return [value] + [move(value, s) for s in range(1, 4)]


def scatter_by(move, pieces):
    return [pieces[0]] + [move(pieces[s], -s) for s in range(1, 4)]


def gather_rolled(value):
    return gather_by(shift, value)


def scatter_rolled(pieces):
    return scatter_by(shift, pieces)


def together(*values):
    return lax.optimization_barrier(values)


def shards(tokens, gain_attn, w_q, w_kv, w_o, gain_mlp, w_gate_up, w_down, block_order, cotangent):
    x_t = tokens[0].T
    g_t = cotangent[0].T
    down_t = w_down.T
    order = block_order[0]
    place = lax.axis_index("ctx")
    x_place = place // 8 * 2 + lax.axis_index("seq")
    ids = jnp.stack([lax.axis_index("fsdp"), place % 2, x_place, place // 2 % 4])
    ids = ids.astype(jnp.int32)

    slots = jnp.arange(2 * CTX, dtype=jnp.int32)
    inverse = jnp.sum(jnp.where(order[None, :] == slots[:, None], slots[None, :], 0), axis=1)
    mine = lax.dynamic_slice_in_dim(order, place * 2, 2)
    places = (mine[:, None] * BLK + jnp.arange(BLK, dtype=jnp.int32)[None, :]).reshape(ROWS)
    freq = THETA ** (-(jnp.arange(HALF, dtype=F32) * 2.0 / HEAD))
    angle = freq[:, None] * places.astype(F32)[None, :]
    angle_all = freq[:, None] * jnp.arange(L, dtype=F32)[None, :]

    (message,) = call(
        message_kernel,
        [shape(SHARD, HALFW)],
        [ids, w_q, w_kv, gain_attn, gain_mlp],
        smem=1,
    )
    w_mine = gather_rolled(message)
    chunks = call(chunk_kernel, [shape(SHARD, 2 * FSL)] * FS, [ids, w_gate_up], smem=1)
    w_mine, chunks, w_o, g_t = together(w_mine, chunks, w_o, g_t)
    w_other = [swap_core(message)] + [swap_core(piece) for piece in w_mine[1:]]
    w_out = lax.all_gather(w_o, "fsdp", axis=0, tiled=True)
    gu_pieces = scatter_rolled(chunks)
    g_all = gather_rolled(g_t)

    packed, gains, w_a, w_b, a_t = call(
        qkv_kernel,
        [
            shape(CTX, 3 * HEAD, ROWS),
            shape(8, D, dtype=F32),
            shape(D, HALFW),
            shape(D, HALFW),
            shape(D, ROWS),
        ],
        [ids, x_t] + w_mine + w_other + [jnp.cos(angle), jnp.sin(angle)],
        smem=1,
        flops=2 * ROWS * D * QKV,
    )
    a_all = lax.all_gather(a_t, "ctx", axis=0)
    received = lax.all_to_all(packed, "ctx", 0, 0)
    cos_all, sin_all = jnp.cos(angle_all), jnp.sin(angle_all)
    received, cos_all, sin_all = together(received, cos_all, sin_all)
    o_part, q_t, k_t, k_n, v_t, o_f, lse = call(
        attend_kernel,
        [
            shape(CTX, HEAD, ROWS),
            shape(HEAD, L),
            shape(HEAD, L),
            shape(L, HEAD),
            shape(HEAD, L),
            shape(CTX, HEAD, ROWS, dtype=F32),
            shape(NT, 8, TILE, dtype=F32),
        ],
        [order, inverse, received],
        smem=2,
        scratch=[pltpu.VMEM((L, TILE), F32)],
        flops=2 * L * L * HEAD,
    )
    o_all = lax.all_to_all(o_part, "ctx", 0, 0)
    q_n, v_n = q_t.T, v_t.T
    o_all, w_out, q_n, v_n, gu_pieces[1] = together(o_all, w_out, q_n, v_n, gu_pieces[1])
    h, b, *o_pieces = call(
        resid_kernel,
        [shape(ROWS, D, dtype=F32), shape(ROWS, D)] + [shape(SHARD, ROWS)] * FS,
        [ids, o_all, w_out, x_t, gains],
        smem=1,
        scratch=[pltpu.VMEM((D, ROWS), BF16)],
        flops=2 * ROWS * D * D,
    )
    b, gu_pieces, g_all = together(b, gu_pieces, g_all)
    (w_gu,) = call(place_gate_up_kernel, [shape(D, 2 * FSL)], [ids] + gu_pieces, smem=1)
    b_all = gather_rolled(b)
    db, mm, dgu = [None] * FS, [None] * FS, [None] * FS
    before = None
    for partners in ((0,), (1, 3), (2,)):
        if before is not None:
            b_all[partners[0]], before = together(b_all[partners[0]], before)
        outs = call(
            mlp_kernel,
            [shape(ROWS, D), shape(ROWS, FSL), shape(ROWS, 2 * FSL)] * len(partners),
            [b_all[s] for s in partners] + [g_all[s] for s in partners] + [w_gu, down_t],
            flops=10 * len(partners) * ROWS * D * FSL,
            limit=MLP_BYTES,
        )
        for i, s in enumerate(partners):
            db[s], mm[s], dgu[s] = outs[3 * i : 3 * i + 3]
        before = mm[partners[0]]
    db = scatter_rolled(db)
    *y_parts, keep, give = call(
        mlp_grad_kernel,
        [shape(ROWS, D)] * FS + [shape(HALF_ROWS, FSL)] * 2,
        [ids] + b_all + g_all + mm + dgu + [down_t],
        smem=1,
        scratch=[pltpu.VMEM((D, 2 * FSL), BF16), pltpu.VMEM((D, FSL), BF16)],
        flops=8 * FS * ROWS * D * FSL,
        limit=MLP_BYTES,
    )
    db, keep = together(db, keep)
    dh, do_part, *eo_parts = call(
        mid_kernel,
        [shape(ROWS, D, dtype=F32), shape(CTX, HEAD, ROWS)] + [shape(ROWS, EO)] * FS,
        db + [h, g_t, gains, w_out] + o_pieces,
        flops=2 * ROWS * D * D,
    )
    do_all = lax.all_to_all(do_part, "ctx", 0, 0)
    eo_parts, give = together(eo_parts, give)
    got = swap_core(give)
    x_pieces = call(
        pack_kernel,
        [shape(4, 96, FSL)] * 4,
        [ids, keep, got],
        smem=1,
        scratch=[pltpu.VMEM((HALF_ROWS + 16, FSL), F32)],
    )
    eo_all = scatter_rolled(eo_parts)
    do_all, x_pieces, eo_all[1], eo_all[3] = together(do_all, x_pieces, eo_all[1], eo_all[3])
    x_pieces = scatter_by(shift_x, x_pieces)
    (dqkv_part,) = call(
        attend_back_kernel,
        [shape(CTX, 3 * HEAD, ROWS)],
        [order, inverse, do_all, q_t, q_n, k_t, k_n, v_n, o_f, lse, cos_all, sin_all],
        smem=2,
        scratch=[
            pltpu.VMEM((HEAD, L), BF16),
            pltpu.VMEM((L, HEAD), BF16),
            pltpu.VMEM((8, L), F32),
            pltpu.VMEM((L, HEAD), F32),
            pltpu.VMEM((L, HEAD), F32),
            pltpu.VMEM((CTX, 3 * HEAD, ROWS), F32),
        ],
        flops=5 * L * L * HEAD,
    )
    head_pieces = call(
        head_grad_kernel,
        [shape(HEADROWS, 128)] * FS,
        [ids, a_all, dqkv_part],
        smem=1,
        scratch=[pltpu.VMEM((D, 3 * HEAD), BF16)],
        flops=2 * L * D * 3 * HEAD,
    )
    dqkv_part, head_pieces, eo_all, x_pieces = together(dqkv_part, head_pieces, eo_all, x_pieces)
    (message,) = call(
        out_grad_kernel,
        [shape(CTX, 3 * HEAD + 128, ROWS)],
        eo_all + [dqkv_part],
        flops=2 * FS * ROWS * SHARD * D,
    )
    dqkv = lax.all_to_all(message, "ctx", 0, 0)
    head_pieces = scatter_rolled(head_pieces)
    z_pieces = call(
        sum_x_kernel,
        [shape(96, FSL)] * 4,
        [ids] + x_pieces,
        smem=1,
        scratch=[pltpu.VMEM((4, 96, FSL), BF16)],
    )
    *pieces, down_sum = call(
        sum_z_kernel,
        [shape(16, FSL)] * FS + [shape(32, FSL)],
        [ids] + scatter_by(shift_z, z_pieces),
        smem=1,
        scratch=[pltpu.VMEM((96, FSL), BF16)],
    )
    own = jnp.concatenate(scatter_rolled(pieces) + [down_sum], axis=0)
    dqkv, own, head_pieces, y_parts = together(dqkv, own, head_pieces, y_parts)
    y = scatter_rolled(y_parts)
    mine_all = same_core(jnp.broadcast_to(own[None], (CTX, 96, FSL)))
    (head_sum,) = call(head_sum_kernel, [shape(HEADROWS + 128, 128)], head_pieces + [dqkv])
    head_sum = (head_sum.astype(F32) + swap_seq(head_sum).astype(F32)).astype(BF16)
    (input_grad,) = call(
        last_kernel,
        [shape(D, ROWS, dtype=F32)],
        [dqkv, w_a, w_b, x_t, dh, gains],
        scratch=[pltpu.VMEM((QKV, ROWS), BF16)],
        flops=2 * ROWS * D * QKV,
    )
    (result,) = call(result_kernel, [shape(D, ROWS)], [h] + y)
    mine_all, head_sum, input_grad, result = together(mine_all, head_sum, input_grad, result)
    head_mine = same_core_row(jnp.broadcast_to(head_sum[None], (CTX // 2, HEADROWS + 128, 128)))
    gu_out, down_out, gain_two = call(
        widen_kernel,
        [
            shape(SHARD, 2 * FF, dtype=F32),
            shape(D, FSL, dtype=F32),
            shape(SHARD, dtype=F32),
        ],
        [ids, mine_all, swap_core(mine_all), w_gate_up, gain_mlp],
        smem=1,
    )
    head_mine, gu_out, down_out, gain_two = together(head_mine, gu_out, down_out, gain_two)
    q_out, kv_out, o_out, gain_one = call(
        unpack_kernel,
        [
            shape(SHARD, D, dtype=F32),
            shape(SHARD, KVW, dtype=F32),
            shape(SHARD, D, dtype=F32),
            shape(SHARD, dtype=F32),
        ],
        [ids, head_mine, swap_core(head_mine), w_q, w_kv, gain_attn],
        smem=1,
    )
    return (
        result.T[None],
        input_grad.T[None],
        gain_one,
        q_out,
        kv_out,
        o_out,
        gain_two,
        gu_out,
        down_out.T,
    )


def solution(mesh):
    tokens = P(("seq", "fsdp"), "ctx", None)
    return jax.shard_map(
        shards,
        mesh=mesh,
        in_specs=(
            tokens,
            P("fsdp"),
            P("fsdp", None),
            P("fsdp", None),
            P("fsdp", None),
            P("fsdp"),
            P("fsdp", None),
            P("fsdp", None),
            P(("seq", "fsdp"), None),
            tokens,
        ),
        out_specs=(
            tokens,
            tokens,
            P("fsdp"),
            P("fsdp", None),
            P("fsdp", None),
            P("fsdp", None),
            P("fsdp"),
            P("fsdp", None),
            P("fsdp", None),
        ),
        check_vma=False,
    )
```

```python
import jax
import jax.numpy as jnp
from jax import lax
from jax.experimental import pallas as pl
from jax.experimental.pallas import tpu as pltpu
from jax.sharding import PartitionSpec as P

D = 960
HEADS = 15
KV_HEADS = 5
GROUP = 3
HEAD = 64
HALF = 32
FF = 2560
BLK = 64
L = 2048
CTX = 16
FS = 4
ROWS = 128
QKV = 1600
HEADROWS = 368
EO = 1280
HALFW = 896
KVW = 640
HALF_ROWS = D + D // 2
SHARD = D // FS
FSL = FF // FS
TILE = 256
NT = L // TILE
EPS = 1e-05
THETA = 100000.0
SCALE = HEAD**-0.5
F32 = jnp.float32
BF16 = jnp.bfloat16
VMEM_BYTES = 56 * 1024 * 1024
MLP_BYTES = 24 * 1024 * 1024


def call(kernel, outs, args, smem=0, scratch=(), flops=0, limit=VMEM_BYTES):
    specs = [pl.BlockSpec(memory_space=pltpu.SMEM)] * smem
    specs += [pl.BlockSpec(memory_space=pltpu.VMEM)] * (len(args) - smem)
    moved = sum(a.size * a.dtype.itemsize for a in list(args) + list(outs))
    return pl.pallas_call(
        kernel,
        out_shape=outs,
        in_specs=specs,
        out_specs=[pl.BlockSpec(memory_space=pltpu.VMEM)] * len(outs),
        scratch_shapes=list(scratch),
        cost_estimate=pl.CostEstimate(flops=flops, bytes_accessed=moved, transcendentals=0),
        compiler_params=pltpu.CompilerParams(vmem_limit_bytes=limit),
    )(*args)


def shape(*dims, dtype=BF16):
    return jax.ShapeDtypeStruct(dims, dtype)


def dot(left, right, a=1, b=0):
    return lax.dot_general(left, right, (((a,), (b,)), ((), ())), preferred_element_type=F32)


def inv_norm(rows):
    return lax.rsqrt(jnp.mean(rows * rows, axis=-1, keepdims=True) + EPS)


def message_kernel(ids_ref, wq_ref, wkv_ref, g1_ref, g2_ref, out_ref):
    core = ids_ref[1]

    @pl.when(core == 0)
    def _():
        out_ref[...] = wq_ref[:, 0:HALFW]

    @pl.when(core == 1)
    def _():
        out_ref[:, 0:KVW] = wkv_ref[...]
        one = jnp.broadcast_to(g1_ref[...].astype(F32)[None], (128, SHARD)).T
        two = jnp.broadcast_to(g2_ref[...].astype(F32)[None], (128, SHARD)).T
        lane = lax.broadcasted_iota(jnp.int32, (SHARD, 128), 1)
        rest = wq_ref[:, HALFW:D].astype(F32)
        rest = jnp.concatenate([rest, jnp.zeros((SHARD, 64), F32)], axis=1)
        rest = jnp.where(lane == 64, one, jnp.where(lane == 65, two, rest))
        out_ref[:, KVW : KVW + 128] = rest.astype(BF16)
        out_ref[:, KVW + 128 : HALFW] = jnp.zeros((SHARD, HALFW - KVW - 128), BF16)


def chunk_kernel(ids_ref, gu_ref, *out_refs):
    fs = ids_ref[0]
    core = ids_ref[1]
    for s in range(FS):
        at = lax.rem(fs + s, FS) * FSL + core * FF
        out_refs[s][...] = gu_ref[:, pl.ds(pl.multiple_of(at, 128), FSL)]
    at = fs * FSL + (1 - core) * FF
    out_refs[FS][...] = gu_ref[:, pl.ds(pl.multiple_of(at, 128), FSL)]


def place_gate_up_kernel(ids_ref, *refs):
    out_ref = refs[2 * FS]
    for half in range(2):

        @pl.when(ids_ref[1] == half)
        def _(half=half):
            for s in range(FS):
                at = pl.multiple_of(lax.rem(ids_ref[0] + FS - s, FS) * SHARD, 16)
                for other in range(2):
                    cols = slice(FSL * (half ^ other), FSL * ((half ^ other) + 1))
                    out_ref[pl.ds(at, SHARD), cols] = refs[FS * other + s][...]


def qkv_kernel(ids_ref, xt_ref, *refs):
    mine = refs[0:FS]
    other = refs[FS : 2 * FS]
    cos_ref, sin_ref, out_ref, gains_ref, wa_ref, wb_ref, at_ref = refs[2 * FS :]
    fs = ids_ref[0]
    core = ids_ref[1]

    def fill(first, second):
        for s in range(FS):
            at = pl.multiple_of(lax.rem(fs + s, FS) * SHARD, 16)
            wa_ref[pl.ds(at, SHARD), :] = first[s][...]
            wb_ref[pl.ds(at, SHARD), :] = second[s][...]

    @pl.when(core == 0)
    def _():
        fill(mine, other)

    @pl.when(core == 1)
    def _():
        fill(other, mine)

    xt = xt_ref[...].astype(F32)
    gains = wb_ref[:, KVW : KVW + 128].astype(F32)
    gains_ref[...] = gains.T[64:72, :]
    r1 = lax.rsqrt(jnp.mean(xt * xt, axis=0, keepdims=True) + EPS)
    at = xt * r1 * gains[:, 64:65]
    at_ref[...] = at.astype(BF16)
    a = at.T.astype(BF16)
    lin_a = dot(a, wa_ref[...]).T
    lin_b = dot(a, wb_ref[...]).T
    cos = cos_ref[...]
    sin = sin_ref[...]

    def turned(rows):
        first = rows[0:HALF]
        second = rows[HALF:HEAD]
        return jnp.concatenate(
            [first * cos - second * sin, second * cos + first * sin], axis=0
        ).astype(BF16)

    for j in range(KV_HEADS):
        key = turned(lin_b[HEAD * j : HEAD * (j + 1)])
        value = lin_b[HEAD * (KV_HEADS + j) : HEAD * (KV_HEADS + j + 1)].astype(BF16)
        for g in range(GROUP):
            head = j * GROUP + g
            if head < HEADS - 1:
                rows = lin_a[HEAD * head : HEAD * (head + 1)]
            else:
                rows = lin_b[KVW : KVW + HEAD]
            out_ref[head, 0:HEAD, :] = turned(rows)
            out_ref[head, HEAD : 2 * HEAD, :] = key
            out_ref[head, 2 * HEAD : 3 * HEAD, :] = value
    out_ref[HEADS, :, :] = jnp.zeros((3 * HEAD, ROWS), BF16)


def pick_pair(load, first, second):
    left = load(first // 2).astype(F32)
    right = load(second // 2).astype(F32)
    left = pltpu.roll(left, (first % 2) * BLK, 1)
    right = pltpu.roll(right, (1 - second % 2) * BLK, 1)
    lane = lax.broadcasted_iota(jnp.int32, left.shape, 1)
    return jnp.where(lane < BLK, left, right)


def causal(size):
    key = lax.broadcasted_iota(jnp.int32, (size, size), 0)
    query = lax.broadcasted_iota(jnp.int32, (size, size), 1)
    return key <= query


def attend_kernel(
    order_ref, inv_ref, recv_ref, out_ref, qt_ref, kt_ref, k_ref, vt_ref, of_ref, lse_ref, s_ref
):
    for m in range(CTX):
        got = pick_pair(lambda i: recv_ref[i], inv_ref[2 * m], inv_ref[2 * m + 1])
        at = slice(2 * BLK * m, 2 * BLK * (m + 1))
        qt_ref[:, at] = (got[0:HEAD] * SCALE).astype(BF16)
        key = got[HEAD : 2 * HEAD]
        kt_ref[:, at] = key.astype(BF16)
        k_ref[at, :] = key.T.astype(BF16)
        vt_ref[:, at] = got[2 * HEAD : 3 * HEAD].astype(BF16)
    allowed = causal(TILE)
    for n in range(NT):
        span = slice(TILE * n, TILE * (n + 1))
        query = qt_ref[:, span]
        top = None
        for c in range(n + 1):
            rows = slice(TILE * c, TILE * (c + 1))
            s = dot(k_ref[rows, :], query)
            if c == n:
                s = jnp.where(allowed, s, -1e30)
            s_ref[rows, :] = s
            part = jnp.max(s, axis=0, keepdims=True)
            top = part if top is None else jnp.maximum(top, part)
        total = None
        for c in range(n + 1):
            rows = slice(TILE * c, TILE * (c + 1))
            e = jnp.exp(s_ref[rows, :] - top)
            s_ref[rows, :] = e
            part = jnp.sum(e, axis=0, keepdims=True)
            total = part if total is None else total + part
        recip = 1.0 / total
        lse_ref[n] = jnp.broadcast_to(top + jnp.log(total), (8, TILE))
        prob = (s_ref[0 : TILE * (n + 1), :] * recip).astype(BF16)
        o = dot(vt_ref[:, 0 : TILE * (n + 1)], prob)
        of_ref[2 * n] = o[:, 0 : 2 * BLK]
        of_ref[2 * n + 1] = o[:, 2 * BLK :]
    for i in range(CTX):
        got = pick_pair(lambda g: of_ref[g], order_ref[2 * i], order_ref[2 * i + 1])
        out_ref[i] = got.astype(BF16)


def attend_back_kernel(
    order_ref,
    inv_ref,
    recv_ref,
    qt_ref,
    q_ref,
    kt_ref,
    k_ref,
    v_ref,
    of_ref,
    lse_ref,
    cos_ref,
    sin_ref,
    out_ref,
    dot_ref,
    do_ref,
    delta_ref,
    dk_ref,
    dv_ref,
    st_ref,
):
    for m in range(CTX):
        got = pick_pair(lambda i: recv_ref[i], inv_ref[2 * m], inv_ref[2 * m + 1])
        at = slice(2 * BLK * m, 2 * BLK * (m + 1))
        dot_ref[:, at] = got.astype(BF16)
        do_ref[at, :] = got.T.astype(BF16)
        delta_ref[:, at] = jnp.broadcast_to(
            jnp.sum(got * of_ref[m], axis=0, keepdims=True), (8, 2 * BLK)
        )
    allowed = causal(TILE)
    for n in range(NT):
        span = slice(TILE * n, TILE * (n + 1))
        query = qt_ref[:, span]
        out_grad = dot_ref[:, span]
        lse = lse_ref[n][0:1, :]
        delta = delta_ref[0:1, span]
        dq = None
        for c in range(n + 1):
            rows = slice(TILE * c, TILE * (c + 1))
            prob = jnp.exp(dot(k_ref[rows, :], query) - lse)
            if c == n:
                prob = jnp.where(allowed, prob, 0.0)
            ds = (prob * (dot(v_ref[rows, :], out_grad) - delta)).astype(BF16)
            part = dot(kt_ref[:, rows], ds)
            dq = part if dq is None else dq + part
            dk = dot(ds, q_ref[span, :])
            dv = dot(prob.astype(BF16), do_ref[span, :])
            if c == n:
                dk_ref[rows, :] = dk
                dv_ref[rows, :] = dv
            else:
                dk_ref[rows, :] += dk
                dv_ref[rows, :] += dv
        st_ref[2 * n, 0:HEAD, :] = dq[:, 0 : 2 * BLK] * SCALE
        st_ref[2 * n + 1, 0:HEAD, :] = dq[:, 2 * BLK :] * SCALE
    for m in range(CTX):
        at = slice(2 * BLK * m, 2 * BLK * (m + 1))
        cos = cos_ref[:, at]
        sin = sin_ref[:, at]

        def turned(value):
            first = value[0:HALF]
            second = value[HALF:HEAD]
            return jnp.concatenate(
                [first * cos + second * sin, second * cos - first * sin], axis=0
            )

        st_ref[m, 0:HEAD, :] = turned(st_ref[m, 0:HEAD, :])
        st_ref[m, HEAD : 2 * HEAD, :] = turned(dk_ref[at, :].T)
        st_ref[m, 2 * HEAD : 3 * HEAD, :] = dv_ref[at, :].T
    for i in range(CTX):
        got = pick_pair(lambda g: st_ref[g], order_ref[2 * i], order_ref[2 * i + 1])
        out_ref[i] = got.astype(BF16)


def resid_kernel(ids_ref, ot_ref, w_ref, xt_ref, gains_ref, h_ref, b_ref, *refs):
    full_ref = refs[FS]
    flat = jnp.concatenate([ot_ref[h] for h in range(HEADS)], axis=0)
    full_ref[...] = flat
    for s in range(FS):
        at = pl.multiple_of(lax.rem(ids_ref[0] + s, FS) * SHARD, 16)
        refs[s][...] = full_ref[pl.ds(at, SHARD), :]
    mixed = flat.astype(F32).T.astype(BF16)
    h = xt_ref[...].astype(F32).T + dot(mixed, w_ref[...])
    h_ref[...] = h
    b_ref[...] = (h * inv_norm(h) * gains_ref[1:2, :]).astype(BF16)


def mlp_kernel(*refs):
    count = (len(refs) - 2) // 5
    b_refs = refs[0:count]
    g_refs = refs[count : 2 * count]
    gu_ref, down_ref = refs[2 * count : 2 * count + 2]
    outs = refs[2 * count + 2 :]
    for i in range(count):
        db_ref, mm_ref, dgu_ref = outs[3 * i : 3 * i + 3]
        gu = dot(b_refs[i][...], gu_ref[...])
        gate = gu[:, :FSL]
        up = gu[:, FSL:]
        sig = 1.0 / (1.0 + jnp.exp(-gate))
        act = gate * sig
        dm = dot(g_refs[i][...], down_ref[...], 0, 0)
        dgate = dm * up * sig * (1.0 + gate * (1.0 - sig))
        dgu = jnp.concatenate([dgate, dm * act], axis=1).astype(BF16)
        mm_ref[...] = (act * up).astype(BF16)
        dgu_ref[...] = dgu
        db_ref[...] = dot(dgu, gu_ref[...], 1, 1).astype(BF16)


def mlp_grad_kernel(ids_ref, *refs):
    b_refs = refs[0:FS]
    g_refs = refs[FS : 2 * FS]
    mm_refs = refs[2 * FS : 3 * FS]
    dgu_refs = refs[3 * FS : 4 * FS]
    down_ref = refs[4 * FS]
    y_refs = refs[4 * FS + 1 : 5 * FS + 1]
    keep_ref, give_ref, gu_ref, dd_ref = refs[5 * FS + 1 :]
    b = jnp.concatenate([r[...] for r in b_refs], axis=0)
    gt = jnp.concatenate([r[...] for r in g_refs], axis=1)
    mm = jnp.concatenate([r[...] for r in mm_refs], axis=0)
    dgu = jnp.concatenate([r[...] for r in dgu_refs], axis=0)
    gu_ref[...] = dot(b, dgu, 0, 0).astype(BF16)
    dd_ref[...] = dot(gt, mm).astype(BF16)

    def put(out_ref, half):
        out_ref[0:D, :] = gu_ref[:, FSL * half : FSL * (half + 1)]
        out_ref[D : D + D // 2, :] = dd_ref[D // 2 * half : D // 2 * (half + 1), :]

    for core in range(2):

        @pl.when(ids_ref[1] == core)
        def _(core=core):
            put(keep_ref, core)
            put(give_ref, 1 - core)

    for s in range(FS):
        y_refs[s][...] = dot(mm_refs[s][...], down_ref[...], 1, 1).astype(BF16)


def result_kernel(h_ref, y0, y1, y2, y3, out_ref):
    total = h_ref[...]
    for piece in (y0, y1, y2, y3):
        total += piece[...].astype(F32)
    out_ref[...] = total.T.astype(BF16)


def pack_kernel(ids_ref, keep_ref, got_ref, *refs):
    sum_ref = refs[4]
    for at in range(0, HALF_ROWS, 240):
        rows = slice(at, at + 240)
        sum_ref[rows, :] = keep_ref[rows, :].astype(F32) + got_ref[rows, :].astype(F32)
    sum_ref[HALF_ROWS:, :] = jnp.zeros((16, FSL), F32)

    def put(out_ref, first):
        for r in range(first, first + 4):
            for k in range(FS):
                at = SHARD * k + 15 * r
                out_ref[r - first, 16 * k : 16 * (k + 1), :] = sum_ref[at : at + 16, :].astype(BF16)
            at = D + 30 * r
            out_ref[r - first, 64:96, :] = sum_ref[at : at + 32, :].astype(BF16)

    for x in range(4):

        @pl.when(ids_ref[2] == x)
        def _(x=x):
            for step in range(4):
                owner = (x + step) % 4
                put(refs[step], 4 * (owner % 2 * 2 + owner // 2))


def sum_x_kernel(ids_ref, *refs):
    total = refs[0][...].astype(F32)
    for step in range(1, 4):
        total += refs[step][...].astype(F32)
    refs[8][...] = total.astype(BF16)
    for step in range(4):
        refs[4 + step][...] = refs[8][lax.rem(ids_ref[3] + step, 4)]


def sum_z_kernel(ids_ref, *refs):
    total = refs[0][...].astype(F32)
    for step in range(1, 4):
        total += refs[step][...].astype(F32)
    sum_ref = refs[9]
    sum_ref[...] = total.astype(BF16)
    for s in range(FS):
        at = pl.multiple_of(lax.rem(ids_ref[0] + s, FS) * 16, 16)
        refs[4 + s][...] = sum_ref[pl.ds(at, 16), :]
    refs[8][...] = sum_ref[64:96, :]


def mid_kernel(*refs):
    db_refs = refs[0:FS]
    h_ref, gt_ref, gains_ref, w_ref = refs[FS : FS + 4]
    o_refs = refs[FS + 4 : 2 * FS + 4]
    dh_ref, do_ref = refs[2 * FS + 4 : 2 * FS + 6]
    out_refs = refs[2 * FS + 6 :]
    db = db_refs[0][...].astype(F32)
    for ref in db_refs[1:]:
        db += ref[...].astype(F32)
    h = h_ref[...]
    r2 = inv_norm(h)
    scaled = gains_ref[1:2, :] * db
    dh = (
        gt_ref[...].astype(F32).T
        + r2 * scaled
        - h * (r2 * r2 * r2) * jnp.mean(scaled * h, axis=-1, keepdims=True)
    )
    dh_ref[...] = dh
    e = dh.astype(BF16)
    back = dot(w_ref[...], e, 1, 1).astype(BF16)
    for head in range(HEADS):
        do_ref[head] = back[HEAD * head : HEAD * (head + 1)]
    do_ref[HEADS] = jnp.zeros((HEAD, ROWS), BF16)
    for s in range(FS):
        out_refs[s][:, 0:D] = e
        o = jnp.concatenate([o_refs[s][...].astype(F32), jnp.zeros((80, ROWS), F32)], axis=0)
        out_refs[s][:, D:EO] = o.T.astype(BF16)


def head_grad_kernel(ids_ref, at_ref, d_ref, *refs):
    full_ref = refs[FS]
    total = None
    for i in range(0, CTX, 2):
        left = jnp.concatenate([at_ref[i], at_ref[i + 1]], axis=1)
        right = jnp.concatenate([d_ref[i], d_ref[i + 1]], axis=1)
        part = dot(left, right, 1, 1)
        total = part if total is None else total + part
    full_ref[...] = total.astype(BF16)
    for s in range(FS):
        at = pl.multiple_of(lax.rem(ids_ref[0] + s, FS) * SHARD, 16)
        rows = full_ref[pl.ds(at, SHARD), :]
        refs[s][0:SHARD, :] = rows[:, 0:128]
        value = rows[:, 128:192].astype(F32)
        value = jnp.concatenate([value[0 : SHARD // 2], value[SHARD // 2 :]], axis=1)
        value = jnp.concatenate([value, jnp.zeros((8, 128), F32)], axis=0)
        refs[s][SHARD:HEADROWS, :] = value.astype(BF16)


def out_grad_kernel(*refs):
    out_ref = refs[FS]
    total = None
    for s in range(FS):
        message = refs[s]
        part = dot(message[:, D:EO], message[:, 0:D], 0, 0)[0:SHARD]
        total = part if total is None else total + part
    pad = jnp.zeros((SHARD, 64), F32)
    total = jnp.concatenate([total, pad], axis=1).astype(BF16)
    for i in range(HEADS):
        for j in range(8):
            out_ref[i, 16 * j : 16 * (j + 1), :] = total[
                16 * i : 16 * (i + 1), 128 * j : 128 * (j + 1)
            ]
    out_ref[HEADS, :, :] = jnp.zeros((128, 128), BF16)


def head_sum_kernel(p0, p1, p2, p3, recv_ref, out_ref):
    total = p0[...].astype(F32)
    for piece in (p1, p2, p3):
        total += piece[...].astype(F32)
    out_ref[0:HEADROWS, :] = total.astype(BF16)
    total = recv_ref[0].astype(F32)
    for i in range(1, CTX):
        total += recv_ref[i].astype(F32)
    out_ref[HEADROWS:, :] = total.astype(BF16)


def last_kernel(recv_ref, wa_ref, wb_ref, xt_ref, dh_ref, gains_ref, ig_ref, msg_ref):
    for head in range(HEADS):
        msg_ref[HEAD * head : HEAD * (head + 1), :] = recv_ref[head, 0:HEAD, :]
    for part in range(2):
        for j in range(KV_HEADS):
            total = None
            for g in range(GROUP):
                piece = recv_ref[j * GROUP + g, HEAD * (part + 1) : HEAD * (part + 2), :]
                piece = piece.astype(F32)
                total = piece if total is None else total + piece
            base = D + HEAD * (KV_HEADS * part + j)
            msg_ref[base : base + HEAD, :] = total.astype(BF16)
    da = dot(wa_ref[...], msg_ref[0:HALFW, :])
    da += dot(wb_ref[:, 0:KVW], msg_ref[D:QKV, :])
    da += dot(wb_ref[:, KVW : KVW + HEAD], msg_ref[HALFW:D, :])
    x = xt_ref[...].astype(F32)
    r1 = lax.rsqrt(jnp.mean(x * x, axis=0, keepdims=True) + EPS)
    scaled = wb_ref[:, KVW : KVW + 128].astype(F32)[:, 64:65] * da
    ig_ref[...] = (
        dh_ref[...].T
        + r1 * scaled
        - x * (r1 * r1 * r1) * jnp.mean(scaled * x, axis=0, keepdims=True)
    )


def unpack_kernel(
    ids_ref, mine_ref, other_ref, wq_ref, wkv_ref, gain_in, q_ref, kv_ref, o_ref, gain_ref
):
    for core in range(2):

        @pl.when(ids_ref[1] == core)
        def _(core=core):
            blocks = []
            for head in range(HEADS):
                src = mine_ref if head % 2 == core else other_ref
                blocks.append(src[head // 2].astype(F32))
            parts = [b[0:SHARD] for b in blocks]
            tails = [b[SHARD : SHARD + SHARD // 2] for b in blocks]
            zero = jnp.zeros((SHARD, HEAD), F32)
            query = [p[:, 0:HEAD] for p in parts]
            key = []
            value = []
            for j in range(KV_HEADS):
                group = parts[GROUP * j] + parts[GROUP * j + 1] + parts[GROUP * j + 2]
                key.append(group[:, HEAD:])
                group = tails[GROUP * j] + tails[GROUP * j + 1] + tails[GROUP * j + 2]
                value.append(jnp.concatenate([group[:, 0:HEAD], group[:, HEAD:]], axis=0))
            q = jnp.concatenate(query + [zero], axis=1)[:, 0:D]
            kv = jnp.concatenate(key + value, axis=1)
            q_ref[...] = q
            kv_ref[...] = kv
            total = jnp.sum(q * wq_ref[...].astype(F32), axis=1, keepdims=True)
            total += jnp.sum(kv * wkv_ref[...].astype(F32), axis=1, keepdims=True)
            total = jnp.broadcast_to(total, (SHARD, 128)).T[0:8]
            gain_ref[...] = total[0] / gain_in[...].astype(F32)
            for i, b in enumerate(blocks):
                cols = [b[HEADROWS + 16 * j : HEADROWS + 16 * (j + 1)] for j in range(8)]
                o_ref[16 * i : 16 * (i + 1), :] = jnp.concatenate(cols, axis=1)[:, 0:D]


def widen_kernel(
    ids_ref, mine_ref, other_ref, gu_in, gain_in, gu_out, down_out, gain_ref
):
    for core in range(2):

        @pl.when(ids_ref[1] == core)
        def _(core=core):
            halves = (mine_ref, other_ref) if core == 0 else (other_ref, mine_ref)
            total = None
            down = []
            for half, src in enumerate(halves):
                for s in range(FS):
                    at = lax.rem(ids_ref[0] + FS - s, FS) * FSL + FF * half
                    cols = pl.ds(pl.multiple_of(at, 128), FSL)
                    rows = [
                        src[r, 16 * s : 16 * (s + 1), :].astype(F32)[0:15] for r in range(CTX)
                    ]
                    rows = jnp.concatenate(rows, axis=0)
                    gu_out[:, cols] = rows
                    part = jnp.sum(rows * gu_in[:, cols].astype(F32), axis=1, keepdims=True)
                    total = part if total is None else total + part
                down += [src[r, 64:96, :].astype(F32)[0:30] for r in range(CTX)]
            down_out[...] = jnp.concatenate(down, axis=0)
            total = jnp.broadcast_to(total, (SHARD, 128)).T[0:8]
            gain_ref[...] = total[0] / gain_in[...].astype(F32)


def swap_core(value):
    return lax.ppermute(value, "ctx", [(i, i ^ 1) for i in range(CTX)])


def shift(value, step):
    return lax.ppermute(value, "fsdp", [((i + step) % FS, i) for i in range(FS)])


def same_core(value):
    groups = [[2 * i + core for i in range(CTX)] for core in range(2)]
    return lax.all_to_all(value, ("seq", "ctx"), 0, 0, axis_index_groups=groups)


def shift_x(value, step):
    def at(x, z, core):
        return (x % 2) * CTX + (x // 2) * 8 + z * 2 + core

    pairs = [
        (at((x + step) % 4, z, core), at(x, z, core))
        for x in range(4)
        for z in range(4)
        for core in range(2)
    ]
    return lax.ppermute(value, ("seq", "ctx"), pairs)


def shift_z(value, step):
    def at(high, z, core):
        return high * 8 + z * 2 + core

    pairs = [
        (at(high, (z + step) % 4, core), at(high, z, core))
        for high in range(2)
        for z in range(4)
        for core in range(2)
    ]
    return lax.ppermute(value, "ctx", pairs)


def same_core_row(value):
    groups = [[2 * i + core for i in range(CTX // 2)] for core in range(2)]
    return lax.all_to_all(value, "ctx", 0, 0, axis_index_groups=groups)


def swap_seq(value):
    return lax.ppermute(value, "seq", [(0, 1), (1, 0)])


def gather_by(move, value):
    return [value] + [move(value, s) for s in range(1, 4)]


def scatter_by(move, pieces):
    return [pieces[0]] + [move(pieces[s], -s) for s in range(1, 4)]


def gather_rolled(value):
    return gather_by(shift, value)


def scatter_rolled(pieces):
    return scatter_by(shift, pieces)


def together(*values):
    return lax.optimization_barrier(values)


def shards(tokens, gain_attn, w_q, w_kv, w_o, gain_mlp, w_gate_up, w_down, block_order, cotangent):
    x_t = tokens[0].T
    g_t = cotangent[0].T
    down_t = w_down.T
    order = block_order[0]
    place = lax.axis_index("ctx")
    x_place = place // 8 * 2 + lax.axis_index("seq")
    ids = jnp.stack([lax.axis_index("fsdp"), place % 2, x_place, place // 2 % 4])
    ids = ids.astype(jnp.int32)

    slots = jnp.arange(2 * CTX, dtype=jnp.int32)
    inverse = jnp.sum(jnp.where(order[None, :] == slots[:, None], slots[None, :], 0), axis=1)
    mine = lax.dynamic_slice_in_dim(order, place * 2, 2)
    places = (mine[:, None] * BLK + jnp.arange(BLK, dtype=jnp.int32)[None, :]).reshape(ROWS)
    freq = THETA ** (-(jnp.arange(HALF, dtype=F32) * 2.0 / HEAD))
    angle = freq[:, None] * places.astype(F32)[None, :]
    angle_all = freq[:, None] * jnp.arange(L, dtype=F32)[None, :]

    (message,) = call(
        message_kernel,
        [shape(SHARD, HALFW)],
        [ids, w_q, w_kv, gain_attn, gain_mlp],
        smem=1,
    )
    w_mine = gather_rolled(message)
    *chunks, gu_local = call(
        chunk_kernel, [shape(SHARD, FSL)] * (FS + 1), [ids, w_gate_up], smem=1
    )
    w_mine, chunks, w_o, g_t = together(w_mine, chunks, w_o, g_t)
    w_other = [swap_core(message)] + [swap_core(piece) for piece in w_mine[1:]]
    w_out = lax.all_gather(w_o, "fsdp", axis=0, tiled=True)
    gu_pieces = scatter_rolled(chunks)
    g_all = gather_rolled(g_t)

    packed, gains, w_a, w_b, a_t = call(
        qkv_kernel,
        [
            shape(CTX, 3 * HEAD, ROWS),
            shape(8, D, dtype=F32),
            shape(D, HALFW),
            shape(D, HALFW),
            shape(D, ROWS),
        ],
        [ids, x_t] + w_mine + w_other + [jnp.cos(angle), jnp.sin(angle)],
        smem=1,
        flops=2 * ROWS * D * QKV,
    )
    a_all = lax.all_gather(a_t, "ctx", axis=0)
    received = lax.all_to_all(packed, "ctx", 0, 0)
    cos_all, sin_all = jnp.cos(angle_all), jnp.sin(angle_all)
    received, cos_all, sin_all = together(received, cos_all, sin_all)
    o_part, q_t, k_t, k_n, v_t, o_f, lse = call(
        attend_kernel,
        [
            shape(CTX, HEAD, ROWS),
            shape(HEAD, L),
            shape(HEAD, L),
            shape(L, HEAD),
            shape(HEAD, L),
            shape(CTX, HEAD, ROWS, dtype=F32),
            shape(NT, 8, TILE, dtype=F32),
        ],
        [order, inverse, received],
        smem=2,
        scratch=[pltpu.VMEM((L, TILE), F32)],
        flops=2 * L * L * HEAD,
    )
    o_all = lax.all_to_all(o_part, "ctx", 0, 0)
    q_n, v_n = q_t.T, v_t.T
    o_all, w_out, q_n, v_n, gu_pieces = together(o_all, w_out, q_n, v_n, gu_pieces)
    h, b, *o_pieces = call(
        resid_kernel,
        [shape(ROWS, D, dtype=F32), shape(ROWS, D)] + [shape(SHARD, ROWS)] * FS,
        [ids, o_all, w_out, x_t, gains],
        smem=1,
        scratch=[pltpu.VMEM((D, ROWS), BF16)],
        flops=2 * ROWS * D * D,
    )
    b, g_all = together(b, g_all)
    gu_other = [gu_local] + [swap_core(piece) for piece in gu_pieces[1:]]
    (w_gu,) = call(
        place_gate_up_kernel, [shape(D, 2 * FSL)], [ids] + gu_pieces + gu_other, smem=1
    )
    b_all = gather_rolled(b)
    db, mm, dgu = [None] * FS, [None] * FS, [None] * FS
    before = None
    for partners in ((0,), (1, 3), (2,)):
        if before is not None:
            b_all[partners[0]], before = together(b_all[partners[0]], before)
        outs = call(
            mlp_kernel,
            [shape(ROWS, D), shape(ROWS, FSL), shape(ROWS, 2 * FSL)] * len(partners),
            [b_all[s] for s in partners] + [g_all[s] for s in partners] + [w_gu, down_t],
            flops=10 * len(partners) * ROWS * D * FSL,
            limit=MLP_BYTES,
        )
        for i, s in enumerate(partners):
            db[s], mm[s], dgu[s] = outs[3 * i : 3 * i + 3]
        before = mm[partners[0]]
    db = scatter_rolled(db)
    *y_parts, keep, give = call(
        mlp_grad_kernel,
        [shape(ROWS, D)] * FS + [shape(HALF_ROWS, FSL)] * 2,
        [ids] + b_all + g_all + mm + dgu + [down_t],
        smem=1,
        scratch=[pltpu.VMEM((D, 2 * FSL), BF16), pltpu.VMEM((D, FSL), BF16)],
        flops=8 * FS * ROWS * D * FSL,
        limit=MLP_BYTES,
    )
    db, keep = together(db, keep)
    dh, do_part, *eo_parts = call(
        mid_kernel,
        [shape(ROWS, D, dtype=F32), shape(CTX, HEAD, ROWS)] + [shape(ROWS, EO)] * FS,
        db + [h, g_t, gains, w_out] + o_pieces,
        flops=2 * ROWS * D * D,
    )
    do_all = lax.all_to_all(do_part, "ctx", 0, 0)
    eo_parts, give = together(eo_parts, give)
    got = swap_core(give)
    x_pieces = call(
        pack_kernel,
        [shape(4, 96, FSL)] * 4,
        [ids, keep, got],
        smem=1,
        scratch=[pltpu.VMEM((HALF_ROWS + 16, FSL), F32)],
    )
    eo_all = scatter_rolled(eo_parts)
    do_all, x_pieces, eo_all[1], eo_all[3] = together(do_all, x_pieces, eo_all[1], eo_all[3])
    x_pieces = scatter_by(shift_x, x_pieces)
    (dqkv_part,) = call(
        attend_back_kernel,
        [shape(CTX, 3 * HEAD, ROWS)],
        [order, inverse, do_all, q_t, q_n, k_t, k_n, v_n, o_f, lse, cos_all, sin_all],
        smem=2,
        scratch=[
            pltpu.VMEM((HEAD, L), BF16),
            pltpu.VMEM((L, HEAD), BF16),
            pltpu.VMEM((8, L), F32),
            pltpu.VMEM((L, HEAD), F32),
            pltpu.VMEM((L, HEAD), F32),
            pltpu.VMEM((CTX, 3 * HEAD, ROWS), F32),
        ],
        flops=5 * L * L * HEAD,
    )
    head_pieces = call(
        head_grad_kernel,
        [shape(HEADROWS, 128)] * FS,
        [ids, a_all, dqkv_part],
        smem=1,
        scratch=[pltpu.VMEM((D, 3 * HEAD), BF16)],
        flops=2 * L * D * 3 * HEAD,
    )
    dqkv_part, eo_all, x_pieces = together(dqkv_part, eo_all, x_pieces)
    dqkv = lax.all_to_all(dqkv_part, "ctx", 0, 0)
    (message,) = call(
        out_grad_kernel,
        [shape(CTX, 128, 128)],
        eo_all,
        flops=2 * FS * ROWS * SHARD * D,
    )
    dqkv, message = together(dqkv, message)
    o_recv = lax.all_to_all(message, "ctx", 0, 0)
    head_pieces = scatter_rolled(head_pieces)
    z_pieces = call(
        sum_x_kernel,
        [shape(96, FSL)] * 4,
        [ids] + x_pieces,
        smem=1,
        scratch=[pltpu.VMEM((4, 96, FSL), BF16)],
    )
    *pieces, down_sum = call(
        sum_z_kernel,
        [shape(16, FSL)] * FS + [shape(32, FSL)],
        [ids] + scatter_by(shift_z, z_pieces),
        smem=1,
        scratch=[pltpu.VMEM((96, FSL), BF16)],
    )
    own = jnp.concatenate(scatter_rolled(pieces) + [down_sum], axis=0)
    o_recv, own, head_pieces, y_parts = together(o_recv, own, head_pieces, y_parts)
    y = scatter_rolled(y_parts)
    mine_all = same_core(jnp.broadcast_to(own[None], (CTX, 96, FSL)))
    (head_sum,) = call(head_sum_kernel, [shape(HEADROWS + 128, 128)], head_pieces + [o_recv])
    head_sum = (head_sum.astype(F32) + swap_seq(head_sum).astype(F32)).astype(BF16)
    (input_grad,) = call(
        last_kernel,
        [shape(D, ROWS, dtype=F32)],
        [dqkv, w_a, w_b, x_t, dh, gains],
        scratch=[pltpu.VMEM((QKV, ROWS), BF16)],
        flops=2 * ROWS * D * QKV,
    )
    (result,) = call(result_kernel, [shape(D, ROWS)], [h] + y)
    mine_all, head_sum, input_grad, result = together(mine_all, head_sum, input_grad, result)
    head_mine = same_core_row(jnp.broadcast_to(head_sum[None], (CTX // 2, HEADROWS + 128, 128)))
    gu_out, down_out, gain_two = call(
        widen_kernel,
        [
            shape(SHARD, 2 * FF, dtype=F32),
            shape(D, FSL, dtype=F32),
            shape(SHARD, dtype=F32),
        ],
        [ids, mine_all, swap_core(mine_all), w_gate_up, gain_mlp],
        smem=1,
    )
    head_mine, gu_out, down_out, gain_two = together(head_mine, gu_out, down_out, gain_two)
    q_out, kv_out, o_out, gain_one = call(
        unpack_kernel,
        [
            shape(SHARD, D, dtype=F32),
            shape(SHARD, KVW, dtype=F32),
            shape(SHARD, D, dtype=F32),
            shape(SHARD, dtype=F32),
        ],
        [ids, head_mine, swap_core(head_mine), w_q, w_kv, gain_attn],
        smem=1,
    )
    return (
        result.T[None],
        input_grad.T[None],
        gain_one,
        q_out,
        kv_out,
        o_out,
        gain_two,
        gu_out,
        down_out.T,
    )


def solution(mesh):
    tokens = P(("seq", "fsdp"), "ctx", None)
    return jax.shard_map(
        shards,
        mesh=mesh,
        in_specs=(
            tokens,
            P("fsdp"),
            P("fsdp", None),
            P("fsdp", None),
            P("fsdp", None),
            P("fsdp"),
            P("fsdp", None),
            P("fsdp", None),
            P(("seq", "fsdp"), None),
            tokens,
        ),
        out_specs=(
            tokens,
            tokens,
            P("fsdp"),
            P("fsdp", None),
            P("fsdp", None),
            P("fsdp", None),
            P("fsdp"),
            P("fsdp", None),
            P("fsdp", None),
        ),
        check_vma=False,
    )
```

```python
import jax
import jax.numpy as jnp
from jax import lax
from jax.experimental import pallas as pl
from jax.experimental.pallas import tpu as pltpu
from jax.sharding import PartitionSpec as P

D = 960
HEADS = 15
KV_HEADS = 5
GROUP = 3
HEAD = 64
HALF = 32
FF = 2560
BLK = 64
L = 2048
CTX = 16
FS = 4
ROWS = 128
QKV = 1600
HEADROWS = 368
EO = 1280
HALFW = 896
KVW = 640
HALF_ROWS = D + D // 2
SHARD = D // FS
FSL = FF // FS
TILE = 256
NT = L // TILE
EPS = 1e-05
THETA = 100000.0
SCALE = HEAD**-0.5
F32 = jnp.float32
BF16 = jnp.bfloat16
VMEM_BYTES = 56 * 1024 * 1024
MLP_BYTES = 24 * 1024 * 1024


def call(kernel, outs, args, smem=0, scratch=(), flops=0, limit=VMEM_BYTES):
    specs = [pl.BlockSpec(memory_space=pltpu.SMEM)] * smem
    specs += [pl.BlockSpec(memory_space=pltpu.VMEM)] * (len(args) - smem)
    moved = sum(a.size * a.dtype.itemsize for a in list(args) + list(outs))
    return pl.pallas_call(
        kernel,
        out_shape=outs,
        in_specs=specs,
        out_specs=[pl.BlockSpec(memory_space=pltpu.VMEM)] * len(outs),
        scratch_shapes=list(scratch),
        cost_estimate=pl.CostEstimate(flops=flops, bytes_accessed=moved, transcendentals=0),
        compiler_params=pltpu.CompilerParams(vmem_limit_bytes=limit),
    )(*args)


def shape(*dims, dtype=BF16):
    return jax.ShapeDtypeStruct(dims, dtype)


def dot(left, right, a=1, b=0):
    return lax.dot_general(left, right, (((a,), (b,)), ((), ())), preferred_element_type=F32)


def inv_norm(rows):
    return lax.rsqrt(jnp.mean(rows * rows, axis=-1, keepdims=True) + EPS)


def message_kernel(ids_ref, wq_ref, wkv_ref, g1_ref, g2_ref, out_ref):
    core = ids_ref[1]

    @pl.when(core == 0)
    def _():
        out_ref[...] = wq_ref[:, 0:HALFW]

    @pl.when(core == 1)
    def _():
        out_ref[:, 0:KVW] = wkv_ref[...]
        one = jnp.broadcast_to(g1_ref[...].astype(F32)[None], (128, SHARD)).T
        two = jnp.broadcast_to(g2_ref[...].astype(F32)[None], (128, SHARD)).T
        lane = lax.broadcasted_iota(jnp.int32, (SHARD, 128), 1)
        rest = wq_ref[:, HALFW:D].astype(F32)
        rest = jnp.concatenate([rest, jnp.zeros((SHARD, 64), F32)], axis=1)
        rest = jnp.where(lane == 64, one, jnp.where(lane == 65, two, rest))
        out_ref[:, KVW : KVW + 128] = rest.astype(BF16)
        out_ref[:, KVW + 128 : HALFW] = jnp.zeros((SHARD, HALFW - KVW - 128), BF16)


def chunk_kernel(ids_ref, gu_ref, *out_refs):
    fs = ids_ref[0]
    core = ids_ref[1]
    for s in range(FS):
        at = lax.rem(fs + s, FS) * FSL + core * FF
        out_refs[s][...] = gu_ref[:, pl.ds(pl.multiple_of(at, 128), FSL)]
    at = fs * FSL + (1 - core) * FF
    out_refs[FS][...] = gu_ref[:, pl.ds(pl.multiple_of(at, 128), FSL)]


def place_gate_up_kernel(ids_ref, *refs):
    out_ref = refs[2 * FS]
    for half in range(2):

        @pl.when(ids_ref[1] == half)
        def _(half=half):
            for s in range(FS):
                at = pl.multiple_of(lax.rem(ids_ref[0] + FS - s, FS) * SHARD, 16)
                for other in range(2):
                    cols = slice(FSL * (half ^ other), FSL * ((half ^ other) + 1))
                    out_ref[pl.ds(at, SHARD), cols] = refs[FS * other + s][...]


def qkv_kernel(ids_ref, xt_ref, *refs):
    mine = refs[0:FS]
    other = refs[FS : 2 * FS]
    cos_ref, sin_ref, out_ref, gains_ref, wa_ref, wb_ref, at_ref = refs[2 * FS :]
    fs = ids_ref[0]
    core = ids_ref[1]

    def fill(first, second):
        for s in range(FS):
            at = pl.multiple_of(lax.rem(fs + s, FS) * SHARD, 16)
            wa_ref[pl.ds(at, SHARD), :] = first[s][...]
            wb_ref[pl.ds(at, SHARD), :] = second[s][...]

    @pl.when(core == 0)
    def _():
        fill(mine, other)

    @pl.when(core == 1)
    def _():
        fill(other, mine)

    xt = xt_ref[...].astype(F32)
    gains = wb_ref[:, KVW : KVW + 128].astype(F32)
    gains_ref[...] = gains.T[64:72, :]
    r1 = lax.rsqrt(jnp.mean(xt * xt, axis=0, keepdims=True) + EPS)
    at = xt * r1 * gains[:, 64:65]
    at_ref[...] = at.astype(BF16)
    a = at.T.astype(BF16)
    lin_a = dot(a, wa_ref[...]).T
    lin_b = dot(a, wb_ref[...]).T
    cos = cos_ref[...]
    sin = sin_ref[...]

    def turned(rows):
        first = rows[0:HALF]
        second = rows[HALF:HEAD]
        return jnp.concatenate(
            [first * cos - second * sin, second * cos + first * sin], axis=0
        ).astype(BF16)

    for j in range(KV_HEADS):
        key = turned(lin_b[HEAD * j : HEAD * (j + 1)])
        value = lin_b[HEAD * (KV_HEADS + j) : HEAD * (KV_HEADS + j + 1)].astype(BF16)
        for g in range(GROUP):
            head = j * GROUP + g
            if head < HEADS - 1:
                rows = lin_a[HEAD * head : HEAD * (head + 1)]
            else:
                rows = lin_b[KVW : KVW + HEAD]
            out_ref[head, 0:HEAD, :] = turned(rows)
            out_ref[head, HEAD : 2 * HEAD, :] = key
            out_ref[head, 2 * HEAD : 3 * HEAD, :] = value
    out_ref[HEADS, :, :] = jnp.zeros((3 * HEAD, ROWS), BF16)


def pick_pair(load, first, second):
    left = load(first // 2).astype(F32)
    right = load(second // 2).astype(F32)
    left = pltpu.roll(left, (first % 2) * BLK, 1)
    right = pltpu.roll(right, (1 - second % 2) * BLK, 1)
    lane = lax.broadcasted_iota(jnp.int32, left.shape, 1)
    return jnp.where(lane < BLK, left, right)


def causal(size):
    key = lax.broadcasted_iota(jnp.int32, (size, size), 0)
    query = lax.broadcasted_iota(jnp.int32, (size, size), 1)
    return key <= query


def attend_kernel(
    order_ref, inv_ref, recv_ref, out_ref, qt_ref, kt_ref, k_ref, vt_ref, of_ref, lse_ref, s_ref
):
    for m in range(CTX):
        got = pick_pair(lambda i: recv_ref[i], inv_ref[2 * m], inv_ref[2 * m + 1])
        at = slice(2 * BLK * m, 2 * BLK * (m + 1))
        qt_ref[:, at] = (got[0:HEAD] * SCALE).astype(BF16)
        key = got[HEAD : 2 * HEAD]
        kt_ref[:, at] = key.astype(BF16)
        k_ref[at, :] = key.T.astype(BF16)
        vt_ref[:, at] = got[2 * HEAD : 3 * HEAD].astype(BF16)
    allowed = causal(TILE)
    for n in range(NT):
        span = slice(TILE * n, TILE * (n + 1))
        query = qt_ref[:, span]
        top = None
        for c in range(n + 1):
            rows = slice(TILE * c, TILE * (c + 1))
            s = dot(k_ref[rows, :], query)
            if c == n:
                s = jnp.where(allowed, s, -1e30)
            s_ref[rows, :] = s
            part = jnp.max(s, axis=0, keepdims=True)
            top = part if top is None else jnp.maximum(top, part)
        total = None
        for c in range(n + 1):
            rows = slice(TILE * c, TILE * (c + 1))
            e = jnp.exp(s_ref[rows, :] - top)
            s_ref[rows, :] = e
            part = jnp.sum(e, axis=0, keepdims=True)
            total = part if total is None else total + part
        recip = 1.0 / total
        lse_ref[n] = jnp.broadcast_to(top + jnp.log(total), (8, TILE))
        prob = (s_ref[0 : TILE * (n + 1), :] * recip).astype(BF16)
        o = dot(vt_ref[:, 0 : TILE * (n + 1)], prob)
        of_ref[2 * n] = o[:, 0 : 2 * BLK]
        of_ref[2 * n + 1] = o[:, 2 * BLK :]
    for i in range(CTX):
        got = pick_pair(lambda g: of_ref[g], order_ref[2 * i], order_ref[2 * i + 1])
        out_ref[i] = got.astype(BF16)


def attend_back_kernel(
    order_ref,
    inv_ref,
    recv_ref,
    qt_ref,
    q_ref,
    kt_ref,
    k_ref,
    v_ref,
    of_ref,
    lse_ref,
    cos_ref,
    sin_ref,
    out_ref,
    dot_ref,
    do_ref,
    delta_ref,
    dk_ref,
    dv_ref,
    st_ref,
):
    for m in range(CTX):
        got = pick_pair(lambda i: recv_ref[i], inv_ref[2 * m], inv_ref[2 * m + 1])
        at = slice(2 * BLK * m, 2 * BLK * (m + 1))
        dot_ref[:, at] = got.astype(BF16)
        do_ref[at, :] = got.T.astype(BF16)
        delta_ref[:, at] = jnp.broadcast_to(
            jnp.sum(got * of_ref[m], axis=0, keepdims=True), (8, 2 * BLK)
        )
    allowed = causal(TILE)
    for n in range(NT):
        span = slice(TILE * n, TILE * (n + 1))
        query = qt_ref[:, span]
        out_grad = dot_ref[:, span]
        lse = lse_ref[n][0:1, :]
        delta = delta_ref[0:1, span]
        dq = None
        for c in range(n + 1):
            rows = slice(TILE * c, TILE * (c + 1))
            prob = jnp.exp(dot(k_ref[rows, :], query) - lse)
            if c == n:
                prob = jnp.where(allowed, prob, 0.0)
            ds = (prob * (dot(v_ref[rows, :], out_grad) - delta)).astype(BF16)
            part = dot(kt_ref[:, rows], ds)
            dq = part if dq is None else dq + part
            dk = dot(ds, q_ref[span, :])
            dv = dot(prob.astype(BF16), do_ref[span, :])
            if c == n:
                dk_ref[rows, :] = dk
                dv_ref[rows, :] = dv
            else:
                dk_ref[rows, :] += dk
                dv_ref[rows, :] += dv
        st_ref[2 * n, 0:HEAD, :] = dq[:, 0 : 2 * BLK] * SCALE
        st_ref[2 * n + 1, 0:HEAD, :] = dq[:, 2 * BLK :] * SCALE
    for m in range(CTX):
        at = slice(2 * BLK * m, 2 * BLK * (m + 1))
        cos = cos_ref[:, at]
        sin = sin_ref[:, at]

        def turned(value):
            first = value[0:HALF]
            second = value[HALF:HEAD]
            return jnp.concatenate(
                [first * cos + second * sin, second * cos - first * sin], axis=0
            )

        st_ref[m, 0:HEAD, :] = turned(st_ref[m, 0:HEAD, :])
        st_ref[m, HEAD : 2 * HEAD, :] = turned(dk_ref[at, :].T)
        st_ref[m, 2 * HEAD : 3 * HEAD, :] = dv_ref[at, :].T
    for i in range(CTX):
        got = pick_pair(lambda g: st_ref[g], order_ref[2 * i], order_ref[2 * i + 1])
        out_ref[i] = got.astype(BF16)


def resid_kernel(ids_ref, ot_ref, w_ref, xt_ref, gains_ref, h_ref, b_ref, *refs):
    full_ref = refs[FS]
    flat = jnp.concatenate([ot_ref[h] for h in range(HEADS)], axis=0)
    full_ref[...] = flat
    for s in range(FS):
        at = pl.multiple_of(lax.rem(ids_ref[0] + s, FS) * SHARD, 16)
        refs[s][...] = full_ref[pl.ds(at, SHARD), :]
    mixed = flat.astype(F32).T.astype(BF16)
    h = xt_ref[...].astype(F32).T + dot(mixed, w_ref[...])
    h_ref[...] = h
    b_ref[...] = (h * inv_norm(h) * gains_ref[1:2, :]).astype(BF16)


def mlp_kernel(*refs):
    count = (len(refs) - 2) // 5
    b_refs = refs[0:count]
    g_refs = refs[count : 2 * count]
    gu_ref, down_ref = refs[2 * count : 2 * count + 2]
    outs = refs[2 * count + 2 :]
    for i in range(count):
        db_ref, mm_ref, dgu_ref = outs[3 * i : 3 * i + 3]
        gu = dot(b_refs[i][...], gu_ref[...])
        gate = gu[:, :FSL]
        up = gu[:, FSL:]
        sig = 1.0 / (1.0 + jnp.exp(-gate))
        act = gate * sig
        dm = dot(g_refs[i][...], down_ref[...], 0, 0)
        dgate = dm * up * sig * (1.0 + gate * (1.0 - sig))
        dgu = jnp.concatenate([dgate, dm * act], axis=1).astype(BF16)
        mm_ref[...] = (act * up).astype(BF16)
        dgu_ref[...] = dgu
        db_ref[...] = dot(dgu, gu_ref[...], 1, 1).astype(BF16)


def mlp_grad_kernel(ids_ref, *refs):
    b_refs = refs[0:FS]
    g_refs = refs[FS : 2 * FS]
    mm_refs = refs[2 * FS : 3 * FS]
    dgu_refs = refs[3 * FS : 4 * FS]
    down_ref = refs[4 * FS]
    y_refs = refs[4 * FS + 1 : 5 * FS + 1]
    keep_ref, give_ref, gu_ref, dd_ref = refs[5 * FS + 1 :]
    b = jnp.concatenate([r[...] for r in b_refs], axis=0)
    gt = jnp.concatenate([r[...] for r in g_refs], axis=1)
    mm = jnp.concatenate([r[...] for r in mm_refs], axis=0)
    dgu = jnp.concatenate([r[...] for r in dgu_refs], axis=0)
    gu_ref[...] = dot(b, dgu, 0, 0).astype(BF16)
    dd_ref[...] = dot(gt, mm).astype(BF16)

    def put(out_ref, half):
        out_ref[0:D, :] = gu_ref[:, FSL * half : FSL * (half + 1)]
        out_ref[D : D + D // 2, :] = dd_ref[D // 2 * half : D // 2 * (half + 1), :]

    for core in range(2):

        @pl.when(ids_ref[1] == core)
        def _(core=core):
            put(keep_ref, core)
            put(give_ref, 1 - core)

    for s in range(FS):
        y_refs[s][...] = dot(mm_refs[s][...], down_ref[...], 1, 1).astype(BF16)


def result_kernel(h_ref, y0, y1, y2, y3, out_ref):
    total = h_ref[...]
    for piece in (y0, y1, y2, y3):
        total += piece[...].astype(F32)
    out_ref[...] = total.T.astype(BF16)


def pack_kernel(ids_ref, keep_ref, got_ref, *refs):
    sum_ref = refs[4]
    for at in range(0, HALF_ROWS, 240):
        rows = slice(at, at + 240)
        sum_ref[rows, :] = keep_ref[rows, :].astype(F32) + got_ref[rows, :].astype(F32)
    sum_ref[HALF_ROWS:, :] = jnp.zeros((16, FSL), F32)

    def put(out_ref, first):
        for r in range(first, first + 4):
            for k in range(FS):
                at = SHARD * k + 15 * r
                out_ref[r - first, 16 * k : 16 * (k + 1), :] = sum_ref[at : at + 16, :].astype(BF16)
            at = D + 30 * r
            out_ref[r - first, 64:96, :] = sum_ref[at : at + 32, :].astype(BF16)

    for x in range(4):

        @pl.when(ids_ref[2] == x)
        def _(x=x):
            for step in range(4):
                owner = (x + step) % 4
                put(refs[step], 4 * (owner % 2 * 2 + owner // 2))


def sum_x_kernel(ids_ref, *refs):
    total = refs[0][...].astype(F32)
    for step in range(1, 4):
        total += refs[step][...].astype(F32)
    refs[8][...] = total.astype(BF16)
    for step in range(4):
        refs[4 + step][...] = refs[8][lax.rem(ids_ref[3] + step, 4)]


def sum_z_kernel(ids_ref, *refs):
    total = refs[0][...].astype(F32)
    for step in range(1, 4):
        total += refs[step][...].astype(F32)
    sum_ref = refs[9]
    sum_ref[...] = total.astype(BF16)
    for s in range(FS):
        at = pl.multiple_of(lax.rem(ids_ref[0] + s, FS) * 16, 16)
        refs[4 + s][...] = sum_ref[pl.ds(at, 16), :]
    refs[8][...] = sum_ref[64:96, :]


def mid_kernel(*refs):
    db_refs = refs[0:FS]
    h_ref, gt_ref, gains_ref, w_ref = refs[FS : FS + 4]
    o_refs = refs[FS + 4 : 2 * FS + 4]
    dh_ref, do_ref = refs[2 * FS + 4 : 2 * FS + 6]
    out_refs = refs[2 * FS + 6 :]
    db = db_refs[0][...].astype(F32)
    for ref in db_refs[1:]:
        db += ref[...].astype(F32)
    h = h_ref[...]
    r2 = inv_norm(h)
    scaled = gains_ref[1:2, :] * db
    dh = (
        gt_ref[...].astype(F32).T
        + r2 * scaled
        - h * (r2 * r2 * r2) * jnp.mean(scaled * h, axis=-1, keepdims=True)
    )
    dh_ref[...] = dh
    e = dh.astype(BF16)
    back = dot(w_ref[...], e, 1, 1).astype(BF16)
    for head in range(HEADS):
        do_ref[head] = back[HEAD * head : HEAD * (head + 1)]
    do_ref[HEADS] = jnp.zeros((HEAD, ROWS), BF16)
    for s in range(FS):
        out_refs[s][:, 0:D] = e
        o = jnp.concatenate([o_refs[s][...].astype(F32), jnp.zeros((80, ROWS), F32)], axis=0)
        out_refs[s][:, D:EO] = o.T.astype(BF16)


def head_grad_kernel(ids_ref, at_ref, d_ref, *refs):
    full_ref = refs[FS]
    total = None
    for i in range(0, CTX, 2):
        left = jnp.concatenate([at_ref[i], at_ref[i + 1]], axis=1)
        right = jnp.concatenate([d_ref[i], d_ref[i + 1]], axis=1)
        part = dot(left, right, 1, 1)
        total = part if total is None else total + part
    full_ref[...] = total.astype(BF16)
    for s in range(FS):
        at = pl.multiple_of(lax.rem(ids_ref[0] + s, FS) * SHARD, 16)
        rows = full_ref[pl.ds(at, SHARD), :]
        refs[s][0:SHARD, :] = rows[:, 0:128]
        value = rows[:, 128:192].astype(F32)
        value = jnp.concatenate([value[0 : SHARD // 2], value[SHARD // 2 :]], axis=1)
        value = jnp.concatenate([value, jnp.zeros((8, 128), F32)], axis=0)
        refs[s][SHARD:HEADROWS, :] = value.astype(BF16)


def out_grad_kernel(*refs):
    part_ref, out_ref = refs[FS:]
    total = None
    for s in range(FS):
        message = refs[s]
        part = dot(message[:, D:EO], message[:, 0:D], 0, 0)[0:SHARD]
        total = part if total is None else total + part
    pad = jnp.zeros((SHARD, 64), F32)
    total = jnp.concatenate([total, pad], axis=1).astype(BF16)
    out_ref[:, 0 : 3 * HEAD, :] = part_ref[...]
    for i in range(HEADS):
        for j in range(8):
            at = 3 * HEAD + 16 * j
            out_ref[i, at : at + 16, :] = total[16 * i : 16 * (i + 1), 128 * j : 128 * (j + 1)]
    out_ref[HEADS, 3 * HEAD :, :] = jnp.zeros((128, 128), BF16)


def head_sum_kernel(p0, p1, p2, p3, recv_ref, out_ref):
    total = p0[...].astype(F32)
    for piece in (p1, p2, p3):
        total += piece[...].astype(F32)
    out_ref[0:HEADROWS, :] = total.astype(BF16)
    total = recv_ref[0, 3 * HEAD :, :].astype(F32)
    for i in range(1, CTX):
        total += recv_ref[i, 3 * HEAD :, :].astype(F32)
    out_ref[HEADROWS:, :] = total.astype(BF16)


def last_kernel(recv_ref, wa_ref, wb_ref, xt_ref, dh_ref, gains_ref, ig_ref, msg_ref):
    for head in range(HEADS):
        msg_ref[HEAD * head : HEAD * (head + 1), :] = recv_ref[head, 0:HEAD, :]
    for part in range(2):
        for j in range(KV_HEADS):
            total = None
            for g in range(GROUP):
                piece = recv_ref[j * GROUP + g, HEAD * (part + 1) : HEAD * (part + 2), :]
                piece = piece.astype(F32)
                total = piece if total is None else total + piece
            base = D + HEAD * (KV_HEADS * part + j)
            msg_ref[base : base + HEAD, :] = total.astype(BF16)
    da = dot(wa_ref[...], msg_ref[0:HALFW, :])
    da += dot(wb_ref[:, 0:KVW], msg_ref[D:QKV, :])
    da += dot(wb_ref[:, KVW : KVW + HEAD], msg_ref[HALFW:D, :])
    x = xt_ref[...].astype(F32)
    r1 = lax.rsqrt(jnp.mean(x * x, axis=0, keepdims=True) + EPS)
    scaled = wb_ref[:, KVW : KVW + 128].astype(F32)[:, 64:65] * da
    ig_ref[...] = (
        dh_ref[...].T
        + r1 * scaled
        - x * (r1 * r1 * r1) * jnp.mean(scaled * x, axis=0, keepdims=True)
    )


def unpack_kernel(
    ids_ref, mine_ref, other_ref, wq_ref, wkv_ref, gain_in, q_ref, kv_ref, o_ref, gain_ref
):
    for core in range(2):

        @pl.when(ids_ref[1] == core)
        def _(core=core):
            blocks = []
            for head in range(HEADS):
                src = mine_ref if head % 2 == core else other_ref
                blocks.append(src[head // 2].astype(F32))
            parts = [b[0:SHARD] for b in blocks]
            tails = [b[SHARD : SHARD + SHARD // 2] for b in blocks]
            zero = jnp.zeros((SHARD, HEAD), F32)
            query = [p[:, 0:HEAD] for p in parts]
            key = []
            value = []
            for j in range(KV_HEADS):
                group = parts[GROUP * j] + parts[GROUP * j + 1] + parts[GROUP * j + 2]
                key.append(group[:, HEAD:])
                group = tails[GROUP * j] + tails[GROUP * j + 1] + tails[GROUP * j + 2]
                value.append(jnp.concatenate([group[:, 0:HEAD], group[:, HEAD:]], axis=0))
            q = jnp.concatenate(query + [zero], axis=1)[:, 0:D]
            kv = jnp.concatenate(key + value, axis=1)
            q_ref[...] = q
            kv_ref[...] = kv
            total = jnp.sum(q * wq_ref[...].astype(F32), axis=1, keepdims=True)
            total += jnp.sum(kv * wkv_ref[...].astype(F32), axis=1, keepdims=True)
            total = jnp.broadcast_to(total, (SHARD, 128)).T[0:8]
            gain_ref[...] = total[0] / gain_in[...].astype(F32)
            for i, b in enumerate(blocks):
                cols = [b[HEADROWS + 16 * j : HEADROWS + 16 * (j + 1)] for j in range(8)]
                o_ref[16 * i : 16 * (i + 1), :] = jnp.concatenate(cols, axis=1)[:, 0:D]


def widen_kernel(
    ids_ref, mine_ref, other_ref, gu_in, gain_in, gu_out, down_out, gain_ref
):
    for core in range(2):

        @pl.when(ids_ref[1] == core)
        def _(core=core):
            halves = (mine_ref, other_ref) if core == 0 else (other_ref, mine_ref)
            total = None
            down = []
            for half, src in enumerate(halves):
                for s in range(FS):
                    at = lax.rem(ids_ref[0] + FS - s, FS) * FSL + FF * half
                    cols = pl.ds(pl.multiple_of(at, 128), FSL)
                    rows = [
                        src[r, 16 * s : 16 * (s + 1), :].astype(F32)[0:15] for r in range(CTX)
                    ]
                    rows = jnp.concatenate(rows, axis=0)
                    gu_out[:, cols] = rows
                    part = jnp.sum(rows * gu_in[:, cols].astype(F32), axis=1, keepdims=True)
                    total = part if total is None else total + part
                down += [src[r, 64:96, :].astype(F32)[0:30] for r in range(CTX)]
            down_out[...] = jnp.concatenate(down, axis=0)
            total = jnp.broadcast_to(total, (SHARD, 128)).T[0:8]
            gain_ref[...] = total[0] / gain_in[...].astype(F32)


def swap_core(value):
    return lax.ppermute(value, "ctx", [(i, i ^ 1) for i in range(CTX)])


def shift(value, step):
    return lax.ppermute(value, "fsdp", [((i + step) % FS, i) for i in range(FS)])


def same_core(value):
    groups = [[2 * i + core for i in range(CTX)] for core in range(2)]
    return lax.all_to_all(value, ("seq", "ctx"), 0, 0, axis_index_groups=groups)


def shift_x(value, step):
    def at(x, z, core):
        return (x % 2) * CTX + (x // 2) * 8 + z * 2 + core

    pairs = [
        (at((x + step) % 4, z, core), at(x, z, core))
        for x in range(4)
        for z in range(4)
        for core in range(2)
    ]
    return lax.ppermute(value, ("seq", "ctx"), pairs)


def shift_z(value, step):
    def at(high, z, core):
        return high * 8 + z * 2 + core

    pairs = [
        (at(high, (z + step) % 4, core), at(high, z, core))
        for high in range(2)
        for z in range(4)
        for core in range(2)
    ]
    return lax.ppermute(value, "ctx", pairs)


def same_core_row(value):
    groups = [[2 * i + core for i in range(CTX // 2)] for core in range(2)]
    return lax.all_to_all(value, "ctx", 0, 0, axis_index_groups=groups)


def swap_seq(value):
    return lax.ppermute(value, "seq", [(0, 1), (1, 0)])


def gather_by(move, value):
    return [value] + [move(value, s) for s in range(1, 4)]


def scatter_by(move, pieces):
    return [pieces[0]] + [move(pieces[s], -s) for s in range(1, 4)]


def gather_rolled(value):
    return gather_by(shift, value)


def scatter_rolled(pieces):
    return scatter_by(shift, pieces)


def together(*values):
    return lax.optimization_barrier(values)


def shards(tokens, gain_attn, w_q, w_kv, w_o, gain_mlp, w_gate_up, w_down, block_order, cotangent):
    x_t = tokens[0].T
    g_t = cotangent[0].T
    down_t = w_down.T
    order = block_order[0]
    place = lax.axis_index("ctx")
    x_place = place // 8 * 2 + lax.axis_index("seq")
    ids = jnp.stack([lax.axis_index("fsdp"), place % 2, x_place, place // 2 % 4])
    ids = ids.astype(jnp.int32)

    slots = jnp.arange(2 * CTX, dtype=jnp.int32)
    inverse = jnp.sum(jnp.where(order[None, :] == slots[:, None], slots[None, :], 0), axis=1)
    mine = lax.dynamic_slice_in_dim(order, place * 2, 2)
    places = (mine[:, None] * BLK + jnp.arange(BLK, dtype=jnp.int32)[None, :]).reshape(ROWS)
    freq = THETA ** (-(jnp.arange(HALF, dtype=F32) * 2.0 / HEAD))
    angle = freq[:, None] * places.astype(F32)[None, :]
    angle_all = freq[:, None] * jnp.arange(L, dtype=F32)[None, :]

    (message,) = call(
        message_kernel,
        [shape(SHARD, HALFW)],
        [ids, w_q, w_kv, gain_attn, gain_mlp],
        smem=1,
    )
    w_mine = gather_rolled(message)
    *chunks, gu_local = call(
        chunk_kernel, [shape(SHARD, FSL)] * (FS + 1), [ids, w_gate_up], smem=1
    )
    w_mine, chunks, w_o, g_t = together(w_mine, chunks, w_o, g_t)
    w_other = [swap_core(message)] + [swap_core(piece) for piece in w_mine[1:]]
    w_out = lax.all_gather(w_o, "fsdp", axis=0, tiled=True)
    gu_pieces = scatter_rolled(chunks)
    g_all = gather_rolled(g_t)

    packed, gains, w_a, w_b, a_t = call(
        qkv_kernel,
        [
            shape(CTX, 3 * HEAD, ROWS),
            shape(8, D, dtype=F32),
            shape(D, HALFW),
            shape(D, HALFW),
            shape(D, ROWS),
        ],
        [ids, x_t] + w_mine + w_other + [jnp.cos(angle), jnp.sin(angle)],
        smem=1,
        flops=2 * ROWS * D * QKV,
    )
    a_all = lax.all_gather(a_t, "ctx", axis=0)
    received = lax.all_to_all(packed, "ctx", 0, 0)
    cos_all, sin_all = jnp.cos(angle_all), jnp.sin(angle_all)
    received, cos_all, sin_all = together(received, cos_all, sin_all)
    o_part, q_t, k_t, k_n, v_t, o_f, lse = call(
        attend_kernel,
        [
            shape(CTX, HEAD, ROWS),
            shape(HEAD, L),
            shape(HEAD, L),
            shape(L, HEAD),
            shape(HEAD, L),
            shape(CTX, HEAD, ROWS, dtype=F32),
            shape(NT, 8, TILE, dtype=F32),
        ],
        [order, inverse, received],
        smem=2,
        scratch=[pltpu.VMEM((L, TILE), F32)],
        flops=2 * L * L * HEAD,
    )
    o_all = lax.all_to_all(o_part, "ctx", 0, 0)
    q_n, v_n = q_t.T, v_t.T
    o_all, w_out, q_n, v_n, gu_pieces = together(o_all, w_out, q_n, v_n, gu_pieces)
    h, b, *o_pieces = call(
        resid_kernel,
        [shape(ROWS, D, dtype=F32), shape(ROWS, D)] + [shape(SHARD, ROWS)] * FS,
        [ids, o_all, w_out, x_t, gains],
        smem=1,
        scratch=[pltpu.VMEM((D, ROWS), BF16)],
        flops=2 * ROWS * D * D,
    )
    b, g_all = together(b, g_all)
    gu_other = [gu_local] + [swap_core(piece) for piece in gu_pieces[1:]]
    (w_gu,) = call(
        place_gate_up_kernel, [shape(D, 2 * FSL)], [ids] + gu_pieces + gu_other, smem=1
    )
    b_all = gather_rolled(b)
    db, mm, dgu = [None] * FS, [None] * FS, [None] * FS
    before = None
    for partners in ((0,), (1, 3), (2,)):
        if before is not None:
            b_all[partners[0]], before = together(b_all[partners[0]], before)
        outs = call(
            mlp_kernel,
            [shape(ROWS, D), shape(ROWS, FSL), shape(ROWS, 2 * FSL)] * len(partners),
            [b_all[s] for s in partners] + [g_all[s] for s in partners] + [w_gu, down_t],
            flops=10 * len(partners) * ROWS * D * FSL,
            limit=MLP_BYTES,
        )
        for i, s in enumerate(partners):
            db[s], mm[s], dgu[s] = outs[3 * i : 3 * i + 3]
        before = mm[partners[0]]
    db = scatter_rolled(db)
    *y_parts, keep, give = call(
        mlp_grad_kernel,
        [shape(ROWS, D)] * FS + [shape(HALF_ROWS, FSL)] * 2,
        [ids] + b_all + g_all + mm + dgu + [down_t],
        smem=1,
        scratch=[pltpu.VMEM((D, 2 * FSL), BF16), pltpu.VMEM((D, FSL), BF16)],
        flops=8 * FS * ROWS * D * FSL,
        limit=MLP_BYTES,
    )
    db, keep = together(db, keep)
    dh, do_part, *eo_parts = call(
        mid_kernel,
        [shape(ROWS, D, dtype=F32), shape(CTX, HEAD, ROWS)] + [shape(ROWS, EO)] * FS,
        db + [h, g_t, gains, w_out] + o_pieces,
        flops=2 * ROWS * D * D,
    )
    do_all = lax.all_to_all(do_part, "ctx", 0, 0)
    eo_parts, give = together(eo_parts, give)
    got = swap_core(give)
    x_pieces = call(
        pack_kernel,
        [shape(4, 96, FSL)] * 4,
        [ids, keep, got],
        smem=1,
        scratch=[pltpu.VMEM((HALF_ROWS + 16, FSL), F32)],
    )
    eo_all = scatter_rolled(eo_parts)
    do_all, x_pieces, eo_all[1], eo_all[3] = together(do_all, x_pieces, eo_all[1], eo_all[3])
    x_pieces = scatter_by(shift_x, x_pieces)
    (dqkv_part,) = call(
        attend_back_kernel,
        [shape(CTX, 3 * HEAD, ROWS)],
        [order, inverse, do_all, q_t, q_n, k_t, k_n, v_n, o_f, lse, cos_all, sin_all],
        smem=2,
        scratch=[
            pltpu.VMEM((HEAD, L), BF16),
            pltpu.VMEM((L, HEAD), BF16),
            pltpu.VMEM((8, L), F32),
            pltpu.VMEM((L, HEAD), F32),
            pltpu.VMEM((L, HEAD), F32),
            pltpu.VMEM((CTX, 3 * HEAD, ROWS), F32),
        ],
        flops=5 * L * L * HEAD,
    )
    head_pieces = call(
        head_grad_kernel,
        [shape(HEADROWS, 128)] * FS,
        [ids, a_all, dqkv_part],
        smem=1,
        scratch=[pltpu.VMEM((D, 3 * HEAD), BF16)],
        flops=2 * L * D * 3 * HEAD,
    )
    dqkv_part, head_pieces, eo_all, x_pieces = together(dqkv_part, head_pieces, eo_all, x_pieces)
    (message,) = call(
        out_grad_kernel,
        [shape(CTX, 3 * HEAD + 128, ROWS)],
        eo_all + [dqkv_part],
        flops=2 * FS * ROWS * SHARD * D,
    )
    dqkv = lax.all_to_all(message, "ctx", 0, 0)
    z_pieces = call(
        sum_x_kernel,
        [shape(96, FSL)] * 4,
        [ids] + x_pieces,
        smem=1,
        scratch=[pltpu.VMEM((4, 96, FSL), BF16)],
    )
    *pieces, down_sum = call(
        sum_z_kernel,
        [shape(16, FSL)] * FS + [shape(32, FSL)],
        [ids] + scatter_by(shift_z, z_pieces),
        smem=1,
        scratch=[pltpu.VMEM((96, FSL), BF16)],
    )
    own = jnp.concatenate(scatter_rolled(pieces) + [down_sum], axis=0)
    dqkv, own, head_pieces, y_parts = together(dqkv, own, head_pieces, y_parts)
    head_pieces = scatter_rolled(head_pieces)
    y = scatter_rolled(y_parts)
    mine_all = same_core(jnp.broadcast_to(own[None], (CTX, 96, FSL)))
    (head_sum,) = call(head_sum_kernel, [shape(HEADROWS + 128, 128)], head_pieces + [dqkv])
    head_sum = (head_sum.astype(F32) + swap_seq(head_sum).astype(F32)).astype(BF16)
    (input_grad,) = call(
        last_kernel,
        [shape(D, ROWS, dtype=F32)],
        [dqkv, w_a, w_b, x_t, dh, gains],
        scratch=[pltpu.VMEM((QKV, ROWS), BF16)],
        flops=2 * ROWS * D * QKV,
    )
    (result,) = call(result_kernel, [shape(D, ROWS)], [h] + y)
    mine_all, head_sum, input_grad, result = together(mine_all, head_sum, input_grad, result)
    head_mine = same_core_row(jnp.broadcast_to(head_sum[None], (CTX // 2, HEADROWS + 128, 128)))
    gu_out, down_out, gain_two = call(
        widen_kernel,
        [
            shape(SHARD, 2 * FF, dtype=F32),
            shape(D, FSL, dtype=F32),
            shape(SHARD, dtype=F32),
        ],
        [ids, mine_all, swap_core(mine_all), w_gate_up, gain_mlp],
        smem=1,
    )
    head_mine, gu_out, down_out, gain_two = together(head_mine, gu_out, down_out, gain_two)
    q_out, kv_out, o_out, gain_one = call(
        unpack_kernel,
        [
            shape(SHARD, D, dtype=F32),
            shape(SHARD, KVW, dtype=F32),
            shape(SHARD, D, dtype=F32),
            shape(SHARD, dtype=F32),
        ],
        [ids, head_mine, swap_core(head_mine), w_q, w_kv, gain_attn],
        smem=1,
    )
    return (
        result.T[None],
        input_grad.T[None],
        gain_one,
        q_out,
        kv_out,
        o_out,
        gain_two,
        gu_out,
        down_out.T,
    )


def solution(mesh):
    tokens = P(("seq", "fsdp"), "ctx", None)
    return jax.shard_map(
        shards,
        mesh=mesh,
        in_specs=(
            tokens,
            P("fsdp"),
            P("fsdp", None),
            P("fsdp", None),
            P("fsdp", None),
            P("fsdp"),
            P("fsdp", None),
            P("fsdp", None),
            P(("seq", "fsdp"), None),
            tokens,
        ),
        out_specs=(
            tokens,
            tokens,
            P("fsdp"),
            P("fsdp", None),
            P("fsdp", None),
            P("fsdp", None),
            P("fsdp"),
            P("fsdp", None),
            P("fsdp", None),
        ),
        check_vma=False,
    )
```

```python
import jax
import jax.numpy as jnp
from jax import lax
from jax.experimental import pallas as pl
from jax.experimental.pallas import tpu as pltpu
from jax.sharding import PartitionSpec as P

D = 960
HEADS = 15
KV_HEADS = 5
GROUP = 3
HEAD = 64
HALF = 32
FF = 2560
BLK = 64
L = 2048
CTX = 16
FS = 4
ROWS = 128
QKV = 1600
HEADROWS = 368
EO = 1280
HALFW = 896
KVW = 640
HALF_ROWS = D + D // 2
SHARD = D // FS
FSL = FF // FS
TILE = 256
NT = L // TILE
EPS = 1e-05
THETA = 100000.0
SCALE = HEAD**-0.5
F32 = jnp.float32
BF16 = jnp.bfloat16
VMEM_BYTES = 56 * 1024 * 1024
MLP_BYTES = 24 * 1024 * 1024


def call(kernel, outs, args, smem=0, scratch=(), flops=0, limit=VMEM_BYTES):
    specs = [pl.BlockSpec(memory_space=pltpu.SMEM)] * smem
    specs += [pl.BlockSpec(memory_space=pltpu.VMEM)] * (len(args) - smem)
    moved = sum(a.size * a.dtype.itemsize for a in list(args) + list(outs))
    return pl.pallas_call(
        kernel,
        out_shape=outs,
        in_specs=specs,
        out_specs=[pl.BlockSpec(memory_space=pltpu.VMEM)] * len(outs),
        scratch_shapes=list(scratch),
        cost_estimate=pl.CostEstimate(flops=flops, bytes_accessed=moved, transcendentals=0),
        compiler_params=pltpu.CompilerParams(vmem_limit_bytes=limit),
    )(*args)


def shape(*dims, dtype=BF16):
    return jax.ShapeDtypeStruct(dims, dtype)


def dot(left, right, a=1, b=0):
    return lax.dot_general(left, right, (((a,), (b,)), ((), ())), preferred_element_type=F32)


def inv_norm(rows):
    return lax.rsqrt(jnp.mean(rows * rows, axis=-1, keepdims=True) + EPS)


def message_kernel(ids_ref, wq_ref, wkv_ref, g1_ref, g2_ref, out_ref):
    core = ids_ref[1]

    @pl.when(core == 0)
    def _():
        out_ref[...] = wq_ref[:, 0:HALFW]

    @pl.when(core == 1)
    def _():
        out_ref[:, 0:KVW] = wkv_ref[...]
        one = jnp.broadcast_to(g1_ref[...].astype(F32)[None], (128, SHARD)).T
        two = jnp.broadcast_to(g2_ref[...].astype(F32)[None], (128, SHARD)).T
        lane = lax.broadcasted_iota(jnp.int32, (SHARD, 128), 1)
        rest = wq_ref[:, HALFW:D].astype(F32)
        rest = jnp.concatenate([rest, jnp.zeros((SHARD, 64), F32)], axis=1)
        rest = jnp.where(lane == 64, one, jnp.where(lane == 65, two, rest))
        out_ref[:, KVW : KVW + 128] = rest.astype(BF16)
        out_ref[:, KVW + 128 : HALFW] = jnp.zeros((SHARD, HALFW - KVW - 128), BF16)


def chunk_kernel(ids_ref, gu_ref, *out_refs):
    fs = ids_ref[0]
    core = ids_ref[1]
    for s in range(FS):
        at = lax.rem(fs + s, FS) * FSL + core * FF
        out_refs[s][...] = gu_ref[:, pl.ds(pl.multiple_of(at, 128), FSL)]
    at = fs * FSL + (1 - core) * FF
    out_refs[FS][...] = gu_ref[:, pl.ds(pl.multiple_of(at, 128), FSL)]


def place_gate_up_kernel(ids_ref, *refs):
    out_ref = refs[2 * FS]
    for half in range(2):

        @pl.when(ids_ref[1] == half)
        def _(half=half):
            for s in range(FS):
                at = pl.multiple_of(lax.rem(ids_ref[0] + FS - s, FS) * SHARD, 16)
                for other in range(2):
                    cols = slice(FSL * (half ^ other), FSL * ((half ^ other) + 1))
                    out_ref[pl.ds(at, SHARD), cols] = refs[FS * other + s][...]


def qkv_kernel(ids_ref, xt_ref, *refs):
    mine = refs[0:FS]
    other = refs[FS : 2 * FS]
    cos_ref, sin_ref, out_ref, gains_ref, wa_ref, wb_ref, at_ref = refs[2 * FS :]
    fs = ids_ref[0]
    core = ids_ref[1]

    def fill(first, second):
        for s in range(FS):
            at = pl.multiple_of(lax.rem(fs + s, FS) * SHARD, 16)
            wa_ref[pl.ds(at, SHARD), :] = first[s][...]
            wb_ref[pl.ds(at, SHARD), :] = second[s][...]

    @pl.when(core == 0)
    def _():
        fill(mine, other)

    @pl.when(core == 1)
    def _():
        fill(other, mine)

    xt = xt_ref[...].astype(F32)
    gains = wb_ref[:, KVW : KVW + 128].astype(F32)
    gains_ref[...] = gains.T[64:72, :]
    r1 = lax.rsqrt(jnp.mean(xt * xt, axis=0, keepdims=True) + EPS)
    at = xt * r1 * gains[:, 64:65]
    at_ref[...] = at.astype(BF16)
    a = at.T.astype(BF16)
    lin_a = dot(a, wa_ref[...]).T
    lin_b = dot(a, wb_ref[...]).T
    cos = cos_ref[...]
    sin = sin_ref[...]

    def turned(rows):
        first = rows[0:HALF]
        second = rows[HALF:HEAD]
        return jnp.concatenate(
            [first * cos - second * sin, second * cos + first * sin], axis=0
        ).astype(BF16)

    for j in range(KV_HEADS):
        key = turned(lin_b[HEAD * j : HEAD * (j + 1)])
        value = lin_b[HEAD * (KV_HEADS + j) : HEAD * (KV_HEADS + j + 1)].astype(BF16)
        for g in range(GROUP):
            head = j * GROUP + g
            if head < HEADS - 1:
                rows = lin_a[HEAD * head : HEAD * (head + 1)]
            else:
                rows = lin_b[KVW : KVW + HEAD]
            out_ref[head, 0:HEAD, :] = turned(rows)
            out_ref[head, HEAD : 2 * HEAD, :] = key
            out_ref[head, 2 * HEAD : 3 * HEAD, :] = value
    out_ref[HEADS, :, :] = jnp.zeros((3 * HEAD, ROWS), BF16)


def pick_pair(load, first, second):
    left = load(first // 2).astype(F32)
    right = load(second // 2).astype(F32)
    left = pltpu.roll(left, (first % 2) * BLK, 1)
    right = pltpu.roll(right, (1 - second % 2) * BLK, 1)
    lane = lax.broadcasted_iota(jnp.int32, left.shape, 1)
    return jnp.where(lane < BLK, left, right)


def causal(size):
    key = lax.broadcasted_iota(jnp.int32, (size, size), 0)
    query = lax.broadcasted_iota(jnp.int32, (size, size), 1)
    return key <= query


def attend_kernel(
    order_ref, inv_ref, recv_ref, out_ref, qt_ref, kt_ref, k_ref, vt_ref, of_ref, lse_ref, s_ref
):
    for m in range(CTX):
        got = pick_pair(lambda i: recv_ref[i], inv_ref[2 * m], inv_ref[2 * m + 1])
        at = slice(2 * BLK * m, 2 * BLK * (m + 1))
        qt_ref[:, at] = (got[0:HEAD] * SCALE).astype(BF16)
        key = got[HEAD : 2 * HEAD]
        kt_ref[:, at] = key.astype(BF16)
        k_ref[at, :] = key.T.astype(BF16)
        vt_ref[:, at] = got[2 * HEAD : 3 * HEAD].astype(BF16)
    allowed = causal(TILE)
    for n in range(NT):
        span = slice(TILE * n, TILE * (n + 1))
        query = qt_ref[:, span]
        top = None
        for c in range(n + 1):
            rows = slice(TILE * c, TILE * (c + 1))
            s = dot(k_ref[rows, :], query)
            if c == n:
                s = jnp.where(allowed, s, -1e30)
            s_ref[rows, :] = s
            part = jnp.max(s, axis=0, keepdims=True)
            top = part if top is None else jnp.maximum(top, part)
        total = None
        for c in range(n + 1):
            rows = slice(TILE * c, TILE * (c + 1))
            e = jnp.exp(s_ref[rows, :] - top)
            s_ref[rows, :] = e
            part = jnp.sum(e, axis=0, keepdims=True)
            total = part if total is None else total + part
        recip = 1.0 / total
        lse_ref[n] = jnp.broadcast_to(top + jnp.log(total), (8, TILE))
        prob = (s_ref[0 : TILE * (n + 1), :] * recip).astype(BF16)
        o = dot(vt_ref[:, 0 : TILE * (n + 1)], prob)
        of_ref[2 * n] = o[:, 0 : 2 * BLK]
        of_ref[2 * n + 1] = o[:, 2 * BLK :]
    for i in range(CTX):
        got = pick_pair(lambda g: of_ref[g], order_ref[2 * i], order_ref[2 * i + 1])
        out_ref[i] = got.astype(BF16)


def attend_back_kernel(
    order_ref,
    inv_ref,
    recv_ref,
    qt_ref,
    q_ref,
    kt_ref,
    k_ref,
    v_ref,
    of_ref,
    lse_ref,
    cos_ref,
    sin_ref,
    out_ref,
    dot_ref,
    do_ref,
    delta_ref,
    dk_ref,
    dv_ref,
    st_ref,
):
    for m in range(CTX):
        got = pick_pair(lambda i: recv_ref[i], inv_ref[2 * m], inv_ref[2 * m + 1])
        at = slice(2 * BLK * m, 2 * BLK * (m + 1))
        dot_ref[:, at] = got.astype(BF16)
        do_ref[at, :] = got.T.astype(BF16)
        delta_ref[:, at] = jnp.broadcast_to(
            jnp.sum(got * of_ref[m], axis=0, keepdims=True), (8, 2 * BLK)
        )
    allowed = causal(TILE)
    for n in range(NT):
        span = slice(TILE * n, TILE * (n + 1))
        query = qt_ref[:, span]
        out_grad = dot_ref[:, span]
        lse = lse_ref[n][0:1, :]
        delta = delta_ref[0:1, span]
        dq = None
        for c in range(n + 1):
            rows = slice(TILE * c, TILE * (c + 1))
            prob = jnp.exp(dot(k_ref[rows, :], query) - lse)
            if c == n:
                prob = jnp.where(allowed, prob, 0.0)
            ds = (prob * (dot(v_ref[rows, :], out_grad) - delta)).astype(BF16)
            part = dot(kt_ref[:, rows], ds)
            dq = part if dq is None else dq + part
            dk = dot(ds, q_ref[span, :])
            dv = dot(prob.astype(BF16), do_ref[span, :])
            if c == n:
                dk_ref[rows, :] = dk
                dv_ref[rows, :] = dv
            else:
                dk_ref[rows, :] += dk
                dv_ref[rows, :] += dv
        st_ref[2 * n, 0:HEAD, :] = dq[:, 0 : 2 * BLK] * SCALE
        st_ref[2 * n + 1, 0:HEAD, :] = dq[:, 2 * BLK :] * SCALE
    for m in range(CTX):
        at = slice(2 * BLK * m, 2 * BLK * (m + 1))
        cos = cos_ref[:, at]
        sin = sin_ref[:, at]

        def turned(value):
            first = value[0:HALF]
            second = value[HALF:HEAD]
            return jnp.concatenate(
                [first * cos + second * sin, second * cos - first * sin], axis=0
            )

        st_ref[m, 0:HEAD, :] = turned(st_ref[m, 0:HEAD, :])
        st_ref[m, HEAD : 2 * HEAD, :] = turned(dk_ref[at, :].T)
        st_ref[m, 2 * HEAD : 3 * HEAD, :] = dv_ref[at, :].T
    for i in range(CTX):
        got = pick_pair(lambda g: st_ref[g], order_ref[2 * i], order_ref[2 * i + 1])
        out_ref[i] = got.astype(BF16)


def resid_kernel(ids_ref, ot_ref, w_ref, xt_ref, gains_ref, h_ref, b_ref, *refs):
    full_ref = refs[FS]
    flat = jnp.concatenate([ot_ref[h] for h in range(HEADS)], axis=0)
    full_ref[...] = flat
    for s in range(FS):
        at = pl.multiple_of(lax.rem(ids_ref[0] + s, FS) * SHARD, 16)
        refs[s][...] = full_ref[pl.ds(at, SHARD), :]
    mixed = flat.astype(F32).T.astype(BF16)
    h = xt_ref[...].astype(F32).T + dot(mixed, w_ref[...])
    h_ref[...] = h
    b_ref[...] = (h * inv_norm(h) * gains_ref[1:2, :]).astype(BF16)


def mlp_kernel(*refs):
    count = (len(refs) - 2) // 5
    b_refs = refs[0:count]
    g_refs = refs[count : 2 * count]
    gu_ref, down_ref = refs[2 * count : 2 * count + 2]
    outs = refs[2 * count + 2 :]
    for i in range(count):
        db_ref, mm_ref, dgu_ref = outs[3 * i : 3 * i + 3]
        gu = dot(b_refs[i][...], gu_ref[...])
        gate = gu[:, :FSL]
        up = gu[:, FSL:]
        sig = 1.0 / (1.0 + jnp.exp(-gate))
        act = gate * sig
        dm = dot(g_refs[i][...], down_ref[...], 0, 0)
        dgate = dm * up * sig * (1.0 + gate * (1.0 - sig))
        dgu = jnp.concatenate([dgate, dm * act], axis=1).astype(BF16)
        mm_ref[...] = (act * up).astype(BF16)
        dgu_ref[...] = dgu
        db_ref[...] = dot(dgu, gu_ref[...], 1, 1).astype(BF16)


def mlp_grad_kernel(ids_ref, *refs):
    b_refs = refs[0:FS]
    g_refs = refs[FS : 2 * FS]
    mm_refs = refs[2 * FS : 3 * FS]
    dgu_refs = refs[3 * FS : 4 * FS]
    down_ref = refs[4 * FS]
    y_refs = refs[4 * FS + 1 : 5 * FS + 1]
    keep_ref, give_ref, gu_ref, dd_ref = refs[5 * FS + 1 :]
    b = jnp.concatenate([r[...] for r in b_refs], axis=0)
    gt = jnp.concatenate([r[...] for r in g_refs], axis=1)
    mm = jnp.concatenate([r[...] for r in mm_refs], axis=0)
    dgu = jnp.concatenate([r[...] for r in dgu_refs], axis=0)
    gu_ref[...] = dot(b, dgu, 0, 0).astype(BF16)
    dd_ref[...] = dot(gt, mm).astype(BF16)

    def put(out_ref, half):
        out_ref[0:D, :] = gu_ref[:, FSL * half : FSL * (half + 1)]
        out_ref[D : D + D // 2, :] = dd_ref[D // 2 * half : D // 2 * (half + 1), :]

    for core in range(2):

        @pl.when(ids_ref[1] == core)
        def _(core=core):
            put(keep_ref, core)
            put(give_ref, 1 - core)

    for s in range(FS):
        y_refs[s][...] = dot(mm_refs[s][...], down_ref[...], 1, 1).astype(BF16)


def result_kernel(h_ref, y0, y1, y2, y3, out_ref):
    total = h_ref[...]
    for piece in (y0, y1, y2, y3):
        total += piece[...].astype(F32)
    out_ref[...] = total.T.astype(BF16)


def pack_kernel(ids_ref, keep_ref, got_ref, *refs):
    sum_ref = refs[4]
    for at in range(0, HALF_ROWS, 240):
        rows = slice(at, at + 240)
        sum_ref[rows, :] = keep_ref[rows, :].astype(F32) + got_ref[rows, :].astype(F32)
    sum_ref[HALF_ROWS:, :] = jnp.zeros((16, FSL), F32)

    def put(out_ref, first):
        for r in range(first, first + 4):
            for k in range(FS):
                at = SHARD * k + 15 * r
                out_ref[r - first, 16 * k : 16 * (k + 1), :] = sum_ref[at : at + 16, :].astype(BF16)
            at = D + 30 * r
            out_ref[r - first, 64:96, :] = sum_ref[at : at + 32, :].astype(BF16)

    for x in range(4):

        @pl.when(ids_ref[2] == x)
        def _(x=x):
            for step in range(4):
                owner = (x + step) % 4
                put(refs[step], 4 * (owner % 2 * 2 + owner // 2))


def sum_x_kernel(ids_ref, *refs):
    total = refs[0][...].astype(F32)
    for step in range(1, 4):
        total += refs[step][...].astype(F32)
    refs[8][...] = total.astype(BF16)
    for step in range(4):
        refs[4 + step][...] = refs[8][lax.rem(ids_ref[3] + step, 4)]


def sum_z_kernel(ids_ref, *refs):
    total = refs[0][...].astype(F32)
    for step in range(1, 4):
        total += refs[step][...].astype(F32)
    sum_ref = refs[9]
    sum_ref[...] = total.astype(BF16)
    for s in range(FS):
        at = pl.multiple_of(lax.rem(ids_ref[0] + s, FS) * 16, 16)
        refs[4 + s][...] = sum_ref[pl.ds(at, 16), :]
    refs[8][...] = sum_ref[64:96, :]


def copies_kernel(*refs):
    out_ref = refs[-1]
    own = jnp.concatenate([r[...] for r in refs[:-1]], axis=0)
    for i in range(CTX):
        out_ref[i] = own


def add_kernel(own_ref, got_ref, out_ref):
    total = (own_ref[...].astype(F32) + got_ref[...].astype(F32)).astype(BF16)
    for i in range(CTX // 2):
        out_ref[i] = total


def mid_kernel(*refs):
    db_refs = refs[0:FS]
    h_ref, gt_ref, gains_ref, w_ref = refs[FS : FS + 4]
    o_refs = refs[FS + 4 : 2 * FS + 4]
    dh_ref, do_ref = refs[2 * FS + 4 : 2 * FS + 6]
    out_refs = refs[2 * FS + 6 :]
    db = db_refs[0][...].astype(F32)
    for ref in db_refs[1:]:
        db += ref[...].astype(F32)
    h = h_ref[...]
    r2 = inv_norm(h)
    scaled = gains_ref[1:2, :] * db
    dh = (
        gt_ref[...].astype(F32).T
        + r2 * scaled
        - h * (r2 * r2 * r2) * jnp.mean(scaled * h, axis=-1, keepdims=True)
    )
    dh_ref[...] = dh
    e = dh.astype(BF16)
    back = dot(w_ref[...], e, 1, 1).astype(BF16)
    for head in range(HEADS):
        do_ref[head] = back[HEAD * head : HEAD * (head + 1)]
    do_ref[HEADS] = jnp.zeros((HEAD, ROWS), BF16)
    for s in range(FS):
        out_refs[s][:, 0:D] = e
        o = jnp.concatenate([o_refs[s][...].astype(F32), jnp.zeros((80, ROWS), F32)], axis=0)
        out_refs[s][:, D:EO] = o.T.astype(BF16)


def head_grad_kernel(ids_ref, at_ref, d_ref, *refs):
    full_ref = refs[FS]
    total = None
    for i in range(0, CTX, 2):
        left = jnp.concatenate([at_ref[i], at_ref[i + 1]], axis=1)
        right = jnp.concatenate([d_ref[i], d_ref[i + 1]], axis=1)
        part = dot(left, right, 1, 1)
        total = part if total is None else total + part
    full_ref[...] = total.astype(BF16)
    for s in range(FS):
        at = pl.multiple_of(lax.rem(ids_ref[0] + s, FS) * SHARD, 16)
        rows = full_ref[pl.ds(at, SHARD), :]
        refs[s][0:SHARD, :] = rows[:, 0:128]
        value = rows[:, 128:192].astype(F32)
        value = jnp.concatenate([value[0 : SHARD // 2], value[SHARD // 2 :]], axis=1)
        value = jnp.concatenate([value, jnp.zeros((8, 128), F32)], axis=0)
        refs[s][SHARD:HEADROWS, :] = value.astype(BF16)


def out_grad_kernel(*refs):
    part_ref, out_ref = refs[FS:]
    total = None
    for s in range(FS):
        message = refs[s]
        part = dot(message[:, D:EO], message[:, 0:D], 0, 0)[0:SHARD]
        total = part if total is None else total + part
    pad = jnp.zeros((SHARD, 64), F32)
    total = jnp.concatenate([total, pad], axis=1).astype(BF16)
    out_ref[:, 0 : 3 * HEAD, :] = part_ref[...]
    for i in range(HEADS):
        for j in range(8):
            at = 3 * HEAD + 16 * j
            out_ref[i, at : at + 16, :] = total[16 * i : 16 * (i + 1), 128 * j : 128 * (j + 1)]
    out_ref[HEADS, 3 * HEAD :, :] = jnp.zeros((128, 128), BF16)


def head_sum_kernel(p0, p1, p2, p3, recv_ref, out_ref):
    total = p0[...].astype(F32)
    for piece in (p1, p2, p3):
        total += piece[...].astype(F32)
    out_ref[0:HEADROWS, :] = total.astype(BF16)
    total = recv_ref[0, 3 * HEAD :, :].astype(F32)
    for i in range(1, CTX):
        total += recv_ref[i, 3 * HEAD :, :].astype(F32)
    out_ref[HEADROWS:, :] = total.astype(BF16)


def last_kernel(recv_ref, wa_ref, wb_ref, xt_ref, dh_ref, gains_ref, ig_ref, msg_ref):
    for head in range(HEADS):
        msg_ref[HEAD * head : HEAD * (head + 1), :] = recv_ref[head, 0:HEAD, :]
    for part in range(2):
        for j in range(KV_HEADS):
            total = None
            for g in range(GROUP):
                piece = recv_ref[j * GROUP + g, HEAD * (part + 1) : HEAD * (part + 2), :]
                piece = piece.astype(F32)
                total = piece if total is None else total + piece
            base = D + HEAD * (KV_HEADS * part + j)
            msg_ref[base : base + HEAD, :] = total.astype(BF16)
    da = dot(wa_ref[...], msg_ref[0:HALFW, :])
    da += dot(wb_ref[:, 0:KVW], msg_ref[D:QKV, :])
    da += dot(wb_ref[:, KVW : KVW + HEAD], msg_ref[HALFW:D, :])
    x = xt_ref[...].astype(F32)
    r1 = lax.rsqrt(jnp.mean(x * x, axis=0, keepdims=True) + EPS)
    scaled = wb_ref[:, KVW : KVW + 128].astype(F32)[:, 64:65] * da
    ig_ref[...] = (
        dh_ref[...].T
        + r1 * scaled
        - x * (r1 * r1 * r1) * jnp.mean(scaled * x, axis=0, keepdims=True)
    )


def unpack_kernel(
    ids_ref, mine_ref, other_ref, wq_ref, wkv_ref, gain_in, q_ref, kv_ref, o_ref, gain_ref
):
    for core in range(2):

        @pl.when(ids_ref[1] == core)
        def _(core=core):
            blocks = []
            for head in range(HEADS):
                src = mine_ref if head % 2 == core else other_ref
                blocks.append(src[head // 2].astype(F32))
            parts = [b[0:SHARD] for b in blocks]
            tails = [b[SHARD : SHARD + SHARD // 2] for b in blocks]
            zero = jnp.zeros((SHARD, HEAD), F32)
            query = [p[:, 0:HEAD] for p in parts]
            key = []
            value = []
            for j in range(KV_HEADS):
                group = parts[GROUP * j] + parts[GROUP * j + 1] + parts[GROUP * j + 2]
                key.append(group[:, HEAD:])
                group = tails[GROUP * j] + tails[GROUP * j + 1] + tails[GROUP * j + 2]
                value.append(jnp.concatenate([group[:, 0:HEAD], group[:, HEAD:]], axis=0))
            q = jnp.concatenate(query + [zero], axis=1)[:, 0:D]
            kv = jnp.concatenate(key + value, axis=1)
            q_ref[...] = q
            kv_ref[...] = kv
            total = jnp.sum(q * wq_ref[...].astype(F32), axis=1, keepdims=True)
            total += jnp.sum(kv * wkv_ref[...].astype(F32), axis=1, keepdims=True)
            total = jnp.broadcast_to(total, (SHARD, 128)).T[0:8]
            gain_ref[...] = total[0] / gain_in[...].astype(F32)
            for i, b in enumerate(blocks):
                cols = [b[HEADROWS + 16 * j : HEADROWS + 16 * (j + 1)] for j in range(8)]
                o_ref[16 * i : 16 * (i + 1), :] = jnp.concatenate(cols, axis=1)[:, 0:D]


def widen_kernel(
    ids_ref, mine_ref, other_ref, gu_in, gain_in, gu_out, down_out, gain_ref
):
    for core in range(2):

        @pl.when(ids_ref[1] == core)
        def _(core=core):
            halves = (mine_ref, other_ref) if core == 0 else (other_ref, mine_ref)
            total = None
            down = []
            for half, src in enumerate(halves):
                for s in range(FS):
                    at = lax.rem(ids_ref[0] + FS - s, FS) * FSL + FF * half
                    cols = pl.ds(pl.multiple_of(at, 128), FSL)
                    rows = [
                        src[r, 16 * s : 16 * (s + 1), :].astype(F32)[0:15] for r in range(CTX)
                    ]
                    rows = jnp.concatenate(rows, axis=0)
                    gu_out[:, cols] = rows
                    part = jnp.sum(rows * gu_in[:, cols].astype(F32), axis=1, keepdims=True)
                    total = part if total is None else total + part
                down += [src[r, 64:96, :].astype(F32)[0:30] for r in range(CTX)]
            down_out[...] = jnp.concatenate(down, axis=0)
            total = jnp.broadcast_to(total, (SHARD, 128)).T[0:8]
            gain_ref[...] = total[0] / gain_in[...].astype(F32)


def swap_core(value):
    return lax.ppermute(value, "ctx", [(i, i ^ 1) for i in range(CTX)])


def shift(value, step):
    return lax.ppermute(value, "fsdp", [((i + step) % FS, i) for i in range(FS)])


def same_core(value):
    groups = [[2 * i + core for i in range(CTX)] for core in range(2)]
    return lax.all_to_all(value, ("seq", "ctx"), 0, 0, axis_index_groups=groups)


def shift_x(value, step):
    def at(x, z, core):
        return (x % 2) * CTX + (x // 2) * 8 + z * 2 + core

    pairs = [
        (at((x + step) % 4, z, core), at(x, z, core))
        for x in range(4)
        for z in range(4)
        for core in range(2)
    ]
    return lax.ppermute(value, ("seq", "ctx"), pairs)


def shift_z(value, step):
    def at(high, z, core):
        return high * 8 + z * 2 + core

    pairs = [
        (at(high, (z + step) % 4, core), at(high, z, core))
        for high in range(2)
        for z in range(4)
        for core in range(2)
    ]
    return lax.ppermute(value, "ctx", pairs)


def same_core_row(value):
    groups = [[2 * i + core for i in range(CTX // 2)] for core in range(2)]
    return lax.all_to_all(value, "ctx", 0, 0, axis_index_groups=groups)


def swap_seq(value):
    return lax.ppermute(value, "seq", [(0, 1), (1, 0)])


def gather_by(move, value):
    return [value] + [move(value, s) for s in range(1, 4)]


def scatter_by(move, pieces):
    return [pieces[0]] + [move(pieces[s], -s) for s in range(1, 4)]


def gather_rolled(value):
    return gather_by(shift, value)


def scatter_rolled(pieces):
    return scatter_by(shift, pieces)


def together(*values):
    return lax.optimization_barrier(values)


def shards(tokens, gain_attn, w_q, w_kv, w_o, gain_mlp, w_gate_up, w_down, block_order, cotangent):
    x_t = tokens[0].T
    g_t = cotangent[0].T
    down_t = w_down.T
    order = block_order[0]
    place = lax.axis_index("ctx")
    x_place = place // 8 * 2 + lax.axis_index("seq")
    ids = jnp.stack([lax.axis_index("fsdp"), place % 2, x_place, place // 2 % 4])
    ids = ids.astype(jnp.int32)

    slots = jnp.arange(2 * CTX, dtype=jnp.int32)
    inverse = jnp.sum(jnp.where(order[None, :] == slots[:, None], slots[None, :], 0), axis=1)
    mine = lax.dynamic_slice_in_dim(order, place * 2, 2)
    places = (mine[:, None] * BLK + jnp.arange(BLK, dtype=jnp.int32)[None, :]).reshape(ROWS)
    freq = THETA ** (-(jnp.arange(HALF, dtype=F32) * 2.0 / HEAD))
    angle = freq[:, None] * places.astype(F32)[None, :]
    angle_all = freq[:, None] * jnp.arange(L, dtype=F32)[None, :]

    (message,) = call(
        message_kernel,
        [shape(SHARD, HALFW)],
        [ids, w_q, w_kv, gain_attn, gain_mlp],
        smem=1,
    )
    w_mine = gather_rolled(message)
    *chunks, gu_local = call(
        chunk_kernel, [shape(SHARD, FSL)] * (FS + 1), [ids, w_gate_up], smem=1
    )
    w_mine, chunks, w_o, g_t = together(w_mine, chunks, w_o, g_t)
    w_other = [swap_core(message)] + [swap_core(piece) for piece in w_mine[1:]]
    w_out = lax.all_gather(w_o, "fsdp", axis=0, tiled=True)
    gu_pieces = scatter_rolled(chunks)
    g_all = gather_rolled(g_t)

    packed, gains, w_a, w_b, a_t = call(
        qkv_kernel,
        [
            shape(CTX, 3 * HEAD, ROWS),
            shape(8, D, dtype=F32),
            shape(D, HALFW),
            shape(D, HALFW),
            shape(D, ROWS),
        ],
        [ids, x_t] + w_mine + w_other + [jnp.cos(angle), jnp.sin(angle)],
        smem=1,
        flops=2 * ROWS * D * QKV,
    )
    a_all = lax.all_gather(a_t, "ctx", axis=0)
    received = lax.all_to_all(packed, "ctx", 0, 0)
    cos_all, sin_all = jnp.cos(angle_all), jnp.sin(angle_all)
    received, cos_all, sin_all = together(received, cos_all, sin_all)
    o_part, q_t, k_t, k_n, v_t, o_f, lse = call(
        attend_kernel,
        [
            shape(CTX, HEAD, ROWS),
            shape(HEAD, L),
            shape(HEAD, L),
            shape(L, HEAD),
            shape(HEAD, L),
            shape(CTX, HEAD, ROWS, dtype=F32),
            shape(NT, 8, TILE, dtype=F32),
        ],
        [order, inverse, received],
        smem=2,
        scratch=[pltpu.VMEM((L, TILE), F32)],
        flops=2 * L * L * HEAD,
    )
    o_all = lax.all_to_all(o_part, "ctx", 0, 0)
    q_n, v_n = q_t.T, v_t.T
    o_all, w_out, q_n, v_n, gu_pieces = together(o_all, w_out, q_n, v_n, gu_pieces)
    h, b, *o_pieces = call(
        resid_kernel,
        [shape(ROWS, D, dtype=F32), shape(ROWS, D)] + [shape(SHARD, ROWS)] * FS,
        [ids, o_all, w_out, x_t, gains],
        smem=1,
        scratch=[pltpu.VMEM((D, ROWS), BF16)],
        flops=2 * ROWS * D * D,
    )
    b, g_all = together(b, g_all)
    gu_other = [gu_local] + [swap_core(piece) for piece in gu_pieces[1:]]
    (w_gu,) = call(
        place_gate_up_kernel, [shape(D, 2 * FSL)], [ids] + gu_pieces + gu_other, smem=1
    )
    b_all = gather_rolled(b)
    db, mm, dgu = [None] * FS, [None] * FS, [None] * FS
    before = None
    for partners in ((0,), (1, 3), (2,)):
        if before is not None:
            b_all[partners[0]], before = together(b_all[partners[0]], before)
        outs = call(
            mlp_kernel,
            [shape(ROWS, D), shape(ROWS, FSL), shape(ROWS, 2 * FSL)] * len(partners),
            [b_all[s] for s in partners] + [g_all[s] for s in partners] + [w_gu, down_t],
            flops=10 * len(partners) * ROWS * D * FSL,
            limit=MLP_BYTES,
        )
        for i, s in enumerate(partners):
            db[s], mm[s], dgu[s] = outs[3 * i : 3 * i + 3]
        before = mm[partners[0]]
    db = scatter_rolled(db)
    *y_parts, keep, give = call(
        mlp_grad_kernel,
        [shape(ROWS, D)] * FS + [shape(HALF_ROWS, FSL)] * 2,
        [ids] + b_all + g_all + mm + dgu + [down_t],
        smem=1,
        scratch=[pltpu.VMEM((D, 2 * FSL), BF16), pltpu.VMEM((D, FSL), BF16)],
        flops=8 * FS * ROWS * D * FSL,
        limit=MLP_BYTES,
    )
    db, keep = together(db, keep)
    dh, do_part, *eo_parts = call(
        mid_kernel,
        [shape(ROWS, D, dtype=F32), shape(CTX, HEAD, ROWS)] + [shape(ROWS, EO)] * FS,
        db + [h, g_t, gains, w_out] + o_pieces,
        flops=2 * ROWS * D * D,
    )
    do_all = lax.all_to_all(do_part, "ctx", 0, 0)
    eo_parts, give = together(eo_parts, give)
    got = swap_core(give)
    x_pieces = call(
        pack_kernel,
        [shape(4, 96, FSL)] * 4,
        [ids, keep, got],
        smem=1,
        scratch=[pltpu.VMEM((HALF_ROWS + 16, FSL), F32)],
    )
    eo_all = scatter_rolled(eo_parts)
    do_all, x_pieces, eo_all[1], eo_all[3] = together(do_all, x_pieces, eo_all[1], eo_all[3])
    x_pieces = scatter_by(shift_x, x_pieces)
    (dqkv_part,) = call(
        attend_back_kernel,
        [shape(CTX, 3 * HEAD, ROWS)],
        [order, inverse, do_all, q_t, q_n, k_t, k_n, v_n, o_f, lse, cos_all, sin_all],
        smem=2,
        scratch=[
            pltpu.VMEM((HEAD, L), BF16),
            pltpu.VMEM((L, HEAD), BF16),
            pltpu.VMEM((8, L), F32),
            pltpu.VMEM((L, HEAD), F32),
            pltpu.VMEM((L, HEAD), F32),
            pltpu.VMEM((CTX, 3 * HEAD, ROWS), F32),
        ],
        flops=5 * L * L * HEAD,
    )
    head_pieces = call(
        head_grad_kernel,
        [shape(HEADROWS, 128)] * FS,
        [ids, a_all, dqkv_part],
        smem=1,
        scratch=[pltpu.VMEM((D, 3 * HEAD), BF16)],
        flops=2 * L * D * 3 * HEAD,
    )
    dqkv_part, head_pieces, eo_all, x_pieces = together(dqkv_part, head_pieces, eo_all, x_pieces)
    (message,) = call(
        out_grad_kernel,
        [shape(CTX, 3 * HEAD + 128, ROWS)],
        eo_all + [dqkv_part],
        flops=2 * FS * ROWS * SHARD * D,
    )
    dqkv = lax.all_to_all(message, "ctx", 0, 0)
    z_pieces = call(
        sum_x_kernel,
        [shape(96, FSL)] * 4,
        [ids] + x_pieces,
        smem=1,
        scratch=[pltpu.VMEM((4, 96, FSL), BF16)],
    )
    *pieces, down_sum = call(
        sum_z_kernel,
        [shape(16, FSL)] * FS + [shape(32, FSL)],
        [ids] + scatter_by(shift_z, z_pieces),
        smem=1,
        scratch=[pltpu.VMEM((96, FSL), BF16)],
    )
    (own,) = call(
        copies_kernel, [shape(CTX, 96, FSL)], scatter_rolled(pieces) + [down_sum]
    )
    dqkv, own, head_pieces = together(dqkv, own, head_pieces)
    head_pieces = scatter_rolled(head_pieces)
    mine_all = same_core(own)
    (head_sum,) = call(head_sum_kernel, [shape(HEADROWS + 128, 128)], head_pieces + [dqkv])
    _, y_parts = together(head_sum, y_parts)
    y = scatter_rolled(y_parts)
    (head_parts,) = call(
        add_kernel, [shape(CTX // 2, HEADROWS + 128, 128)], [head_sum, swap_seq(head_sum)]
    )
    (input_grad,) = call(
        last_kernel,
        [shape(D, ROWS, dtype=F32)],
        [dqkv, w_a, w_b, x_t, dh, gains],
        scratch=[pltpu.VMEM((QKV, ROWS), BF16)],
        flops=2 * ROWS * D * QKV,
    )
    (result,) = call(result_kernel, [shape(D, ROWS)], [h] + y)
    mine_all, head_parts, result = together(mine_all, head_parts, result)
    head_mine = same_core_row(head_parts)
    gu_out, down_out, gain_two = call(
        widen_kernel,
        [
            shape(SHARD, 2 * FF, dtype=F32),
            shape(D, FSL, dtype=F32),
            shape(SHARD, dtype=F32),
        ],
        [ids, mine_all, swap_core(mine_all), w_gate_up, gain_mlp],
        smem=1,
    )
    head_mine, gu_out, down_out, gain_two, input_grad = together(
        head_mine, gu_out, down_out, gain_two, input_grad
    )
    q_out, kv_out, o_out, gain_one = call(
        unpack_kernel,
        [
            shape(SHARD, D, dtype=F32),
            shape(SHARD, KVW, dtype=F32),
            shape(SHARD, D, dtype=F32),
            shape(SHARD, dtype=F32),
        ],
        [ids, head_mine, swap_core(head_mine), w_q, w_kv, gain_attn],
        smem=1,
    )
    return (
        result.T[None],
        input_grad.T[None],
        gain_one,
        q_out,
        kv_out,
        o_out,
        gain_two,
        gu_out,
        down_out.T,
    )


def solution(mesh):
    tokens = P(("seq", "fsdp"), "ctx", None)
    return jax.shard_map(
        shards,
        mesh=mesh,
        in_specs=(
            tokens,
            P("fsdp"),
            P("fsdp", None),
            P("fsdp", None),
            P("fsdp", None),
            P("fsdp"),
            P("fsdp", None),
            P("fsdp", None),
            P(("seq", "fsdp"), None),
            tokens,
        ),
        out_specs=(
            tokens,
            tokens,
            P("fsdp"),
            P("fsdp", None),
            P("fsdp", None),
            P("fsdp", None),
            P("fsdp"),
            P("fsdp", None),
            P("fsdp", None),
        ),
        check_vma=False,
    )
```

```python
import jax
import jax.numpy as jnp
from jax import lax
from jax.experimental import pallas as pl
from jax.experimental.pallas import tpu as pltpu
from jax.sharding import PartitionSpec as P

D = 960
HEADS = 15
KV_HEADS = 5
GROUP = 3
HEAD = 64
HALF = 32
FF = 2560
BLK = 64
L = 2048
CTX = 16
FS = 4
ROWS = 128
QKV = 1600
HEADROWS = 368
EO = 1280
HALFW = 896
KVW = 640
HALF_ROWS = D + D // 2
SHARD = D // FS
FSL = FF // FS
TILE = 256
NT = L // TILE
EPS = 1e-05
THETA = 100000.0
SCALE = HEAD**-0.5
F32 = jnp.float32
BF16 = jnp.bfloat16
VMEM_BYTES = 56 * 1024 * 1024
MLP_BYTES = 24 * 1024 * 1024


def call(kernel, outs, args, smem=0, scratch=(), flops=0, limit=VMEM_BYTES):
    specs = [pl.BlockSpec(memory_space=pltpu.SMEM)] * smem
    specs += [pl.BlockSpec(memory_space=pltpu.VMEM)] * (len(args) - smem)
    moved = sum(a.size * a.dtype.itemsize for a in list(args) + list(outs))
    return pl.pallas_call(
        kernel,
        out_shape=outs,
        in_specs=specs,
        out_specs=[pl.BlockSpec(memory_space=pltpu.VMEM)] * len(outs),
        scratch_shapes=list(scratch),
        cost_estimate=pl.CostEstimate(flops=flops, bytes_accessed=moved, transcendentals=0),
        compiler_params=pltpu.CompilerParams(vmem_limit_bytes=limit),
    )(*args)


def shape(*dims, dtype=BF16):
    return jax.ShapeDtypeStruct(dims, dtype)


def dot(left, right, a=1, b=0):
    return lax.dot_general(left, right, (((a,), (b,)), ((), ())), preferred_element_type=F32)


def inv_norm(rows):
    return lax.rsqrt(jnp.mean(rows * rows, axis=-1, keepdims=True) + EPS)


def message_kernel(ids_ref, wq_ref, wkv_ref, g1_ref, g2_ref, out_ref):
    core = ids_ref[1]

    @pl.when(core == 0)
    def _():
        out_ref[...] = wq_ref[:, 0:HALFW]

    @pl.when(core == 1)
    def _():
        out_ref[:, 0:KVW] = wkv_ref[...]
        one = jnp.broadcast_to(g1_ref[...].astype(F32)[None], (128, SHARD)).T
        two = jnp.broadcast_to(g2_ref[...].astype(F32)[None], (128, SHARD)).T
        lane = lax.broadcasted_iota(jnp.int32, (SHARD, 128), 1)
        rest = wq_ref[:, HALFW:D].astype(F32)
        rest = jnp.concatenate([rest, jnp.zeros((SHARD, 64), F32)], axis=1)
        rest = jnp.where(lane == 64, one, jnp.where(lane == 65, two, rest))
        out_ref[:, KVW : KVW + 128] = rest.astype(BF16)
        out_ref[:, KVW + 128 : HALFW] = jnp.zeros((SHARD, HALFW - KVW - 128), BF16)


def chunk_kernel(ids_ref, gu_ref, *out_refs):
    fs = ids_ref[0]
    core = ids_ref[1]
    for s in range(FS):
        at = lax.rem(fs + s, FS) * FSL + core * FF
        out_refs[s][...] = gu_ref[:, pl.ds(pl.multiple_of(at, 128), FSL)]
    at = fs * FSL + (1 - core) * FF
    out_refs[FS][...] = gu_ref[:, pl.ds(pl.multiple_of(at, 128), FSL)]


def place_gate_up_kernel(ids_ref, *refs):
    out_ref = refs[2 * FS]
    for half in range(2):

        @pl.when(ids_ref[1] == half)
        def _(half=half):
            for s in range(FS):
                at = pl.multiple_of(lax.rem(ids_ref[0] + FS - s, FS) * SHARD, 16)
                for other in range(2):
                    cols = slice(FSL * (half ^ other), FSL * ((half ^ other) + 1))
                    out_ref[pl.ds(at, SHARD), cols] = refs[FS * other + s][...]


def qkv_kernel(ids_ref, xt_ref, *refs):
    mine = refs[0:FS]
    other = refs[FS : 2 * FS]
    cos_ref, sin_ref, out_ref, gains_ref, wa_ref, wb_ref, at_ref = refs[2 * FS :]
    fs = ids_ref[0]
    core = ids_ref[1]

    def fill(first, second):
        for s in range(FS):
            at = pl.multiple_of(lax.rem(fs + s, FS) * SHARD, 16)
            wa_ref[pl.ds(at, SHARD), :] = first[s][...]
            wb_ref[pl.ds(at, SHARD), :] = second[s][...]

    @pl.when(core == 0)
    def _():
        fill(mine, other)

    @pl.when(core == 1)
    def _():
        fill(other, mine)

    xt = xt_ref[...].astype(F32)
    gains = wb_ref[:, KVW : KVW + 128].astype(F32)
    gains_ref[...] = gains.T[64:72, :]
    r1 = lax.rsqrt(jnp.mean(xt * xt, axis=0, keepdims=True) + EPS)
    at = xt * r1 * gains[:, 64:65]
    at_ref[...] = at.astype(BF16)
    a = at.T.astype(BF16)
    lin_a = dot(a, wa_ref[...]).T
    lin_b = dot(a, wb_ref[...]).T
    cos = cos_ref[...]
    sin = sin_ref[...]

    def turned(rows):
        first = rows[0:HALF]
        second = rows[HALF:HEAD]
        return jnp.concatenate(
            [first * cos - second * sin, second * cos + first * sin], axis=0
        ).astype(BF16)

    for j in range(KV_HEADS):
        key = turned(lin_b[HEAD * j : HEAD * (j + 1)])
        value = lin_b[HEAD * (KV_HEADS + j) : HEAD * (KV_HEADS + j + 1)].astype(BF16)
        for g in range(GROUP):
            head = j * GROUP + g
            if head < HEADS - 1:
                rows = lin_a[HEAD * head : HEAD * (head + 1)]
            else:
                rows = lin_b[KVW : KVW + HEAD]
            out_ref[head, 0:HEAD, :] = turned(rows)
            out_ref[head, HEAD : 2 * HEAD, :] = key
            out_ref[head, 2 * HEAD : 3 * HEAD, :] = value
    out_ref[HEADS, :, :] = jnp.zeros((3 * HEAD, ROWS), BF16)


def pick_pair(load, first, second):
    left = load(first // 2).astype(F32)
    right = load(second // 2).astype(F32)
    left = pltpu.roll(left, (first % 2) * BLK, 1)
    right = pltpu.roll(right, (1 - second % 2) * BLK, 1)
    lane = lax.broadcasted_iota(jnp.int32, left.shape, 1)
    return jnp.where(lane < BLK, left, right)


def causal(size):
    key = lax.broadcasted_iota(jnp.int32, (size, size), 0)
    query = lax.broadcasted_iota(jnp.int32, (size, size), 1)
    return key <= query


def attend_kernel(
    order_ref, inv_ref, recv_ref, out_ref, qt_ref, kt_ref, k_ref, vt_ref, of_ref, lse_ref, s_ref
):
    for m in range(CTX):
        got = pick_pair(lambda i: recv_ref[i], inv_ref[2 * m], inv_ref[2 * m + 1])
        at = slice(2 * BLK * m, 2 * BLK * (m + 1))
        qt_ref[:, at] = (got[0:HEAD] * SCALE).astype(BF16)
        key = got[HEAD : 2 * HEAD]
        kt_ref[:, at] = key.astype(BF16)
        k_ref[at, :] = key.T.astype(BF16)
        vt_ref[:, at] = got[2 * HEAD : 3 * HEAD].astype(BF16)
    allowed = causal(TILE)
    for n in range(NT):
        span = slice(TILE * n, TILE * (n + 1))
        query = qt_ref[:, span]
        top = None
        for c in range(n + 1):
            rows = slice(TILE * c, TILE * (c + 1))
            s = dot(k_ref[rows, :], query)
            if c == n:
                s = jnp.where(allowed, s, -1e30)
            s_ref[rows, :] = s
            part = jnp.max(s, axis=0, keepdims=True)
            top = part if top is None else jnp.maximum(top, part)
        total = None
        for c in range(n + 1):
            rows = slice(TILE * c, TILE * (c + 1))
            e = jnp.exp(s_ref[rows, :] - top)
            s_ref[rows, :] = e
            part = jnp.sum(e, axis=0, keepdims=True)
            total = part if total is None else total + part
        recip = 1.0 / total
        lse_ref[n] = jnp.broadcast_to(top + jnp.log(total), (8, TILE))
        prob = (s_ref[0 : TILE * (n + 1), :] * recip).astype(BF16)
        o = dot(vt_ref[:, 0 : TILE * (n + 1)], prob)
        of_ref[2 * n] = o[:, 0 : 2 * BLK]
        of_ref[2 * n + 1] = o[:, 2 * BLK :]
    for i in range(CTX):
        got = pick_pair(lambda g: of_ref[g], order_ref[2 * i], order_ref[2 * i + 1])
        out_ref[i] = got.astype(BF16)


def attend_back_kernel(
    order_ref,
    inv_ref,
    recv_ref,
    qt_ref,
    q_ref,
    kt_ref,
    k_ref,
    v_ref,
    of_ref,
    lse_ref,
    cos_ref,
    sin_ref,
    out_ref,
    dot_ref,
    do_ref,
    delta_ref,
    dk_ref,
    dv_ref,
    st_ref,
):
    for m in range(CTX):
        got = pick_pair(lambda i: recv_ref[i], inv_ref[2 * m], inv_ref[2 * m + 1])
        at = slice(2 * BLK * m, 2 * BLK * (m + 1))
        dot_ref[:, at] = got.astype(BF16)
        do_ref[at, :] = got.T.astype(BF16)
        delta_ref[:, at] = jnp.broadcast_to(
            jnp.sum(got * of_ref[m], axis=0, keepdims=True), (8, 2 * BLK)
        )
    allowed = causal(TILE)
    for n in range(NT):
        span = slice(TILE * n, TILE * (n + 1))
        query = qt_ref[:, span]
        out_grad = dot_ref[:, span]
        lse = lse_ref[n][0:1, :]
        delta = delta_ref[0:1, span]
        dq = None
        for c in range(n + 1):
            rows = slice(TILE * c, TILE * (c + 1))
            prob = jnp.exp(dot(k_ref[rows, :], query) - lse)
            if c == n:
                prob = jnp.where(allowed, prob, 0.0)
            ds = (prob * (dot(v_ref[rows, :], out_grad) - delta)).astype(BF16)
            part = dot(kt_ref[:, rows], ds)
            dq = part if dq is None else dq + part
            dk = dot(ds, q_ref[span, :])
            dv = dot(prob.astype(BF16), do_ref[span, :])
            if c == n:
                dk_ref[rows, :] = dk
                dv_ref[rows, :] = dv
            else:
                dk_ref[rows, :] += dk
                dv_ref[rows, :] += dv
        st_ref[2 * n, 0:HEAD, :] = dq[:, 0 : 2 * BLK] * SCALE
        st_ref[2 * n + 1, 0:HEAD, :] = dq[:, 2 * BLK :] * SCALE
    for m in range(CTX):
        at = slice(2 * BLK * m, 2 * BLK * (m + 1))
        cos = cos_ref[:, at]
        sin = sin_ref[:, at]

        def turned(value):
            first = value[0:HALF]
            second = value[HALF:HEAD]
            return jnp.concatenate(
                [first * cos + second * sin, second * cos - first * sin], axis=0
            )

        st_ref[m, 0:HEAD, :] = turned(st_ref[m, 0:HEAD, :])
        st_ref[m, HEAD : 2 * HEAD, :] = turned(dk_ref[at, :].T)
        st_ref[m, 2 * HEAD : 3 * HEAD, :] = dv_ref[at, :].T
    for i in range(CTX):
        got = pick_pair(lambda g: st_ref[g], order_ref[2 * i], order_ref[2 * i + 1])
        out_ref[i] = got.astype(BF16)


def resid_kernel(ids_ref, ot_ref, w_ref, xt_ref, gains_ref, h_ref, b_ref, *refs):
    full_ref = refs[FS]
    flat = jnp.concatenate([ot_ref[h] for h in range(HEADS)], axis=0)
    full_ref[...] = flat
    for s in range(FS):
        at = pl.multiple_of(lax.rem(ids_ref[0] + s, FS) * SHARD, 16)
        refs[s][...] = full_ref[pl.ds(at, SHARD), :]
    mixed = flat.astype(F32).T.astype(BF16)
    h = xt_ref[...].astype(F32).T + dot(mixed, w_ref[...])
    h_ref[...] = h
    b_ref[...] = (h * inv_norm(h) * gains_ref[1:2, :]).astype(BF16)


def mlp_kernel(*refs):
    count = (len(refs) - 2) // 5
    b_refs = refs[0:count]
    g_refs = refs[count : 2 * count]
    gu_ref, down_ref = refs[2 * count : 2 * count + 2]
    outs = refs[2 * count + 2 :]
    for i in range(count):
        db_ref, mm_ref, dgu_ref = outs[3 * i : 3 * i + 3]
        gu = dot(b_refs[i][...], gu_ref[...])
        gate = gu[:, :FSL]
        up = gu[:, FSL:]
        sig = 1.0 / (1.0 + jnp.exp(-gate))
        act = gate * sig
        dm = dot(g_refs[i][...], down_ref[...], 0, 0)
        dgate = dm * up * sig * (1.0 + gate * (1.0 - sig))
        dgu = jnp.concatenate([dgate, dm * act], axis=1).astype(BF16)
        mm_ref[...] = (act * up).astype(BF16)
        dgu_ref[...] = dgu
        db_ref[...] = dot(dgu, gu_ref[...], 1, 1).astype(BF16)


def mlp_grad_kernel(ids_ref, *refs):
    b_refs = refs[0:FS]
    g_refs = refs[FS : 2 * FS]
    mm_refs = refs[2 * FS : 3 * FS]
    dgu_refs = refs[3 * FS : 4 * FS]
    down_ref = refs[4 * FS]
    y_refs = refs[4 * FS + 1 : 5 * FS + 1]
    keep_ref, give_ref, gu_ref, dd_ref = refs[5 * FS + 1 :]
    b = jnp.concatenate([r[...] for r in b_refs], axis=0)
    gt = jnp.concatenate([r[...] for r in g_refs], axis=1)
    mm = jnp.concatenate([r[...] for r in mm_refs], axis=0)
    dgu = jnp.concatenate([r[...] for r in dgu_refs], axis=0)
    gu_ref[...] = dot(b, dgu, 0, 0).astype(BF16)
    dd_ref[...] = dot(gt, mm).astype(BF16)

    def put(out_ref, half):
        out_ref[0:D, :] = gu_ref[:, FSL * half : FSL * (half + 1)]
        out_ref[D : D + D // 2, :] = dd_ref[D // 2 * half : D // 2 * (half + 1), :]

    for core in range(2):

        @pl.when(ids_ref[1] == core)
        def _(core=core):
            put(keep_ref, core)
            put(give_ref, 1 - core)

    for s in range(FS):
        y_refs[s][...] = dot(mm_refs[s][...], down_ref[...], 1, 1).astype(BF16)


def result_kernel(h_ref, y0, y1, y2, y3, out_ref):
    total = h_ref[...]
    for piece in (y0, y1, y2, y3):
        total += piece[...].astype(F32)
    out_ref[...] = total.T.astype(BF16)


def pack_kernel(ids_ref, keep_ref, got_ref, *refs):
    sum_ref = refs[4]
    for at in range(0, HALF_ROWS, 240):
        rows = slice(at, at + 240)
        sum_ref[rows, :] = keep_ref[rows, :].astype(F32) + got_ref[rows, :].astype(F32)
    sum_ref[HALF_ROWS:, :] = jnp.zeros((16, FSL), F32)

    def put(out_ref, first):
        for r in range(first, first + 4):
            for k in range(FS):
                at = SHARD * k + 15 * r
                out_ref[r - first, 16 * k : 16 * (k + 1), :] = sum_ref[at : at + 16, :].astype(BF16)
            at = D + 30 * r
            out_ref[r - first, 64:96, :] = sum_ref[at : at + 32, :].astype(BF16)

    for x in range(4):

        @pl.when(ids_ref[2] == x)
        def _(x=x):
            for step in range(4):
                owner = (x + step) % 4
                put(refs[step], 4 * (owner % 2 * 2 + owner // 2))


def sum_x_kernel(ids_ref, *refs):
    total = refs[0][...].astype(F32)
    for step in range(1, 4):
        total += refs[step][...].astype(F32)
    refs[8][...] = total.astype(BF16)
    for step in range(4):
        refs[4 + step][...] = refs[8][lax.rem(ids_ref[3] + step, 4)]


def sum_z_kernel(ids_ref, *refs):
    total = refs[0][...].astype(F32)
    for step in range(1, 4):
        total += refs[step][...].astype(F32)
    sum_ref = refs[9]
    sum_ref[...] = total.astype(BF16)
    for s in range(FS):
        at = pl.multiple_of(lax.rem(ids_ref[0] + s, FS) * 16, 16)
        refs[4 + s][...] = sum_ref[pl.ds(at, 16), :]
    refs[8][...] = sum_ref[64:96, :]


def copies_kernel(*refs):
    out_ref = refs[-1]
    own = jnp.concatenate([r[...] for r in refs[:-1]], axis=0)
    for i in range(CTX):
        out_ref[i] = own


def add_kernel(own_ref, got_ref, out_ref):
    total = (own_ref[...].astype(F32) + got_ref[...].astype(F32)).astype(BF16)
    for i in range(CTX // 2):
        out_ref[i] = total


def mid_kernel(*refs):
    db_refs = refs[0:FS]
    h_ref, gt_ref, gains_ref, w_ref = refs[FS : FS + 4]
    o_refs = refs[FS + 4 : 2 * FS + 4]
    dh_ref, do_ref = refs[2 * FS + 4 : 2 * FS + 6]
    out_refs = refs[2 * FS + 6 :]
    db = db_refs[0][...].astype(F32)
    for ref in db_refs[1:]:
        db += ref[...].astype(F32)
    h = h_ref[...]
    r2 = inv_norm(h)
    scaled = gains_ref[1:2, :] * db
    dh = (
        gt_ref[...].astype(F32).T
        + r2 * scaled
        - h * (r2 * r2 * r2) * jnp.mean(scaled * h, axis=-1, keepdims=True)
    )
    dh_ref[...] = dh
    e = dh.astype(BF16)
    back = dot(w_ref[...], e, 1, 1).astype(BF16)
    for head in range(HEADS):
        do_ref[head] = back[HEAD * head : HEAD * (head + 1)]
    do_ref[HEADS] = jnp.zeros((HEAD, ROWS), BF16)
    for s in range(FS):
        out_refs[s][:, 0:D] = e
        o = jnp.concatenate([o_refs[s][...].astype(F32), jnp.zeros((80, ROWS), F32)], axis=0)
        out_refs[s][:, D:EO] = o.T.astype(BF16)


def head_grad_kernel(ids_ref, at_ref, d_ref, *refs):
    full_ref = refs[FS]
    total = None
    for i in range(0, CTX, 2):
        left = jnp.concatenate([at_ref[i], at_ref[i + 1]], axis=1)
        right = jnp.concatenate([d_ref[i], d_ref[i + 1]], axis=1)
        part = dot(left, right, 1, 1)
        total = part if total is None else total + part
    full_ref[...] = total.astype(BF16)
    for s in range(FS):
        at = pl.multiple_of(lax.rem(ids_ref[0] + s, FS) * SHARD, 16)
        rows = full_ref[pl.ds(at, SHARD), :]
        refs[s][0:SHARD, :] = rows[:, 0:128]
        value = rows[:, 128:192].astype(F32)
        value = jnp.concatenate([value[0 : SHARD // 2], value[SHARD // 2 :]], axis=1)
        value = jnp.concatenate([value, jnp.zeros((8, 128), F32)], axis=0)
        refs[s][SHARD:HEADROWS, :] = value.astype(BF16)


def out_grad_kernel(*refs):
    part_ref, out_ref = refs[FS:]
    total = None
    for s in range(FS):
        message = refs[s]
        part = dot(message[:, D:EO], message[:, 0:D], 0, 0)[0:SHARD]
        total = part if total is None else total + part
    pad = jnp.zeros((SHARD, 64), F32)
    total = jnp.concatenate([total, pad], axis=1).astype(BF16)
    out_ref[:, 0 : 3 * HEAD, :] = part_ref[...]
    for i in range(HEADS):
        for j in range(8):
            at = 3 * HEAD + 16 * j
            out_ref[i, at : at + 16, :] = total[16 * i : 16 * (i + 1), 128 * j : 128 * (j + 1)]
    out_ref[HEADS, 3 * HEAD :, :] = jnp.zeros((128, 128), BF16)


def head_sum_kernel(p0, p1, p2, p3, recv_ref, out_ref):
    total = p0[...].astype(F32)
    for piece in (p1, p2, p3):
        total += piece[...].astype(F32)
    out_ref[0:HEADROWS, :] = total.astype(BF16)
    total = recv_ref[0, 3 * HEAD :, :].astype(F32)
    for i in range(1, CTX):
        total += recv_ref[i, 3 * HEAD :, :].astype(F32)
    out_ref[HEADROWS:, :] = total.astype(BF16)


def last_kernel(recv_ref, wa_ref, wb_ref, xt_ref, dh_ref, gains_ref, ig_ref, msg_ref):
    for head in range(HEADS):
        msg_ref[HEAD * head : HEAD * (head + 1), :] = recv_ref[head, 0:HEAD, :]
    for part in range(2):
        for j in range(KV_HEADS):
            total = None
            for g in range(GROUP):
                piece = recv_ref[j * GROUP + g, HEAD * (part + 1) : HEAD * (part + 2), :]
                piece = piece.astype(F32)
                total = piece if total is None else total + piece
            base = D + HEAD * (KV_HEADS * part + j)
            msg_ref[base : base + HEAD, :] = total.astype(BF16)
    da = dot(wa_ref[...], msg_ref[0:HALFW, :])
    da += dot(wb_ref[:, 0:KVW], msg_ref[D:QKV, :])
    da += dot(wb_ref[:, KVW : KVW + HEAD], msg_ref[HALFW:D, :])
    x = xt_ref[...].astype(F32)
    r1 = lax.rsqrt(jnp.mean(x * x, axis=0, keepdims=True) + EPS)
    scaled = wb_ref[:, KVW : KVW + 128].astype(F32)[:, 64:65] * da
    ig_ref[...] = (
        dh_ref[...].T
        + r1 * scaled
        - x * (r1 * r1 * r1) * jnp.mean(scaled * x, axis=0, keepdims=True)
    )


def unpack_kernel(
    ids_ref, mine_ref, other_ref, wq_ref, wkv_ref, gain_in, q_ref, kv_ref, o_ref, gain_ref
):
    for core in range(2):

        @pl.when(ids_ref[1] == core)
        def _(core=core):
            blocks = []
            for head in range(HEADS):
                src = mine_ref if head % 2 == core else other_ref
                blocks.append(src[head // 2].astype(F32))
            parts = [b[0:SHARD] for b in blocks]
            tails = [b[SHARD : SHARD + SHARD // 2] for b in blocks]
            zero = jnp.zeros((SHARD, HEAD), F32)
            query = [p[:, 0:HEAD] for p in parts]
            key = []
            value = []
            for j in range(KV_HEADS):
                group = parts[GROUP * j] + parts[GROUP * j + 1] + parts[GROUP * j + 2]
                key.append(group[:, HEAD:])
                group = tails[GROUP * j] + tails[GROUP * j + 1] + tails[GROUP * j + 2]
                value.append(jnp.concatenate([group[:, 0:HEAD], group[:, HEAD:]], axis=0))
            q = jnp.concatenate(query + [zero], axis=1)[:, 0:D]
            kv = jnp.concatenate(key + value, axis=1)
            q_ref[...] = q
            kv_ref[...] = kv
            total = jnp.sum(q * wq_ref[...].astype(F32), axis=1, keepdims=True)
            total += jnp.sum(kv * wkv_ref[...].astype(F32), axis=1, keepdims=True)
            total = jnp.broadcast_to(total, (SHARD, 128)).T[0:8]
            gain_ref[...] = total[0] / gain_in[...].astype(F32)
            for i, b in enumerate(blocks):
                cols = [b[HEADROWS + 16 * j : HEADROWS + 16 * (j + 1)] for j in range(8)]
                o_ref[16 * i : 16 * (i + 1), :] = jnp.concatenate(cols, axis=1)[:, 0:D]


def widen_kernel(
    ids_ref, mine_ref, other_ref, gu_in, gain_in, gu_out, down_out, gain_ref
):
    for core in range(2):

        @pl.when(ids_ref[1] == core)
        def _(core=core):
            halves = (mine_ref, other_ref) if core == 0 else (other_ref, mine_ref)
            total = None
            down = []
            for half, src in enumerate(halves):
                for s in range(FS):
                    at = lax.rem(ids_ref[0] + FS - s, FS) * FSL + FF * half
                    cols = pl.ds(pl.multiple_of(at, 128), FSL)
                    rows = [
                        src[r, 16 * s : 16 * (s + 1), :].astype(F32)[0:15] for r in range(CTX)
                    ]
                    rows = jnp.concatenate(rows, axis=0)
                    gu_out[:, cols] = rows
                    part = jnp.sum(rows * gu_in[:, cols].astype(F32), axis=1, keepdims=True)
                    total = part if total is None else total + part
                down += [src[r, 64:96, :].astype(F32)[0:30] for r in range(CTX)]
            down_out[...] = jnp.concatenate(down, axis=0)
            total = jnp.broadcast_to(total, (SHARD, 128)).T[0:8]
            gain_ref[...] = total[0] / gain_in[...].astype(F32)


def swap_core(value):
    return lax.ppermute(value, "ctx", [(i, i ^ 1) for i in range(CTX)])


def shift(value, step):
    return lax.ppermute(value, "fsdp", [((i + step) % FS, i) for i in range(FS)])


def same_core(value):
    groups = [[2 * i + core for i in range(CTX)] for core in range(2)]
    return lax.all_to_all(value, ("seq", "ctx"), 0, 0, axis_index_groups=groups)


def shift_x(value, step):
    def at(x, z, core):
        return (x % 2) * CTX + (x // 2) * 8 + z * 2 + core

    pairs = [
        (at((x + step) % 4, z, core), at(x, z, core))
        for x in range(4)
        for z in range(4)
        for core in range(2)
    ]
    return lax.ppermute(value, ("seq", "ctx"), pairs)


def shift_z(value, step):
    def at(high, z, core):
        return high * 8 + z * 2 + core

    pairs = [
        (at(high, (z + step) % 4, core), at(high, z, core))
        for high in range(2)
        for z in range(4)
        for core in range(2)
    ]
    return lax.ppermute(value, "ctx", pairs)


def same_core_row(value):
    groups = [[2 * i + core for i in range(CTX // 2)] for core in range(2)]
    return lax.all_to_all(value, "ctx", 0, 0, axis_index_groups=groups)


def swap_seq(value):
    return lax.ppermute(value, "seq", [(0, 1), (1, 0)])


def gather_by(move, value):
    return [value] + [move(value, s) for s in range(1, 4)]


def scatter_by(move, pieces):
    return [pieces[0]] + [move(pieces[s], -s) for s in range(1, 4)]


def gather_rolled(value):
    return gather_by(shift, value)


def scatter_rolled(pieces):
    return scatter_by(shift, pieces)


def together(*values):
    return lax.optimization_barrier(values)


def shards(tokens, gain_attn, w_q, w_kv, w_o, gain_mlp, w_gate_up, w_down, block_order, cotangent):
    x_t = tokens[0].T
    g_t = cotangent[0].T
    down_t = w_down.T
    order = block_order[0]
    place = lax.axis_index("ctx")
    x_place = place // 8 * 2 + lax.axis_index("seq")
    ids = jnp.stack([lax.axis_index("fsdp"), place % 2, x_place, place // 2 % 4])
    ids = ids.astype(jnp.int32)

    slots = jnp.arange(2 * CTX, dtype=jnp.int32)
    inverse = jnp.sum(jnp.where(order[None, :] == slots[:, None], slots[None, :], 0), axis=1)
    mine = lax.dynamic_slice_in_dim(order, place * 2, 2)
    places = (mine[:, None] * BLK + jnp.arange(BLK, dtype=jnp.int32)[None, :]).reshape(ROWS)
    freq = THETA ** (-(jnp.arange(HALF, dtype=F32) * 2.0 / HEAD))
    angle = freq[:, None] * places.astype(F32)[None, :]
    angle_all = freq[:, None] * jnp.arange(L, dtype=F32)[None, :]

    (message,) = call(
        message_kernel,
        [shape(SHARD, HALFW)],
        [ids, w_q, w_kv, gain_attn, gain_mlp],
        smem=1,
    )
    w_mine = gather_rolled(message)
    *chunks, gu_local = call(
        chunk_kernel, [shape(SHARD, FSL)] * (FS + 1), [ids, w_gate_up], smem=1
    )
    w_mine, chunks, w_o, g_t = together(w_mine, chunks, w_o, g_t)
    w_other = [swap_core(message)] + [swap_core(piece) for piece in w_mine[1:]]
    w_out = lax.all_gather(w_o, "fsdp", axis=0, tiled=True)
    gu_pieces = scatter_rolled(chunks)
    g_all = gather_rolled(g_t)

    packed, gains, w_a, w_b, a_t = call(
        qkv_kernel,
        [
            shape(CTX, 3 * HEAD, ROWS),
            shape(8, D, dtype=F32),
            shape(D, HALFW),
            shape(D, HALFW),
            shape(D, ROWS),
        ],
        [ids, x_t] + w_mine + w_other + [jnp.cos(angle), jnp.sin(angle)],
        smem=1,
        flops=2 * ROWS * D * QKV,
    )
    a_all = lax.all_gather(a_t, "ctx", axis=0)
    received = lax.all_to_all(packed, "ctx", 0, 0)
    cos_all, sin_all = jnp.cos(angle_all), jnp.sin(angle_all)
    received, cos_all, sin_all = together(received, cos_all, sin_all)
    o_part, q_t, k_t, k_n, v_t, o_f, lse = call(
        attend_kernel,
        [
            shape(CTX, HEAD, ROWS),
            shape(HEAD, L),
            shape(HEAD, L),
            shape(L, HEAD),
            shape(HEAD, L),
            shape(CTX, HEAD, ROWS, dtype=F32),
            shape(NT, 8, TILE, dtype=F32),
        ],
        [order, inverse, received],
        smem=2,
        scratch=[pltpu.VMEM((L, TILE), F32)],
        flops=2 * L * L * HEAD,
    )
    o_all = lax.all_to_all(o_part, "ctx", 0, 0)
    q_n, v_n = q_t.T, v_t.T
    o_all, w_out, q_n, v_n, gu_pieces = together(o_all, w_out, q_n, v_n, gu_pieces)
    h, b, *o_pieces = call(
        resid_kernel,
        [shape(ROWS, D, dtype=F32), shape(ROWS, D)] + [shape(SHARD, ROWS)] * FS,
        [ids, o_all, w_out, x_t, gains],
        smem=1,
        scratch=[pltpu.VMEM((D, ROWS), BF16)],
        flops=2 * ROWS * D * D,
    )
    b, g_all = together(b, g_all)
    gu_other = [gu_local] + [swap_core(piece) for piece in gu_pieces[1:]]
    (w_gu,) = call(
        place_gate_up_kernel, [shape(D, 2 * FSL)], [ids] + gu_pieces + gu_other, smem=1
    )
    b_all = gather_rolled(b)
    db, mm, dgu = [None] * FS, [None] * FS, [None] * FS
    before = None
    for partners in ((0,), (1, 3), (2,)):
        if before is not None:
            b_all[partners[0]], before = together(b_all[partners[0]], before)
        outs = call(
            mlp_kernel,
            [shape(ROWS, D), shape(ROWS, FSL), shape(ROWS, 2 * FSL)] * len(partners),
            [b_all[s] for s in partners] + [g_all[s] for s in partners] + [w_gu, down_t],
            flops=10 * len(partners) * ROWS * D * FSL,
            limit=MLP_BYTES,
        )
        for i, s in enumerate(partners):
            db[s], mm[s], dgu[s] = outs[3 * i : 3 * i + 3]
        before = mm[partners[0]]
    db = scatter_rolled(db)
    *y_parts, keep, give = call(
        mlp_grad_kernel,
        [shape(ROWS, D)] * FS + [shape(HALF_ROWS, FSL)] * 2,
        [ids] + b_all + g_all + mm + dgu + [down_t],
        smem=1,
        scratch=[pltpu.VMEM((D, 2 * FSL), BF16), pltpu.VMEM((D, FSL), BF16)],
        flops=8 * FS * ROWS * D * FSL,
        limit=MLP_BYTES,
    )
    db, keep = together(db, keep)
    dh, do_part, *eo_parts = call(
        mid_kernel,
        [shape(ROWS, D, dtype=F32), shape(CTX, HEAD, ROWS)] + [shape(ROWS, EO)] * FS,
        db + [h, g_t, gains, w_out] + o_pieces,
        flops=2 * ROWS * D * D,
    )
    do_all = lax.all_to_all(do_part, "ctx", 0, 0)
    eo_parts, give = together(eo_parts, give)
    got = swap_core(give)
    x_pieces = call(
        pack_kernel,
        [shape(4, 96, FSL)] * 4,
        [ids, keep, got],
        smem=1,
        scratch=[pltpu.VMEM((HALF_ROWS + 16, FSL), F32)],
    )
    eo_all = scatter_rolled(eo_parts)
    do_all, x_pieces, eo_all[1], eo_all[3] = together(do_all, x_pieces, eo_all[1], eo_all[3])
    x_pieces = scatter_by(shift_x, x_pieces)
    (dqkv_part,) = call(
        attend_back_kernel,
        [shape(CTX, 3 * HEAD, ROWS)],
        [order, inverse, do_all, q_t, q_n, k_t, k_n, v_n, o_f, lse, cos_all, sin_all],
        smem=2,
        scratch=[
            pltpu.VMEM((HEAD, L), BF16),
            pltpu.VMEM((L, HEAD), BF16),
            pltpu.VMEM((8, L), F32),
            pltpu.VMEM((L, HEAD), F32),
            pltpu.VMEM((L, HEAD), F32),
            pltpu.VMEM((CTX, 3 * HEAD, ROWS), F32),
        ],
        flops=5 * L * L * HEAD,
    )
    head_pieces = call(
        head_grad_kernel,
        [shape(HEADROWS, 128)] * FS,
        [ids, a_all, dqkv_part],
        smem=1,
        scratch=[pltpu.VMEM((D, 3 * HEAD), BF16)],
        flops=2 * L * D * 3 * HEAD,
    )
    dqkv_part, head_pieces, eo_all, x_pieces = together(dqkv_part, head_pieces, eo_all, x_pieces)
    (message,) = call(
        out_grad_kernel,
        [shape(CTX, 3 * HEAD + 128, ROWS)],
        eo_all + [dqkv_part],
        flops=2 * FS * ROWS * SHARD * D,
    )
    dqkv = lax.all_to_all(message, "ctx", 0, 0)
    z_pieces = call(
        sum_x_kernel,
        [shape(96, FSL)] * 4,
        [ids] + x_pieces,
        smem=1,
        scratch=[pltpu.VMEM((4, 96, FSL), BF16)],
    )
    *pieces, down_sum = call(
        sum_z_kernel,
        [shape(16, FSL)] * FS + [shape(32, FSL)],
        [ids] + scatter_by(shift_z, z_pieces),
        smem=1,
        scratch=[pltpu.VMEM((96, FSL), BF16)],
    )
    (own,) = call(
        copies_kernel, [shape(CTX, 96, FSL)], scatter_rolled(pieces) + [down_sum]
    )
    head_pieces = scatter_rolled(head_pieces)
    dqkv, own, head_pieces, y_parts = together(dqkv, own, head_pieces, y_parts)
    y = scatter_rolled(y_parts)
    mine_all = same_core(own)
    (head_sum,) = call(head_sum_kernel, [shape(HEADROWS + 128, 128)], head_pieces + [dqkv])
    (head_parts,) = call(
        add_kernel, [shape(CTX // 2, HEADROWS + 128, 128)], [head_sum, swap_seq(head_sum)]
    )
    (input_grad,) = call(
        last_kernel,
        [shape(D, ROWS, dtype=F32)],
        [dqkv, w_a, w_b, x_t, dh, gains],
        scratch=[pltpu.VMEM((QKV, ROWS), BF16)],
        flops=2 * ROWS * D * QKV,
    )
    (result,) = call(result_kernel, [shape(D, ROWS)], [h] + y)
    mine_all, head_parts, input_grad = together(mine_all, head_parts, input_grad)
    head_mine = same_core_row(head_parts)
    gu_out, down_out, gain_two = call(
        widen_kernel,
        [
            shape(SHARD, 2 * FF, dtype=F32),
            shape(D, FSL, dtype=F32),
            shape(SHARD, dtype=F32),
        ],
        [ids, mine_all, swap_core(mine_all), w_gate_up, gain_mlp],
        smem=1,
    )
    head_mine, gu_out, down_out, gain_two, result = together(
        head_mine, gu_out, down_out, gain_two, result
    )
    q_out, kv_out, o_out, gain_one = call(
        unpack_kernel,
        [
            shape(SHARD, D, dtype=F32),
            shape(SHARD, KVW, dtype=F32),
            shape(SHARD, D, dtype=F32),
            shape(SHARD, dtype=F32),
        ],
        [ids, head_mine, swap_core(head_mine), w_q, w_kv, gain_attn],
        smem=1,
    )
    return (
        result.T[None],
        input_grad.T[None],
        gain_one,
        q_out,
        kv_out,
        o_out,
        gain_two,
        gu_out,
        down_out.T,
    )


def solution(mesh):
    tokens = P(("seq", "fsdp"), "ctx", None)
    return jax.shard_map(
        shards,
        mesh=mesh,
        in_specs=(
            tokens,
            P("fsdp"),
            P("fsdp", None),
            P("fsdp", None),
            P("fsdp", None),
            P("fsdp"),
            P("fsdp", None),
            P("fsdp", None),
            P(("seq", "fsdp"), None),
            tokens,
        ),
        out_specs=(
            tokens,
            tokens,
            P("fsdp"),
            P("fsdp", None),
            P("fsdp", None),
            P("fsdp", None),
            P("fsdp"),
            P("fsdp", None),
            P("fsdp", None),
        ),
        check_vma=False,
    )
```
